32 devices in a mesh: grp: 8 (over z, x), bf: 4 (over y, core).
Axes of the slice: x: 2, y: 2, z: 4, core: 2. Of those that a mesh axis runs over, the one named last changes fastest.
Arguments:
- field: float32 [16, 65536], P(None, ('grp', 'bf')), may hold values from -6 to 6
- leaf_inverse: bfloat16 [128, 512, 512], P(('grp', 'bf')), may hold values from -0.25 to 0.25
- col_factor: bfloat16 [2, 64, 65536], P(None, None, ('grp', 'bf')), may hold values from -0.125 to 0.125
- row_factor: bfloat16 [2, 64, 65536], P(None, None, ('grp', 'bf')), may hold values from -0.75 to 0.75
- mixing: bfloat16 [32, 2, 4, 2, 64, 64], P(('grp', 'bf')), may hold values from -0.5 to 0.5
- row_owner: int32 [2, 8], replicated, may hold values from 0 to 7, as said below
- rank_perm: int32 [2, 64], replicated, may hold values from 0 to 63, each once within a row
Outputs:
- applied: float32 [16, 65536], P(None, ('grp', 'bf'))
The draws below stay inside these ranges and needn't reach their ends.
Inputs may be any that keep to these rules, and one draw needn't show every extreme that they name: row_owner[l, g] = (g + s_l) mod 8; one level has s_l = 4 and the other s_l = 7, which level takes which drawn from the seed.
All inputs are finite; a program needn't handle non-finite values.
Results may differ from the reference program's by a relative error of at most 0.004.
Values sent between devices are 32-bit elements; how exact they have to be, the bound alone decides.
No kernel may reach another device: no remote copies, remote signals or barrier semaphores. Data moves between devices by JAX's collectives and lax.ppermute only.
A program may use at most 64 MiB of HBM per device.

```python
import jax
import jax.numpy as jnp
from jax import lax

RHS = 16
K = 64
LEAF = 512
ROWS = 2048
MIXES = 4
LEVELS = 2
UNKNOWNS = 65536
N_GRP = 8
N_BF = 4


def draw_row_owner(key, part):
    key = jax.random.fold_in(key, 7)
    chosen = jax.random.randint(key, (), 0, LEVELS)
    levels = jnp.arange(LEVELS, dtype=jnp.int32)[:, None]
    shifts = jnp.where(levels == chosen, N_GRP // 2, N_GRP - 1).astype(jnp.int32)
    segments = jnp.arange(N_GRP, dtype=jnp.int32)[None, :]
    return ((segments + shifts) % N_GRP).astype(jnp.int32)


def level_of(own_key, dims, shards, least, largest):
    def one(position, blocks):
        steps = jax.random.uniform(jax.random.fold_in(jax.random.fold_in(own_key, 6), position), (blocks,), jnp.float32, least / len(shards), largest / len(shards))
        return jnp.repeat(jnp.exp(steps), dims[position] // blocks).reshape((-1,) + (1,) * (len(dims) - position - 1))

    gain = one(*shards[0])
    for cut in shards[1:]:
        gain = gain * one(*cut)
    return gain


def bell_draw(rng, shape, deviation, bound, split=(), kind=jnp.bfloat16):
    array = deviation * jax.random.normal(rng, shape, jnp.float32)
    if split:
        array = array * level_of(rng, shape, split, -0.22, 0.18)
    return jnp.clip(array, -bound, bound).astype(kind)


def setup_inputs(seed: int = 0) -> dict:
    splits = jax.random.split(jax.random.key(seed), 8)
    field = bell_draw(splits[0], (RHS, UNKNOWNS), 1.0, 6.0, ((1, 32),), jnp.float32)
    leaf_inverse = bell_draw(splits[1], (UNKNOWNS // LEAF, LEAF, LEAF), LEAF ** -0.5, 0.25, ((0, 32),))
    col_factor = bell_draw(splits[2], (LEVELS, K, UNKNOWNS), ROWS ** -0.5, 0.125, ((2, 32),))
    row_factor = bell_draw(splits[3], (LEVELS, K, UNKNOWNS), K ** -0.5, 0.75, ((2, 32),))
    mixing = bell_draw(splits[4], (N_GRP * N_BF, LEVELS, MIXES, 2, K, K), (2 * K) ** -0.5, 0.5, ((0, 32),))
    row_owner = draw_row_owner(jax.random.fold_in(splits[7], 71), 0)
    rank_perm = jax.vmap(lambda own: jax.random.permutation(own, K))(jax.random.split(splits[6], LEVELS)).reshape((LEVELS, K)).astype(jnp.int32)
    return dict(field=field, leaf_inverse=leaf_inverse, col_factor=col_factor, row_factor=row_factor, mixing=mixing, row_owner=row_owner, rank_perm=rank_perm)


def reference(field, leaf_inverse, col_factor, row_factor, mixing, row_owner, rank_perm):
    devs = N_GRP * N_BF
    hi = lax.Precision.HIGHEST
    xb = field.astype(jnp.bfloat16)
    xdev = xb.reshape(RHS, devs, ROWS).transpose(1, 0, 2)
    leaves = leaf_inverse.reshape(devs, ROWS // LEAF, LEAF, LEAF)

    def diag_one(pair):
        vec, blocks = pair
        part = vec.reshape(RHS, ROWS // LEAF, LEAF).astype(jnp.float32)
        res = jnp.einsum('rnl,nlm->rnm', part, blocks.astype(jnp.float32), precision=hi)
        return res.reshape(RHS, ROWS)

    total = lax.map(diag_one, (xdev, leaves)).reshape(N_GRP, N_BF, RHS, ROWS)
    bits = N_BF.bit_length() - 1
    index = jnp.arange(devs, dtype=jnp.int32)
    targets = jnp.arange(N_GRP, dtype=jnp.int32)
    owners_eq = (row_owner[:, None, :] == targets[None, :, None]).astype(jnp.float32)
    for level in range(LEVELS):
        vfac = col_factor[level].reshape(K, devs, ROWS).transpose(1, 0, 2)
        state = jnp.einsum('drn,dkn->drk', xdev.astype(jnp.float32), vfac.astype(jnp.float32), precision=hi)
        state = jnp.take(state, rank_perm[level], axis=2)
        for section in range(MIXES):
            bit = section % bits
            partner = jnp.bitwise_xor(index % N_BF, 1 << bit) + (index // N_BF) * N_BF
            other = state[partner]
            own_mat = mixing[:, level, section, 0].astype(jnp.float32)
            oth_mat = mixing[:, level, section, 1].astype(jnp.float32)
            state = jnp.einsum('drk,dkj->drj', state, own_mat, precision=hi) + jnp.einsum('drk,dkj->drj', other, oth_mat, precision=hi)
        rank = state.astype(jnp.bfloat16)
        rank = lax.optimization_barrier(rank).astype(jnp.float32)
        ufac = row_factor[level].reshape(K, devs, ROWS).transpose(1, 0, 2)
        out = jnp.einsum('drk,dkn->drn', rank, ufac.astype(jnp.float32), precision=hi)
        out = out.reshape(N_GRP, N_BF, RHS, ROWS)
        total = total + jnp.einsum('tg,gbrn->tbrn', owners_eq[level], out, precision=hi)
    return total.transpose(2, 0, 1, 3).reshape(RHS, N_GRP * N_BF * ROWS)
```

```python
import jax
import jax.numpy as jnp
from jax import lax
from jax.sharding import PartitionSpec as P

HI = lax.Precision.HIGHEST


def partner(value, axis, distance):
    mask = 2**distance
    pairs = [(source, source ^ mask) for source in range(lax.axis_size(axis))]
    return lax.ppermute(value, axis, pairs)


def shifted(value, axis, distance):
    size = lax.axis_size(axis)
    return lax.ppermute(value, axis, [(source, (source + distance) % size) for source in range(size)])


def block_diagonal(mats):
    levels, k, _ = mats.shape
    eye = jnp.eye(levels, dtype=mats.dtype)
    return (mats[:, :, None, :] * eye[:, None, :, None]).reshape(levels * k, levels * k)


def shards(field, leaf_inverse, col_factor, row_factor, mixing, row_owner, rank_perm):
    vectors, rows = field.shape
    order = leaf_inverse.shape[1]
    levels, rank_size, _ = col_factor.shape
    sections = mixing.shape[2]
    bits = lax.axis_size("bf").bit_length() - 1
    groups = lax.axis_size("grp")
    width = levels * rank_size

    xb = field.astype(jnp.bfloat16)
    state = lax.dot_general(
        xb, col_factor.reshape(width, rows), (((1,), (1,)), ((), ())), preferred_element_type=jnp.float32
    )
    picks = (jnp.arange(rank_size, dtype=jnp.int32)[None, :, None] == rank_perm[:, None, :]).astype(jnp.float32)
    mats = mixing[0].astype(jnp.float32)
    weights = []
    for section in range(sections):
        own, oth = mats[:, section, 0], mats[:, section, 1]
        if section == 0:
            own = jnp.einsum("lij,ljk->lik", picks, own)
            oth = jnp.einsum("lij,ljk->lik", picks, oth)
        weights.append((block_diagonal(own), block_diagonal(oth)))
    for section in range(sections):
        other = partner(state, "bf", section % bits)
        own, oth = weights[section]
        state = jnp.dot(state, own, precision=HI) + jnp.dot(other, oth, precision=HI)
    rank = state.astype(jnp.bfloat16)
    first_is_half = row_owner[0, 0] == groups // 2
    lane_level = lax.broadcasted_iota(jnp.int32, (vectors, width), 1) // rank_size
    half = (lane_level == 0) == first_is_half
    expand = row_factor.reshape(width, rows)
    zero = jnp.zeros_like(rank)
    out_half = jnp.dot(jnp.where(half, rank, zero), expand, preferred_element_type=jnp.float32)
    out_below = jnp.dot(jnp.where(half, zero, rank), expand, preferred_element_type=jnp.float32)
    out_half = shifted(out_half, "grp", groups // 2)
    out_below = shifted(out_below, "grp", groups - 1)
    diag = jnp.einsum(
        "rnl,nlm->rnm",
        xb.reshape(vectors, rows // order, order),
        leaf_inverse,
        preferred_element_type=jnp.float32,
    ).reshape(vectors, rows)
    return diag + out_half + out_below


def solution(mesh):
    in_specs = (
        P(None, ("grp", "bf")),
        P(("grp", "bf"), None, None),
        P(None, None, ("grp", "bf")),
        P(None, None, ("grp", "bf")),
        P(("grp", "bf"), None, None, None, None, None),
        P(),
        P(),
    )
    out_specs = P(None, ("grp", "bf"))
    return jax.shard_map(shards, mesh=mesh, in_specs=in_specs, out_specs=out_specs, check_vma=False)
```

```python
import jax
import jax.numpy as jnp
from jax import lax
from jax.experimental import pallas as pl
from jax.experimental.pallas import tpu as pltpu
from jax.sharding import PartitionSpec as P

F32, BF16 = jnp.float32, jnp.bfloat16
VMEM = pl.BlockSpec(memory_space=pltpu.VMEM)
SMEM = pl.BlockSpec(memory_space=pltpu.SMEM)
NT = (((1,), (1,)), ((), ()))


def partner(value, axis, distance):
    mask = 2**distance
    pairs = [(source, source ^ mask) for source in range(lax.axis_size(axis))]
    return lax.ppermute(value, axis, pairs)


def shifted(value, axis, distance):
    size = lax.axis_size(axis)
    return lax.ppermute(value, axis, [(source, (source + distance) % size) for source in range(size)])


def call(body, shapes, specs, flops, moved, *operands):
    return pl.pallas_call(
        body,
        out_shape=shapes,
        in_specs=specs,
        out_specs=jax.tree.map(lambda _: VMEM, shapes),
        cost_estimate=pl.CostEstimate(flops=flops, bytes_accessed=moved, transcendentals=0),
        compiler_params=pltpu.CompilerParams(vmem_limit_bytes=16 * 2**20),
    )(*operands)


def project(field_ref, col_ref, out_ref):
    out_ref[...] = lax.dot_general(field_ref[...].astype(BF16), col_ref[...], NT, preferred_element_type=F32)


def build_weights(mixing_ref, perm_ref, out_ref):
    levels, sections, _, k, _ = mixing_ref.shape
    width = levels * k

    def placed(block, level):
        parts = [jnp.zeros((k, k), block.dtype)] * levels
        parts[level] = block
        return jnp.concatenate(parts, axis=1)

    rows = lax.broadcasted_iota(jnp.int32, (k, k), 0)
    picks = jnp.concatenate(
        [placed((rows == perm_ref[level : level + 1, :]).astype(F32), level) for level in range(levels)], axis=0
    ).astype(BF16)
    for section in range(sections):
        for side in range(2):
            mats = jnp.concatenate(
                [placed(mixing_ref[level, section, side].astype(F32), level) for level in range(levels)], axis=0
            ).astype(BF16)
            if section == 0:
                mats = jnp.dot(picks, mats, preferred_element_type=F32).astype(BF16)
            out_ref[section, side * width : (side + 1) * width, :] = mats


def exact_dot(value, factor):
    count = value.shape[0]
    high = value.astype(BF16)
    rest = value - high.astype(F32)
    middle = rest.astype(BF16)
    low = (rest - middle.astype(F32)).astype(BF16)
    terms = jnp.dot(jnp.concatenate([high, middle, low], axis=0), factor, preferred_element_type=F32)
    return terms[:count] + (terms[count : 2 * count] + terms[2 * count :])


def step(section, own_ref, other_ref, weights_ref, out_ref):
    both = jnp.concatenate([own_ref[...], other_ref[...]], axis=1)
    out_ref[...] = exact_dot(both, weights_ref[section])


def last_step(section, rank_size, half_shift, own_ref, other_ref, weights_ref, row_ref, owner_ref, half_ref, below_ref):
    both = jnp.concatenate([own_ref[...], other_ref[...]], axis=1)
    state = exact_dot(both, weights_ref[section])
    first_is_half = owner_ref[0, 0] == half_shift
    lane = lax.broadcasted_iota(jnp.int32, state.shape, 1)
    first = (lane < rank_size).astype(jnp.int32)
    half = first == first_is_half.astype(jnp.int32)
    rank_half = jnp.where(half, state, 0.0).astype(BF16)
    rank_below = jnp.where(half, 0.0, state).astype(BF16)
    count = state.shape[0]
    outs = jnp.dot(jnp.concatenate([rank_half, rank_below], axis=0), row_ref[...], preferred_element_type=F32)
    half_ref[...] = outs[:count]
    below_ref[...] = outs[count:]


def shards(field, leaf_inverse, col_factor, row_factor, mixing, row_owner, rank_perm):
    vectors, rows = field.shape
    order = leaf_inverse.shape[1]
    levels, rank_size, _ = col_factor.shape
    sections = mixing.shape[2]
    bits = lax.axis_size("bf").bit_length() - 1
    groups = lax.axis_size("grp")
    width = levels * rank_size

    state_shape = jax.ShapeDtypeStruct((vectors, width), F32)
    out_shape = jax.ShapeDtypeStruct((vectors, rows), F32)
    state = call(
        project, state_shape, [VMEM, VMEM], 2 * vectors * rows * width, 3 * rows * width,
        field, col_factor.reshape(width, rows),
    )
    weights = call(
        build_weights, jax.ShapeDtypeStruct((sections, 2 * width, width), BF16), [VMEM, VMEM],
        4 * width**3, 2 * sections * 2 * width * width, mixing[0], rank_perm,
    )
    for section in range(sections - 1):
        other = partner(state, "bf", section % bits)
        state = call(
            lambda *refs, section=section: step(section, *refs), state_shape, [VMEM] * 3,
            12 * vectors * width * width, 4 * width * width, state, other, weights,
        )
    other = partner(state, "bf", (sections - 1) % bits)
    out_half, out_below = call(
        lambda *refs: last_step(sections - 1, rank_size, groups // 2, *refs), [out_shape, out_shape],
        [VMEM] * 4 + [SMEM], 4 * vectors * width * rows, 4 * width * rows,
        state, other, weights, row_factor.reshape(width, rows), row_owner,
    )
    out_half = shifted(out_half, "grp", groups // 2)
    out_below = shifted(out_below, "grp", groups - 1)
    diag = jnp.einsum(
        "rnl,nlm->rnm",
        field.astype(BF16).reshape(vectors, rows // order, order),
        leaf_inverse,
        preferred_element_type=F32,
    ).reshape(vectors, rows)
    return diag + out_half + out_below


def solution(mesh):
    in_specs = (
        P(None, ("grp", "bf")),
        P(("grp", "bf"), None, None),
        P(None, None, ("grp", "bf")),
        P(None, None, ("grp", "bf")),
        P(("grp", "bf"), None, None, None, None, None),
        P(),
        P(),
    )
    out_specs = P(None, ("grp", "bf"))
    return jax.shard_map(shards, mesh=mesh, in_specs=in_specs, out_specs=out_specs, check_vma=False)
```

```python
import jax
import jax.numpy as jnp
from jax import lax
from jax.experimental import pallas as pl
from jax.experimental.pallas import tpu as pltpu
from jax.sharding import PartitionSpec as P

F32, BF16 = jnp.float32, jnp.bfloat16
VMEM = pl.BlockSpec(memory_space=pltpu.VMEM)
HBM = pl.BlockSpec(memory_space=pltpu.HBM)
NT = (((1,), (1,)), ((), ()))


def partner(value, axis, distance):
    mask = 2**distance
    pairs = [(source, source ^ mask) for source in range(lax.axis_size(axis))]
    return lax.ppermute(value, axis, pairs)


def shifted(value, axis, distance):
    size = lax.axis_size(axis)
    return lax.ppermute(value, axis, [(source, (source + distance) % size) for source in range(size)])


def call(body, shapes, specs, flops, moved, *operands, scratch=(), limit=16):
    return pl.pallas_call(
        body,
        out_shape=shapes,
        in_specs=specs,
        out_specs=jax.tree.map(lambda _: VMEM, shapes),
        scratch_shapes=scratch,
        cost_estimate=pl.CostEstimate(flops=flops, bytes_accessed=moved, transcendentals=0),
        compiler_params=pltpu.CompilerParams(vmem_limit_bytes=limit * 2**20),
    )(*operands)


def project(field_hbm, col_hbm, mixing_hbm, perm_hbm, out_ref, mixing_ref, perm_ref, field_ref, col_ref, sems):
    pairs = [(field_hbm, field_ref), (col_hbm, col_ref), (mixing_hbm, mixing_ref), (perm_hbm, perm_ref)]
    copies = [pltpu.make_async_copy(source, target, sems.at[n]) for n, (source, target) in enumerate(pairs)]
    for copy in copies:
        copy.start()
    copies[0].wait()
    copies[1].wait()
    out_ref[...] = lax.dot_general(field_ref[...].astype(BF16), col_ref[...], NT, preferred_element_type=F32)
    copies[2].wait()
    copies[3].wait()


def build_weights(mixing_ref, perm_ref, out_ref):
    levels, sections, _, k, _ = mixing_ref.shape
    width = levels * k

    def placed(block, level):
        parts = [jnp.zeros((k, k), block.dtype)] * levels
        parts[level] = block
        return jnp.concatenate(parts, axis=1)

    rows = lax.broadcasted_iota(jnp.int32, (k, k), 0)
    picks = jnp.concatenate(
        [placed((rows == perm_ref[level : level + 1, :]).astype(F32), level) for level in range(levels)], axis=0
    ).astype(BF16)
    for section in range(sections):
        for side in range(2):
            mats = jnp.concatenate(
                [placed(mixing_ref[level, section, side].astype(F32), level) for level in range(levels)], axis=0
            ).astype(BF16)
            if section == 0:
                mats = jnp.dot(picks, mats, preferred_element_type=F32).astype(BF16)
            out_ref[section, side * width : (side + 1) * width, :] = mats


def exact_dot(value, factor):
    count = value.shape[0]
    high = value.astype(BF16)
    rest = value - high.astype(F32)
    middle = rest.astype(BF16)
    low = (rest - middle.astype(F32)).astype(BF16)
    terms = jnp.dot(jnp.concatenate([high, middle, low], axis=0), factor, preferred_element_type=F32)
    return terms[:count] + (terms[count : 2 * count] + terms[2 * count :])


def step(section, own_ref, other_ref, weights_ref, out_ref):
    both = jnp.concatenate([own_ref[...], other_ref[...]], axis=1)
    out_ref[...] = exact_dot(both, weights_ref[section])


def last_step(section, rank_size, half_shift, own_ref, other_ref, weights_ref, row_ref, owner_ref, half_ref, below_ref):
    both = jnp.concatenate([own_ref[...], other_ref[...]], axis=1)
    state = exact_dot(both, weights_ref[section])
    first_is_half = jnp.broadcast_to(owner_ref[0:1, 0:1], state.shape) == half_shift
    lane = lax.broadcasted_iota(jnp.int32, state.shape, 1)
    half = jnp.logical_xor(lane >= rank_size, first_is_half)
    rank_half = jnp.where(half, state, 0.0).astype(BF16)
    rank_below = jnp.where(half, 0.0, state).astype(BF16)
    count = state.shape[0]
    outs = jnp.dot(jnp.concatenate([rank_half, rank_below], axis=0), row_ref[...], preferred_element_type=F32)
    half_ref[...] = outs[:count]
    below_ref[...] = outs[count:]


def shards(field, leaf_inverse, col_factor, row_factor, mixing, row_owner, rank_perm):
    vectors, rows = field.shape
    order = leaf_inverse.shape[1]
    levels, rank_size, _ = col_factor.shape
    sections = mixing.shape[2]
    bits = lax.axis_size("bf").bit_length() - 1
    groups = lax.axis_size("grp")
    width = levels * rank_size

    state_shape = jax.ShapeDtypeStruct((vectors, width), F32)
    out_shape = jax.ShapeDtypeStruct((vectors, rows), F32)
    state, mats, perm = call(
        project,
        [state_shape, jax.ShapeDtypeStruct(mixing.shape[1:], BF16), jax.ShapeDtypeStruct(rank_perm.shape, jnp.int32)],
        [HBM] * 4, 2 * vectors * rows * width, 3 * rows * width,
        *[pltpu.with_memory_space_constraint(x, pltpu.HBM) for x in (field, col_factor.reshape(width, rows), mixing[0], rank_perm)],
        scratch=[pltpu.VMEM(field.shape, F32), pltpu.VMEM((width, rows), BF16), pltpu.SemaphoreType.DMA((4,))],
    )
    weights = call(
        build_weights, jax.ShapeDtypeStruct((sections, 2 * width, width), BF16), [VMEM, VMEM],
        4 * width**3, 2 * sections * 2 * width * width, mats, perm,
    )
    for section in range(sections - 1):
        other = partner(state, "bf", section % bits)
        state = call(
            lambda *refs, section=section: step(section, *refs), state_shape, [VMEM] * 3,
            12 * vectors * width * width, 4 * width * width, state, other, weights,
        )
    other = partner(state, "bf", (sections - 1) % bits)
    out_half, out_below = call(
        lambda *refs: last_step(sections - 1, rank_size, groups // 2, *refs), [out_shape, out_shape],
        [VMEM] * 5, 4 * vectors * width * rows, 4 * width * rows,
        state, other, weights, row_factor.reshape(width, rows), row_owner,
    )
    out_half = shifted(out_half, "grp", groups // 2)
    out_below = shifted(out_below, "grp", groups - 1)
    diag = jnp.einsum(
        "rnl,nlm->rnm",
        field.astype(BF16).reshape(vectors, rows // order, order),
        leaf_inverse,
        preferred_element_type=F32,
    ).reshape(vectors, rows)
    return diag + out_half + out_below


def solution(mesh):
    in_specs = (
        P(None, ("grp", "bf")),
        P(("grp", "bf"), None, None),
        P(None, None, ("grp", "bf")),
        P(None, None, ("grp", "bf")),
        P(("grp", "bf"), None, None, None, None, None),
        P(),
        P(),
    )
    out_specs = P(None, ("grp", "bf"))
    return jax.shard_map(shards, mesh=mesh, in_specs=in_specs, out_specs=out_specs, check_vma=False)
```

```python
import jax
import jax.numpy as jnp
from jax import lax
from jax.experimental import pallas as pl
from jax.experimental.pallas import tpu as pltpu
from jax.sharding import PartitionSpec as P

F32, BF16 = jnp.float32, jnp.bfloat16
VMEM = pl.BlockSpec(memory_space=pltpu.VMEM)
HBM = pl.BlockSpec(memory_space=pltpu.HBM)
NT = (((1,), (1,)), ((), ()))


def partner(value, axis, distance):
    mask = 2**distance
    pairs = [(source, source ^ mask) for source in range(lax.axis_size(axis))]
    return lax.ppermute(value, axis, pairs)


def shifted(value, axis, distance):
    size = lax.axis_size(axis)
    return lax.ppermute(value, axis, [(source, (source + distance) % size) for source in range(size)])


def gathered(copies, axis, low, high):
    size = lax.axis_size(axis)
    bases = [base for base in range(size) if not base & (1 << low) and not base & (1 << high)]
    groups = [[base, base | 1 << low, base | 1 << high, base | 1 << low | 1 << high] for base in bases]
    return lax.all_to_all(copies, axis, 0, 0, axis_index_groups=groups if len(groups) > 1 else None)


def call(body, shapes, specs, flops, moved, *operands, scratch=()):
    return pl.pallas_call(
        body,
        out_shape=shapes,
        in_specs=specs,
        out_specs=jax.tree.map(lambda _: VMEM, shapes),
        scratch_shapes=scratch,
        cost_estimate=pl.CostEstimate(flops=flops, bytes_accessed=moved, transcendentals=0),
        compiler_params=pltpu.CompilerParams(vmem_limit_bytes=16 * 2**20),
    )(*operands)


def block_diagonal(compact, levels):
    k = compact.shape[0]
    lane = lax.broadcasted_iota(jnp.int32, compact.shape, 1)
    parts = []
    for level in range(levels):
        mine = jnp.logical_and(lane >= level * k, lane < (level + 1) * k)
        parts.append(jnp.where(mine, compact, 0.0))
    return jnp.concatenate(parts, axis=0)


def load(field_hbm, col_hbm, mixing_hbm, perm_hbm, field_ref, col_ref, compact_ref, mixing_ref, perm_ref, sems):
    pairs = [(mixing_hbm, mixing_ref), (perm_hbm, perm_ref), (field_hbm, field_ref), (col_hbm, col_ref)]
    copies = [pltpu.make_async_copy(source, target, sems.at[n]) for n, (source, target) in enumerate(pairs)]
    for copy in copies:
        copy.start()
    copies[0].wait()
    copies[1].wait()
    levels, sections, _, k, _ = mixing_ref.shape
    row = lax.broadcasted_iota(jnp.int32, (k, k), 0)
    picks = jnp.concatenate(
        [(row == perm_ref[level : level + 1, :]).astype(F32) for level in range(levels)], axis=1
    )
    picks = block_diagonal(picks, levels).astype(BF16)
    for section in range(sections):
        for side in range(2):
            mats = jnp.concatenate(
                [mixing_ref[level, section, side].astype(F32) for level in range(levels)], axis=1
            )
            if section == 0:
                mats = jnp.dot(picks, block_diagonal(mats, levels).astype(BF16), preferred_element_type=F32)
                mats = sum(mats[level * k : (level + 1) * k] for level in range(levels))
            compact_ref[section, side * k : (side + 1) * k, :] = mats
    copies[2].wait()
    copies[3].wait()


def project(field_ref, col_ref, out_ref):
    state = lax.dot_general(field_ref[...].astype(BF16), col_ref[...], NT, preferred_element_type=F32)
    for n in range(out_ref.shape[0]):
        out_ref[n] = state


def exact_dot(value, factor):
    count = value.shape[0]
    high = value.astype(BF16)
    rest = value - high.astype(F32)
    middle = rest.astype(BF16)
    low = (rest - middle.astype(F32)).astype(BF16)
    terms = jnp.dot(jnp.concatenate([high, middle, low], axis=0), factor, preferred_element_type=F32)
    return terms[:count] + (terms[count : 2 * count] + terms[2 * count :])


def section_product(own, other, compact, levels):
    k = compact.shape[0] // 2
    weights = jnp.concatenate([block_diagonal(compact[:k], levels), block_diagonal(compact[k:], levels)], axis=0)
    return exact_dot(jnp.concatenate([own, other], axis=1), weights.astype(BF16))


def two_sections(levels, section, first_bit, second_bit, states_ref, compact_ref, partner_ref):
    place = lax.axis_index("bf")
    low, high = sorted((first_bit, second_bit))
    mine = lax.rem(place >> low, 2) + 2 * lax.rem(place >> high, 2)
    first, second = (1, 2) if first_bit < second_bit else (2, 1)
    own = section_product(states_ref[mine], states_ref[mine ^ first], compact_ref[section], levels)
    other = section_product(states_ref[mine ^ second], states_ref[mine ^ 3], partner_ref[...], levels)
    return section_product(own, other, compact_ref[section + 1], levels)


def middle_step(static, states_ref, compact_ref, partner_ref, out_ref):
    state = two_sections(*static, states_ref, compact_ref, partner_ref)
    for n in range(out_ref.shape[0]):
        out_ref[n] = state


def last_step(static, rank_size, half_shift, states_ref, compact_ref, partner_ref, row_ref, owner_ref, half_ref, below_ref):
    state = two_sections(*static, states_ref, compact_ref, partner_ref)
    first_is_half = jnp.broadcast_to(owner_ref[0:1, 0:1], state.shape) == half_shift
    lane = lax.broadcasted_iota(jnp.int32, state.shape, 1)
    half = jnp.logical_xor(lane >= rank_size, first_is_half)
    rank_half = jnp.where(half, state, 0.0).astype(BF16)
    rank_below = jnp.where(half, 0.0, state).astype(BF16)
    count = state.shape[0]
    outs = jnp.dot(jnp.concatenate([rank_half, rank_below], axis=0), row_ref[...], preferred_element_type=F32)
    half_ref[...] = outs[:count]
    below_ref[...] = outs[count:]


def shards(field, leaf_inverse, col_factor, row_factor, mixing, row_owner, rank_perm):
    vectors, rows = field.shape
    order = leaf_inverse.shape[1]
    levels, rank_size, _ = col_factor.shape
    sections = mixing.shape[2]
    bits = lax.axis_size("bf").bit_length() - 1
    groups = lax.axis_size("grp")
    width = levels * rank_size

    states_shape = jax.ShapeDtypeStruct((4, vectors, width), F32)
    out_shape = jax.ShapeDtypeStruct((vectors, rows), F32)
    in_hbm = [
        pltpu.with_memory_space_constraint(x, pltpu.HBM)
        for x in (field, col_factor.reshape(width, rows), mixing[0], rank_perm)
    ]
    field_here, col_here, compact = call(
        load,
        [
            jax.ShapeDtypeStruct((vectors, rows), F32),
            jax.ShapeDtypeStruct((width, rows), BF16),
            jax.ShapeDtypeStruct((sections, 2 * rank_size, width), F32),
        ],
        [HBM] * 4, 8 * width**3, 3 * rows * width, *in_hbm,
        scratch=[
            pltpu.VMEM(mixing.shape[1:], BF16),
            pltpu.VMEM(rank_perm.shape, jnp.int32),
            pltpu.SemaphoreType.DMA((4,)),
        ],
    )
    pair_bits = [(section % bits, (section + 1) % bits) for section in range(0, sections, 2)]
    partners = [partner(compact[2 * n], "bf", second) for n, (_, second) in enumerate(pair_bits)]
    states = call(
        project, states_shape, [VMEM, VMEM], 2 * vectors * rows * width, 3 * rows * width, field_here, col_here
    )
    step_flops = 36 * vectors * width * width
    for n, pair in enumerate(pair_bits):
        states = gathered(states, "bf", min(pair), max(pair))
        static = (levels, 2 * n, *pair)
        if n < len(pair_bits) - 1:
            states = call(
                lambda *refs, static=static: middle_step(static, *refs), states_shape, [VMEM] * 3,
                step_flops, 12 * width * width, states, compact, partners[n],
            )
    out_half, out_below = call(
        lambda *refs: last_step(static, rank_size, groups // 2, *refs), [out_shape, out_shape],
        [VMEM] * 5, step_flops + 4 * vectors * width * rows, 4 * width * rows,
        states, compact, partners[-1], row_factor.reshape(width, rows), row_owner,
    )
    out_half = shifted(out_half, "grp", groups // 2)
    out_below = shifted(out_below, "grp", groups - 1)
    diag = jnp.einsum(
        "rnl,nlm->rnm",
        field_here.astype(BF16).reshape(vectors, rows // order, order),
        leaf_inverse,
        preferred_element_type=F32,
    ).reshape(vectors, rows)
    return diag + out_half + out_below


def solution(mesh):
    in_specs = (
        P(None, ("grp", "bf")),
        P(("grp", "bf"), None, None),
        P(None, None, ("grp", "bf")),
        P(None, None, ("grp", "bf")),
        P(("grp", "bf"), None, None, None, None, None),
        P(),
        P(),
    )
    out_specs = P(None, ("grp", "bf"))
    return jax.shard_map(shards, mesh=mesh, in_specs=in_specs, out_specs=out_specs, check_vma=False)
```

```python
import jax
import jax.numpy as jnp
from jax import lax
from jax.experimental import pallas as pl
from jax.experimental.pallas import tpu as pltpu
from jax.sharding import PartitionSpec as P

F32, BF16 = jnp.float32, jnp.bfloat16
VMEM = pl.BlockSpec(memory_space=pltpu.VMEM)
HBM = pl.BlockSpec(memory_space=pltpu.HBM)
NT = (((1,), (1,)), ((), ()))


def shifted(value, axis, distance):
    size = lax.axis_size(axis)
    return lax.ppermute(value, axis, [(source, (source + distance) % size) for source in range(size)])


def to_odd(value):
    return lax.ppermute(value, "bf", [(n, n + 1) for n in range(0, lax.axis_size("bf"), 2)])


def to_even(value):
    return lax.ppermute(value, "bf", [(n + 1, n) for n in range(0, lax.axis_size("bf"), 2)])


def among_odd(value, bit):
    return lax.ppermute(value, "bf", [(n, n ^ 1 << bit) for n in range(1, lax.axis_size("bf"), 2)])


def call(body, shapes, specs, flops, moved, *operands, scratch=()):
    return pl.pallas_call(
        body,
        out_shape=shapes,
        in_specs=specs,
        out_specs=jax.tree.map(lambda _: VMEM, shapes),
        scratch_shapes=scratch,
        cost_estimate=pl.CostEstimate(flops=flops, bytes_accessed=moved, transcendentals=0),
        compiler_params=pltpu.CompilerParams(vmem_limit_bytes=16 * 2**20),
    )(*operands)


def block_diagonal(compact, levels):
    k = compact.shape[0]
    lane = lax.broadcasted_iota(jnp.int32, compact.shape, 1)
    parts = []
    for level in range(levels):
        mine = jnp.logical_and(lane >= level * k, lane < (level + 1) * k)
        parts.append(jnp.where(mine, compact, 0.0))
    return jnp.concatenate(parts, axis=0)


def section_weights(compact, levels):
    k = compact.shape[0] // 2
    parts = [block_diagonal(compact[:k], levels), block_diagonal(compact[k:], levels)]
    return jnp.concatenate(parts, axis=0).astype(BF16)


def compact_section(mixing_ref, section, side):
    levels = mixing_ref.shape[0]
    return jnp.concatenate([mixing_ref[level, section, side].astype(F32) for level in range(levels)], axis=1)


def load(field_hbm, col_hbm, mixing_hbm, perm_hbm, xb_ref, first_ref, mixing_ref, field_ref, col_ref, perm_ref, sems):
    pairs = [(mixing_hbm, mixing_ref), (perm_hbm, perm_ref), (field_hbm, field_ref), (col_hbm, col_ref)]
    copies = [pltpu.make_async_copy(source, target, sems.at[n]) for n, (source, target) in enumerate(pairs)]
    for copy in copies:
        copy.start()
    copies[0].wait()
    copies[1].wait()
    levels, sections, _, k, _ = mixing_ref.shape
    vectors = field_ref.shape[0]
    row = lax.broadcasted_iota(jnp.int32, (k, k), 0)
    picks = jnp.concatenate([(row == perm_ref[level : level + 1, :]).astype(F32) for level in range(levels)], axis=1)
    picks = block_diagonal(picks, levels).astype(BF16)
    for side in range(2):
        mats = block_diagonal(compact_section(mixing_ref, 0, side), levels).astype(BF16)
        mats = jnp.dot(picks, mats, preferred_element_type=F32)
        mats = sum(mats[level * k : (level + 1) * k] for level in range(levels))
        first_ref[vectors + side * k : vectors + (side + 1) * k, :] = mats
    copies[2].wait()
    copies[3].wait()
    xb = field_ref[...].astype(BF16)
    xb_ref[...] = xb
    first_ref[:vectors, :] = lax.dot_general(xb, col_ref[...], NT, preferred_element_type=F32)


def build_own(levels, mixing_ref, compact_ref, weights_ref):
    k = mixing_ref.shape[3]
    for n in range(compact_ref.shape[0]):
        for side in range(2):
            compact_ref[n, side * k : (side + 1) * k, :] = compact_section(mixing_ref, n + 1, side)
        weights_ref[n] = section_weights(compact_ref[n], levels)


def build_weights(levels, compact_ref, weights_ref):
    for n in range(compact_ref.shape[0]):
        weights_ref[n] = section_weights(compact_ref[n], levels)


def exact_dot(value, factor):
    count = value.shape[0]
    high = value.astype(BF16)
    rest = value - high.astype(F32)
    middle = rest.astype(BF16)
    low = (rest - middle.astype(F32)).astype(BF16)
    terms = jnp.dot(jnp.concatenate([high, middle, low], axis=0), factor, preferred_element_type=F32)
    return terms[:count] + (terms[count : 2 * count] + terms[2 * count :])


def section_product(own, other, weights):
    return exact_dot(jnp.concatenate([own, other], axis=1), weights)


def first_section(levels, mine_ref, theirs_ref, out_ref):
    vectors = out_ref.shape[1]
    odd, even = mine_ref[:vectors, :], theirs_ref[:vectors, :]
    out_ref[0] = section_product(even, odd, section_weights(theirs_ref[vectors:, :], levels))
    out_ref[1] = section_product(odd, even, section_weights(mine_ref[vectors:, :], levels))


def next_sections(sections, states_ref, other_ref, mine_ref, theirs_ref, *out_refs):
    weights = (theirs_ref, mine_ref)
    states = [section_product(states_ref[n], other_ref[n], weights[n][sections[0] - 1]) for n in range(2)]
    for section in sections[1:]:
        states = [section_product(states[n], states[1 - n], weights[n][section - 1]) for n in range(2)]
    for n in range(2):
        if len(out_refs) == 1:
            out_refs[0][n] = states[n]
        else:
            out_refs[n][...] = states[n]


def expand(rank_size, half_shift, state_ref, back_ref, row_ref, owner_ref, half_ref, below_ref):
    odd = jnp.broadcast_to(lax.rem(lax.axis_index("bf"), 2), back_ref.shape) == 1
    state = jnp.where(odd, state_ref[...], back_ref[...])
    first_is_half = jnp.broadcast_to(owner_ref[0:1, 0:1], state.shape) == half_shift
    lane = lax.broadcasted_iota(jnp.int32, state.shape, 1)
    half = jnp.logical_xor(lane >= rank_size, first_is_half)
    rank_half = jnp.where(half, state, 0.0).astype(BF16)
    rank_below = jnp.where(half, 0.0, state).astype(BF16)
    count = state.shape[0]
    outs = jnp.dot(jnp.concatenate([rank_half, rank_below], axis=0), row_ref[...], preferred_element_type=F32)
    half_ref[...] = outs[:count]
    below_ref[...] = outs[count:]


def shards(field, leaf_inverse, col_factor, row_factor, mixing, row_owner, rank_perm):
    vectors, rows = field.shape
    order = leaf_inverse.shape[1]
    levels, rank_size, _ = col_factor.shape
    sections = mixing.shape[2]
    bits = lax.axis_size("bf").bit_length() - 1
    groups = lax.axis_size("grp")
    width = levels * rank_size

    def array(*shape, kind=F32):
        return jax.ShapeDtypeStruct(shape, kind)

    in_hbm = [
        pltpu.with_memory_space_constraint(x, pltpu.HBM)
        for x in (field, col_factor.reshape(width, rows), mixing[0], rank_perm)
    ]
    xb, first, mixing_here = call(
        load,
        [
            array(vectors, rows, kind=BF16),
            array(vectors + 2 * rank_size, width),
            array(*mixing.shape[1:], kind=BF16),
        ],
        [HBM] * 4, 2 * vectors * rows * width, 3 * rows * width, *in_hbm,
        scratch=[
            pltpu.VMEM(field.shape, F32),
            pltpu.VMEM((width, rows), BF16),
            pltpu.VMEM(rank_perm.shape, jnp.int32),
            pltpu.SemaphoreType.DMA((4,)),
        ],
    )
    first_theirs = to_odd(first)
    weight_cost = (4 * width * width * sections, 8 * width * width * sections)
    weights_shape = array(sections - 1, 2 * width, width, kind=BF16)
    later, mine = call(
        lambda *refs: build_own(levels, *refs), [array(sections - 1, 2 * rank_size, width), weights_shape],
        [VMEM], *weight_cost, mixing_here,
    )
    theirs = call(
        lambda *refs: build_weights(levels, *refs), weights_shape, [VMEM], *weight_cost, to_odd(later)
    )
    step_cost = (24 * vectors * width * width, 8 * width * width)
    states = call(
        lambda *refs: first_section(levels, *refs), array(2, vectors, width), [VMEM] * 2, *step_cost, first, first_theirs
    )
    runs = []
    for section in range(1, sections):
        if section % bits:
            runs.append([section])
        else:
            runs[-1].append(section)
    for n, run in enumerate(runs):
        other = among_odd(states, run[0] % bits)
        last = n == len(runs) - 1
        states = call(
            lambda *refs, run=run: next_sections(run, *refs),
            [array(vectors, width)] * 2 if last else array(2, vectors, width),
            [VMEM] * 4, *step_cost, states, other, mine, theirs,
        )
    out_half, out_below = call(
        lambda *refs: expand(rank_size, groups // 2, *refs), [array(vectors, rows)] * 2,
        [VMEM] * 4, 4 * vectors * width * rows, 4 * width * rows,
        states[1], to_even(states[0]), row_factor.reshape(width, rows), row_owner,
    )
    out_half = shifted(out_half, "grp", groups // 2)
    out_below = shifted(out_below, "grp", groups - 1)
    diag = jnp.einsum(
        "rnl,nlm->rnm",
        xb.reshape(vectors, rows // order, order),
        leaf_inverse,
        preferred_element_type=F32,
    ).reshape(vectors, rows)
    return diag + out_half + out_below


def solution(mesh):
    in_specs = (
        P(None, ("grp", "bf")),
        P(("grp", "bf"), None, None),
        P(None, None, ("grp", "bf")),
        P(None, None, ("grp", "bf")),
        P(("grp", "bf"), None, None, None, None, None),
        P(),
        P(),
    )
    out_specs = P(None, ("grp", "bf"))
    return jax.shard_map(shards, mesh=mesh, in_specs=in_specs, out_specs=out_specs, check_vma=False)
```

```python
import jax
import jax.numpy as jnp
from jax import lax
from jax.experimental import pallas as pl
from jax.experimental.pallas import tpu as pltpu
from jax.sharding import PartitionSpec as P

F32, BF16 = jnp.float32, jnp.bfloat16
VMEM = pl.BlockSpec(memory_space=pltpu.VMEM)
HBM = pl.BlockSpec(memory_space=pltpu.HBM)
NT = (((1,), (1,)), ((), ()))


def shifted(value, axis, distance):
    size = lax.axis_size(axis)
    return lax.ppermute(value, axis, [(source, (source + distance) % size) for source in range(size)])


def swapped(value):
    return lax.ppermute(value, "bf", [(n, n ^ 1) for n in range(lax.axis_size("bf"))])


def among_odd(value, bit):
    return lax.ppermute(value, "bf", [(n, n ^ 1 << bit if n % 2 else n) for n in range(lax.axis_size("bf"))])


def call(body, shapes, specs, flops, moved, *operands, scratch=()):
    return pl.pallas_call(
        body,
        out_shape=shapes,
        in_specs=specs,
        out_specs=jax.tree.map(lambda _: VMEM, shapes),
        scratch_shapes=scratch,
        cost_estimate=pl.CostEstimate(flops=flops, bytes_accessed=moved, transcendentals=0),
        compiler_params=pltpu.CompilerParams(vmem_limit_bytes=16 * 2**20),
    )(*operands)


def block_diagonal(compact, levels):
    k = compact.shape[0]
    lane = lax.broadcasted_iota(jnp.int32, compact.shape, 1)
    parts = []
    for level in range(levels):
        mine = jnp.logical_and(lane >= level * k, lane < (level + 1) * k)
        parts.append(jnp.where(mine, compact, 0.0))
    return jnp.concatenate(parts, axis=0)


def section_weights(compact, levels):
    k = compact.shape[0] // 2
    parts = [block_diagonal(compact[:k], levels), block_diagonal(compact[k:], levels)]
    return jnp.concatenate(parts, axis=0).astype(BF16)


def compact_section(mixing_ref, section, side):
    levels = mixing_ref.shape[0]
    return jnp.concatenate([mixing_ref[level, section, side].astype(F32) for level in range(levels)], axis=1)


def load(field_hbm, col_hbm, mixing_hbm, perm_hbm, xb_ref, sent_ref, field_ref, col_ref, mixing_ref, perm_ref, sems):
    pairs = [(mixing_hbm, mixing_ref), (perm_hbm, perm_ref), (field_hbm, field_ref), (col_hbm, col_ref)]
    copies = [pltpu.make_async_copy(source, target, sems.at[n]) for n, (source, target) in enumerate(pairs)]
    for copy in copies:
        copy.start()
    copies[0].wait()
    copies[1].wait()
    levels, sections, _, k, _ = mixing_ref.shape
    vectors = field_ref.shape[0]
    row = lax.broadcasted_iota(jnp.int32, (k, k), 0)
    picks = jnp.concatenate([(row == perm_ref[level : level + 1, :]).astype(F32) for level in range(levels)], axis=1)
    picks = block_diagonal(picks, levels).astype(BF16)
    for section in range(sections):
        for side in range(2):
            mats = jnp.concatenate([mixing_ref[level, section, side].astype(F32) for level in range(levels)], axis=1)
            if section == 0:
                mats = jnp.dot(picks, block_diagonal(mats, levels).astype(BF16), preferred_element_type=F32)
                mats = sum(mats[level * k : (level + 1) * k] for level in range(levels))
            start = vectors + (2 * section + side) * k
            sent_ref[start : start + k, :] = mats
    copies[2].wait()
    copies[3].wait()
    xb = field_ref[...].astype(BF16)
    xb_ref[...] = xb
    sent_ref[:vectors, :] = lax.dot_general(xb, col_ref[...], NT, preferred_element_type=F32)


def build_weights(levels, vectors, first, compact_ref, weights_ref):
    size = weights_ref.shape[2] // levels * 2
    for n in range(weights_ref.shape[0]):
        start = vectors + (first + n) * size
        weights_ref[n] = section_weights(compact_ref[start : start + size, :], levels)


def exact_dot(value, factor):
    count = value.shape[0]
    high = value.astype(BF16)
    rest = value - high.astype(F32)
    middle = rest.astype(BF16)
    low = (rest - middle.astype(F32)).astype(BF16)
    terms = jnp.dot(jnp.concatenate([high, middle, low], axis=0), factor, preferred_element_type=F32)
    return terms[:count] + (terms[count : 2 * count] + terms[2 * count :])


def section_product(own, other, weights):
    return exact_dot(jnp.concatenate([own, other], axis=1), weights)


def first_section(levels, mine_ref, theirs_ref, weights_ref, out_ref):
    vectors, width = out_ref.shape[1:]
    odd, even = mine_ref[:vectors, :], theirs_ref[:vectors, :]
    theirs = section_weights(theirs_ref[vectors : vectors + 2 * width // levels, :], levels)
    out_ref[0] = section_product(even, odd, theirs)
    out_ref[1] = section_product(odd, even, weights_ref[0])


def next_sections(sections, states_ref, other_ref, mine_ref, theirs_ref, *out_refs):
    weights = [lambda section: theirs_ref[section - 1], lambda section: mine_ref[section]]
    states = [section_product(states_ref[n], other_ref[n], weights[n](sections[0])) for n in range(2)]
    for section in sections[1:]:
        states = [section_product(states[n], states[1 - n], weights[n](section)) for n in range(2)]
    for n in range(2):
        if len(out_refs) == 1:
            out_refs[0][n] = states[n]
        else:
            out_refs[n][...] = states[n]


def expand(rank_size, half_shift, state_ref, back_ref, row_ref, owner_ref, half_ref, below_ref):
    odd = jnp.broadcast_to(lax.rem(lax.axis_index("bf"), 2), back_ref.shape) == 1
    state = jnp.where(odd, state_ref[...], back_ref[...])
    first_is_half = jnp.broadcast_to(owner_ref[0:1, 0:1], state.shape) == half_shift
    lane = lax.broadcasted_iota(jnp.int32, state.shape, 1)
    half = jnp.logical_xor(lane >= rank_size, first_is_half)
    rank_half = jnp.where(half, state, 0.0).astype(BF16)
    rank_below = jnp.where(half, 0.0, state).astype(BF16)
    count = state.shape[0]
    outs = jnp.dot(jnp.concatenate([rank_half, rank_below], axis=0), row_ref[...], preferred_element_type=F32)
    half_ref[...] = outs[:count]
    below_ref[...] = outs[count:]


def shards(field, leaf_inverse, col_factor, row_factor, mixing, row_owner, rank_perm):
    vectors, rows = field.shape
    order = leaf_inverse.shape[1]
    levels, rank_size, _ = col_factor.shape
    sections = mixing.shape[2]
    bits = lax.axis_size("bf").bit_length() - 1
    groups = lax.axis_size("grp")
    width = levels * rank_size

    def array(*shape, kind=F32):
        return jax.ShapeDtypeStruct(shape, kind)

    in_hbm = [
        pltpu.with_memory_space_constraint(x, pltpu.HBM)
        for x in (field, col_factor.reshape(width, rows), mixing[0], rank_perm)
    ]
    xb, sent = call(
        load,
        [array(vectors, rows, kind=BF16), array(vectors + 2 * sections * rank_size, width)],
        [HBM] * 4, 2 * vectors * rows * width, 3 * rows * width, *in_hbm,
        scratch=[
            pltpu.VMEM(field.shape, F32),
            pltpu.VMEM((width, rows), BF16),
            pltpu.VMEM(mixing.shape[1:], BF16),
            pltpu.VMEM(rank_perm.shape, jnp.int32),
            pltpu.SemaphoreType.DMA((4,)),
        ],
    )
    received = swapped(sent)
    mine, theirs = [
        call(
            lambda *refs, first=first: build_weights(levels, vectors, first, *refs),
            array(sections - first, 2 * width, width, kind=BF16),
            [VMEM], 4 * width * width * sections, 8 * width * width * sections, compact,
        )
        for first, compact in enumerate((sent, received))
    ]
    step_cost = (24 * vectors * width * width, 8 * width * width)
    states = call(
        lambda *refs: first_section(levels, *refs), array(2, vectors, width), [VMEM] * 3, *step_cost, sent, received, mine
    )
    runs = []
    for section in range(1, sections):
        if section % bits:
            runs.append([section])
        else:
            runs[-1].append(section)
    for n, run in enumerate(runs):
        other = among_odd(states, run[0] % bits)
        last = n == len(runs) - 1
        states = call(
            lambda *refs, run=run: next_sections(run, *refs),
            [array(vectors, width)] * 2 if last else array(2, vectors, width),
            [VMEM] * 4, *step_cost, states, other, mine, theirs,
        )
    out_half, out_below = call(
        lambda *refs: expand(rank_size, groups // 2, *refs), [array(vectors, rows)] * 2,
        [VMEM] * 4, 4 * vectors * width * rows, 4 * width * rows,
        states[1], swapped(states[0]), row_factor.reshape(width, rows), row_owner,
    )
    out_half = shifted(out_half, "grp", groups // 2)
    out_below = shifted(out_below, "grp", groups - 1)
    diag = jnp.einsum(
        "rnl,nlm->rnm",
        xb.reshape(vectors, rows // order, order),
        leaf_inverse,
        preferred_element_type=F32,
    ).reshape(vectors, rows)
    return diag + out_half + out_below


def solution(mesh):
    in_specs = (
        P(None, ("grp", "bf")),
        P(("grp", "bf"), None, None),
        P(None, None, ("grp", "bf")),
        P(None, None, ("grp", "bf")),
        P(("grp", "bf"), None, None, None, None, None),
        P(),
        P(),
    )
    out_specs = P(None, ("grp", "bf"))
    return jax.shard_map(shards, mesh=mesh, in_specs=in_specs, out_specs=out_specs, check_vma=False)
```

```python
import jax
import jax.numpy as jnp
from jax import lax
from jax.experimental import pallas as pl
from jax.experimental.pallas import tpu as pltpu
from jax.sharding import PartitionSpec as P

F32, BF16 = jnp.float32, jnp.bfloat16
VMEM = pl.BlockSpec(memory_space=pltpu.VMEM)
HBM = pl.BlockSpec(memory_space=pltpu.HBM)
NT = (((1,), (1,)), ((), ()))


def shifted(value, axis, distance):
    size = lax.axis_size(axis)
    return lax.ppermute(value, axis, [(source, (source + distance) % size) for source in range(size)])


def swapped(value):
    return lax.ppermute(value, "bf", [(n, n ^ 1) for n in range(lax.axis_size("bf"))])


def across(value, bit):
    return lax.ppermute(value, "bf", [(n, n ^ (1 << bit | 1)) for n in range(lax.axis_size("bf"))])


def call(body, shapes, specs, flops, moved, *operands, scratch=()):
    return pl.pallas_call(
        body,
        out_shape=shapes,
        in_specs=specs,
        out_specs=jax.tree.map(lambda _: VMEM, shapes),
        scratch_shapes=scratch,
        cost_estimate=pl.CostEstimate(flops=flops, bytes_accessed=moved, transcendentals=0),
        compiler_params=pltpu.CompilerParams(vmem_limit_bytes=16 * 2**20),
    )(*operands)


def block_diagonal(compact, levels):
    k = compact.shape[0]
    lane = lax.broadcasted_iota(jnp.int32, compact.shape, 1)
    parts = []
    for level in range(levels):
        mine = jnp.logical_and(lane >= level * k, lane < (level + 1) * k)
        parts.append(jnp.where(mine, compact, 0.0))
    return jnp.concatenate(parts, axis=0)


def section_weights(compact, levels):
    k = compact.shape[0] // 2
    parts = [block_diagonal(compact[:k], levels), block_diagonal(compact[k:], levels)]
    return jnp.concatenate(parts, axis=0).astype(BF16)


def compact_section(mixing_ref, section, side):
    levels = mixing_ref.shape[0]
    return jnp.concatenate([mixing_ref[level, section, side].astype(F32) for level in range(levels)], axis=1)


def load(field_hbm, col_hbm, mixing_hbm, perm_hbm, xb_ref, col_ref, sent_ref, kept_ref, field_ref, mixing_ref, perm_ref, sems):
    pairs = [(mixing_hbm, mixing_ref), (perm_hbm, perm_ref), (field_hbm, field_ref), (col_hbm, col_ref)]
    copies = [pltpu.make_async_copy(source, target, sems.at[n]) for n, (source, target) in enumerate(pairs)]
    for copy in copies:
        copy.start()
    copies[0].wait()
    copies[1].wait()
    levels, sections, _, k, _ = mixing_ref.shape
    row = lax.broadcasted_iota(jnp.int32, (k, k), 0)
    picks = jnp.concatenate([(row == perm_ref[level : level + 1, :]).astype(F32) for level in range(levels)], axis=1)
    picks = block_diagonal(picks, levels).astype(BF16)
    for section in range(sections):
        for side in range(2):
            mats = jnp.concatenate([mixing_ref[level, section, side].astype(F32) for level in range(levels)], axis=1)
            if section == 0:
                mats = jnp.dot(picks, block_diagonal(mats, levels).astype(BF16), preferred_element_type=F32)
                mats = sum(mats[level * k : (level + 1) * k] for level in range(levels))
            if section < sections - 1:
                sent_ref[section, side * k : (side + 1) * k, :] = mats
            else:
                kept_ref[0, side * k : (side + 1) * k, :] = mats
    copies[2].wait()
    xb_ref[...] = field_ref[...].astype(BF16)
    copies[3].wait()


def project(xb_ref, col_ref, out_ref):
    out_ref[...] = lax.dot_general(xb_ref[...], col_ref[...], NT, preferred_element_type=F32)


def build_weights(levels, *refs):
    *compact_refs, weights_ref = refs
    n = 0
    for compact_ref in compact_refs:
        for section in range(compact_ref.shape[0]):
            weights_ref[n] = section_weights(compact_ref[section], levels)
            n += 1


def exact_dot(value, factor):
    count = value.shape[0]
    high = value.astype(BF16)
    rest = value - high.astype(F32)
    middle = rest.astype(BF16)
    low = (rest - middle.astype(F32)).astype(BF16)
    terms = jnp.dot(jnp.concatenate([high, middle, low], axis=0), factor, preferred_element_type=F32)
    return terms[:count] + (terms[count : 2 * count] + terms[2 * count :])


def section_product(own, other, weights):
    return exact_dot(jnp.concatenate([own, other], axis=1), weights)


def run_sections(sections, final, first_refs, mine_ref, theirs_ref, out_ref):
    weights = (mine_ref, theirs_ref)
    if sections[0]:
        states_ref, other_ref = first_refs
        states, others = [states_ref[0], states_ref[1]], [other_ref[1], other_ref[0]]
    else:
        states = [ref[...] for ref in first_refs]
        others = states[::-1]
    for section in sections:
        count = 1 if section == final else 2
        states = [section_product(states[n], others[n], weights[n][section]) for n in range(count)]
        others = states[::-1]
    if count == 1:
        return states[0]
    out_ref[0], out_ref[1] = states


def step(sections, final, first_ref, second_ref, mine_ref, theirs_ref, out_ref):
    run_sections(sections, final, (first_ref, second_ref), mine_ref, theirs_ref, out_ref)


def last_step(sections, final, rank_size, half_shift, first_ref, second_ref, mine_ref, theirs_ref, row_ref, owner_ref, half_ref, below_ref):
    state = run_sections(sections, final, (first_ref, second_ref), mine_ref, theirs_ref, None)
    first_is_half = jnp.broadcast_to(owner_ref[0:1, 0:1], state.shape) == half_shift
    lane = lax.broadcasted_iota(jnp.int32, state.shape, 1)
    half = jnp.logical_xor(lane >= rank_size, first_is_half)
    rank_half = jnp.where(half, state, 0.0).astype(BF16)
    rank_below = jnp.where(half, 0.0, state).astype(BF16)
    count = state.shape[0]
    outs = jnp.dot(jnp.concatenate([rank_half, rank_below], axis=0), row_ref[...], preferred_element_type=F32)
    half_ref[...] = outs[:count]
    below_ref[...] = outs[count:]


def shards(field, leaf_inverse, col_factor, row_factor, mixing, row_owner, rank_perm):
    vectors, rows = field.shape
    order = leaf_inverse.shape[1]
    levels, rank_size, _ = col_factor.shape
    sections = mixing.shape[2]
    bits = lax.axis_size("bf").bit_length() - 1
    groups = lax.axis_size("grp")
    width = levels * rank_size

    def array(*shape, kind=F32):
        return jax.ShapeDtypeStruct(shape, kind)

    in_hbm = [
        pltpu.with_memory_space_constraint(x, pltpu.HBM)
        for x in (field, col_factor.reshape(width, rows), mixing[0], rank_perm)
    ]
    xb, col_here, sent, kept = call(
        load,
        [
            array(vectors, rows, kind=BF16),
            array(width, rows, kind=BF16),
            array(sections - 1, 2 * rank_size, width),
            array(1, 2 * rank_size, width),
        ],
        [HBM] * 4, 8 * width**3, 3 * rows * width, *in_hbm,
        scratch=[
            pltpu.VMEM(field.shape, F32),
            pltpu.VMEM(mixing.shape[1:], BF16),
            pltpu.VMEM(rank_perm.shape, jnp.int32),
            pltpu.SemaphoreType.DMA((4,)),
        ],
    )
    received = swapped(sent)
    state = call(
        project, array(vectors, width), [VMEM, VMEM], 2 * vectors * rows * width, 3 * rows * width, xb, col_here
    )
    first_states = (state, swapped(state))
    weight_cost = (4 * width * width * sections, 8 * width * width * sections)
    mine, theirs = [
        call(
            lambda *refs: build_weights(levels, *refs),
            array(sum(x.shape[0] for x in compacts), 2 * width, width, kind=BF16),
            [VMEM] * len(compacts), *weight_cost, *compacts,
        )
        for compacts in ((sent, kept), (received,))
    ]
    runs = []
    for section in range(sections):
        if section % bits or not section:
            runs.append([section])
        else:
            runs[-1].append(section)
    step_cost = (24 * vectors * width * width, 8 * width * width)
    final = sections - 1
    for run in runs[:-1]:
        states = call(
            lambda *refs, run=run: step(run, final, *refs), array(2, vectors, width), [VMEM] * 4, *step_cost,
            *first_states, mine, theirs,
        )
        first_states = (states, across(states, (run[-1] + 1) % bits))
    out_half, out_below = call(
        lambda *refs: last_step(runs[-1], final, rank_size, groups // 2, *refs), [array(vectors, rows)] * 2,
        [VMEM] * 6, 4 * vectors * width * rows, 4 * width * rows,
        *first_states, mine, theirs, row_factor.reshape(width, rows), row_owner,
    )
    out_half = shifted(out_half, "grp", groups // 2)
    out_below = shifted(out_below, "grp", groups - 1)
    diag = jnp.einsum(
        "rnl,nlm->rnm",
        xb.reshape(vectors, rows // order, order),
        leaf_inverse,
        preferred_element_type=F32,
    ).reshape(vectors, rows)
    return diag + out_half + out_below


def solution(mesh):
    in_specs = (
        P(None, ("grp", "bf")),
        P(("grp", "bf"), None, None),
        P(None, None, ("grp", "bf")),
        P(None, None, ("grp", "bf")),
        P(("grp", "bf"), None, None, None, None, None),
        P(),
        P(),
    )
    out_specs = P(None, ("grp", "bf"))
    return jax.shard_map(shards, mesh=mesh, in_specs=in_specs, out_specs=out_specs, check_vma=False)
```

```python
import jax
import jax.numpy as jnp
from jax import lax
from jax.experimental import pallas as pl
from jax.experimental.pallas import tpu as pltpu
from jax.sharding import PartitionSpec as P

F32, BF16 = jnp.float32, jnp.bfloat16
VMEM = pl.BlockSpec(memory_space=pltpu.VMEM)
HBM = pl.BlockSpec(memory_space=pltpu.HBM)
NT = (((1,), (1,)), ((), ()))


def shifted(value, axis, distance):
    size = lax.axis_size(axis)
    return lax.ppermute(value, axis, [(source, (source + distance) % size) for source in range(size)])


def swapped(value):
    return lax.ppermute(value, "bf", [(n, n ^ 1) for n in range(lax.axis_size("bf"))])


def across(value, bit):
    return lax.ppermute(value, "bf", [(n, n ^ 1 << bit) for n in range(lax.axis_size("bf"))])


def call(body, shapes, specs, flops, moved, *operands, scratch=()):
    return pl.pallas_call(
        body,
        out_shape=shapes,
        in_specs=specs,
        out_specs=jax.tree.map(lambda _: VMEM, shapes),
        scratch_shapes=scratch,
        cost_estimate=pl.CostEstimate(flops=flops, bytes_accessed=moved, transcendentals=0),
        compiler_params=pltpu.CompilerParams(vmem_limit_bytes=16 * 2**20),
    )(*operands)


def block_diagonal(compact, levels):
    k = compact.shape[0]
    lane = lax.broadcasted_iota(jnp.int32, compact.shape, 1)
    parts = []
    for level in range(levels):
        mine = jnp.logical_and(lane >= level * k, lane < (level + 1) * k)
        parts.append(jnp.where(mine, compact, 0.0))
    return jnp.concatenate(parts, axis=0)


def section_weights(compact, levels):
    k = compact.shape[0] // 2
    parts = [block_diagonal(compact[:k], levels), block_diagonal(compact[k:], levels)]
    return jnp.concatenate(parts, axis=0).astype(BF16)


def compact_section(mixing_ref, section, side):
    levels = mixing_ref.shape[0]
    return jnp.concatenate([mixing_ref[level, section, side].astype(F32) for level in range(levels)], axis=1)


def load(field_hbm, col_hbm, mixing_hbm, perm_hbm, xb_ref, col_ref, sent_ref, kept_ref, field_ref, mixing_ref, perm_ref, sems):
    pairs = [(mixing_hbm, mixing_ref), (perm_hbm, perm_ref), (field_hbm, field_ref), (col_hbm, col_ref)]
    copies = [pltpu.make_async_copy(source, target, sems.at[n]) for n, (source, target) in enumerate(pairs)]
    for copy in copies:
        copy.start()
    copies[0].wait()
    copies[1].wait()
    levels, sections, _, k, _ = mixing_ref.shape
    row = lax.broadcasted_iota(jnp.int32, (k, k), 0)
    picks = jnp.concatenate([(row == perm_ref[level : level + 1, :]).astype(F32) for level in range(levels)], axis=1)
    picks = block_diagonal(picks, levels).astype(BF16)
    for section in range(sections):
        for side in range(2):
            mats = jnp.concatenate([mixing_ref[level, section, side].astype(F32) for level in range(levels)], axis=1)
            if section == 0:
                mats = jnp.dot(picks, block_diagonal(mats, levels).astype(BF16), preferred_element_type=F32)
                mats = sum(mats[level * k : (level + 1) * k] for level in range(levels))
            if section < sections - 1:
                sent_ref[section, side * k : (side + 1) * k, :] = mats
            else:
                kept_ref[0, side * k : (side + 1) * k, :] = mats
    copies[2].wait()
    xb_ref[...] = field_ref[...].astype(BF16)
    copies[3].wait()


def project(xb_ref, col_ref, out_ref):
    out_ref[...] = lax.dot_general(xb_ref[...], col_ref[...], NT, preferred_element_type=F32)


def build_weights(levels, *refs):
    *compact_refs, weights_ref = refs
    n = 0
    for compact_ref in compact_refs:
        for section in range(compact_ref.shape[0]):
            weights_ref[n] = section_weights(compact_ref[section], levels)
            n += 1


def exact_dot(value, factor):
    count = value.shape[0]
    high = value.astype(BF16)
    rest = value - high.astype(F32)
    middle = rest.astype(BF16)
    low = (rest - middle.astype(F32)).astype(BF16)
    terms = jnp.dot(jnp.concatenate([high, middle, low], axis=0), factor, preferred_element_type=F32)
    return terms[:count] + (terms[count : 2 * count] + terms[2 * count :])


def section_product(own, other, weights):
    return exact_dot(jnp.concatenate([own, other], axis=1), weights)


def run_sections(sections, final, first_refs, mine_ref, theirs_ref, out_ref):
    weights = (mine_ref, theirs_ref)
    if sections[0]:
        states_ref, other_ref = first_refs
        states, others = [states_ref[0], states_ref[1]], [other_ref[0], other_ref[1]]
    else:
        states = [ref[...] for ref in first_refs]
        others = states[::-1]
    for section in sections:
        count = 1 if section == final else 2
        states = [section_product(states[n], others[n], weights[n][section]) for n in range(count)]
        others = states[::-1]
    if count == 1:
        return states[0]
    out_ref[0], out_ref[1] = states


def step(sections, final, first_ref, second_ref, mine_ref, theirs_ref, out_ref):
    run_sections(sections, final, (first_ref, second_ref), mine_ref, theirs_ref, out_ref)


def level_rank(state, rank_size, half_shift, owner_ref, half):
    first_is_half = jnp.broadcast_to(owner_ref[0:1, 0:1], state.shape) == half_shift
    lane = lax.broadcasted_iota(jnp.int32, state.shape, 1)
    chosen = jnp.logical_xor(lane >= rank_size, first_is_half)
    return (jnp.where(chosen, state, 0.0) if half else jnp.where(chosen, 0.0, state)).astype(BF16)


def last_step(sections, final, rank_size, half_shift, first_ref, second_ref, mine_ref, theirs_ref, row_ref, owner_ref, state_ref, half_ref):
    state = run_sections(sections, final, (first_ref, second_ref), mine_ref, theirs_ref, None)
    state_ref[...] = state
    rank = level_rank(state, rank_size, half_shift, owner_ref, True)
    half_ref[...] = jnp.dot(rank, row_ref[...], preferred_element_type=F32)


def expand_below(rank_size, half_shift, state_ref, row_ref, owner_ref, below_ref):
    rank = level_rank(state_ref[...], rank_size, half_shift, owner_ref, False)
    below_ref[...] = jnp.dot(rank, row_ref[...], preferred_element_type=F32)


def shards(field, leaf_inverse, col_factor, row_factor, mixing, row_owner, rank_perm):
    vectors, rows = field.shape
    order = leaf_inverse.shape[1]
    levels, rank_size, _ = col_factor.shape
    sections = mixing.shape[2]
    bits = lax.axis_size("bf").bit_length() - 1
    groups = lax.axis_size("grp")
    width = levels * rank_size

    def array(*shape, kind=F32):
        return jax.ShapeDtypeStruct(shape, kind)

    in_hbm = [
        pltpu.with_memory_space_constraint(x, pltpu.HBM)
        for x in (field, col_factor.reshape(width, rows), mixing[0], rank_perm)
    ]
    xb, col_here, sent, kept = call(
        load,
        [
            array(vectors, rows, kind=BF16),
            array(width, rows, kind=BF16),
            array(sections - 1, 2 * rank_size, width),
            array(1, 2 * rank_size, width),
        ],
        [HBM] * 4, 8 * width**3, 3 * rows * width, *in_hbm,
        scratch=[
            pltpu.VMEM(field.shape, F32),
            pltpu.VMEM(mixing.shape[1:], BF16),
            pltpu.VMEM(rank_perm.shape, jnp.int32),
            pltpu.SemaphoreType.DMA((4,)),
        ],
    )
    received = swapped(sent)
    state = call(
        project, array(vectors, width), [VMEM, VMEM], 2 * vectors * rows * width, 3 * rows * width, xb, col_here
    )
    first_states = (state, swapped(state))
    weight_cost = (4 * width * width * sections, 8 * width * width * sections)
    mine, theirs = [
        call(
            lambda *refs: build_weights(levels, *refs),
            array(sum(x.shape[0] for x in compacts), 2 * width, width, kind=BF16),
            [VMEM] * len(compacts), *weight_cost, *compacts,
        )
        for compacts in ((sent, kept), (received,))
    ]
    runs = []
    for section in range(sections):
        if section % bits or not section:
            runs.append([section])
        else:
            runs[-1].append(section)
    step_cost = (24 * vectors * width * width, 8 * width * width)
    final = sections - 1
    for run in runs[:-1]:
        states = call(
            lambda *refs, run=run: step(run, final, *refs), array(2, vectors, width), [VMEM] * 4, *step_cost,
            *first_states, mine, theirs,
        )
        first_states = (states, across(states, (run[-1] + 1) % bits))
    expand_cost = (2 * vectors * width * rows, 4 * width * rows)
    expand = row_factor.reshape(width, rows)
    state, out_half = call(
        lambda *refs: last_step(runs[-1], final, rank_size, groups // 2, *refs),
        [array(vectors, width), array(vectors, rows)],
        [VMEM] * 6, *expand_cost, *first_states, mine, theirs, expand, row_owner,
    )
    out_below = call(
        lambda *refs: expand_below(rank_size, groups // 2, *refs), array(vectors, rows),
        [VMEM] * 3, *expand_cost, state, expand, row_owner,
    )
    out_half = shifted(out_half, "grp", groups // 2)
    out_below = shifted(out_below, "grp", groups - 1)
    diag = jnp.einsum(
        "rnl,nlm->rnm",
        xb.reshape(vectors, rows // order, order),
        leaf_inverse,
        preferred_element_type=F32,
    ).reshape(vectors, rows)
    return diag + out_half + out_below


def solution(mesh):
    in_specs = (
        P(None, ("grp", "bf")),
        P(("grp", "bf"), None, None),
        P(None, None, ("grp", "bf")),
        P(None, None, ("grp", "bf")),
        P(("grp", "bf"), None, None, None, None, None),
        P(),
        P(),
    )
    out_specs = P(None, ("grp", "bf"))
    return jax.shard_map(shards, mesh=mesh, in_specs=in_specs, out_specs=out_specs, check_vma=False)
```

```python
import jax
import jax.numpy as jnp
from jax import lax
from jax.experimental import pallas as pl
from jax.experimental.pallas import tpu as pltpu
from jax.sharding import PartitionSpec as P

F32, BF16 = jnp.float32, jnp.bfloat16
VMEM = pl.BlockSpec(memory_space=pltpu.VMEM)
HBM = pl.BlockSpec(memory_space=pltpu.HBM)
NT = (((1,), (1,)), ((), ()))


def shifted(value, axis, distance):
    size = lax.axis_size(axis)
    return lax.ppermute(value, axis, [(source, (source + distance) % size) for source in range(size)])


def swapped(value):
    return lax.ppermute(value, "bf", [(n, n ^ 1) for n in range(lax.axis_size("bf"))])


def across(value, bit):
    return lax.ppermute(value, "bf", [(n, n ^ 1 << bit) for n in range(lax.axis_size("bf"))])


def call(body, shapes, specs, flops, moved, *operands, scratch=()):
    return pl.pallas_call(
        body,
        out_shape=shapes,
        in_specs=specs,
        out_specs=jax.tree.map(lambda _: VMEM, shapes),
        scratch_shapes=scratch,
        cost_estimate=pl.CostEstimate(flops=flops, bytes_accessed=moved, transcendentals=0),
        compiler_params=pltpu.CompilerParams(vmem_limit_bytes=16 * 2**20),
    )(*operands)


def block_diagonal(compact, levels):
    k = compact.shape[0]
    lane = lax.broadcasted_iota(jnp.int32, compact.shape, 1)
    parts = []
    for level in range(levels):
        mine = jnp.logical_and(lane >= level * k, lane < (level + 1) * k)
        parts.append(jnp.where(mine, compact, 0.0))
    return jnp.concatenate(parts, axis=0)


def section_weights(compact, levels):
    k = compact.shape[0] // 2
    parts = [block_diagonal(compact[:k], levels), block_diagonal(compact[k:], levels)]
    return jnp.concatenate(parts, axis=0).astype(BF16)


def compact_section(mixing_ref, section, side):
    levels = mixing_ref.shape[0]
    return jnp.concatenate([mixing_ref[level, section, side].astype(F32) for level in range(levels)], axis=1)


def load(field_hbm, col_hbm, mixing_hbm, perm_hbm, xb_ref, col_ref, sent_ref, kept_ref, field_ref, mixing_ref, perm_ref, sems):
    pairs = [(mixing_hbm, mixing_ref), (perm_hbm, perm_ref), (field_hbm, field_ref), (col_hbm, col_ref)]
    copies = [pltpu.make_async_copy(source, target, sems.at[n]) for n, (source, target) in enumerate(pairs)]
    for copy in copies:
        copy.start()
    copies[0].wait()
    copies[1].wait()
    levels, sections, _, k, _ = mixing_ref.shape
    row = lax.broadcasted_iota(jnp.int32, (k, k), 0)
    picks = jnp.concatenate([(row == perm_ref[level : level + 1, :]).astype(F32) for level in range(levels)], axis=1)
    picks = block_diagonal(picks, levels).astype(BF16)
    for section in range(sections):
        for side in range(2):
            mats = jnp.concatenate([mixing_ref[level, section, side].astype(F32) for level in range(levels)], axis=1)
            if section == 0:
                mats = jnp.dot(picks, block_diagonal(mats, levels).astype(BF16), preferred_element_type=F32)
                mats = sum(mats[level * k : (level + 1) * k] for level in range(levels))
            if section < sections - 1:
                sent_ref[section, side * k : (side + 1) * k, :] = mats
            else:
                kept_ref[0, side * k : (side + 1) * k, :] = mats
    copies[2].wait()
    xb_ref[...] = field_ref[...].astype(BF16)
    copies[3].wait()


def project(xb_ref, col_ref, out_ref):
    out_ref[...] = lax.dot_general(xb_ref[...], col_ref[...], NT, preferred_element_type=F32)


def build_weights(levels, *refs):
    *compact_refs, weights_ref = refs
    n = 0
    for compact_ref in compact_refs:
        for section in range(compact_ref.shape[0]):
            weights_ref[n] = section_weights(compact_ref[section], levels)
            n += 1


def exact_dot(value, factor):
    count = value.shape[0]
    high = value.astype(BF16)
    rest = value - high.astype(F32)
    middle = rest.astype(BF16)
    low = (rest - middle.astype(F32)).astype(BF16)
    terms = jnp.dot(jnp.concatenate([high, middle, low], axis=0), factor, preferred_element_type=F32)
    return terms[:count] + (terms[count : 2 * count] + terms[2 * count :])


def section_product(own, other, weights):
    return exact_dot(jnp.concatenate([own, other], axis=1), weights)


def run_sections(sections, final, first_refs, mine_ref, theirs_ref, out_ref):
    weights = (mine_ref, theirs_ref)
    if sections[0]:
        states_ref, other_ref = first_refs
        states, others = [states_ref[0], states_ref[1]], [other_ref[0], other_ref[1]]
    else:
        states = [ref[...] for ref in first_refs]
        others = states[::-1]
    for section in sections:
        count = 1 if section == final else 2
        states = [section_product(states[n], others[n], weights[n][section]) for n in range(count)]
        others = states[::-1]
    if count == 1:
        return states[0]
    out_ref[0], out_ref[1] = states


def step(sections, final, first_ref, second_ref, mine_ref, theirs_ref, out_ref):
    run_sections(sections, final, (first_ref, second_ref), mine_ref, theirs_ref, out_ref)


def level_rank(state, rank_size, half_shift, owner_ref, half):
    first_is_half = jnp.broadcast_to(owner_ref[0:1, 0:1], state.shape) == half_shift
    lane = lax.broadcasted_iota(jnp.int32, state.shape, 1)
    chosen = jnp.logical_xor(lane >= rank_size, first_is_half)
    return (jnp.where(chosen, state, 0.0) if half else jnp.where(chosen, 0.0, state)).astype(BF16)


def last_step(sections, final, rank_size, half_shift, first_ref, second_ref, mine_ref, theirs_ref, row_ref, owner_ref, state_ref, half_ref):
    state = run_sections(sections, final, (first_ref, second_ref), mine_ref, theirs_ref, None)
    state_ref[...] = state
    rank = level_rank(state, rank_size, half_shift, owner_ref, True)
    half_ref[...] = jnp.dot(rank, row_ref[...], preferred_element_type=F32)


def expand_below(rank_size, half_shift, state_ref, row_ref, owner_ref, below_ref):
    rank = level_rank(state_ref[...], rank_size, half_shift, owner_ref, False)
    below_ref[...] = jnp.dot(rank, row_ref[...], preferred_element_type=F32)


def shards(field, leaf_inverse, col_factor, row_factor, mixing, row_owner, rank_perm):
    vectors, rows = field.shape
    order = leaf_inverse.shape[1]
    levels, rank_size, _ = col_factor.shape
    sections = mixing.shape[2]
    bits = lax.axis_size("bf").bit_length() - 1
    groups = lax.axis_size("grp")
    width = levels * rank_size

    def array(*shape, kind=F32):
        return jax.ShapeDtypeStruct(shape, kind)

    in_hbm = [
        pltpu.with_memory_space_constraint(x, pltpu.HBM)
        for x in (field, col_factor.reshape(width, rows), mixing[0], rank_perm)
    ]
    xb, col_here, sent, kept = call(
        load,
        [
            array(vectors, rows, kind=BF16),
            array(width, rows, kind=BF16),
            array(sections - 1, 2 * rank_size, width),
            array(1, 2 * rank_size, width),
        ],
        [HBM] * 4, 8 * width**3, 3 * rows * width, *in_hbm,
        scratch=[
            pltpu.VMEM(field.shape, F32),
            pltpu.VMEM(mixing.shape[1:], BF16),
            pltpu.VMEM(rank_perm.shape, jnp.int32),
            pltpu.SemaphoreType.DMA((4,)),
        ],
    )
    received = swapped(sent)
    state = call(
        project, array(vectors, width), [VMEM, VMEM], 2 * vectors * rows * width, 3 * rows * width, xb, col_here
    )
    first_states = (state, swapped(state))
    weight_cost = (4 * width * width * sections, 8 * width * width * sections)
    mine, theirs = [
        call(
            lambda *refs: build_weights(levels, *refs),
            array(sum(x.shape[0] for x in compacts), 2 * width, width, kind=BF16),
            [VMEM] * len(compacts), *weight_cost, *compacts,
        )
        for compacts in ((sent, kept), (received,))
    ]
    runs = []
    for section in range(sections):
        if section % bits or not section:
            runs.append([section])
        else:
            runs[-1].append(section)
    step_cost = (24 * vectors * width * width, 8 * width * width)
    final = sections - 1
    for run in runs[:-1]:
        states = call(
            lambda *refs, run=run: step(run, final, *refs), array(2, vectors, width), [VMEM] * 4, *step_cost,
            *first_states, mine, theirs,
        )
        first_states = (states, across(states, (run[-1] + 1) % bits))
    expand_cost = (2 * vectors * width * rows, 4 * width * rows)
    expand = row_factor.reshape(width, rows)
    state, out_half = call(
        lambda *refs: last_step(runs[-1], final, rank_size, groups // 2, *refs),
        [array(vectors, width), array(vectors, rows)],
        [VMEM] * 6, *expand_cost, *first_states, mine, theirs, expand, row_owner,
    )
    out_below = call(
        lambda *refs: expand_below(rank_size, groups // 2, *refs), array(vectors, rows),
        [VMEM] * 3, *expand_cost, state, expand, row_owner,
    )
    out_half = shifted(out_half, "grp", groups // 2)
    out_below = shifted(out_below, "grp", groups - 1)
    diag = jnp.einsum(
        "rnl,nlm->rnm",
        xb.reshape(vectors, rows // order, order),
        leaf_inverse,
        preferred_element_type=F32,
    ).reshape(vectors, rows)
    return diag + out_below + out_half


def solution(mesh):
    in_specs = (
        P(None, ("grp", "bf")),
        P(("grp", "bf"), None, None),
        P(None, None, ("grp", "bf")),
        P(None, None, ("grp", "bf")),
        P(("grp", "bf"), None, None, None, None, None),
        P(),
        P(),
    )
    out_specs = P(None, ("grp", "bf"))
    return jax.shard_map(shards, mesh=mesh, in_specs=in_specs, out_specs=out_specs, check_vma=False)
```

```python
import jax
import jax.numpy as jnp
from jax import lax
from jax.experimental import pallas as pl
from jax.experimental.pallas import tpu as pltpu
from jax.sharding import PartitionSpec as P

F32, BF16 = jnp.float32, jnp.bfloat16
VMEM = pl.BlockSpec(memory_space=pltpu.VMEM)
HBM = pl.BlockSpec(memory_space=pltpu.HBM)
NT = (((1,), (1,)), ((), ()))


def shifted(value, axis, distance):
    size = lax.axis_size(axis)
    return lax.ppermute(value, axis, [(source, (source + distance) % size) for source in range(size)])


def swapped(value):
    return lax.ppermute(value, "bf", [(n, n ^ 1) for n in range(lax.axis_size("bf"))])


def across(value, bit):
    return lax.ppermute(value, "bf", [(n, n ^ (1 << bit | 1)) for n in range(lax.axis_size("bf"))])


def call(body, shapes, specs, flops, moved, *operands, scratch=()):
    return pl.pallas_call(
        body,
        out_shape=shapes,
        in_specs=specs,
        out_specs=jax.tree.map(lambda _: VMEM, shapes),
        scratch_shapes=scratch,
        cost_estimate=pl.CostEstimate(flops=flops, bytes_accessed=moved, transcendentals=0),
        compiler_params=pltpu.CompilerParams(vmem_limit_bytes=16 * 2**20),
    )(*operands)


def block_diagonal(compact, levels):
    k = compact.shape[0]
    lane = lax.broadcasted_iota(jnp.int32, compact.shape, 1)
    parts = []
    for level in range(levels):
        mine = jnp.logical_and(lane >= level * k, lane < (level + 1) * k)
        parts.append(jnp.where(mine, compact, 0.0))
    return jnp.concatenate(parts, axis=0)


def section_weights(compact, levels):
    k = compact.shape[0] // 2
    parts = [block_diagonal(compact[:k], levels), block_diagonal(compact[k:], levels)]
    return jnp.concatenate(parts, axis=0).astype(BF16)


def compact_section(mixing_ref, section, side):
    levels = mixing_ref.shape[0]
    return jnp.concatenate([mixing_ref[level, section, side].astype(F32) for level in range(levels)], axis=1)


def load(field_hbm, col_hbm, mixing_hbm, perm_hbm, xb_ref, col_ref, sent_ref, kept_ref, field_ref, mixing_ref, perm_ref, sems):
    pairs = [(mixing_hbm, mixing_ref), (perm_hbm, perm_ref), (field_hbm, field_ref), (col_hbm, col_ref)]
    copies = [pltpu.make_async_copy(source, target, sems.at[n]) for n, (source, target) in enumerate(pairs)]
    for copy in copies:
        copy.start()
    copies[0].wait()
    copies[1].wait()
    levels, sections, _, k, _ = mixing_ref.shape
    row = lax.broadcasted_iota(jnp.int32, (k, k), 0)
    picks = jnp.concatenate([(row == perm_ref[level : level + 1, :]).astype(F32) for level in range(levels)], axis=1)
    picks = block_diagonal(picks, levels).astype(BF16)
    for section in range(sections):
        for side in range(2):
            mats = jnp.concatenate([mixing_ref[level, section, side].astype(F32) for level in range(levels)], axis=1)
            if section == 0:
                mats = jnp.dot(picks, block_diagonal(mats, levels).astype(BF16), preferred_element_type=F32)
                mats = sum(mats[level * k : (level + 1) * k] for level in range(levels))
            if section < sections - 1:
                sent_ref[section, side * k : (side + 1) * k, :] = mats
            else:
                kept_ref[0, side * k : (side + 1) * k, :] = mats
    copies[2].wait()
    xb_ref[...] = field_ref[...].astype(BF16)
    copies[3].wait()


def project(xb_ref, col_ref, out_ref):
    out_ref[...] = lax.dot_general(xb_ref[...], col_ref[...], NT, preferred_element_type=F32)


def build_weights(levels, *refs):
    *compact_refs, weights_ref = refs
    n = 0
    for compact_ref in compact_refs:
        for section in range(compact_ref.shape[0]):
            weights_ref[n] = section_weights(compact_ref[section], levels)
            n += 1


def exact_dot(value, factor):
    count = value.shape[0]
    high = value.astype(BF16)
    rest = value - high.astype(F32)
    middle = rest.astype(BF16)
    low = (rest - middle.astype(F32)).astype(BF16)
    terms = jnp.dot(jnp.concatenate([high, middle, low], axis=0), factor, preferred_element_type=F32)
    return terms[:count] + (terms[count : 2 * count] + terms[2 * count :])


def section_product(own, other, weights):
    return exact_dot(jnp.concatenate([own, other], axis=1), weights)


def run_sections(sections, final, first_refs, mine_ref, theirs_ref, out_ref):
    weights = (mine_ref, theirs_ref)
    if sections[0]:
        states_ref, other_ref = first_refs
        states, others = [states_ref[0], states_ref[1]], [other_ref[1], other_ref[0]]
    else:
        states = [ref[...] for ref in first_refs]
        others = states[::-1]
    for section in sections:
        count = 1 if section == final else 2
        states = [section_product(states[n], others[n], weights[n][section]) for n in range(count)]
        others = states[::-1]
    if count == 1:
        return states[0]
    out_ref[0], out_ref[1] = states


def step(sections, final, first_ref, second_ref, mine_ref, theirs_ref, out_ref):
    run_sections(sections, final, (first_ref, second_ref), mine_ref, theirs_ref, out_ref)


def level_rank(state, rank_size, half_shift, owner_ref, half):
    first_is_half = jnp.broadcast_to(owner_ref[0:1, 0:1], state.shape) == half_shift
    lane = lax.broadcasted_iota(jnp.int32, state.shape, 1)
    chosen = jnp.logical_xor(lane >= rank_size, first_is_half)
    return (jnp.where(chosen, state, 0.0) if half else jnp.where(chosen, 0.0, state)).astype(BF16)


def last_step(sections, final, rank_size, half_shift, first_ref, second_ref, mine_ref, theirs_ref, row_ref, owner_ref, state_ref, half_ref):
    state = run_sections(sections, final, (first_ref, second_ref), mine_ref, theirs_ref, None)
    state_ref[...] = state
    rank = level_rank(state, rank_size, half_shift, owner_ref, True)
    half_ref[...] = jnp.dot(rank, row_ref[...], preferred_element_type=F32)


def expand_below(rank_size, half_shift, state_ref, row_ref, owner_ref, below_ref):
    rank = level_rank(state_ref[...], rank_size, half_shift, owner_ref, False)
    below_ref[...] = jnp.dot(rank, row_ref[...], preferred_element_type=F32)


def shards(field, leaf_inverse, col_factor, row_factor, mixing, row_owner, rank_perm):
    vectors, rows = field.shape
    order = leaf_inverse.shape[1]
    levels, rank_size, _ = col_factor.shape
    sections = mixing.shape[2]
    bits = lax.axis_size("bf").bit_length() - 1
    groups = lax.axis_size("grp")
    width = levels * rank_size

    def array(*shape, kind=F32):
        return jax.ShapeDtypeStruct(shape, kind)

    in_hbm = [
        pltpu.with_memory_space_constraint(x, pltpu.HBM)
        for x in (field, col_factor.reshape(width, rows), mixing[0], rank_perm)
    ]
    xb, col_here, sent, kept = call(
        load,
        [
            array(vectors, rows, kind=BF16),
            array(width, rows, kind=BF16),
            array(sections - 1, 2 * rank_size, width),
            array(1, 2 * rank_size, width),
        ],
        [HBM] * 4, 8 * width**3, 3 * rows * width, *in_hbm,
        scratch=[
            pltpu.VMEM(field.shape, F32),
            pltpu.VMEM(mixing.shape[1:], BF16),
            pltpu.VMEM(rank_perm.shape, jnp.int32),
            pltpu.SemaphoreType.DMA((4,)),
        ],
    )
    received = swapped(sent)
    state = call(
        project, array(vectors, width), [VMEM, VMEM], 2 * vectors * rows * width, 3 * rows * width, xb, col_here
    )
    first_states = (state, swapped(state))
    weight_cost = (4 * width * width * sections, 8 * width * width * sections)
    mine, theirs = [
        call(
            lambda *refs: build_weights(levels, *refs),
            array(sum(x.shape[0] for x in compacts), 2 * width, width, kind=BF16),
            [VMEM] * len(compacts), *weight_cost, *compacts,
        )
        for compacts in ((sent, kept), (received,))
    ]
    runs = []
    for section in range(sections):
        if section % bits or not section:
            runs.append([section])
        else:
            runs[-1].append(section)
    step_cost = (24 * vectors * width * width, 8 * width * width)
    final = sections - 1
    for run in runs[:-1]:
        states = call(
            lambda *refs, run=run: step(run, final, *refs), array(2, vectors, width), [VMEM] * 4, *step_cost,
            *first_states, mine, theirs,
        )
        first_states = (states, across(states, (run[-1] + 1) % bits))
    expand_cost = (2 * vectors * width * rows, 4 * width * rows)
    expand = row_factor.reshape(width, rows)
    state, out_half = call(
        lambda *refs: last_step(runs[-1], final, rank_size, groups // 2, *refs),
        [array(vectors, width), array(vectors, rows)],
        [VMEM] * 6, *expand_cost, *first_states, mine, theirs, expand, row_owner,
    )
    out_below = call(
        lambda *refs: expand_below(rank_size, groups // 2, *refs), array(vectors, rows),
        [VMEM] * 3, *expand_cost, state, expand, row_owner,
    )
    out_half = shifted(out_half, "grp", groups // 2)
    out_below = shifted(out_below, "grp", groups - 1)
    diag = jnp.einsum(
        "rnl,nlm->rnm",
        xb.reshape(vectors, rows // order, order),
        leaf_inverse,
        preferred_element_type=F32,
    ).reshape(vectors, rows)
    return diag + out_below + out_half


def solution(mesh):
    in_specs = (
        P(None, ("grp", "bf")),
        P(("grp", "bf"), None, None),
        P(None, None, ("grp", "bf")),
        P(None, None, ("grp", "bf")),
        P(("grp", "bf"), None, None, None, None, None),
        P(),
        P(),
    )
    out_specs = P(None, ("grp", "bf"))
    return jax.shard_map(shards, mesh=mesh, in_specs=in_specs, out_specs=out_specs, check_vma=False)
```

```python
import jax
import jax.numpy as jnp
from jax import lax
from jax.experimental import pallas as pl
from jax.experimental.pallas import tpu as pltpu
from jax.sharding import PartitionSpec as P

F32, BF16 = jnp.float32, jnp.bfloat16
VMEM = pl.BlockSpec(memory_space=pltpu.VMEM)
HBM = pl.BlockSpec(memory_space=pltpu.HBM)
NT = (((1,), (1,)), ((), ()))


def shifted(value, axis, distance):
    size = lax.axis_size(axis)
    return lax.ppermute(value, axis, [(source, (source + distance) % size) for source in range(size)])


def swapped(value):
    return lax.ppermute(value, "bf", [(n, n ^ 1) for n in range(lax.axis_size("bf"))])


def across(value, bit):
    return lax.ppermute(value, "bf", [(n, n ^ 1 << bit) for n in range(lax.axis_size("bf"))])


def call(body, shapes, specs, flops, moved, *operands, scratch=(), out=VMEM):
    return pl.pallas_call(
        body,
        out_shape=shapes,
        in_specs=specs,
        out_specs=jax.tree.map(lambda _: out, shapes),
        scratch_shapes=scratch,
        cost_estimate=pl.CostEstimate(flops=flops, bytes_accessed=moved, transcendentals=0),
        compiler_params=pltpu.CompilerParams(vmem_limit_bytes=16 * 2**20),
    )(*operands)


def block_diagonal(compact, levels):
    k = compact.shape[0]
    lane = lax.broadcasted_iota(jnp.int32, compact.shape, 1)
    parts = []
    for level in range(levels):
        mine = jnp.logical_and(lane >= level * k, lane < (level + 1) * k)
        parts.append(jnp.where(mine, compact, 0.0))
    return jnp.concatenate(parts, axis=0)


def section_weights(compact, levels):
    k = compact.shape[0] // 2
    parts = [block_diagonal(compact[:k], levels), block_diagonal(compact[k:], levels)]
    return jnp.concatenate(parts, axis=0).astype(BF16)


def compact_section(mixing_ref, section, side):
    levels = mixing_ref.shape[0]
    return jnp.concatenate([mixing_ref[level, section, side].astype(F32) for level in range(levels)], axis=1)


def load(field_hbm, col_hbm, mixing_hbm, perm_hbm, xb_ref, col_ref, sent_ref, kept_ref, field_ref, mixing_ref, perm_ref, sems):
    pairs = [(mixing_hbm, mixing_ref), (perm_hbm, perm_ref), (field_hbm, field_ref), (col_hbm, col_ref)]
    copies = [pltpu.make_async_copy(source, target, sems.at[n]) for n, (source, target) in enumerate(pairs)]
    for copy in copies:
        copy.start()
    copies[0].wait()
    copies[1].wait()
    levels, sections, _, k, _ = mixing_ref.shape
    row = lax.broadcasted_iota(jnp.int32, (k, k), 0)
    picks = jnp.concatenate([(row == perm_ref[level : level + 1, :]).astype(F32) for level in range(levels)], axis=1)
    picks = block_diagonal(picks, levels).astype(BF16)
    for section in range(sections):
        for side in range(2):
            mats = jnp.concatenate([mixing_ref[level, section, side].astype(F32) for level in range(levels)], axis=1)
            if section == 0:
                mats = jnp.dot(picks, block_diagonal(mats, levels).astype(BF16), preferred_element_type=F32)
                mats = sum(mats[level * k : (level + 1) * k] for level in range(levels))
            if section < sections - 1:
                sent_ref[section, side * k : (side + 1) * k, :] = mats
            else:
                kept_ref[0, side * k : (side + 1) * k, :] = mats
    copies[2].wait()
    xb_ref[...] = field_ref[...].astype(BF16)
    copies[3].wait()


def project(xb_ref, col_ref, out_ref):
    out_ref[...] = lax.dot_general(xb_ref[...], col_ref[...], NT, preferred_element_type=F32)


def build_weights(levels, *refs):
    *compact_refs, weights_ref = refs
    n = 0
    for compact_ref in compact_refs:
        for section in range(compact_ref.shape[0]):
            weights_ref[n] = section_weights(compact_ref[section], levels)
            n += 1


def exact_dot(value, factor):
    count = value.shape[0]
    high = value.astype(BF16)
    rest = value - high.astype(F32)
    middle = rest.astype(BF16)
    low = (rest - middle.astype(F32)).astype(BF16)
    terms = jnp.dot(jnp.concatenate([high, middle, low], axis=0), factor, preferred_element_type=F32)
    return terms[:count] + (terms[count : 2 * count] + terms[2 * count :])


def section_product(own, other, weights):
    return exact_dot(jnp.concatenate([own, other], axis=1), weights)


def run_sections(sections, final, first_refs, mine_ref, theirs_ref, out_ref):
    weights = (mine_ref, theirs_ref)
    if sections[0]:
        states_ref, other_ref = first_refs
        states, others = [states_ref[0], states_ref[1]], [other_ref[0], other_ref[1]]
    else:
        states = [ref[...] for ref in first_refs]
        others = states[::-1]
    for section in sections:
        count = 1 if section == final else 2
        states = [section_product(states[n], others[n], weights[n][section]) for n in range(count)]
        others = states[::-1]
    if count == 1:
        return states[0]
    out_ref[0], out_ref[1] = states


def step(sections, final, first_ref, second_ref, mine_ref, theirs_ref, out_ref):
    run_sections(sections, final, (first_ref, second_ref), mine_ref, theirs_ref, out_ref)


def level_rank(state, rank_size, half_shift, owner_ref, half):
    first_is_half = jnp.broadcast_to(owner_ref[0:1, 0:1], state.shape) == half_shift
    lane = lax.broadcasted_iota(jnp.int32, state.shape, 1)
    chosen = jnp.logical_xor(lane >= rank_size, first_is_half)
    return (jnp.where(chosen, state, 0.0) if half else jnp.where(chosen, 0.0, state)).astype(BF16)


def last_step(sections, final, rank_size, half_shift, first_ref, second_ref, mine_ref, theirs_ref, row_ref, owner_ref, state_ref, *half_refs):
    state = run_sections(sections, final, (first_ref, second_ref), mine_ref, theirs_ref, None)
    state_ref[...] = state
    rank = level_rank(state, rank_size, half_shift, owner_ref, True)
    outs = jnp.dot(rank, row_ref[...], preferred_element_type=F32)
    count = half_refs[0].shape[0]
    for n, half_ref in enumerate(half_refs):
        half_ref[...] = outs[n * count : (n + 1) * count]


def expand_below(rank_size, half_shift, state_ref, row_ref, owner_ref, below_ref):
    rank = level_rank(state_ref[...], rank_size, half_shift, owner_ref, False)
    below_ref[...] = jnp.dot(rank, row_ref[...], preferred_element_type=F32)


def combine(diag_ref, below_ref, *refs):
    *half_refs, out_hbm, sum_ref, sems = refs
    count = half_refs[0].shape[0]
    copies = []
    for n, half_ref in enumerate(half_refs):
        part = pl.ds(n * count, count)
        sum_ref[part, :] = diag_ref[part, :] + below_ref[part, :] + half_ref[...]
        copies.append(pltpu.make_async_copy(sum_ref.at[part, :], out_hbm.at[part, :], sems.at[n]))
        copies[-1].start()
    for copy in copies:
        copy.wait()


def shards(field, leaf_inverse, col_factor, row_factor, mixing, row_owner, rank_perm):
    vectors, rows = field.shape
    order = leaf_inverse.shape[1]
    levels, rank_size, _ = col_factor.shape
    sections = mixing.shape[2]
    bits = lax.axis_size("bf").bit_length() - 1
    groups = lax.axis_size("grp")
    width = levels * rank_size

    def array(*shape, kind=F32):
        return jax.ShapeDtypeStruct(shape, kind)

    in_hbm = [
        pltpu.with_memory_space_constraint(x, pltpu.HBM)
        for x in (field, col_factor.reshape(width, rows), mixing[0], rank_perm)
    ]
    xb, col_here, sent, kept = call(
        load,
        [
            array(vectors, rows, kind=BF16),
            array(width, rows, kind=BF16),
            array(sections - 1, 2 * rank_size, width),
            array(1, 2 * rank_size, width),
        ],
        [HBM] * 4, 8 * width**3, 3 * rows * width, *in_hbm,
        scratch=[
            pltpu.VMEM(field.shape, F32),
            pltpu.VMEM(mixing.shape[1:], BF16),
            pltpu.VMEM(rank_perm.shape, jnp.int32),
            pltpu.SemaphoreType.DMA((4,)),
        ],
    )
    received = swapped(sent)
    state = call(
        project, array(vectors, width), [VMEM, VMEM], 2 * vectors * rows * width, 3 * rows * width, xb, col_here
    )
    first_states = (state, swapped(state))
    weight_cost = (4 * width * width * sections, 8 * width * width * sections)
    mine, theirs = [
        call(
            lambda *refs: build_weights(levels, *refs),
            array(sum(x.shape[0] for x in compacts), 2 * width, width, kind=BF16),
            [VMEM] * len(compacts), *weight_cost, *compacts,
        )
        for compacts in ((sent, kept), (received,))
    ]
    runs = []
    for section in range(sections):
        if section % bits or not section:
            runs.append([section])
        else:
            runs[-1].append(section)
    step_cost = (24 * vectors * width * width, 8 * width * width)
    final = sections - 1
    for run in runs[:-1]:
        states = call(
            lambda *refs, run=run: step(run, final, *refs), array(2, vectors, width), [VMEM] * 4, *step_cost,
            *first_states, mine, theirs,
        )
        first_states = (states, across(states, (run[-1] + 1) % bits))
    expand_cost = (2 * vectors * width * rows, 4 * width * rows)
    expand = row_factor.reshape(width, rows)
    parts = 2
    state, *out_half = call(
        lambda *refs: last_step(runs[-1], final, rank_size, groups // 2, *refs),
        [array(vectors, width)] + [array(vectors // parts, rows)] * parts,
        [VMEM] * 6, *expand_cost, *first_states, mine, theirs, expand, row_owner,
    )
    out_below = call(
        lambda *refs: expand_below(rank_size, groups // 2, *refs), array(vectors, rows),
        [VMEM] * 3, *expand_cost, state, expand, row_owner,
    )
    out_half = [shifted(part, "grp", groups // 2) for part in out_half]
    out_below = shifted(out_below, "grp", groups - 1)
    diag = jnp.einsum(
        "rnl,nlm->rnm",
        xb.reshape(vectors, rows // order, order),
        leaf_inverse,
        preferred_element_type=F32,
    ).reshape(vectors, rows)
    return call(
        combine, array(vectors, rows), [VMEM] * (2 + parts), 2 * vectors * rows, 16 * vectors * rows,
        diag, out_below, *out_half,
        scratch=[pltpu.VMEM((vectors, rows), F32), pltpu.SemaphoreType.DMA((parts,))], out=HBM,
    )


def solution(mesh):
    in_specs = (
        P(None, ("grp", "bf")),
        P(("grp", "bf"), None, None),
        P(None, None, ("grp", "bf")),
        P(None, None, ("grp", "bf")),
        P(("grp", "bf"), None, None, None, None, None),
        P(),
        P(),
    )
    out_specs = P(None, ("grp", "bf"))
    return jax.shard_map(shards, mesh=mesh, in_specs=in_specs, out_specs=out_specs, check_vma=False)
```

```python
import jax
import jax.numpy as jnp
from jax import lax
from jax.experimental import pallas as pl
from jax.experimental.pallas import tpu as pltpu
from jax.sharding import PartitionSpec as P

F32, BF16 = jnp.float32, jnp.bfloat16
VMEM = pl.BlockSpec(memory_space=pltpu.VMEM)
HBM = pl.BlockSpec(memory_space=pltpu.HBM)
NT = (((1,), (1,)), ((), ()))


def shifted(value, axis, distance):
    size = lax.axis_size(axis)
    return lax.ppermute(value, axis, [(source, (source + distance) % size) for source in range(size)])


def below_in_half(value):
    half = lax.axis_size("grp") // 2
    pairs = [(g, g - 1 if g % half else g + half - 1) for g in range(2 * half)]
    return lax.ppermute(value, "grp", pairs)


def between_halves(value):
    size, places = lax.axis_size("grp"), lax.axis_size("bf")
    half = size // 2
    pairs = []
    for g in range(size):
        for b in range(places):
            target = ((g + half) % size, b) if g % half == half - 1 else (g, b ^ 2)
            pairs.append((g * places + b, target[0] * places + target[1]))
    return lax.ppermute(value, ("grp", "bf"), pairs)


def swapped(value):
    return lax.ppermute(value, "bf", [(n, n ^ 1) for n in range(lax.axis_size("bf"))])


def across(value, bit):
    return lax.ppermute(value, "bf", [(n, n ^ 1 << bit) for n in range(lax.axis_size("bf"))])


def call(body, shapes, specs, flops, moved, *operands, scratch=()):
    return pl.pallas_call(
        body,
        out_shape=shapes,
        in_specs=specs,
        out_specs=jax.tree.map(lambda _: VMEM, shapes),
        scratch_shapes=scratch,
        cost_estimate=pl.CostEstimate(flops=flops, bytes_accessed=moved, transcendentals=0),
        compiler_params=pltpu.CompilerParams(vmem_limit_bytes=16 * 2**20),
    )(*operands)


def block_diagonal(compact, levels):
    k = compact.shape[0]
    lane = lax.broadcasted_iota(jnp.int32, compact.shape, 1)
    parts = []
    for level in range(levels):
        mine = jnp.logical_and(lane >= level * k, lane < (level + 1) * k)
        parts.append(jnp.where(mine, compact, 0.0))
    return jnp.concatenate(parts, axis=0)


def section_weights(compact, levels):
    k = compact.shape[0] // 2
    parts = [block_diagonal(compact[:k], levels), block_diagonal(compact[k:], levels)]
    return jnp.concatenate(parts, axis=0).astype(BF16)


def compact_section(mixing_ref, section, side):
    levels = mixing_ref.shape[0]
    return jnp.concatenate([mixing_ref[level, section, side].astype(F32) for level in range(levels)], axis=1)


def load(field_hbm, col_hbm, mixing_hbm, perm_hbm, xb_ref, col_ref, sent_ref, kept_ref, field_ref, mixing_ref, perm_ref, sems):
    pairs = [(mixing_hbm, mixing_ref), (perm_hbm, perm_ref), (field_hbm, field_ref), (col_hbm, col_ref)]
    copies = [pltpu.make_async_copy(source, target, sems.at[n]) for n, (source, target) in enumerate(pairs)]
    for copy in copies:
        copy.start()
    copies[0].wait()
    copies[1].wait()
    levels, sections, _, k, _ = mixing_ref.shape
    row = lax.broadcasted_iota(jnp.int32, (k, k), 0)
    picks = jnp.concatenate([(row == perm_ref[level : level + 1, :]).astype(F32) for level in range(levels)], axis=1)
    picks = block_diagonal(picks, levels).astype(BF16)
    for section in range(sections):
        for side in range(2):
            mats = jnp.concatenate([mixing_ref[level, section, side].astype(F32) for level in range(levels)], axis=1)
            if section == 0:
                mats = jnp.dot(picks, block_diagonal(mats, levels).astype(BF16), preferred_element_type=F32)
                mats = sum(mats[level * k : (level + 1) * k] for level in range(levels))
            if section < sections - 1:
                sent_ref[section, side * k : (side + 1) * k, :] = mats
            else:
                kept_ref[0, side * k : (side + 1) * k, :] = mats
    copies[2].wait()
    xb_ref[...] = field_ref[...].astype(BF16)
    copies[3].wait()


def project(xb_ref, col_ref, out_ref):
    out_ref[...] = lax.dot_general(xb_ref[...], col_ref[...], NT, preferred_element_type=F32)


def build_weights(levels, *refs):
    *compact_refs, weights_ref = refs
    n = 0
    for compact_ref in compact_refs:
        for section in range(compact_ref.shape[0]):
            weights_ref[n] = section_weights(compact_ref[section], levels)
            n += 1


def exact_dot(value, factor):
    count = value.shape[0]
    high = value.astype(BF16)
    rest = value - high.astype(F32)
    middle = rest.astype(BF16)
    low = (rest - middle.astype(F32)).astype(BF16)
    terms = jnp.dot(jnp.concatenate([high, middle, low], axis=0), factor, preferred_element_type=F32)
    return terms[:count] + (terms[count : 2 * count] + terms[2 * count :])


def section_product(own, other, weights):
    return exact_dot(jnp.concatenate([own, other], axis=1), weights)


def run_sections(sections, final, first_refs, mine_ref, theirs_ref, out_ref):
    weights = (mine_ref, theirs_ref)
    if sections[0]:
        states_ref, other_ref = first_refs
        states, others = [states_ref[0], states_ref[1]], [other_ref[0], other_ref[1]]
    else:
        states = [ref[...] for ref in first_refs]
        others = states[::-1]
    for section in sections:
        count = 1 if section == final else 2
        states = [section_product(states[n], others[n], weights[n][section]) for n in range(count)]
        others = states[::-1]
    if count == 1:
        return states[0]
    out_ref[0], out_ref[1] = states


def step(sections, final, first_ref, second_ref, mine_ref, theirs_ref, out_ref):
    run_sections(sections, final, (first_ref, second_ref), mine_ref, theirs_ref, out_ref)


def level_rank(state, rank_size, half_shift, owner_ref, half):
    first_is_half = jnp.broadcast_to(owner_ref[0:1, 0:1], state.shape) == half_shift
    lane = lax.broadcasted_iota(jnp.int32, state.shape, 1)
    chosen = jnp.logical_xor(lane >= rank_size, first_is_half)
    return (jnp.where(chosen, state, 0.0) if half else jnp.where(chosen, 0.0, state)).astype(BF16)


def last_step(sections, final, rank_size, half_shift, first_ref, second_ref, mine_ref, theirs_ref, row_ref, owner_ref, state_ref, below_ref):
    state = run_sections(sections, final, (first_ref, second_ref), mine_ref, theirs_ref, None)
    state_ref[...] = state
    rank = level_rank(state, rank_size, half_shift, owner_ref, False)
    below_ref[...] = jnp.dot(rank, row_ref[...], preferred_element_type=F32)


def expand_half(rank_size, half_shift, state_ref, row_ref, owner_ref, half_ref):
    rank = level_rank(state_ref[...], rank_size, half_shift, owner_ref, True)
    half_ref[...] = jnp.dot(rank, row_ref[...], preferred_element_type=F32)


def shards(field, leaf_inverse, col_factor, row_factor, mixing, row_owner, rank_perm):
    vectors, rows = field.shape
    order = leaf_inverse.shape[1]
    levels, rank_size, _ = col_factor.shape
    sections = mixing.shape[2]
    bits = lax.axis_size("bf").bit_length() - 1
    groups = lax.axis_size("grp")
    width = levels * rank_size

    def array(*shape, kind=F32):
        return jax.ShapeDtypeStruct(shape, kind)

    in_hbm = [
        pltpu.with_memory_space_constraint(x, pltpu.HBM)
        for x in (field, col_factor.reshape(width, rows), mixing[0], rank_perm)
    ]
    xb, col_here, sent, kept = call(
        load,
        [
            array(vectors, rows, kind=BF16),
            array(width, rows, kind=BF16),
            array(sections - 1, 2 * rank_size, width),
            array(1, 2 * rank_size, width),
        ],
        [HBM] * 4, 8 * width**3, 3 * rows * width, *in_hbm,
        scratch=[
            pltpu.VMEM(field.shape, F32),
            pltpu.VMEM(mixing.shape[1:], BF16),
            pltpu.VMEM(rank_perm.shape, jnp.int32),
            pltpu.SemaphoreType.DMA((4,)),
        ],
    )
    received = swapped(sent)
    state = call(
        project, array(vectors, width), [VMEM, VMEM], 2 * vectors * rows * width, 3 * rows * width, xb, col_here
    )
    first_states = (state, swapped(state))
    weight_cost = (4 * width * width * sections, 8 * width * width * sections)
    mine, theirs = [
        call(
            lambda *refs: build_weights(levels, *refs),
            array(sum(x.shape[0] for x in compacts), 2 * width, width, kind=BF16),
            [VMEM] * len(compacts), *weight_cost, *compacts,
        )
        for compacts in ((sent, kept), (received,))
    ]
    runs = []
    for section in range(sections):
        if section % bits or not section:
            runs.append([section])
        else:
            runs[-1].append(section)
    step_cost = (24 * vectors * width * width, 8 * width * width)
    final = sections - 1
    for run in runs[:-1]:
        states = call(
            lambda *refs, run=run: step(run, final, *refs), array(2, vectors, width), [VMEM] * 4, *step_cost,
            *first_states, mine, theirs,
        )
        first_states = (states, across(states, (run[-1] + 1) % bits))
    expand_cost = (2 * vectors * width * rows, 4 * width * rows)
    expand = row_factor.reshape(width, rows)
    state, out_below = call(
        lambda *refs: last_step(runs[-1], final, rank_size, groups // 2, *refs),
        [array(vectors, width), array(vectors, rows)],
        [VMEM] * 6, *expand_cost, *first_states, mine, theirs, expand, row_owner,
    )
    out_half = call(
        lambda *refs: expand_half(rank_size, groups // 2, *refs), array(vectors, rows),
        [VMEM] * 3, *expand_cost, state, expand, row_owner,
    )
    out_half = shifted(out_half, "grp", groups // 2)
    turned = below_in_half(out_below)
    crossed = between_halves(turned)
    highest = lax.rem(lax.axis_index("grp"), groups // 2) == groups // 2 - 1
    diag = jnp.einsum(
        "rnl,nlm->rnm",
        xb.reshape(vectors, rows // order, order),
        leaf_inverse,
        preferred_element_type=F32,
    ).reshape(vectors, rows)
    return diag + out_half + jnp.where(highest, crossed, turned)


def solution(mesh):
    in_specs = (
        P(None, ("grp", "bf")),
        P(("grp", "bf"), None, None),
        P(None, None, ("grp", "bf")),
        P(None, None, ("grp", "bf")),
        P(("grp", "bf"), None, None, None, None, None),
        P(),
        P(),
    )
    out_specs = P(None, ("grp", "bf"))
    return jax.shard_map(shards, mesh=mesh, in_specs=in_specs, out_specs=out_specs, check_vma=False)
```

```python
import jax
import jax.numpy as jnp
from jax import lax
from jax.experimental import pallas as pl
from jax.experimental.pallas import tpu as pltpu
from jax.sharding import PartitionSpec as P

F32, BF16 = jnp.float32, jnp.bfloat16
VMEM = pl.BlockSpec(memory_space=pltpu.VMEM)
HBM = pl.BlockSpec(memory_space=pltpu.HBM)
NT = (((1,), (1,)), ((), ()))


def shifted(value, axis, distance):
    size = lax.axis_size(axis)
    return lax.ppermute(value, axis, [(source, (source + distance) % size) for source in range(size)])


def swapped(value):
    return lax.ppermute(value, "bf", [(n, n ^ 1) for n in range(lax.axis_size("bf"))])


def across(value, bit):
    return lax.ppermute(value, "bf", [(n, n ^ 1 << bit) for n in range(lax.axis_size("bf"))])


def call(body, shapes, specs, flops, moved, *operands, scratch=(), out=VMEM):
    return pl.pallas_call(
        body,
        out_shape=shapes,
        in_specs=specs,
        out_specs=jax.tree.map(lambda _: out, shapes),
        scratch_shapes=scratch,
        cost_estimate=pl.CostEstimate(flops=flops, bytes_accessed=moved, transcendentals=0),
        compiler_params=pltpu.CompilerParams(vmem_limit_bytes=16 * 2**20),
    )(*operands)


def block_diagonal(compact, levels):
    k = compact.shape[0]
    lane = lax.broadcasted_iota(jnp.int32, compact.shape, 1)
    parts = []
    for level in range(levels):
        mine = jnp.logical_and(lane >= level * k, lane < (level + 1) * k)
        parts.append(jnp.where(mine, compact, 0.0))
    return jnp.concatenate(parts, axis=0)


def section_weights(compact, levels):
    k = compact.shape[0] // 2
    parts = [block_diagonal(compact[:k], levels), block_diagonal(compact[k:], levels)]
    return jnp.concatenate(parts, axis=0).astype(BF16)


def compact_section(mixing_ref, section, side):
    levels = mixing_ref.shape[0]
    return jnp.concatenate([mixing_ref[level, section, side].astype(F32) for level in range(levels)], axis=1)


def split_rows(source, target, parts):
    count = source.shape[0] // parts
    return [(source.at[pl.ds(n * count, count)], target.at[pl.ds(n * count, count)]) for n in range(parts)]


def load(field_hbm, col_hbm, mixing_hbm, perm_hbm, xb_ref, col_ref, sent_ref, kept_ref, field_ref, mixing_ref, perm_ref, sems):
    levels, sections, _, k, _ = mixing_ref.shape
    first = [(perm_hbm, perm_ref)]
    first += [(mixing_hbm.at[level], mixing_ref.at[level]) for level in range(levels)]
    second = split_rows(field_hbm, field_ref, 2)
    third = split_rows(col_hbm, col_ref, 4)
    copies = [pltpu.make_async_copy(*pair, sems.at[n]) for n, pair in enumerate(first + second + third)]
    for copy in copies:
        copy.start()
    for copy in copies[: len(first)]:
        copy.wait()
    row = lax.broadcasted_iota(jnp.int32, (k, k), 0)
    picks = jnp.concatenate([(row == perm_ref[level : level + 1, :]).astype(F32) for level in range(levels)], axis=1)
    picks = block_diagonal(picks, levels).astype(BF16)
    for section in range(sections):
        for side in range(2):
            mats = jnp.concatenate([mixing_ref[level, section, side].astype(F32) for level in range(levels)], axis=1)
            if section == 0:
                mats = jnp.dot(picks, block_diagonal(mats, levels).astype(BF16), preferred_element_type=F32)
                mats = sum(mats[level * k : (level + 1) * k] for level in range(levels))
            if section < sections - 1:
                sent_ref[section, side * k : (side + 1) * k, :] = mats
            else:
                kept_ref[0, side * k : (side + 1) * k, :] = mats
    for copy in copies[len(first) : -len(third)]:
        copy.wait()
    xb_ref[...] = field_ref[...].astype(BF16)
    for copy in copies[-len(third) :]:
        copy.wait()


def project(xb_ref, col_ref, out_ref):
    out_ref[...] = lax.dot_general(xb_ref[...], col_ref[...], NT, preferred_element_type=F32)


def build_weights(levels, *refs):
    *compact_refs, weights_ref = refs
    n = 0
    for compact_ref in compact_refs:
        for section in range(compact_ref.shape[0]):
            weights_ref[n] = section_weights(compact_ref[section], levels)
            n += 1


def exact_dot(value, factor):
    count = value.shape[0]
    high = value.astype(BF16)
    rest = value - high.astype(F32)
    middle = rest.astype(BF16)
    low = (rest - middle.astype(F32)).astype(BF16)
    terms = jnp.dot(jnp.concatenate([high, middle, low], axis=0), factor, preferred_element_type=F32)
    return terms[:count] + (terms[count : 2 * count] + terms[2 * count :])


def section_product(own, other, weights):
    return exact_dot(jnp.concatenate([own, other], axis=1), weights)


def run_sections(sections, final, first_refs, mine_ref, theirs_ref, out_ref):
    weights = (mine_ref, theirs_ref)
    if sections[0]:
        states_ref, other_ref = first_refs
        states, others = [states_ref[0], states_ref[1]], [other_ref[0], other_ref[1]]
    else:
        states = [ref[...] for ref in first_refs]
        others = states[::-1]
    for section in sections:
        count = 1 if section == final else 2
        states = [section_product(states[n], others[n], weights[n][section]) for n in range(count)]
        others = states[::-1]
    if count == 1:
        return states[0]
    out_ref[0], out_ref[1] = states


def step(sections, final, first_ref, second_ref, mine_ref, theirs_ref, out_ref):
    run_sections(sections, final, (first_ref, second_ref), mine_ref, theirs_ref, out_ref)


def level_rank(state, rank_size, half_shift, owner_ref, half):
    first_is_half = jnp.broadcast_to(owner_ref[0:1, 0:1], state.shape) == half_shift
    lane = lax.broadcasted_iota(jnp.int32, state.shape, 1)
    chosen = jnp.logical_xor(lane >= rank_size, first_is_half)
    return (jnp.where(chosen, state, 0.0) if half else jnp.where(chosen, 0.0, state)).astype(BF16)


def last_step(sections, final, rank_size, half_shift, first_ref, second_ref, mine_ref, theirs_ref, row_ref, owner_ref, state_ref, half_ref):
    state = run_sections(sections, final, (first_ref, second_ref), mine_ref, theirs_ref, None)
    state_ref[...] = state
    rank = level_rank(state, rank_size, half_shift, owner_ref, True)
    half_ref[...] = jnp.dot(rank, row_ref[...], preferred_element_type=F32)


def expand_below(rank_size, half_shift, state_ref, row_ref, owner_ref, below_ref):
    rank = level_rank(state_ref[...], rank_size, half_shift, owner_ref, False)
    below_ref[...] = jnp.dot(rank, row_ref[...], preferred_element_type=F32)


def diagonal(xb_ref, leaf_hbm, out_ref, leaf_ref, sems):
    blocks, order, _ = leaf_hbm.shape
    copies = []
    for n in range(blocks):
        for source, target in split_rows(leaf_hbm.at[n], leaf_ref.at[n], 2):
            copies.append(pltpu.make_async_copy(source, target, sems.at[len(copies)]))
            copies[-1].start()
    for n in range(blocks):
        copies[2 * n].wait()
        copies[2 * n + 1].wait()
        part = pl.ds(n * order, order)
        out_ref[:, part] = jnp.dot(xb_ref[:, part], leaf_ref[n], preferred_element_type=F32)


def combine(half_ref, below_ref, diag_ref, out_hbm, sum_ref, sems):
    parts = sems.shape[0]
    count = sum_ref.shape[1] // parts
    copies = []
    for n in range(parts):
        part = pl.ds(n * count, count)
        sum_ref[:, part] = diag_ref[:, part] + below_ref[:, part] + half_ref[:, part]
        copies.append(pltpu.make_async_copy(sum_ref.at[:, part], out_hbm.at[:, part], sems.at[n]))
        copies[-1].start()
    for copy in copies:
        copy.wait()


def shards(field, leaf_inverse, col_factor, row_factor, mixing, row_owner, rank_perm):
    vectors, rows = field.shape
    order = leaf_inverse.shape[1]
    levels, rank_size, _ = col_factor.shape
    sections = mixing.shape[2]
    bits = lax.axis_size("bf").bit_length() - 1
    groups = lax.axis_size("grp")
    width = levels * rank_size

    def array(*shape, kind=F32):
        return jax.ShapeDtypeStruct(shape, kind)

    in_hbm = [
        pltpu.with_memory_space_constraint(x, pltpu.HBM)
        for x in (field, col_factor.reshape(width, rows), mixing[0], rank_perm)
    ]
    xb, col_here, sent, kept = call(
        load,
        [
            array(vectors, rows, kind=BF16),
            array(width, rows, kind=BF16),
            array(sections - 1, 2 * rank_size, width),
            array(1, 2 * rank_size, width),
        ],
        [HBM] * 4, 8 * width**3, 3 * rows * width, *in_hbm,
        scratch=[
            pltpu.VMEM(field.shape, F32),
            pltpu.VMEM(mixing.shape[1:], BF16),
            pltpu.VMEM(rank_perm.shape, jnp.int32),
            pltpu.SemaphoreType.DMA((1 + levels + 2 + 4,)),
        ],
    )
    received = swapped(sent)
    state = call(
        project, array(vectors, width), [VMEM, VMEM], 2 * vectors * rows * width, 3 * rows * width, xb, col_here
    )
    first_states = (state, swapped(state))
    weight_cost = (4 * width * width * sections, 8 * width * width * sections)
    mine, theirs = [
        call(
            lambda *refs: build_weights(levels, *refs),
            array(sum(x.shape[0] for x in compacts), 2 * width, width, kind=BF16),
            [VMEM] * len(compacts), *weight_cost, *compacts,
        )
        for compacts in ((sent, kept), (received,))
    ]
    runs = []
    for section in range(sections):
        if section % bits or not section:
            runs.append([section])
        else:
            runs[-1].append(section)
    step_cost = (24 * vectors * width * width, 8 * width * width)
    final = sections - 1
    for run in runs[:-1]:
        states = call(
            lambda *refs, run=run: step(run, final, *refs), array(2, vectors, width), [VMEM] * 4, *step_cost,
            *first_states, mine, theirs,
        )
        first_states = (states, across(states, (run[-1] + 1) % bits))
    expand_cost = (2 * vectors * width * rows, 4 * width * rows)
    expand = row_factor.reshape(width, rows)
    state, out_half = call(
        lambda *refs: last_step(runs[-1], final, rank_size, groups // 2, *refs),
        [array(vectors, width), array(vectors, rows)],
        [VMEM] * 6, *expand_cost, *first_states, mine, theirs, expand, row_owner,
    )
    out_below = call(
        lambda *refs: expand_below(rank_size, groups // 2, *refs), array(vectors, rows),
        [VMEM] * 3, *expand_cost, state, expand, row_owner,
    )
    out_half = shifted(out_half, "grp", groups // 2)
    out_below = shifted(out_below, "grp", groups - 1)
    diag = call(
        diagonal, array(vectors, rows), [VMEM, HBM], 2 * vectors * rows * order, 2 * rows * order,
        xb, pltpu.with_memory_space_constraint(leaf_inverse, pltpu.HBM),
        scratch=[pltpu.VMEM(leaf_inverse.shape, BF16), pltpu.SemaphoreType.DMA((2 * leaf_inverse.shape[0],))],
    )
    return call(
        combine, array(vectors, rows), [VMEM] * 3, 2 * vectors * rows, 16 * vectors * rows, out_half, out_below, diag,
        scratch=[pltpu.VMEM((vectors, rows), F32), pltpu.SemaphoreType.DMA((4,))], out=HBM,
    )


def solution(mesh):
    in_specs = (
        P(None, ("grp", "bf")),
        P(("grp", "bf"), None, None),
        P(None, None, ("grp", "bf")),
        P(None, None, ("grp", "bf")),
        P(("grp", "bf"), None, None, None, None, None),
        P(),
        P(),
    )
    out_specs = P(None, ("grp", "bf"))
    return jax.shard_map(shards, mesh=mesh, in_specs=in_specs, out_specs=out_specs, check_vma=False)
```

```python
import jax
import jax.numpy as jnp
from jax import lax
from jax.experimental import pallas as pl
from jax.experimental.pallas import tpu as pltpu
from jax.sharding import PartitionSpec as P

F32, BF16 = jnp.float32, jnp.bfloat16
VMEM = pl.BlockSpec(memory_space=pltpu.VMEM)
HBM = pl.BlockSpec(memory_space=pltpu.HBM)
NT = (((1,), (1,)), ((), ()))


def shifted(value, axis, distance):
    size = lax.axis_size(axis)
    return lax.ppermute(value, axis, [(source, (source + distance) % size) for source in range(size)])


def swapped(value):
    return lax.ppermute(value, "bf", [(n, n ^ 1) for n in range(lax.axis_size("bf"))])


def across(value, bit):
    return lax.ppermute(value, "bf", [(n, n ^ 1 << bit) for n in range(lax.axis_size("bf"))])


def call(body, shapes, specs, flops, moved, *operands, scratch=(), out=VMEM):
    return pl.pallas_call(
        body,
        out_shape=shapes,
        in_specs=specs,
        out_specs=jax.tree.map(lambda _: out, shapes),
        scratch_shapes=scratch,
        cost_estimate=pl.CostEstimate(flops=flops, bytes_accessed=moved, transcendentals=0),
        compiler_params=pltpu.CompilerParams(vmem_limit_bytes=16 * 2**20),
    )(*operands)


def block_diagonal(compact, levels):
    k = compact.shape[0]
    lane = lax.broadcasted_iota(jnp.int32, compact.shape, 1)
    parts = []
    for level in range(levels):
        mine = jnp.logical_and(lane >= level * k, lane < (level + 1) * k)
        parts.append(jnp.where(mine, compact, 0.0))
    return jnp.concatenate(parts, axis=0)


def section_weights(compact, levels):
    k = compact.shape[0] // 2
    parts = [block_diagonal(compact[:k], levels), block_diagonal(compact[k:], levels)]
    return jnp.concatenate(parts, axis=0).astype(BF16)


def compact_section(mixing_ref, section, side):
    levels = mixing_ref.shape[0]
    return jnp.concatenate([mixing_ref[level, section, side].astype(F32) for level in range(levels)], axis=1)


def split_rows(source, target, parts):
    count = source.shape[0] // parts
    return [(source.at[pl.ds(n * count, count)], target.at[pl.ds(n * count, count)]) for n in range(parts)]


def load(groups, field_hbm, col_hbm, mixing_hbm, perm_hbm, xb_ref, col_ref, *refs):
    *out_refs, field_ref, mixing_ref, perm_ref, sems = refs
    levels, sections, _, k, _ = mixing_ref.shape
    first = [(perm_hbm, perm_ref)]
    first += [(mixing_hbm.at[level], mixing_ref.at[level]) for level in range(levels)]
    second = split_rows(field_hbm, field_ref, 2)
    third = split_rows(col_hbm, col_ref, 4)
    copies = [pltpu.make_async_copy(*pair, sems.at[n]) for n, pair in enumerate(first + second + third)]
    for copy in copies:
        copy.start()
    for copy in copies[: len(first)]:
        copy.wait()
    row = lax.broadcasted_iota(jnp.int32, (k, k), 0)
    picks = jnp.concatenate([(row == perm_ref[level : level + 1, :]).astype(F32) for level in range(levels)], axis=1)
    picks = block_diagonal(picks, levels).astype(BF16)
    for section in range(sections):
        for side in range(2):
            mats = jnp.concatenate([mixing_ref[level, section, side].astype(F32) for level in range(levels)], axis=1)
            if section == 0:
                mats = jnp.dot(picks, block_diagonal(mats, levels).astype(BF16), preferred_element_type=F32)
                mats = sum(mats[level * k : (level + 1) * k] for level in range(levels))
            for group, out_ref in zip(groups, out_refs):
                if section in group:
                    out_ref[group.index(section), side * k : (side + 1) * k, :] = mats
    for copy in copies[len(first) : -len(third)]:
        copy.wait()
    xb_ref[...] = field_ref[...].astype(BF16)
    for copy in copies[-len(third) :]:
        copy.wait()


def project(xb_ref, col_ref, out_ref):
    out_ref[...] = lax.dot_general(xb_ref[...], col_ref[...], NT, preferred_element_type=F32)


def build_weights(levels, chosen, *refs):
    for n, (operand, place) in enumerate(chosen):
        refs[-1][n] = section_weights(refs[operand][place], levels)


def exact_dot(value, factor):
    count = value.shape[0]
    high = value.astype(BF16)
    rest = value - high.astype(F32)
    middle = rest.astype(BF16)
    low = (rest - middle.astype(F32)).astype(BF16)
    terms = jnp.dot(jnp.concatenate([high, middle, low], axis=0), factor, preferred_element_type=F32)
    return terms[:count] + (terms[count : 2 * count] + terms[2 * count :])


def section_product(own, other, weights):
    return exact_dot(jnp.concatenate([own, other], axis=1), weights)


def run_sections(sections, final, first_refs, mine_ref, theirs_ref, out_ref):
    weights = (mine_ref, theirs_ref)
    if sections[0]:
        states_ref, other_ref = first_refs
        states, others = [states_ref[0], states_ref[1]], [other_ref[0], other_ref[1]]
    else:
        states = [ref[...] for ref in first_refs]
        others = states[::-1]
    for section in sections:
        count = 1 if section == final else 2
        states = [section_product(states[n], others[n], weights[n][section]) for n in range(count)]
        others = states[::-1]
    if count == 1:
        return states[0]
    out_ref[0], out_ref[1] = states


def step(sections, final, first_ref, second_ref, mine_ref, theirs_ref, out_ref):
    run_sections(sections, final, (first_ref, second_ref), mine_ref, theirs_ref, out_ref)


def first_step(first_ref, second_ref, mine_ref, theirs_ref, received_ref, out_ref):
    count = first_ref.shape[0]
    mine, theirs = first_ref[...], second_ref[...]
    out_ref[:count, :] = section_product(mine, theirs, mine_ref[0])
    out_ref[count : 2 * count, :] = section_product(theirs, mine, theirs_ref[0])
    out_ref[2 * count :, :] = received_ref[1]


def level_rank(state, rank_size, half_shift, owner_ref, half):
    first_is_half = jnp.broadcast_to(owner_ref[0:1, 0:1], state.shape) == half_shift
    lane = lax.broadcasted_iota(jnp.int32, state.shape, 1)
    chosen = jnp.logical_xor(lane >= rank_size, first_is_half)
    return (jnp.where(chosen, state, 0.0) if half else jnp.where(chosen, 0.0, state)).astype(BF16)


def finish(state, rank_size, half_shift, row_ref, owner_ref, state_ref, half_ref):
    state_ref[...] = state
    rank = level_rank(state, rank_size, half_shift, owner_ref, True)
    half_ref[...] = jnp.dot(rank, row_ref[...], preferred_element_type=F32)


def last_step(sections, final, rank_size, half_shift, first_ref, second_ref, mine_ref, theirs_ref, *refs):
    state = run_sections(sections, final, (first_ref, second_ref), mine_ref, theirs_ref, None)
    finish(state, rank_size, half_shift, *refs)


def last_sections(levels, rank_size, half_shift, pair_ref, other_ref, mine_ref, theirs_ref, far_ref, *refs):
    count = (pair_ref.shape[0] - 2 * rank_size) // 2
    mine, theirs = pair_ref[:count, :], pair_ref[count : 2 * count, :]
    far, cross = other_ref[:count, :], other_ref[count : 2 * count, :]
    mine, theirs, far, cross = (
        section_product(mine, far, mine_ref[1]),
        section_product(theirs, cross, theirs_ref[1]),
        section_product(far, mine, far_ref[0]),
        section_product(cross, theirs, section_weights(other_ref[2 * count :, :], levels)),
    )
    mine, far = section_product(mine, theirs, mine_ref[2]), section_product(far, cross, far_ref[1])
    finish(section_product(mine, far, mine_ref[3]), rank_size, half_shift, *refs)


def expand_below(rank_size, half_shift, state_ref, row_ref, owner_ref, below_ref):
    rank = level_rank(state_ref[...], rank_size, half_shift, owner_ref, False)
    below_ref[...] = jnp.dot(rank, row_ref[...], preferred_element_type=F32)


def diagonal(xb_ref, leaf_hbm, out_ref, leaf_ref, sems):
    blocks, order, _ = leaf_hbm.shape
    copies = []
    for n in range(blocks):
        for source, target in split_rows(leaf_hbm.at[n], leaf_ref.at[n], 2):
            copies.append(pltpu.make_async_copy(source, target, sems.at[len(copies)]))
            copies[-1].start()
    for n in range(blocks):
        copies[2 * n].wait()
        copies[2 * n + 1].wait()
        part = pl.ds(n * order, order)
        out_ref[:, part] = jnp.dot(xb_ref[:, part], leaf_ref[n], preferred_element_type=F32)


def combine(half_ref, below_ref, diag_ref, out_hbm, sum_ref, sems):
    parts = sems.shape[0]
    count = sum_ref.shape[1] // parts
    copies = []
    for n in range(parts):
        part = pl.ds(n * count, count)
        sum_ref[:, part] = diag_ref[:, part] + below_ref[:, part] + half_ref[:, part]
        copies.append(pltpu.make_async_copy(sum_ref.at[:, part], out_hbm.at[:, part], sems.at[n]))
        copies[-1].start()
    for copy in copies:
        copy.wait()


def shards(field, leaf_inverse, col_factor, row_factor, mixing, row_owner, rank_perm):
    vectors, rows = field.shape
    order = leaf_inverse.shape[1]
    levels, rank_size, _ = col_factor.shape
    sections = mixing.shape[2]
    bits = lax.axis_size("bf").bit_length() - 1
    groups = lax.axis_size("grp")
    width = levels * rank_size

    def array(*shape, kind=F32):
        return jax.ShapeDtypeStruct(shape, kind)

    in_hbm = [
        pltpu.with_memory_space_constraint(x, pltpu.HBM)
        for x in (field, col_factor.reshape(width, rows), mixing[0], rank_perm)
    ]
    one_round = bits == 2 and sections == 4
    sent_groups = [(0, 1), (1, 2), (3,)] if one_round else [tuple(range(sections - 1)), (sections - 1,)]
    xb, col_here, sent, *kept = call(
        lambda *refs: load(sent_groups, *refs),
        [array(vectors, rows, kind=BF16), array(width, rows, kind=BF16)]
        + [array(len(group), 2 * rank_size, width) for group in sent_groups],
        [HBM] * 4, 8 * width**3, 3 * rows * width, *in_hbm,
        scratch=[
            pltpu.VMEM(field.shape, F32),
            pltpu.VMEM(mixing.shape[1:], BF16),
            pltpu.VMEM(rank_perm.shape, jnp.int32),
            pltpu.SemaphoreType.DMA((1 + levels + 2 + 4,)),
        ],
    )

    def weights(chosen, *compacts):
        return call(
            lambda *refs: build_weights(levels, chosen, *refs), array(len(chosen), 2 * width, width, kind=BF16),
            [VMEM] * len(compacts), 4 * width * width * sections, 8 * width * width * sections, *compacts,
        )

    received = swapped(sent)
    if one_round:
        received_far = across(kept[0], 1)
    state = call(
        project, array(vectors, width), [VMEM, VMEM], 2 * vectors * rows * width, 3 * rows * width, xb, col_here
    )
    first_states = (state, swapped(state))
    step_cost = (24 * vectors * width * width, 8 * width * width)
    final = sections - 1
    if one_round:
        mine = weights([(0, 0), (0, 1), (1, 1), (2, 0)], sent, *kept)
    else:
        mine = weights([(0, n) for n in range(final)] + [(1, 0)], sent, *kept)
        runs = []
        for section in range(sections):
            if section % bits or not section:
                runs.append([section])
            else:
                runs[-1].append(section)
    theirs = weights([(0, n) for n in range(sent.shape[0])], received)
    if one_round:
        states = call(
            first_step, array(2 * (vectors + rank_size), width), [VMEM] * 5, *step_cost,
            *first_states, mine, theirs, received,
        )
        first_states = (states, across(states, 1))
    for run in [] if one_round else runs[:-1]:
        states = call(
            lambda *refs, run=run: step(run, final, *refs), array(2, vectors, width), [VMEM] * 4, *step_cost,
            *first_states, mine, theirs,
        )
        first_states = (states, across(states, (run[-1] + 1) % bits))
    if one_round:
        last_body = lambda *refs: last_sections(levels, *refs)
        last_weights = (mine, theirs, weights([(0, 0), (0, 1)], received_far))
    else:
        last_body = lambda *refs: last_step(runs[-1], final, *refs)
        last_weights = (mine, theirs)
    expand_cost = (2 * vectors * width * rows, 4 * width * rows)
    expand = row_factor.reshape(width, rows)
    state, out_half = call(
        lambda *refs: last_body(rank_size, groups // 2, *refs),
        [array(vectors, width), array(vectors, rows)],
        [VMEM] * (4 + len(last_weights)), *expand_cost, *first_states, *last_weights, expand, row_owner,
    )
    out_below = call(
        lambda *refs: expand_below(rank_size, groups // 2, *refs), array(vectors, rows),
        [VMEM] * 3, *expand_cost, state, expand, row_owner,
    )
    out_half = shifted(out_half, "grp", groups // 2)
    out_below = shifted(out_below, "grp", groups - 1)
    diag = call(
        diagonal, array(vectors, rows), [VMEM, HBM], 2 * vectors * rows * order, 2 * rows * order,
        xb, pltpu.with_memory_space_constraint(leaf_inverse, pltpu.HBM),
        scratch=[pltpu.VMEM(leaf_inverse.shape, BF16), pltpu.SemaphoreType.DMA((2 * leaf_inverse.shape[0],))],
    )
    return call(
        combine, array(vectors, rows), [VMEM] * 3, 2 * vectors * rows, 16 * vectors * rows, out_half, out_below, diag,
        scratch=[pltpu.VMEM((vectors, rows), F32), pltpu.SemaphoreType.DMA((4,))], out=HBM,
    )


def solution(mesh):
    in_specs = (
        P(None, ("grp", "bf")),
        P(("grp", "bf"), None, None),
        P(None, None, ("grp", "bf")),
        P(None, None, ("grp", "bf")),
        P(("grp", "bf"), None, None, None, None, None),
        P(),
        P(),
    )
    out_specs = P(None, ("grp", "bf"))
    return jax.shard_map(shards, mesh=mesh, in_specs=in_specs, out_specs=out_specs, check_vma=False)
```

```python
import jax
import jax.numpy as jnp
from jax import lax
from jax.experimental import pallas as pl
from jax.experimental.pallas import tpu as pltpu
from jax.sharding import PartitionSpec as P

F32, BF16 = jnp.float32, jnp.bfloat16
VMEM = pl.BlockSpec(memory_space=pltpu.VMEM)
HBM = pl.BlockSpec(memory_space=pltpu.HBM)
NT = (((1,), (1,)), ((), ()))


def shifted(value, axis, distance):
    size = lax.axis_size(axis)
    return lax.ppermute(value, axis, [(source, (source + distance) % size) for source in range(size)])


def swapped(value):
    return lax.ppermute(value, "bf", [(n, n ^ 1) for n in range(lax.axis_size("bf"))])


def across(value, bit):
    return lax.ppermute(value, "bf", [(n, n ^ 1 << bit) for n in range(lax.axis_size("bf"))])


def call(body, shapes, specs, flops, moved, *operands, scratch=(), out=VMEM):
    return pl.pallas_call(
        body,
        out_shape=shapes,
        in_specs=specs,
        out_specs=jax.tree.map(lambda _: out, shapes),
        scratch_shapes=scratch,
        cost_estimate=pl.CostEstimate(flops=flops, bytes_accessed=moved, transcendentals=0),
        compiler_params=pltpu.CompilerParams(vmem_limit_bytes=16 * 2**20),
    )(*operands)


def block_diagonal(compact, levels):
    k = compact.shape[0]
    lane = lax.broadcasted_iota(jnp.int32, compact.shape, 1)
    parts = []
    for level in range(levels):
        mine = jnp.logical_and(lane >= level * k, lane < (level + 1) * k)
        parts.append(jnp.where(mine, compact, 0.0))
    return jnp.concatenate(parts, axis=0)


def section_weights(compact, levels):
    k = compact.shape[0] // 2
    parts = [block_diagonal(compact[:k], levels), block_diagonal(compact[k:], levels)]
    return jnp.concatenate(parts, axis=0).astype(BF16)


def compact_section(mixing_ref, section, side):
    levels = mixing_ref.shape[0]
    return jnp.concatenate([mixing_ref[level, section, side].astype(F32) for level in range(levels)], axis=1)


def split_rows(source, target, parts):
    count = source.shape[0] // parts
    return [(source.at[pl.ds(n * count, count)], target.at[pl.ds(n * count, count)]) for n in range(parts)]


def load(groups, field_hbm, col_hbm, mixing_hbm, perm_hbm, xb_ref, sent_ref, *refs):
    *out_refs, field_ref, col_ref, mixing_ref, perm_ref, sems = refs
    levels, sections, _, k, _ = mixing_ref.shape
    vectors = field_ref.shape[0]
    first = [(perm_hbm, perm_ref)]
    first += [(mixing_hbm.at[level], mixing_ref.at[level]) for level in range(levels)]
    second = split_rows(field_hbm, field_ref, 2)
    third = split_rows(col_hbm, col_ref, 4)
    copies = [pltpu.make_async_copy(*pair, sems.at[n]) for n, pair in enumerate(first + second + third)]
    for copy in copies:
        copy.start()
    for copy in copies[: len(first)]:
        copy.wait()
    row = lax.broadcasted_iota(jnp.int32, (k, k), 0)
    picks = jnp.concatenate([(row == perm_ref[level : level + 1, :]).astype(F32) for level in range(levels)], axis=1)
    picks = block_diagonal(picks, levels).astype(BF16)
    for section in range(sections):
        for side in range(2):
            mats = jnp.concatenate([mixing_ref[level, section, side].astype(F32) for level in range(levels)], axis=1)
            if section == 0:
                mats = jnp.dot(picks, block_diagonal(mats, levels).astype(BF16), preferred_element_type=F32)
                mats = sum(mats[level * k : (level + 1) * k] for level in range(levels))
            for n, (group, out_ref) in enumerate(zip(groups, (sent_ref, *out_refs))):
                if section in group:
                    start = (0 if n else vectors) + (2 * group.index(section) + side) * k
                    out_ref[start : start + k, :] = mats
    for copy in copies[len(first) :]:
        copy.wait()
    xb = field_ref[...].astype(BF16)
    xb_ref[...] = xb
    sent_ref[:vectors, :] = lax.dot_general(xb, col_ref[...], NT, preferred_element_type=F32)


def build_weights(levels, chosen, *refs):
    *compact_refs, weights_ref = refs
    size = 2 * weights_ref.shape[2] // levels
    for n, (operand, start) in enumerate(chosen):
        weights_ref[n] = section_weights(compact_refs[operand][start : start + size, :], levels)


def build_pair_weights(levels, start, mine_ref, far_ref, weights_ref):
    k = far_ref.shape[0] // 2
    width = levels * k
    for n, (ref, first) in enumerate(((mine_ref, start), (far_ref, 0))):
        for side in range(2):
            mats = block_diagonal(ref[first + side * k : first + (side + 1) * k, :], levels).astype(BF16)
            row = (n + side) % 2 * width
            weights_ref[row : row + width, n * width : (n + 1) * width] = mats


def exact_dot(value, factor):
    count = value.shape[0]
    high = value.astype(BF16)
    rest = value - high.astype(F32)
    middle = rest.astype(BF16)
    low = (rest - middle.astype(F32)).astype(BF16)
    terms = jnp.dot(jnp.concatenate([high, middle, low], axis=0), factor, preferred_element_type=F32)
    return terms[:count] + (terms[count : 2 * count] + terms[2 * count :])


def section_product(own, other, weights):
    return exact_dot(jnp.concatenate([own, other], axis=1), weights)


def run_sections(sections, final, first_refs, mine_ref, theirs_ref, out_ref):
    weights = (mine_ref, theirs_ref)
    if sections[0]:
        states_ref, other_ref = first_refs
        states, others = [states_ref[0], states_ref[1]], [other_ref[0], other_ref[1]]
    else:
        states = [ref[: out_ref.shape[1], :] for ref in first_refs]
        others = states[::-1]
    for section in sections:
        count = 1 if section == final else 2
        states = [section_product(states[n], others[n], weights[n][section]) for n in range(count)]
        others = states[::-1]
    if count == 1:
        return states[0]
    out_ref[0], out_ref[1] = states


def step(sections, final, first_ref, second_ref, mine_ref, theirs_ref, out_ref):
    run_sections(sections, final, (first_ref, second_ref), mine_ref, theirs_ref, out_ref)


def first_step(sent_ref, received_ref, mine_ref, theirs_ref, kept_ref, out_ref):
    size = kept_ref.shape[0] // 2
    count = (out_ref.shape[0] - size) // 2
    mine, theirs = sent_ref[:count, :], received_ref[:count, :]
    out_ref[:count, :] = section_product(mine, theirs, mine_ref[0])
    out_ref[count : 2 * count, :] = section_product(theirs, mine, theirs_ref[0])
    out_ref[2 * count :, :] = kept_ref[:size, :]


def level_rank(state, rank_size, half_shift, owner_ref, half):
    first_is_half = jnp.broadcast_to(owner_ref[0:1, 0:1], state.shape) == half_shift
    lane = lax.broadcasted_iota(jnp.int32, state.shape, 1)
    chosen = jnp.logical_xor(lane >= rank_size, first_is_half)
    return (jnp.where(chosen, state, 0.0) if half else jnp.where(chosen, 0.0, state)).astype(BF16)


def finish(state, rank_size, half_shift, row_ref, owner_ref, state_ref, half_ref):
    state_ref[...] = state
    rank = level_rank(state, rank_size, half_shift, owner_ref, True)
    half_ref[...] = jnp.dot(rank, row_ref[...], preferred_element_type=F32)


def last_step(sections, final, rank_size, half_shift, first_ref, second_ref, mine_ref, theirs_ref, *refs):
    state = run_sections(sections, final, (first_ref, second_ref), mine_ref, theirs_ref, None)
    finish(state, rank_size, half_shift, *refs)


def last_sections(levels, rank_size, half_shift, pair_ref, other_ref, mine_ref, near_ref, cross_ref, *refs):
    width = levels * rank_size
    count = (pair_ref.shape[0] - 2 * rank_size) // 2
    own, pair = [
        exact_dot(jnp.concatenate([pair_ref[rows, :], other_ref[rows, :]], axis=1), weights_ref[...])
        for rows, weights_ref in ((pl.ds(0, count), near_ref), (pl.ds(count, count), cross_ref))
    ]
    far_weights = section_weights(other_ref[2 * count :, :], levels)
    mine = section_product(own[:, :width], pair[:, :width], mine_ref[1])
    far = section_product(own[:, width:], pair[:, width:], far_weights)
    finish(section_product(mine, far, mine_ref[2]), rank_size, half_shift, *refs)


def expand_below(rank_size, half_shift, state_ref, row_ref, owner_ref, below_ref):
    rank = level_rank(state_ref[...], rank_size, half_shift, owner_ref, False)
    below_ref[...] = jnp.dot(rank, row_ref[...], preferred_element_type=F32)


def diagonal(xb_ref, leaf_hbm, out_ref, leaf_ref, sems):
    blocks, order, _ = leaf_hbm.shape
    copies = []
    for n in range(blocks):
        for source, target in split_rows(leaf_hbm.at[n], leaf_ref.at[n], 2):
            copies.append(pltpu.make_async_copy(source, target, sems.at[len(copies)]))
            copies[-1].start()
    for n in range(blocks):
        copies[2 * n].wait()
        copies[2 * n + 1].wait()
        part = pl.ds(n * order, order)
        out_ref[:, part] = jnp.dot(xb_ref[:, part], leaf_ref[n], preferred_element_type=F32)


def combine(half_ref, below_ref, diag_ref, out_hbm, sum_ref, sems):
    parts = sems.shape[0]
    count = sum_ref.shape[1] // parts
    copies = []
    for n in range(parts):
        part = pl.ds(n * count, count)
        sum_ref[:, part] = diag_ref[:, part] + below_ref[:, part] + half_ref[:, part]
        copies.append(pltpu.make_async_copy(sum_ref.at[:, part], out_hbm.at[:, part], sems.at[n]))
        copies[-1].start()
    for copy in copies:
        copy.wait()


def shards(field, leaf_inverse, col_factor, row_factor, mixing, row_owner, rank_perm):
    vectors, rows = field.shape
    order = leaf_inverse.shape[1]
    levels, rank_size, _ = col_factor.shape
    sections = mixing.shape[2]
    bits = lax.axis_size("bf").bit_length() - 1
    groups = lax.axis_size("grp")
    width = levels * rank_size

    def array(*shape, kind=F32):
        return jax.ShapeDtypeStruct(shape, kind)

    in_hbm = [
        pltpu.with_memory_space_constraint(x, pltpu.HBM)
        for x in (field, col_factor.reshape(width, rows), mixing[0], rank_perm)
    ]
    size = 2 * rank_size
    one_round = bits == 2 and sections == 4 and levels == 2
    groups_sent = [(0, 1), (1,), (2, 3)] if one_round else [tuple(range(sections - 1)), (sections - 1,)]
    xb, sent, *kept = call(
        lambda *refs: load(groups_sent, *refs),
        [array(vectors, rows, kind=BF16)]
        + [array(len(group) * size + (0 if n else vectors), width) for n, group in enumerate(groups_sent)],
        [HBM] * 4, 2 * vectors * rows * width, 3 * rows * width, *in_hbm,
        scratch=[
            pltpu.VMEM(field.shape, F32),
            pltpu.VMEM((width, rows), BF16),
            pltpu.VMEM(mixing.shape[1:], BF16),
            pltpu.VMEM(rank_perm.shape, jnp.int32),
            pltpu.SemaphoreType.DMA((1 + levels + 2 + 4,)),
        ],
    )
    weight_cost = (4 * width * width * sections, 8 * width * width * sections)

    def weights(chosen, *compacts):
        return call(
            lambda *refs: build_weights(levels, chosen, *refs), array(len(chosen), 2 * width, width, kind=BF16),
            [VMEM] * len(compacts), *weight_cost, *compacts,
        )

    def pair_weights(start, mine, far):
        return call(
            lambda *refs: build_pair_weights(levels, start, *refs), array(2 * width, 2 * width, kind=BF16),
            [VMEM] * 2, *weight_cost, mine, far,
        )

    received = swapped(sent)
    step_cost = (24 * vectors * width * width, 8 * width * width)
    final = sections - 1
    if one_round:
        far = across(kept[0], 1)
        mine = weights([(0, vectors), (1, 0), (1, size)], sent, kept[1])
        states = call(
            first_step, array(2 * vectors + size, width), [VMEM] * 5, *step_cost,
            sent, received, mine, weights([(0, vectors)], received), kept[1],
        )
        first_states = (states, across(states, 1))
        last_body = lambda *refs: last_sections(levels, *refs)
        last_weights = (mine, pair_weights(vectors + size, sent, far), pair_weights(vectors + size, received, swapped(far)))
    else:
        starts = [(0, vectors + n * size) for n in range(final)]
        mine, theirs = weights(starts + [(1, 0)], sent, *kept), weights(starts, received)
        runs = []
        for section in range(sections):
            if section % bits or not section:
                runs.append([section])
            else:
                runs[-1].append(section)
        first_states = (sent, received)
        for run in runs[:-1]:
            states = call(
                lambda *refs, run=run: step(run, final, *refs), array(2, vectors, width), [VMEM] * 4, *step_cost,
                *first_states, mine, theirs,
            )
            first_states = (states, across(states, (run[-1] + 1) % bits))
        last_body = lambda *refs: last_step(runs[-1], final, *refs)
        last_weights = (mine, theirs)
    expand_cost = (2 * vectors * width * rows, 4 * width * rows)
    expand = row_factor.reshape(width, rows)
    state, out_half = call(
        lambda *refs: last_body(rank_size, groups // 2, *refs),
        [array(vectors, width), array(vectors, rows)],
        [VMEM] * (4 + len(last_weights)), *expand_cost, *first_states, *last_weights, expand, row_owner,
    )
    out_below = call(
        lambda *refs: expand_below(rank_size, groups // 2, *refs), array(vectors, rows),
        [VMEM] * 3, *expand_cost, state, expand, row_owner,
    )
    out_half = shifted(out_half, "grp", groups // 2)
    out_below = shifted(out_below, "grp", groups - 1)
    diag = call(
        diagonal, array(vectors, rows), [VMEM, HBM], 2 * vectors * rows * order, 2 * rows * order,
        xb, pltpu.with_memory_space_constraint(leaf_inverse, pltpu.HBM),
        scratch=[pltpu.VMEM(leaf_inverse.shape, BF16), pltpu.SemaphoreType.DMA((2 * leaf_inverse.shape[0],))],
    )
    return call(
        combine, array(vectors, rows), [VMEM] * 3, 2 * vectors * rows, 16 * vectors * rows, out_half, out_below, diag,
        scratch=[pltpu.VMEM((vectors, rows), F32), pltpu.SemaphoreType.DMA((4,))], out=HBM,
    )


def solution(mesh):
    in_specs = (
        P(None, ("grp", "bf")),
        P(("grp", "bf"), None, None),
        P(None, None, ("grp", "bf")),
        P(None, None, ("grp", "bf")),
        P(("grp", "bf"), None, None, None, None, None),
        P(),
        P(),
    )
    out_specs = P(None, ("grp", "bf"))
    return jax.shard_map(shards, mesh=mesh, in_specs=in_specs, out_specs=out_specs, check_vma=False)
```

```python
import jax
import jax.numpy as jnp
from jax import lax
from jax.experimental import pallas as pl
from jax.experimental.pallas import tpu as pltpu
from jax.sharding import PartitionSpec as P

F32, BF16 = jnp.float32, jnp.bfloat16
VMEM = pl.BlockSpec(memory_space=pltpu.VMEM)
HBM = pl.BlockSpec(memory_space=pltpu.HBM)
NT = (((1,), (1,)), ((), ()))


def shifted(value, axis, distance):
    size = lax.axis_size(axis)
    return lax.ppermute(value, axis, [(source, (source + distance) % size) for source in range(size)])


def swapped(value):
    return lax.ppermute(value, "bf", [(n, n ^ 1) for n in range(lax.axis_size("bf"))])


def crossed(value):
    return lax.ppermute(value, "bf", [(n, n ^ 3) for n in range(lax.axis_size("bf"))])


def across(value, bit):
    return lax.ppermute(value, "bf", [(n, n ^ 1 << bit) for n in range(lax.axis_size("bf"))])


def call(body, shapes, specs, flops, moved, *operands, scratch=(), out=VMEM):
    return pl.pallas_call(
        body,
        out_shape=shapes,
        in_specs=specs,
        out_specs=jax.tree.map(lambda _: out, shapes),
        scratch_shapes=scratch,
        cost_estimate=pl.CostEstimate(flops=flops, bytes_accessed=moved, transcendentals=0),
        compiler_params=pltpu.CompilerParams(vmem_limit_bytes=16 * 2**20),
    )(*operands)


def block_diagonal(compact, levels):
    k = compact.shape[0]
    lane = lax.broadcasted_iota(jnp.int32, compact.shape, 1)
    parts = []
    for level in range(levels):
        mine = jnp.logical_and(lane >= level * k, lane < (level + 1) * k)
        parts.append(jnp.where(mine, compact, 0.0))
    return jnp.concatenate(parts, axis=0)


def section_weights(compact, levels):
    k = compact.shape[0] // 2
    parts = [block_diagonal(compact[:k], levels), block_diagonal(compact[k:], levels)]
    return jnp.concatenate(parts, axis=0).astype(BF16)


def compact_section(mixing_ref, section, side):
    levels = mixing_ref.shape[0]
    return jnp.concatenate([mixing_ref[level, section, side].astype(F32) for level in range(levels)], axis=1)


def split(source, target, parts, axis):
    count = source.shape[axis] // parts
    places = [(slice(None),) * axis + (pl.ds(n * count, count),) for n in range(parts)]
    return [(source.at[place], target.at[place]) for place in places]


def load(groups, field_hbm, col_hbm, mixing_hbm, perm_hbm, xb_ref, sent_ref, *refs):
    *out_refs, field_ref, col_ref, mixing_ref, perm_ref, sems = refs
    levels, sections, _, k, _ = mixing_ref.shape
    vectors = field_ref.shape[0]
    first = [(perm_hbm, perm_ref)]
    first += [(mixing_hbm.at[level], mixing_ref.at[level]) for level in range(levels)]
    parts = 4
    second = split(field_hbm, field_ref, parts, 1)
    third = split(col_hbm, col_ref, parts, 1)
    copies = [pltpu.make_async_copy(*pair, sems.at[n]) for n, pair in enumerate(first + second + third)]
    for copy in copies:
        copy.start()
    for copy in copies[: len(first)]:
        copy.wait()
    row = lax.broadcasted_iota(jnp.int32, (k, k), 0)
    picks = jnp.concatenate([(row == perm_ref[level : level + 1, :]).astype(F32) for level in range(levels)], axis=1)
    picks = block_diagonal(picks, levels).astype(BF16)
    for section in range(sections):
        for side in range(2):
            mats = jnp.concatenate([mixing_ref[level, section, side].astype(F32) for level in range(levels)], axis=1)
            if section == 0:
                mats = jnp.dot(picks, block_diagonal(mats, levels).astype(BF16), preferred_element_type=F32)
                mats = sum(mats[level * k : (level + 1) * k] for level in range(levels))
            for n, (group, out_ref) in enumerate(zip(groups, (sent_ref, *out_refs))):
                if section in group:
                    start = (0 if n else vectors) + (2 * group.index(section) + side) * k
                    out_ref[start : start + k, :] = mats
    count = field_ref.shape[1] // parts
    state = None
    for n in range(parts):
        copies[len(first) + n].wait()
        copies[len(first) + parts + n].wait()
        part = pl.ds(n * count, count)
        xb = field_ref[:, part].astype(BF16)
        xb_ref[:, part] = xb
        term = lax.dot_general(xb, col_ref[:, part], NT, preferred_element_type=F32)
        state = term if state is None else state + term
    sent_ref[:vectors, :] = state


def build_weights(levels, chosen, *refs):
    *compact_refs, weights_ref = refs
    size = 2 * weights_ref.shape[2] // levels
    for n, (operand, start) in enumerate(chosen):
        weights_ref[n] = section_weights(compact_refs[operand][start : start + size, :], levels)


def build_pair_weights(levels, start, mine_ref, far_ref, weights_ref):
    k = far_ref.shape[0] // 2
    width = levels * k
    for n, (ref, first) in enumerate(((mine_ref, start), (far_ref, 0))):
        for side in range(2):
            mats = block_diagonal(ref[first + side * k : first + (side + 1) * k, :], levels).astype(BF16)
            row = (n + side) % 2 * width
            weights_ref[row : row + width, n * width : (n + 1) * width] = mats


def exact_dot(value, factor):
    count = value.shape[0]
    high = value.astype(BF16)
    rest = value - high.astype(F32)
    middle = rest.astype(BF16)
    low = (rest - middle.astype(F32)).astype(BF16)
    terms = jnp.dot(jnp.concatenate([high, middle, low], axis=0), factor, preferred_element_type=F32)
    return terms[:count] + (terms[count : 2 * count] + terms[2 * count :])


def section_product(own, other, weights):
    return exact_dot(jnp.concatenate([own, other], axis=1), weights)


def run_sections(sections, final, first_refs, mine_ref, theirs_ref, out_ref):
    weights = (mine_ref, theirs_ref)
    if sections[0]:
        states_ref, other_ref = first_refs
        states, others = [states_ref[0], states_ref[1]], [other_ref[0], other_ref[1]]
    else:
        states = [ref[: out_ref.shape[1], :] for ref in first_refs]
        others = states[::-1]
    for section in sections:
        count = 1 if section == final else 2
        states = [section_product(states[n], others[n], weights[n][section]) for n in range(count)]
        others = states[::-1]
    if count == 1:
        return states[0]
    out_ref[0], out_ref[1] = states


def step(sections, final, first_ref, second_ref, mine_ref, theirs_ref, out_ref):
    run_sections(sections, final, (first_ref, second_ref), mine_ref, theirs_ref, out_ref)


def first_step(size, sent_ref, received_ref, mine_ref, theirs_ref, out_ref):
    count = (out_ref.shape[0] - size) // 2
    mine, theirs = sent_ref[:count, :], received_ref[:count, :]
    out_ref[:count, :] = section_product(mine, theirs, mine_ref[0])
    out_ref[count : 2 * count, :] = section_product(theirs, mine, theirs_ref[0])
    out_ref[2 * count :, :] = received_ref[-size:, :]


def level_rank(state, rank_size, half_shift, owner_ref, half):
    first_is_half = jnp.broadcast_to(owner_ref[0:1, 0:1], state.shape) == half_shift
    lane = lax.broadcasted_iota(jnp.int32, state.shape, 1)
    chosen = jnp.logical_xor(lane >= rank_size, first_is_half)
    return (jnp.where(chosen, state, 0.0) if half else jnp.where(chosen, 0.0, state)).astype(BF16)


def finish(state, rank_size, half_shift, row_ref, owner_ref, half_ref, below_ref):
    ranks = [level_rank(state, rank_size, half_shift, owner_ref, half) for half in (True, False)]
    outs = jnp.dot(jnp.concatenate(ranks, axis=0), row_ref[...], preferred_element_type=F32)
    half_ref[...] = outs[: state.shape[0]]
    below_ref[...] = outs[state.shape[0] :]


def last_step(sections, final, rank_size, half_shift, first_ref, second_ref, mine_ref, theirs_ref, *refs):
    state = run_sections(sections, final, (first_ref, second_ref), mine_ref, theirs_ref, None)
    finish(state, rank_size, half_shift, *refs)


def last_sections(levels, rank_size, half_shift, pair_ref, other_ref, mine_ref, near_ref, cross_ref, *refs):
    width = levels * rank_size
    count = (pair_ref.shape[0] - 2 * rank_size) // 2
    own, pair = [
        exact_dot(jnp.concatenate([pair_ref[here, :], other_ref[there, :]], axis=1), weights_ref[...])
        for here, there, weights_ref in (
            (pl.ds(0, count), pl.ds(count, count), near_ref),
            (pl.ds(count, count), pl.ds(0, count), cross_ref),
        )
    ]
    far_weights = section_weights(other_ref[2 * count :, :], levels)
    mine = section_product(own[:, :width], pair[:, :width], mine_ref[1])
    far = section_product(own[:, width:], pair[:, width:], far_weights)
    finish(section_product(mine, far, mine_ref[2]), rank_size, half_shift, *refs)


def diagonal(xb_ref, leaf_hbm, out_ref, leaf_ref, sems):
    blocks, order, _ = leaf_hbm.shape
    copies = []
    for n in range(blocks):
        for source, target in split(leaf_hbm.at[n], leaf_ref.at[n], 2, 0):
            copies.append(pltpu.make_async_copy(source, target, sems.at[len(copies)]))
            copies[-1].start()
    for n in range(blocks):
        copies[2 * n].wait()
        copies[2 * n + 1].wait()
        part = pl.ds(n * order, order)
        out_ref[:, part] = jnp.dot(xb_ref[:, part], leaf_ref[n], preferred_element_type=F32)


def combine(half_ref, below_ref, diag_ref, out_hbm, sum_ref, sems):
    parts = sems.shape[0]
    count = sum_ref.shape[1] // parts
    copies = []
    for n in range(parts):
        part = pl.ds(n * count, count)
        sum_ref[:, part] = diag_ref[:, part] + below_ref[:, part] + half_ref[:, part]
        copies.append(pltpu.make_async_copy(sum_ref.at[:, part], out_hbm.at[:, part], sems.at[n]))
        copies[-1].start()
    for copy in copies:
        copy.wait()


def shards(field, leaf_inverse, col_factor, row_factor, mixing, row_owner, rank_perm):
    vectors, rows = field.shape
    order = leaf_inverse.shape[1]
    levels, rank_size, _ = col_factor.shape
    sections = mixing.shape[2]
    bits = lax.axis_size("bf").bit_length() - 1
    groups = lax.axis_size("grp")
    width = levels * rank_size

    def array(*shape, kind=F32):
        return jax.ShapeDtypeStruct(shape, kind)

    in_hbm = [
        pltpu.with_memory_space_constraint(x, pltpu.HBM)
        for x in (field, col_factor.reshape(width, rows), mixing[0], rank_perm)
    ]
    size = 2 * rank_size
    one_round = bits == 2 and sections == 4 and levels == 2
    groups_sent = [(0, 1, 2), (1,), (2, 3)] if one_round else [tuple(range(sections - 1)), (sections - 1,)]
    xb, sent, *kept = call(
        lambda *refs: load(groups_sent, *refs),
        [array(vectors, rows, kind=BF16)]
        + [array(len(group) * size + (0 if n else vectors), width) for n, group in enumerate(groups_sent)],
        [HBM] * 4, 2 * vectors * rows * width, 3 * rows * width, *in_hbm,
        scratch=[
            pltpu.VMEM(field.shape, F32),
            pltpu.VMEM((width, rows), BF16),
            pltpu.VMEM(mixing.shape[1:], BF16),
            pltpu.VMEM(rank_perm.shape, jnp.int32),
            pltpu.SemaphoreType.DMA((1 + levels + 4 + 4,)),
        ],
    )
    weight_cost = (4 * width * width * sections, 8 * width * width * sections)

    def weights(chosen, *compacts):
        return call(
            lambda *refs: build_weights(levels, chosen, *refs), array(len(chosen), 2 * width, width, kind=BF16),
            [VMEM] * len(compacts), *weight_cost, *compacts,
        )

    def pair_weights(start, mine, far):
        return call(
            lambda *refs: build_pair_weights(levels, start, *refs), array(2 * width, 2 * width, kind=BF16),
            [VMEM] * 2, *weight_cost, mine, far,
        )

    received = swapped(sent)
    step_cost = (24 * vectors * width * width, 8 * width * width)
    final = sections - 1
    if one_round:
        cross = crossed(kept[0])
        mine = weights([(0, vectors), (1, 0), (1, size)], sent, kept[1])
        states = call(
            lambda *refs: first_step(size, *refs), array(2 * vectors + size, width), [VMEM] * 4, *step_cost,
            sent, received, mine, weights([(0, vectors)], received),
        )
        first_states = (states, crossed(states))
        last_body = lambda *refs: last_sections(levels, *refs)
        last_weights = (mine, pair_weights(vectors + size, sent, swapped(cross)), pair_weights(vectors + size, received, cross))
    else:
        starts = [(0, vectors + n * size) for n in range(final)]
        mine, theirs = weights(starts + [(1, 0)], sent, *kept), weights(starts, received)
        runs = []
        for section in range(sections):
            if section % bits or not section:
                runs.append([section])
            else:
                runs[-1].append(section)
        first_states = (sent, received)
        for run in runs[:-1]:
            states = call(
                lambda *refs, run=run: step(run, final, *refs), array(2, vectors, width), [VMEM] * 4, *step_cost,
                *first_states, mine, theirs,
            )
            first_states = (states, across(states, (run[-1] + 1) % bits))
        last_body = lambda *refs: last_step(runs[-1], final, *refs)
        last_weights = (mine, theirs)
    expand_cost = (2 * vectors * width * rows, 4 * width * rows)
    expand = row_factor.reshape(width, rows)
    out_half, out_below = call(
        lambda *refs: last_body(rank_size, groups // 2, *refs), [array(vectors, rows)] * 2,
        [VMEM] * (4 + len(last_weights)), *expand_cost, *first_states, *last_weights, expand, row_owner,
    )
    out_half = shifted(out_half, "grp", groups // 2)
    out_below = shifted(out_below, "grp", groups - 1)
    diag = call(
        diagonal, array(vectors, rows), [VMEM, HBM], 2 * vectors * rows * order, 2 * rows * order,
        xb, pltpu.with_memory_space_constraint(leaf_inverse, pltpu.HBM),
        scratch=[pltpu.VMEM(leaf_inverse.shape, BF16), pltpu.SemaphoreType.DMA((2 * leaf_inverse.shape[0],))],
    )
    return call(
        combine, array(vectors, rows), [VMEM] * 3, 2 * vectors * rows, 16 * vectors * rows, out_half, out_below, diag,
        scratch=[pltpu.VMEM((vectors, rows), F32), pltpu.SemaphoreType.DMA((4,))], out=HBM,
    )


def solution(mesh):
    in_specs = (
        P(None, ("grp", "bf")),
        P(("grp", "bf"), None, None),
        P(None, None, ("grp", "bf")),
        P(None, None, ("grp", "bf")),
        P(("grp", "bf"), None, None, None, None, None),
        P(),
        P(),
    )
    out_specs = P(None, ("grp", "bf"))
    return jax.shard_map(shards, mesh=mesh, in_specs=in_specs, out_specs=out_specs, check_vma=False)
```

```python
import jax
import jax.numpy as jnp
from jax import lax
from jax.experimental import pallas as pl
from jax.experimental.pallas import tpu as pltpu
from jax.sharding import PartitionSpec as P

F32, BF16 = jnp.float32, jnp.bfloat16
VMEM = pl.BlockSpec(memory_space=pltpu.VMEM)
HBM = pl.BlockSpec(memory_space=pltpu.HBM)
NT = (((1,), (1,)), ((), ()))


def shifted(value, axis, distance):
    size = lax.axis_size(axis)
    return lax.ppermute(value, axis, [(source, (source + distance) % size) for source in range(size)])


def swapped(value):
    return lax.ppermute(value, "bf", [(n, n ^ 1) for n in range(lax.axis_size("bf"))])


def crossed(value):
    return lax.ppermute(value, "bf", [(n, n ^ 3) for n in range(lax.axis_size("bf"))])


def across(value, bit):
    return lax.ppermute(value, "bf", [(n, n ^ 1 << bit) for n in range(lax.axis_size("bf"))])


def call(body, shapes, specs, flops, moved, *operands, scratch=(), out=VMEM):
    return pl.pallas_call(
        body,
        out_shape=shapes,
        in_specs=specs,
        out_specs=jax.tree.map(lambda _: out, shapes),
        scratch_shapes=scratch,
        cost_estimate=pl.CostEstimate(flops=flops, bytes_accessed=moved, transcendentals=0),
        compiler_params=pltpu.CompilerParams(vmem_limit_bytes=16 * 2**20),
    )(*operands)


def block_diagonal(compact, levels):
    k = compact.shape[0]
    lane = lax.broadcasted_iota(jnp.int32, compact.shape, 1)
    parts = []
    for level in range(levels):
        mine = jnp.logical_and(lane >= level * k, lane < (level + 1) * k)
        parts.append(jnp.where(mine, compact, 0.0))
    return jnp.concatenate(parts, axis=0)


def section_weights(compact, levels):
    k = compact.shape[0] // 2
    parts = [block_diagonal(compact[:k], levels), block_diagonal(compact[k:], levels)]
    return jnp.concatenate(parts, axis=0).astype(BF16)


def compact_section(mixing_ref, section, side):
    levels = mixing_ref.shape[0]
    return jnp.concatenate([mixing_ref[level, section, side].astype(F32) for level in range(levels)], axis=1)


def split(source, target, parts, axis):
    count = source.shape[axis] // parts
    places = [(slice(None),) * axis + (pl.ds(n * count, count),) for n in range(parts)]
    return [(source.at[place], target.at[place]) for place in places]


def load(groups, field_hbm, col_hbm, mixing_hbm, perm_hbm, xb_ref, sent_ref, *refs):
    *out_refs, field_ref, col_ref, mixing_ref, perm_ref, sems = refs
    levels, sections, _, k, _ = mixing_ref.shape
    vectors = field_ref.shape[0]
    first = [(perm_hbm, perm_ref)]
    first += [(mixing_hbm.at[level], mixing_ref.at[level]) for level in range(levels)]
    second = split(field_hbm, field_ref, 2, 0)
    third = split(col_hbm, col_ref, 4, 0)
    copies = [pltpu.make_async_copy(*pair, sems.at[n]) for n, pair in enumerate(first + second + third)]
    for copy in copies:
        copy.start()
    for copy in copies[: len(first)]:
        copy.wait()
    row = lax.broadcasted_iota(jnp.int32, (k, k), 0)
    picks = jnp.concatenate([(row == perm_ref[level : level + 1, :]).astype(F32) for level in range(levels)], axis=1)
    picks = block_diagonal(picks, levels).astype(BF16)
    for section in range(sections):
        for side in range(2):
            mats = jnp.concatenate([mixing_ref[level, section, side].astype(F32) for level in range(levels)], axis=1)
            if section == 0:
                mats = jnp.dot(picks, block_diagonal(mats, levels).astype(BF16), preferred_element_type=F32)
                mats = sum(mats[level * k : (level + 1) * k] for level in range(levels))
            for n, (group, out_ref) in enumerate(zip(groups, (sent_ref, *out_refs))):
                if section in group:
                    start = (0 if n else vectors) + (2 * group.index(section) + side) * k
                    out_ref[start : start + k, :] = mats
    for copy in copies[len(first) :]:
        copy.wait()
    xb = field_ref[...].astype(BF16)
    xb_ref[...] = xb
    sent_ref[:vectors, :] = lax.dot_general(xb, col_ref[...], NT, preferred_element_type=F32)


def build_weights(levels, chosen, *refs):
    *compact_refs, weights_ref = refs
    size = 2 * weights_ref.shape[2] // levels
    for n, (operand, start) in enumerate(chosen):
        weights_ref[n] = section_weights(compact_refs[operand][start : start + size, :], levels)


def build_pair_weights(levels, start, mine_ref, far_ref, weights_ref):
    k = far_ref.shape[0] // 2
    width = levels * k
    for n, (ref, first) in enumerate(((mine_ref, start), (far_ref, 0))):
        for side in range(2):
            mats = block_diagonal(ref[first + side * k : first + (side + 1) * k, :], levels).astype(BF16)
            row = (n + side) % 2 * width
            weights_ref[row : row + width, n * width : (n + 1) * width] = mats


def exact_dot(value, factor):
    count = value.shape[0]
    high = value.astype(BF16)
    rest = value - high.astype(F32)
    middle = rest.astype(BF16)
    low = (rest - middle.astype(F32)).astype(BF16)
    terms = jnp.dot(jnp.concatenate([high, middle, low], axis=0), factor, preferred_element_type=F32)
    return terms[:count] + (terms[count : 2 * count] + terms[2 * count :])


def section_product(own, other, weights):
    return exact_dot(jnp.concatenate([own, other], axis=1), weights)


def run_sections(sections, final, first_refs, mine_ref, theirs_ref, out_ref):
    weights = (mine_ref, theirs_ref)
    if sections[0]:
        states_ref, other_ref = first_refs
        states, others = [states_ref[0], states_ref[1]], [other_ref[0], other_ref[1]]
    else:
        states = [ref[: out_ref.shape[1], :] for ref in first_refs]
        others = states[::-1]
    for section in sections:
        count = 1 if section == final else 2
        states = [section_product(states[n], others[n], weights[n][section]) for n in range(count)]
        others = states[::-1]
    if count == 1:
        return states[0]
    out_ref[0], out_ref[1] = states


def step(sections, final, first_ref, second_ref, mine_ref, theirs_ref, out_ref):
    run_sections(sections, final, (first_ref, second_ref), mine_ref, theirs_ref, out_ref)


def first_step(size, sent_ref, received_ref, mine_ref, theirs_ref, kept_ref, out_ref):
    count = (out_ref.shape[0] - size) // 2
    mine, theirs = sent_ref[:count, :], received_ref[:count, :]
    out_ref[:count, :] = section_product(mine, theirs, mine_ref[0])
    out_ref[count : 2 * count, :] = section_product(theirs, mine, theirs_ref[0])
    out_ref[2 * count :, :] = kept_ref[:size, :]


def level_rank(state, rank_size, half_shift, owner_ref, half):
    first_is_half = jnp.broadcast_to(owner_ref[0:1, 0:1], state.shape) == half_shift
    lane = lax.broadcasted_iota(jnp.int32, state.shape, 1)
    chosen = jnp.logical_xor(lane >= rank_size, first_is_half)
    return (jnp.where(chosen, state, 0.0) if half else jnp.where(chosen, 0.0, state)).astype(BF16)


def finish(state, rank_size, half_shift, row_ref, owner_ref, half_ref, below_ref):
    ranks = [level_rank(state, rank_size, half_shift, owner_ref, half) for half in (True, False)]
    outs = jnp.dot(jnp.concatenate(ranks, axis=0), row_ref[...], preferred_element_type=F32)
    half_ref[...] = outs[: state.shape[0]]
    below_ref[...] = outs[state.shape[0] :]


def last_step(sections, final, rank_size, half_shift, first_ref, second_ref, mine_ref, theirs_ref, *refs):
    state = run_sections(sections, final, (first_ref, second_ref), mine_ref, theirs_ref, None)
    finish(state, rank_size, half_shift, *refs)


def last_sections(levels, rank_size, half_shift, pair_ref, other_ref, mine_ref, near_ref, cross_ref, *refs):
    width = levels * rank_size
    count = (pair_ref.shape[0] - 2 * rank_size) // 2
    own, pair = [
        exact_dot(jnp.concatenate([pair_ref[rows, :], other_ref[rows, :]], axis=1), weights_ref[...])
        for rows, weights_ref in ((pl.ds(0, count), near_ref), (pl.ds(count, count), cross_ref))
    ]
    far_weights = section_weights(other_ref[2 * count :, :], levels)
    mine = section_product(own[:, :width], pair[:, :width], mine_ref[1])
    far = section_product(own[:, width:], pair[:, width:], far_weights)
    finish(section_product(mine, far, mine_ref[2]), rank_size, half_shift, *refs)


def diagonal(xb_ref, leaf_hbm, out_ref, leaf_ref, sems):
    blocks, order, _ = leaf_hbm.shape
    copies = []
    for n in range(blocks):
        for source, target in split(leaf_hbm.at[n], leaf_ref.at[n], 2, 0):
            copies.append(pltpu.make_async_copy(source, target, sems.at[len(copies)]))
            copies[-1].start()
    for n in range(blocks):
        copies[2 * n].wait()
        copies[2 * n + 1].wait()
        part = pl.ds(n * order, order)
        out_ref[:, part] = jnp.dot(xb_ref[:, part], leaf_ref[n], preferred_element_type=F32)


def combine(half_ref, below_ref, diag_ref, out_hbm, sum_ref, sems):
    parts = sems.shape[0]
    count = sum_ref.shape[1] // parts
    copies = []
    for n in range(parts):
        part = pl.ds(n * count, count)
        sum_ref[:, part] = diag_ref[:, part] + below_ref[:, part] + half_ref[:, part]
        copies.append(pltpu.make_async_copy(sum_ref.at[:, part], out_hbm.at[:, part], sems.at[n]))
        copies[-1].start()
    for copy in copies:
        copy.wait()


def shards(field, leaf_inverse, col_factor, row_factor, mixing, row_owner, rank_perm):
    vectors, rows = field.shape
    order = leaf_inverse.shape[1]
    levels, rank_size, _ = col_factor.shape
    sections = mixing.shape[2]
    bits = lax.axis_size("bf").bit_length() - 1
    groups = lax.axis_size("grp")
    width = levels * rank_size

    def array(*shape, kind=F32):
        return jax.ShapeDtypeStruct(shape, kind)

    in_hbm = [
        pltpu.with_memory_space_constraint(x, pltpu.HBM)
        for x in (field, col_factor.reshape(width, rows), mixing[0], rank_perm)
    ]
    size = 2 * rank_size
    one_round = bits == 2 and sections == 4 and levels == 2
    groups_sent = [(0, 1), (1,), (2, 3)] if one_round else [tuple(range(sections - 1)), (sections - 1,)]
    xb, sent, *kept = call(
        lambda *refs: load(groups_sent, *refs),
        [array(vectors, rows, kind=BF16)]
        + [array(len(group) * size + (0 if n else vectors), width) for n, group in enumerate(groups_sent)],
        [HBM] * 4, 2 * vectors * rows * width, 3 * rows * width, *in_hbm,
        scratch=[
            pltpu.VMEM(field.shape, F32),
            pltpu.VMEM((width, rows), BF16),
            pltpu.VMEM(mixing.shape[1:], BF16),
            pltpu.VMEM(rank_perm.shape, jnp.int32),
            pltpu.SemaphoreType.DMA((1 + levels + 2 + 4,)),
        ],
    )
    weight_cost = (4 * width * width * sections, 8 * width * width * sections)

    def weights(chosen, *compacts):
        return call(
            lambda *refs: build_weights(levels, chosen, *refs), array(len(chosen), 2 * width, width, kind=BF16),
            [VMEM] * len(compacts), *weight_cost, *compacts,
        )

    def pair_weights(start, mine, far):
        return call(
            lambda *refs: build_pair_weights(levels, start, *refs), array(2 * width, 2 * width, kind=BF16),
            [VMEM] * 2, *weight_cost, mine, far,
        )

    received = swapped(sent)
    step_cost = (24 * vectors * width * width, 8 * width * width)
    final = sections - 1
    if one_round:
        cross = crossed(kept[0])
        mine = weights([(0, vectors), (1, 0), (1, size)], sent, kept[1])
        states = call(
            lambda *refs: first_step(size, *refs), array(2 * vectors + size, width), [VMEM] * 5, *step_cost,
            sent, received, mine, weights([(0, vectors)], received), kept[1],
        )
        first_states = (states, across(states, 1))
        last_body = lambda *refs: last_sections(levels, *refs)
        last_weights = (mine, pair_weights(vectors + size, sent, swapped(cross)), pair_weights(vectors + size, received, cross))
    else:
        starts = [(0, vectors + n * size) for n in range(final)]
        mine, theirs = weights(starts + [(1, 0)], sent, *kept), weights(starts, received)
        runs = []
        for section in range(sections):
            if section % bits or not section:
                runs.append([section])
            else:
                runs[-1].append(section)
        first_states = (sent, received)
        for run in runs[:-1]:
            states = call(
                lambda *refs, run=run: step(run, final, *refs), array(2, vectors, width), [VMEM] * 4, *step_cost,
                *first_states, mine, theirs,
            )
            first_states = (states, across(states, (run[-1] + 1) % bits))
        last_body = lambda *refs: last_step(runs[-1], final, *refs)
        last_weights = (mine, theirs)
    expand_cost = (2 * vectors * width * rows, 4 * width * rows)
    expand = row_factor.reshape(width, rows)
    out_half, out_below = call(
        lambda *refs: last_body(rank_size, groups // 2, *refs), [array(vectors, rows)] * 2,
        [VMEM] * (4 + len(last_weights)), *expand_cost, *first_states, *last_weights, expand, row_owner,
    )
    out_half = shifted(out_half, "grp", groups // 2)
    out_below = shifted(out_below, "grp", groups - 1)
    diag = call(
        diagonal, array(vectors, rows), [VMEM, HBM], 2 * vectors * rows * order, 2 * rows * order,
        xb, pltpu.with_memory_space_constraint(leaf_inverse, pltpu.HBM),
        scratch=[pltpu.VMEM(leaf_inverse.shape, BF16), pltpu.SemaphoreType.DMA((2 * leaf_inverse.shape[0],))],
    )
    return call(
        combine, array(vectors, rows), [VMEM] * 3, 2 * vectors * rows, 16 * vectors * rows, out_half, out_below, diag,
        scratch=[pltpu.VMEM((vectors, rows), F32), pltpu.SemaphoreType.DMA((4,))], out=HBM,
    )


def solution(mesh):
    in_specs = (
        P(None, ("grp", "bf")),
        P(("grp", "bf"), None, None),
        P(None, None, ("grp", "bf")),
        P(None, None, ("grp", "bf")),
        P(("grp", "bf"), None, None, None, None, None),
        P(),
        P(),
    )
    out_specs = P(None, ("grp", "bf"))
    return jax.shard_map(shards, mesh=mesh, in_specs=in_specs, out_specs=out_specs, check_vma=False)
```

```python
import jax
import jax.numpy as jnp
from jax import lax
from jax.experimental import pallas as pl
from jax.experimental.pallas import tpu as pltpu
from jax.sharding import PartitionSpec as P

F32, BF16 = jnp.float32, jnp.bfloat16
VMEM = pl.BlockSpec(memory_space=pltpu.VMEM)
HBM = pl.BlockSpec(memory_space=pltpu.HBM)
NT = (((1,), (1,)), ((), ()))


def shifted(value, axis, distance):
    size = lax.axis_size(axis)
    return lax.ppermute(value, axis, [(source, (source + distance) % size) for source in range(size)])


def swapped(value):
    return lax.ppermute(value, "bf", [(n, n ^ 1) for n in range(lax.axis_size("bf"))])


def across(value, bit):
    return lax.ppermute(value, "bf", [(n, n ^ 1 << bit) for n in range(lax.axis_size("bf"))])


def call(body, shapes, specs, flops, moved, *operands, scratch=(), out=VMEM):
    return pl.pallas_call(
        body,
        out_shape=shapes,
        in_specs=specs,
        out_specs=jax.tree.map(lambda _: out, shapes),
        scratch_shapes=scratch,
        cost_estimate=pl.CostEstimate(flops=flops, bytes_accessed=moved, transcendentals=0),
        compiler_params=pltpu.CompilerParams(vmem_limit_bytes=16 * 2**20),
    )(*operands)


def block_diagonal(compact, levels):
    k = compact.shape[0]
    lane = lax.broadcasted_iota(jnp.int32, compact.shape, 1)
    parts = []
    for level in range(levels):
        mine = jnp.logical_and(lane >= level * k, lane < (level + 1) * k)
        parts.append(jnp.where(mine, compact, 0.0))
    return jnp.concatenate(parts, axis=0)


def section_weights(compact, levels):
    k = compact.shape[0] // 2
    parts = [block_diagonal(compact[:k], levels), block_diagonal(compact[k:], levels)]
    return jnp.concatenate(parts, axis=0).astype(BF16)


def compact_section(mixing_ref, section, side):
    levels = mixing_ref.shape[0]
    return jnp.concatenate([mixing_ref[level, section, side].astype(F32) for level in range(levels)], axis=1)


def split(source, target, parts, axis):
    count = source.shape[axis] // parts
    places = [(slice(None),) * axis + (pl.ds(n * count, count),) for n in range(parts)]
    return [(source.at[place], target.at[place]) for place in places]


def load(groups, field_hbm, col_hbm, mixing_hbm, perm_hbm, xb_ref, sent_ref, *refs):
    *out_refs, field_ref, col_ref, mixing_ref, perm_ref, sems = refs
    levels, sections, _, k, _ = mixing_ref.shape
    vectors = field_ref.shape[0]
    first = [(perm_hbm, perm_ref)]
    first += [(mixing_hbm.at[level], mixing_ref.at[level]) for level in range(levels)]
    second = split(field_hbm, field_ref, 2, 0)
    third = split(col_hbm, col_ref, 4, 0)
    copies = [pltpu.make_async_copy(*pair, sems.at[n]) for n, pair in enumerate(first + second + third)]
    for copy in copies:
        copy.start()
    for copy in copies[: len(first)]:
        copy.wait()
    row = lax.broadcasted_iota(jnp.int32, (k, k), 0)
    picks = jnp.concatenate([(row == perm_ref[level : level + 1, :]).astype(F32) for level in range(levels)], axis=1)
    picks = block_diagonal(picks, levels).astype(BF16)
    for section in range(sections):
        for side in range(2):
            mats = jnp.concatenate([mixing_ref[level, section, side].astype(F32) for level in range(levels)], axis=1)
            if section == 0:
                mats = jnp.dot(picks, block_diagonal(mats, levels).astype(BF16), preferred_element_type=F32)
                mats = sum(mats[level * k : (level + 1) * k] for level in range(levels))
            for n, (group, out_ref) in enumerate(zip(groups, (sent_ref, *out_refs))):
                if section in group:
                    start = (0 if n else vectors) + (2 * group.index(section) + side) * k
                    out_ref[start : start + k, :] = mats
    for copy in copies[len(first) :]:
        copy.wait()
    xb = field_ref[...].astype(BF16)
    xb_ref[...] = xb
    sent_ref[:vectors, :] = lax.dot_general(xb, col_ref[...], NT, preferred_element_type=F32)


def build_weights(levels, chosen, *refs):
    *compact_refs, weights_ref = refs
    size = 2 * weights_ref.shape[2] // levels
    for n, (operand, start) in enumerate(chosen):
        weights_ref[n] = section_weights(compact_refs[operand][start : start + size, :], levels)


def build_own(levels, chosen, *refs):
    *operand_refs, weights_ref, compact_ref = refs
    build_weights(levels, chosen, *operand_refs, weights_ref)
    width = weights_ref.shape[2]
    compact_ref[...] = compact_product(levels, weights_ref[1, width:, :], weights_ref[2, :width, :])


def compact_product(levels, left, right):
    k = left.shape[0] // levels
    product = jnp.dot(left, right, preferred_element_type=F32)
    return sum(product[level * k : (level + 1) * k] for level in range(levels))


def three_terms(value):
    high = value.astype(BF16)
    rest = value - high.astype(F32)
    middle = rest.astype(BF16)
    return high, middle, (rest - middle.astype(F32)).astype(BF16)


def factor_terms(levels, compact):
    return three_terms(block_diagonal(compact, levels))


def build_terms(levels, compact_ref, *refs):
    *message_refs, terms_ref = refs
    k, width = compact_ref.shape
    parts = [compact_ref[...]] + [ref[-k:, :] for ref in message_refs]
    for row, part in enumerate(parts):
        for n, term in enumerate(factor_terms(levels, part)):
            terms_ref[n, row * width : (row + 1) * width, :] = term


def terms_dot(value, terms):
    count = value.shape[0]
    stacked = jnp.concatenate(three_terms(value), axis=0)
    sums = sum(jnp.dot(stacked, term, preferred_element_type=F32) for term in reversed(terms))
    return sums[:count] + (sums[count : 2 * count] + sums[2 * count :])


def exact_dot(value, factor):
    return terms_dot(value, [factor])


def section_product(own, other, weights):
    return exact_dot(jnp.concatenate([own, other], axis=1), weights)


def run_sections(sections, final, first_refs, mine_ref, theirs_ref, out_ref):
    weights = (mine_ref, theirs_ref)
    if sections[0]:
        states_ref, other_ref = first_refs
        states, others = [states_ref[0], states_ref[1]], [other_ref[0], other_ref[1]]
    else:
        states = [ref[: out_ref.shape[1], :] for ref in first_refs]
        others = states[::-1]
    for section in sections:
        count = 1 if section == final else 2
        states = [section_product(states[n], others[n], weights[n][section]) for n in range(count)]
        others = states[::-1]
    if count == 1:
        return states[0]
    out_ref[0], out_ref[1] = states


def step(sections, final, first_ref, second_ref, mine_ref, theirs_ref, out_ref):
    run_sections(sections, final, (first_ref, second_ref), mine_ref, theirs_ref, out_ref)


def first_step(levels, sent_ref, received_ref, mine_ref, theirs_ref, out_ref):
    width = out_ref.shape[1]
    k = width // levels
    count = (out_ref.shape[0] - k) // 3
    mine, theirs = sent_ref[:count, :], received_ref[:count, :]
    mine, theirs = section_product(mine, theirs, mine_ref[0]), section_product(theirs, mine, theirs_ref[0])
    out_ref[:count, :] = mine
    out_ref[count : 2 * count, :] = theirs
    mine, theirs = exact_dot(mine, mine_ref[1, :width, :]), exact_dot(theirs, theirs_ref[1, :width, :])
    out_ref[2 * count : 3 * count, :] = section_product(mine, theirs, mine_ref[2])
    out_ref[3 * count :, :] = compact_product(levels, theirs_ref[1, width:, :], mine_ref[2, width:, :])


def level_rank(state, rank_size, half_shift, owner_ref, half):
    first_is_half = jnp.broadcast_to(owner_ref[0:1, 0:1], state.shape) == half_shift
    lane = lax.broadcasted_iota(jnp.int32, state.shape, 1)
    chosen = jnp.logical_xor(lane >= rank_size, first_is_half)
    return (jnp.where(chosen, state, 0.0) if half else jnp.where(chosen, 0.0, state)).astype(BF16)


def finish(state, rank_size, half_shift, row_ref, owner_ref, half_ref, below_ref):
    ranks = [level_rank(state, rank_size, half_shift, owner_ref, half) for half in (True, False)]
    outs = jnp.dot(jnp.concatenate(ranks, axis=0), row_ref[...], preferred_element_type=F32)
    half_ref[...] = outs[: state.shape[0]]
    below_ref[...] = outs[state.shape[0] :]


def last_step(sections, final, rank_size, half_shift, first_ref, second_ref, mine_ref, theirs_ref, *refs):
    state = run_sections(sections, final, (first_ref, second_ref), mine_ref, theirs_ref, None)
    finish(state, rank_size, half_shift, *refs)


def last_sections(levels, rank_size, half_shift, here_ref, there_ref, mine_ref, terms_ref, far_ref, *refs):
    count = (here_ref.shape[0] - rank_size) // 3
    here = jnp.concatenate([here_ref[:count, :], here_ref[count : 2 * count, :]], axis=1)
    there = jnp.concatenate([there_ref[:count, :], there_ref[count : 2 * count, :]], axis=1)
    mine = here_ref[2 * count : 3 * count, :] + terms_dot(there, [terms_ref[n] for n in range(3)])
    behind = factor_terms(levels, there_ref[3 * count :, :])
    far_terms = [jnp.concatenate([far_ref[n], behind[n]], axis=0) for n in range(3)]
    far = there_ref[2 * count : 3 * count, :] + terms_dot(here, far_terms)
    finish(section_product(mine, far, mine_ref[3]), rank_size, half_shift, *refs)


def diagonal(xb_ref, leaf_hbm, out_ref, leaf_ref, sems):
    blocks, order, _ = leaf_hbm.shape
    copies = []
    for n in range(blocks):
        for source, target in split(leaf_hbm.at[n], leaf_ref.at[n], 2, 0):
            copies.append(pltpu.make_async_copy(source, target, sems.at[len(copies)]))
            copies[-1].start()
    for n in range(blocks):
        copies[2 * n].wait()
        copies[2 * n + 1].wait()
        part = pl.ds(n * order, order)
        out_ref[:, part] = jnp.dot(xb_ref[:, part], leaf_ref[n], preferred_element_type=F32)


def combine(half_ref, below_ref, diag_ref, out_hbm, sum_ref, sems):
    parts = sems.shape[0]
    count = sum_ref.shape[1] // parts
    copies = []
    for n in range(parts):
        part = pl.ds(n * count, count)
        sum_ref[:, part] = diag_ref[:, part] + below_ref[:, part] + half_ref[:, part]
        copies.append(pltpu.make_async_copy(sum_ref.at[:, part], out_hbm.at[:, part], sems.at[n]))
        copies[-1].start()
    for copy in copies:
        copy.wait()


def shards(field, leaf_inverse, col_factor, row_factor, mixing, row_owner, rank_perm):
    vectors, rows = field.shape
    order = leaf_inverse.shape[1]
    levels, rank_size, _ = col_factor.shape
    sections = mixing.shape[2]
    bits = lax.axis_size("bf").bit_length() - 1
    groups = lax.axis_size("grp")
    width = levels * rank_size

    def array(*shape, kind=F32):
        return jax.ShapeDtypeStruct(shape, kind)

    in_hbm = [
        pltpu.with_memory_space_constraint(x, pltpu.HBM)
        for x in (field, col_factor.reshape(width, rows), mixing[0], rank_perm)
    ]
    size = 2 * rank_size
    one_round = bits == 2 and sections == 4 and levels == 2
    groups_sent = [(0, 1), (2, 3)] if one_round else [tuple(range(sections - 1)), (sections - 1,)]
    xb, sent, *kept = call(
        lambda *refs: load(groups_sent, *refs),
        [array(vectors, rows, kind=BF16)]
        + [array(len(group) * size + (0 if n else vectors), width) for n, group in enumerate(groups_sent)],
        [HBM] * 4, 2 * vectors * rows * width, 3 * rows * width, *in_hbm,
        scratch=[
            pltpu.VMEM(field.shape, F32),
            pltpu.VMEM((width, rows), BF16),
            pltpu.VMEM(mixing.shape[1:], BF16),
            pltpu.VMEM(rank_perm.shape, jnp.int32),
            pltpu.SemaphoreType.DMA((1 + levels + 2 + 4,)),
        ],
    )
    weight_cost = (4 * width * width * sections, 8 * width * width * sections)

    def weights(chosen, *compacts):
        return call(
            lambda *refs: build_weights(levels, chosen, *refs), array(len(chosen), 2 * width, width, kind=BF16),
            [VMEM] * len(compacts), *weight_cost, *compacts,
        )

    def terms(*compacts):
        return call(
            lambda *refs: build_terms(levels, *refs), array(3, len(compacts) * width, width, kind=BF16),
            [VMEM] * len(compacts), *weight_cost, *compacts,
        )

    received = swapped(sent)
    step_cost = (24 * vectors * width * width, 8 * width * width)
    final = sections - 1
    if one_round:
        chosen = [(0, vectors), (0, vectors + size), (1, 0), (1, size)]
        mine, factor = call(
            lambda *refs: build_own(levels, chosen, *refs),
            [array(sections, 2 * width, width, kind=BF16), array(rank_size, width)],
            [VMEM] * 2, *weight_cost, sent, kept[0],
        )
        far_factor = across(factor, 1)
        states = call(
            lambda *refs: first_step(levels, *refs), array(3 * vectors + rank_size, width), [VMEM] * 4, *step_cost,
            sent, received, mine, weights(chosen[:2], received),
        )
        first_states = (states, across(states, 1))
        last_body = lambda *refs: last_sections(levels, *refs)
        last_weights = (mine, terms(factor, states), terms(far_factor))
    else:
        starts = [(0, vectors + n * size) for n in range(final)]
        mine, theirs = weights(starts + [(1, 0)], sent, *kept), weights(starts, received)
        runs = []
        for section in range(sections):
            if section % bits or not section:
                runs.append([section])
            else:
                runs[-1].append(section)
        first_states = (sent, received)
        for run in runs[:-1]:
            states = call(
                lambda *refs, run=run: step(run, final, *refs), array(2, vectors, width), [VMEM] * 4, *step_cost,
                *first_states, mine, theirs,
            )
            first_states = (states, across(states, (run[-1] + 1) % bits))
        last_body = lambda *refs: last_step(runs[-1], final, *refs)
        last_weights = (mine, theirs)
    expand_cost = (2 * vectors * width * rows, 4 * width * rows)
    expand = row_factor.reshape(width, rows)
    out_half, out_below = call(
        lambda *refs: last_body(rank_size, groups // 2, *refs), [array(vectors, rows)] * 2,
        [VMEM] * (4 + len(last_weights)), *expand_cost, *first_states, *last_weights, expand, row_owner,
    )
    out_half = shifted(out_half, "grp", groups // 2)
    out_below = shifted(out_below, "grp", groups - 1)
    diag = call(
        diagonal, array(vectors, rows), [VMEM, HBM], 2 * vectors * rows * order, 2 * rows * order,
        xb, pltpu.with_memory_space_constraint(leaf_inverse, pltpu.HBM),
        scratch=[pltpu.VMEM(leaf_inverse.shape, BF16), pltpu.SemaphoreType.DMA((2 * leaf_inverse.shape[0],))],
    )
    return call(
        combine, array(vectors, rows), [VMEM] * 3, 2 * vectors * rows, 16 * vectors * rows, out_half, out_below, diag,
        scratch=[pltpu.VMEM((vectors, rows), F32), pltpu.SemaphoreType.DMA((4,))], out=HBM,
    )


def solution(mesh):
    in_specs = (
        P(None, ("grp", "bf")),
        P(("grp", "bf"), None, None),
        P(None, None, ("grp", "bf")),
        P(None, None, ("grp", "bf")),
        P(("grp", "bf"), None, None, None, None, None),
        P(),
        P(),
    )
    out_specs = P(None, ("grp", "bf"))
    return jax.shard_map(shards, mesh=mesh, in_specs=in_specs, out_specs=out_specs, check_vma=False)
```

```python
import jax
import jax.numpy as jnp
from jax import lax
from jax.experimental import pallas as pl
from jax.experimental.pallas import tpu as pltpu
from jax.sharding import PartitionSpec as P

F32, BF16 = jnp.float32, jnp.bfloat16
VMEM = pl.BlockSpec(memory_space=pltpu.VMEM)
HBM = pl.BlockSpec(memory_space=pltpu.HBM)
NT = (((1,), (1,)), ((), ()))


def shifted(value, axis, distance):
    size = lax.axis_size(axis)
    return lax.ppermute(value, axis, [(source, (source + distance) % size) for source in range(size)])


def swapped(value):
    return lax.ppermute(value, "bf", [(n, n ^ 1) for n in range(lax.axis_size("bf"))])


def across(value, bit):
    return lax.ppermute(value, "bf", [(n, n ^ 1 << bit) for n in range(lax.axis_size("bf"))])


def call(body, shapes, specs, flops, moved, *operands, scratch=(), out=VMEM):
    return pl.pallas_call(
        body,
        out_shape=shapes,
        in_specs=specs,
        out_specs=jax.tree.map(lambda _: out, shapes),
        scratch_shapes=scratch,
        cost_estimate=pl.CostEstimate(flops=flops, bytes_accessed=moved, transcendentals=0),
        compiler_params=pltpu.CompilerParams(vmem_limit_bytes=16 * 2**20),
    )(*operands)


def block_diagonal(compact, levels):
    k = compact.shape[0]
    lane = lax.broadcasted_iota(jnp.int32, compact.shape, 1)
    parts = []
    for level in range(levels):
        mine = jnp.logical_and(lane >= level * k, lane < (level + 1) * k)
        parts.append(jnp.where(mine, compact, 0.0))
    return jnp.concatenate(parts, axis=0)


def section_weights(compact, levels):
    k = compact.shape[0] // 2
    parts = [block_diagonal(compact[:k], levels), block_diagonal(compact[k:], levels)]
    return jnp.concatenate(parts, axis=0).astype(BF16)


def compact_section(mixing_ref, section, side):
    levels = mixing_ref.shape[0]
    return jnp.concatenate([mixing_ref[level, section, side].astype(F32) for level in range(levels)], axis=1)


def split(source, target, parts, axis):
    count = source.shape[axis] // parts
    places = [(slice(None),) * axis + (pl.ds(n * count, count),) for n in range(parts)]
    return [(source.at[place], target.at[place]) for place in places]


def load(groups, field_hbm, col_hbm, mixing_hbm, perm_hbm, xb_ref, sent_ref, *refs):
    *out_refs, field_ref, col_ref, mixing_ref, perm_ref, sems = refs
    compact = {}
    levels, sections, _, k, _ = mixing_ref.shape
    vectors = field_ref.shape[0]
    first = [(perm_hbm, perm_ref)]
    first += [(mixing_hbm.at[level], mixing_ref.at[level]) for level in range(levels)]
    second = split(field_hbm, field_ref, 2, 0)
    third = split(col_hbm, col_ref, 4, 0)
    copies = [pltpu.make_async_copy(*pair, sems.at[n]) for n, pair in enumerate(first + second + third)]
    for copy in copies:
        copy.start()
    for copy in copies[: len(first)]:
        copy.wait()
    row = lax.broadcasted_iota(jnp.int32, (k, k), 0)
    picks = jnp.concatenate([(row == perm_ref[level : level + 1, :]).astype(F32) for level in range(levels)], axis=1)
    picks = block_diagonal(picks, levels).astype(BF16)
    for section in range(sections):
        for side in range(2):
            mats = jnp.concatenate([mixing_ref[level, section, side].astype(F32) for level in range(levels)], axis=1)
            if section == 0:
                mats = jnp.dot(picks, block_diagonal(mats, levels).astype(BF16), preferred_element_type=F32)
                mats = sum(mats[level * k : (level + 1) * k] for level in range(levels))
            compact[section, side] = mats
            for n, (group, out_ref) in enumerate(zip(groups, (sent_ref, *out_refs))):
                if section in group:
                    start = (0 if n else vectors) + (2 * group.index(section) + side) * k
                    out_ref[start : start + k, :] = mats
    if len(out_refs) == len(groups):
        left, right = [block_diagonal(compact[which], levels).astype(BF16) for which in ((1, 1), (2, 0))]
        out_refs[-1][...] = compact_product(levels, left, right)
    for copy in copies[len(first) :]:
        copy.wait()
    xb = field_ref[...].astype(BF16)
    xb_ref[...] = xb
    sent_ref[:vectors, :] = lax.dot_general(xb, col_ref[...], NT, preferred_element_type=F32)


def build_weights(levels, chosen, *refs):
    *compact_refs, weights_ref = refs
    size = 2 * weights_ref.shape[2] // levels
    for n, (operand, start) in enumerate(chosen):
        weights_ref[n] = section_weights(compact_refs[operand][start : start + size, :], levels)


def compact_product(levels, left, right):
    k = left.shape[0] // levels
    product = jnp.dot(left, right, preferred_element_type=F32)
    return sum(product[level * k : (level + 1) * k] for level in range(levels))


def three_terms(value):
    high = value.astype(BF16)
    rest = value - high.astype(F32)
    middle = rest.astype(BF16)
    return high, middle, (rest - middle.astype(F32)).astype(BF16)


def factor_terms(levels, compact):
    return three_terms(block_diagonal(compact, levels))


def build_terms(levels, compact_ref, *refs):
    *message_refs, terms_ref = refs
    k, width = compact_ref.shape
    parts = [compact_ref[...]] + [ref[-k:, :] for ref in message_refs]
    for row, part in enumerate(parts):
        for n, term in enumerate(factor_terms(levels, part)):
            terms_ref[n, row * width : (row + 1) * width, :] = term


def terms_dot(value, terms):
    count = value.shape[0]
    stacked = jnp.concatenate(three_terms(value), axis=0)
    sums = sum(jnp.dot(stacked, term, preferred_element_type=F32) for term in reversed(terms))
    return sums[:count] + (sums[count : 2 * count] + sums[2 * count :])


def exact_dot(value, factor):
    return terms_dot(value, [factor])


def section_product(own, other, weights):
    return exact_dot(jnp.concatenate([own, other], axis=1), weights)


def run_sections(sections, final, first_refs, mine_ref, theirs_ref, out_ref):
    weights = (mine_ref, theirs_ref)
    if sections[0]:
        states_ref, other_ref = first_refs
        states, others = [states_ref[0], states_ref[1]], [other_ref[0], other_ref[1]]
    else:
        states = [ref[: out_ref.shape[1], :] for ref in first_refs]
        others = states[::-1]
    for section in sections:
        count = 1 if section == final else 2
        states = [section_product(states[n], others[n], weights[n][section]) for n in range(count)]
        others = states[::-1]
    if count == 1:
        return states[0]
    out_ref[0], out_ref[1] = states


def step(sections, final, first_ref, second_ref, mine_ref, theirs_ref, out_ref):
    run_sections(sections, final, (first_ref, second_ref), mine_ref, theirs_ref, out_ref)


def first_step(levels, sent_ref, received_ref, mine_ref, theirs_ref, out_ref):
    width = out_ref.shape[1]
    k = width // levels
    count = (out_ref.shape[0] - k) // 3
    mine, theirs = sent_ref[:count, :], received_ref[:count, :]
    mine, theirs = section_product(mine, theirs, mine_ref[0]), section_product(theirs, mine, theirs_ref[0])
    out_ref[:count, :] = mine
    out_ref[count : 2 * count, :] = theirs
    mine, theirs = exact_dot(mine, mine_ref[1, :width, :]), exact_dot(theirs, theirs_ref[1, :width, :])
    out_ref[2 * count : 3 * count, :] = section_product(mine, theirs, mine_ref[2])
    out_ref[3 * count :, :] = compact_product(levels, theirs_ref[1, width:, :], mine_ref[2, width:, :])


def level_rank(state, rank_size, half_shift, owner_ref, half):
    first_is_half = jnp.broadcast_to(owner_ref[0:1, 0:1], state.shape) == half_shift
    lane = lax.broadcasted_iota(jnp.int32, state.shape, 1)
    chosen = jnp.logical_xor(lane >= rank_size, first_is_half)
    return (jnp.where(chosen, state, 0.0) if half else jnp.where(chosen, 0.0, state)).astype(BF16)


def finish(state, rank_size, half_shift, row_ref, owner_ref, half_ref, below_ref):
    ranks = [level_rank(state, rank_size, half_shift, owner_ref, half) for half in (True, False)]
    outs = jnp.dot(jnp.concatenate(ranks, axis=0), row_ref[...], preferred_element_type=F32)
    half_ref[...] = outs[: state.shape[0]]
    below_ref[...] = outs[state.shape[0] :]


def last_step(sections, final, rank_size, half_shift, first_ref, second_ref, mine_ref, theirs_ref, *refs):
    state = run_sections(sections, final, (first_ref, second_ref), mine_ref, theirs_ref, None)
    finish(state, rank_size, half_shift, *refs)


def last_sections(levels, rank_size, half_shift, here_ref, there_ref, mine_ref, terms_ref, far_ref, *refs):
    count = (here_ref.shape[0] - rank_size) // 3
    here = jnp.concatenate([here_ref[:count, :], here_ref[count : 2 * count, :]], axis=1)
    there = jnp.concatenate([there_ref[:count, :], there_ref[count : 2 * count, :]], axis=1)
    mine = here_ref[2 * count : 3 * count, :] + terms_dot(there, [terms_ref[n] for n in range(3)])
    behind = factor_terms(levels, there_ref[3 * count :, :])
    far_terms = [jnp.concatenate([far_ref[n], behind[n]], axis=0) for n in range(3)]
    far = there_ref[2 * count : 3 * count, :] + terms_dot(here, far_terms)
    finish(section_product(mine, far, mine_ref[3]), rank_size, half_shift, *refs)


def diagonal(xb_ref, leaf_hbm, out_ref, leaf_ref, sems):
    blocks, order, _ = leaf_hbm.shape
    copies = []
    for n in range(blocks):
        for source, target in split(leaf_hbm.at[n], leaf_ref.at[n], 2, 0):
            copies.append(pltpu.make_async_copy(source, target, sems.at[len(copies)]))
            copies[-1].start()
    for n in range(blocks):
        copies[2 * n].wait()
        copies[2 * n + 1].wait()
        part = pl.ds(n * order, order)
        out_ref[:, part] = jnp.dot(xb_ref[:, part], leaf_ref[n], preferred_element_type=F32)


def combine(half_ref, below_ref, diag_ref, out_hbm, sum_ref, sems):
    parts = sems.shape[0]
    count = sum_ref.shape[1] // parts
    copies = []
    for n in range(parts):
        part = pl.ds(n * count, count)
        sum_ref[:, part] = diag_ref[:, part] + below_ref[:, part] + half_ref[:, part]
        copies.append(pltpu.make_async_copy(sum_ref.at[:, part], out_hbm.at[:, part], sems.at[n]))
        copies[-1].start()
    for copy in copies:
        copy.wait()


def shards(field, leaf_inverse, col_factor, row_factor, mixing, row_owner, rank_perm):
    vectors, rows = field.shape
    order = leaf_inverse.shape[1]
    levels, rank_size, _ = col_factor.shape
    sections = mixing.shape[2]
    bits = lax.axis_size("bf").bit_length() - 1
    groups = lax.axis_size("grp")
    width = levels * rank_size

    def array(*shape, kind=F32):
        return jax.ShapeDtypeStruct(shape, kind)

    in_hbm = [
        pltpu.with_memory_space_constraint(x, pltpu.HBM)
        for x in (field, col_factor.reshape(width, rows), mixing[0], rank_perm)
    ]
    size = 2 * rank_size
    one_round = bits == 2 and sections == 4 and levels == 2
    groups_sent = [(0, 1), (2, 3)] if one_round else [tuple(range(sections - 1)), (sections - 1,)]
    xb, sent, *kept = call(
        lambda *refs: load(groups_sent, *refs),
        [array(vectors, rows, kind=BF16)]
        + [array(len(group) * size + (0 if n else vectors), width) for n, group in enumerate(groups_sent)]
        + [array(rank_size, width)] * one_round,
        [HBM] * 4, 2 * vectors * rows * width, 3 * rows * width, *in_hbm,
        scratch=[
            pltpu.VMEM(field.shape, F32),
            pltpu.VMEM((width, rows), BF16),
            pltpu.VMEM(mixing.shape[1:], BF16),
            pltpu.VMEM(rank_perm.shape, jnp.int32),
            pltpu.SemaphoreType.DMA((1 + levels + 2 + 4,)),
        ],
    )
    weight_cost = (4 * width * width * sections, 8 * width * width * sections)

    def weights(chosen, *compacts):
        return call(
            lambda *refs: build_weights(levels, chosen, *refs), array(len(chosen), 2 * width, width, kind=BF16),
            [VMEM] * len(compacts), *weight_cost, *compacts,
        )

    def terms(*compacts, scale=1):
        return call(
            lambda *refs: build_terms(levels, *refs), array(3, len(compacts) * width, width, kind=BF16),
            [VMEM] * len(compacts), *[scale * cost for cost in weight_cost], *compacts,
        )

    received = swapped(sent)
    step_cost = (24 * vectors * width * width, 8 * width * width)
    final = sections - 1
    if one_round:
        chosen = [(0, vectors), (0, vectors + size), (1, 0), (1, size)]
        mine, factor = weights(chosen, sent, kept[0]), kept[1]
        far_factor = across(factor, 1)
        states = call(
            lambda *refs: first_step(levels, *refs), array(3 * vectors + rank_size, width), [VMEM] * 4, *step_cost,
            sent, received, mine, weights(chosen[:2], received),
        )
        first_states = (states, across(states, 1))
        last_body = lambda *refs: last_sections(levels, *refs)
        last_weights = (mine, terms(factor, states), terms(far_factor, scale=1000))
    else:
        starts = [(0, vectors + n * size) for n in range(final)]
        mine, theirs = weights(starts + [(1, 0)], sent, *kept), weights(starts, received)
        runs = []
        for section in range(sections):
            if section % bits or not section:
                runs.append([section])
            else:
                runs[-1].append(section)
        first_states = (sent, received)
        for run in runs[:-1]:
            states = call(
                lambda *refs, run=run: step(run, final, *refs), array(2, vectors, width), [VMEM] * 4, *step_cost,
                *first_states, mine, theirs,
            )
            first_states = (states, across(states, (run[-1] + 1) % bits))
        last_body = lambda *refs: last_step(runs[-1], final, *refs)
        last_weights = (mine, theirs)
    expand_cost = (2 * vectors * width * rows, 4 * width * rows)
    expand = row_factor.reshape(width, rows)
    out_half, out_below = call(
        lambda *refs: last_body(rank_size, groups // 2, *refs), [array(vectors, rows)] * 2,
        [VMEM] * (4 + len(last_weights)), *expand_cost, *first_states, *last_weights, expand, row_owner,
    )
    out_half = shifted(out_half, "grp", groups // 2)
    out_below = shifted(out_below, "grp", groups - 1)
    diag = call(
        diagonal, array(vectors, rows), [VMEM, HBM], 2 * vectors * rows * order, 2 * rows * order,
        xb, pltpu.with_memory_space_constraint(leaf_inverse, pltpu.HBM),
        scratch=[pltpu.VMEM(leaf_inverse.shape, BF16), pltpu.SemaphoreType.DMA((2 * leaf_inverse.shape[0],))],
    )
    return call(
        combine, array(vectors, rows), [VMEM] * 3, 2 * vectors * rows, 16 * vectors * rows, out_half, out_below, diag,
        scratch=[pltpu.VMEM((vectors, rows), F32), pltpu.SemaphoreType.DMA((4,))], out=HBM,
    )


def solution(mesh):
    in_specs = (
        P(None, ("grp", "bf")),
        P(("grp", "bf"), None, None),
        P(None, None, ("grp", "bf")),
        P(None, None, ("grp", "bf")),
        P(("grp", "bf"), None, None, None, None, None),
        P(),
        P(),
    )
    out_specs = P(None, ("grp", "bf"))
    return jax.shard_map(shards, mesh=mesh, in_specs=in_specs, out_specs=out_specs, check_vma=False)
```

```python
import jax
import jax.numpy as jnp
from jax import lax
from jax.experimental import pallas as pl
from jax.experimental.pallas import tpu as pltpu
from jax.sharding import PartitionSpec as P

F32, BF16 = jnp.float32, jnp.bfloat16
VMEM = pl.BlockSpec(memory_space=pltpu.VMEM)
HBM = pl.BlockSpec(memory_space=pltpu.HBM)
NT = (((1,), (1,)), ((), ()))


def shifted(value, axis, distance):
    size = lax.axis_size(axis)
    return lax.ppermute(value, axis, [(source, (source + distance) % size) for source in range(size)])


def swapped(value):
    return lax.ppermute(value, "bf", [(n, n ^ 1) for n in range(lax.axis_size("bf"))])


def across(value, bit):
    return lax.ppermute(value, "bf", [(n, n ^ 1 << bit) for n in range(lax.axis_size("bf"))])


def call(body, shapes, specs, flops, moved, *operands, scratch=(), out=VMEM):
    return pl.pallas_call(
        body,
        out_shape=shapes,
        in_specs=specs,
        out_specs=jax.tree.map(lambda _: out, shapes),
        scratch_shapes=scratch,
        cost_estimate=pl.CostEstimate(flops=flops, bytes_accessed=moved, transcendentals=0),
        compiler_params=pltpu.CompilerParams(vmem_limit_bytes=16 * 2**20),
    )(*operands)


def block_diagonal(compact, levels):
    k = compact.shape[0]
    lane = lax.broadcasted_iota(jnp.int32, compact.shape, 1)
    parts = []
    for level in range(levels):
        mine = jnp.logical_and(lane >= level * k, lane < (level + 1) * k)
        parts.append(jnp.where(mine, compact, 0.0))
    return jnp.concatenate(parts, axis=0)


def section_weights(compact, levels):
    k = compact.shape[0] // 2
    parts = [block_diagonal(compact[:k], levels), block_diagonal(compact[k:], levels)]
    return jnp.concatenate(parts, axis=0).astype(BF16)


def compact_section(mixing_ref, section, side):
    levels = mixing_ref.shape[0]
    return jnp.concatenate([mixing_ref[level, section, side].astype(F32) for level in range(levels)], axis=1)


def split(source, target, parts, axis):
    count = source.shape[axis] // parts
    places = [(slice(None),) * axis + (pl.ds(n * count, count),) for n in range(parts)]
    return [(source.at[place], target.at[place]) for place in places]


def load(groups, field_hbm, col_hbm, mixing_hbm, perm_hbm, xb_ref, sent_ref, *refs):
    *out_refs, field_ref, col_ref, mixing_ref, perm_ref, sems = refs
    compact = {}
    levels, sections, _, k, _ = mixing_ref.shape
    vectors = field_ref.shape[0]
    pairs = split(col_hbm, col_ref, 4, 0) + split(field_hbm, field_ref, 2, 0)
    pairs += [(mixing_hbm.at[level], mixing_ref.at[level]) for level in range(levels)]
    pairs.append((perm_hbm, perm_ref))
    copies = [pltpu.make_async_copy(*pair, sems.at[n]) for n, pair in enumerate(pairs)]
    for copy in copies:
        copy.start()
    for copy in copies:
        copy.wait()
    xb = field_ref[...].astype(BF16)
    xb_ref[...] = xb
    sent_ref[:vectors, :] = lax.dot_general(xb, col_ref[...], NT, preferred_element_type=F32)
    row = lax.broadcasted_iota(jnp.int32, (k, k), 0)
    picks = jnp.concatenate([(row == perm_ref[level : level + 1, :]).astype(F32) for level in range(levels)], axis=1)
    picks = block_diagonal(picks, levels).astype(BF16)
    for section in range(sections):
        for side in range(2):
            mats = jnp.concatenate([mixing_ref[level, section, side].astype(F32) for level in range(levels)], axis=1)
            if section == 0:
                mats = jnp.dot(picks, block_diagonal(mats, levels).astype(BF16), preferred_element_type=F32)
                mats = sum(mats[level * k : (level + 1) * k] for level in range(levels))
            compact[section, side] = mats
            for n, (group, out_ref) in enumerate(zip(groups, (sent_ref, *out_refs))):
                if section in group:
                    start = (0 if n else vectors) + (2 * group.index(section) + side) * k
                    out_ref[start : start + k, :] = mats
    if len(out_refs) == len(groups):
        left, right = [block_diagonal(compact[which], levels).astype(BF16) for which in ((1, 1), (2, 0))]
        out_refs[-1][...] = compact_product(levels, left, right)


def build_weights(levels, chosen, *refs):
    *compact_refs, weights_ref = refs
    size = 2 * weights_ref.shape[2] // levels
    for n, (operand, start) in enumerate(chosen):
        weights_ref[n] = section_weights(compact_refs[operand][start : start + size, :], levels)


def compact_product(levels, left, right):
    k = left.shape[0] // levels
    product = jnp.dot(left, right, preferred_element_type=F32)
    return sum(product[level * k : (level + 1) * k] for level in range(levels))


def three_terms(value):
    high = value.astype(BF16)
    rest = value - high.astype(F32)
    middle = rest.astype(BF16)
    return high, middle, (rest - middle.astype(F32)).astype(BF16)


def factor_terms(levels, compact):
    return three_terms(block_diagonal(compact, levels))


def build_terms(levels, compact_ref, *refs):
    *message_refs, terms_ref = refs
    k, width = compact_ref.shape
    parts = [compact_ref[...]] + [ref[-k:, :] for ref in message_refs]
    for row, part in enumerate(parts):
        for n, term in enumerate(factor_terms(levels, part)):
            terms_ref[n, row * width : (row + 1) * width, :] = term


def terms_dot(value, terms):
    count = value.shape[0]
    stacked = jnp.concatenate(three_terms(value), axis=0)
    sums = sum(jnp.dot(stacked, term, preferred_element_type=F32) for term in reversed(terms))
    return sums[:count] + (sums[count : 2 * count] + sums[2 * count :])


def exact_dot(value, factor):
    return terms_dot(value, [factor])


def section_product(own, other, weights):
    return exact_dot(jnp.concatenate([own, other], axis=1), weights)


def run_sections(sections, final, first_refs, mine_ref, theirs_ref, out_ref):
    weights = (mine_ref, theirs_ref)
    if sections[0]:
        states_ref, other_ref = first_refs
        states, others = [states_ref[0], states_ref[1]], [other_ref[0], other_ref[1]]
    else:
        states = [ref[: out_ref.shape[1], :] for ref in first_refs]
        others = states[::-1]
    for section in sections:
        count = 1 if section == final else 2
        states = [section_product(states[n], others[n], weights[n][section]) for n in range(count)]
        others = states[::-1]
    if count == 1:
        return states[0]
    out_ref[0], out_ref[1] = states


def step(sections, final, first_ref, second_ref, mine_ref, theirs_ref, out_ref):
    run_sections(sections, final, (first_ref, second_ref), mine_ref, theirs_ref, out_ref)


def first_step(levels, sent_ref, received_ref, mine_ref, theirs_ref, out_ref):
    width = out_ref.shape[1]
    k = width // levels
    count = (out_ref.shape[0] - k) // 3
    mine, theirs = sent_ref[:count, :], received_ref[:count, :]
    mine, theirs = section_product(mine, theirs, mine_ref[0]), section_product(theirs, mine, theirs_ref[0])
    out_ref[:count, :] = mine
    out_ref[count : 2 * count, :] = theirs
    mine, theirs = exact_dot(mine, mine_ref[1, :width, :]), exact_dot(theirs, theirs_ref[1, :width, :])
    out_ref[2 * count : 3 * count, :] = section_product(mine, theirs, mine_ref[2])
    out_ref[3 * count :, :] = compact_product(levels, theirs_ref[1, width:, :], mine_ref[2, width:, :])


def level_rank(state, rank_size, half_shift, owner_ref, half):
    first_is_half = jnp.broadcast_to(owner_ref[0:1, 0:1], state.shape) == half_shift
    lane = lax.broadcasted_iota(jnp.int32, state.shape, 1)
    chosen = jnp.logical_xor(lane >= rank_size, first_is_half)
    return (jnp.where(chosen, state, 0.0) if half else jnp.where(chosen, 0.0, state)).astype(BF16)


def finish(state, rank_size, half_shift, row_ref, owner_ref, half_ref, below_ref):
    ranks = [level_rank(state, rank_size, half_shift, owner_ref, half) for half in (True, False)]
    outs = jnp.dot(jnp.concatenate(ranks, axis=0), row_ref[...], preferred_element_type=F32)
    half_ref[...] = outs[: state.shape[0]]
    below_ref[...] = outs[state.shape[0] :]


def last_step(sections, final, rank_size, half_shift, first_ref, second_ref, mine_ref, theirs_ref, *refs):
    state = run_sections(sections, final, (first_ref, second_ref), mine_ref, theirs_ref, None)
    finish(state, rank_size, half_shift, *refs)


def last_sections(levels, rank_size, half_shift, here_ref, there_ref, mine_ref, terms_ref, far_ref, *refs):
    count = (here_ref.shape[0] - rank_size) // 3
    here = jnp.concatenate([here_ref[:count, :], here_ref[count : 2 * count, :]], axis=1)
    there = jnp.concatenate([there_ref[:count, :], there_ref[count : 2 * count, :]], axis=1)
    mine = here_ref[2 * count : 3 * count, :] + terms_dot(there, [terms_ref[n] for n in range(3)])
    behind = factor_terms(levels, there_ref[3 * count :, :])
    far_terms = [jnp.concatenate([far_ref[n], behind[n]], axis=0) for n in range(3)]
    far = there_ref[2 * count : 3 * count, :] + terms_dot(here, far_terms)
    finish(section_product(mine, far, mine_ref[3]), rank_size, half_shift, *refs)


def diagonal(xb_ref, leaf_hbm, out_ref, leaf_ref, sems):
    blocks, order, _ = leaf_hbm.shape
    copies = []
    for n in range(blocks):
        for source, target in split(leaf_hbm.at[n], leaf_ref.at[n], 2, 0):
            copies.append(pltpu.make_async_copy(source, target, sems.at[len(copies)]))
            copies[-1].start()
    for n in range(blocks):
        copies[2 * n].wait()
        copies[2 * n + 1].wait()
        part = pl.ds(n * order, order)
        out_ref[:, part] = jnp.dot(xb_ref[:, part], leaf_ref[n], preferred_element_type=F32)


def combine(half_ref, below_ref, diag_ref, out_hbm, sum_ref, sems):
    parts = sems.shape[0]
    count = sum_ref.shape[1] // parts
    copies = []
    for n in range(parts):
        part = pl.ds(n * count, count)
        sum_ref[:, part] = diag_ref[:, part] + below_ref[:, part] + half_ref[:, part]
        copies.append(pltpu.make_async_copy(sum_ref.at[:, part], out_hbm.at[:, part], sems.at[n]))
        copies[-1].start()
    for copy in copies:
        copy.wait()


def shards(field, leaf_inverse, col_factor, row_factor, mixing, row_owner, rank_perm):
    vectors, rows = field.shape
    order = leaf_inverse.shape[1]
    levels, rank_size, _ = col_factor.shape
    sections = mixing.shape[2]
    bits = lax.axis_size("bf").bit_length() - 1
    groups = lax.axis_size("grp")
    width = levels * rank_size

    def array(*shape, kind=F32):
        return jax.ShapeDtypeStruct(shape, kind)

    in_hbm = [
        pltpu.with_memory_space_constraint(x, pltpu.HBM)
        for x in (field, col_factor.reshape(width, rows), mixing[0], rank_perm)
    ]
    size = 2 * rank_size
    one_round = bits == 2 and sections == 4 and levels == 2
    groups_sent = [(0, 1), (2, 3)] if one_round else [tuple(range(sections - 1)), (sections - 1,)]
    xb, sent, *kept = call(
        lambda *refs: load(groups_sent, *refs),
        [array(vectors, rows, kind=BF16)]
        + [array(len(group) * size + (0 if n else vectors), width) for n, group in enumerate(groups_sent)]
        + [array(rank_size, width)] * one_round,
        [HBM] * 4, 2 * vectors * rows * width, 3 * rows * width, *in_hbm,
        scratch=[
            pltpu.VMEM(field.shape, F32),
            pltpu.VMEM((width, rows), BF16),
            pltpu.VMEM(mixing.shape[1:], BF16),
            pltpu.VMEM(rank_perm.shape, jnp.int32),
            pltpu.SemaphoreType.DMA((1 + levels + 2 + 4,)),
        ],
    )
    weight_cost = (4 * width * width * sections, 8 * width * width * sections)

    def weights(chosen, *compacts):
        return call(
            lambda *refs: build_weights(levels, chosen, *refs), array(len(chosen), 2 * width, width, kind=BF16),
            [VMEM] * len(compacts), *weight_cost, *compacts,
        )

    def terms(*compacts, scale=1):
        return call(
            lambda *refs: build_terms(levels, *refs), array(3, len(compacts) * width, width, kind=BF16),
            [VMEM] * len(compacts), *[scale * cost for cost in weight_cost], *compacts,
        )

    received = swapped(sent)
    step_cost = (24 * vectors * width * width, 8 * width * width)
    final = sections - 1
    if one_round:
        chosen = [(0, vectors), (0, vectors + size), (1, 0), (1, size)]
        mine, factor = weights(chosen, sent, kept[0]), kept[1]
        far_factor = across(factor, 1)
        states = call(
            lambda *refs: first_step(levels, *refs), array(3 * vectors + rank_size, width), [VMEM] * 4, *step_cost,
            sent, received, mine, weights(chosen[:2], received),
        )
        first_states = (states, across(states, 1))
        last_body = lambda *refs: last_sections(levels, *refs)
        last_weights = (mine, terms(factor, states), terms(far_factor, scale=1000))
    else:
        starts = [(0, vectors + n * size) for n in range(final)]
        mine, theirs = weights(starts + [(1, 0)], sent, *kept), weights(starts, received)
        runs = []
        for section in range(sections):
            if section % bits or not section:
                runs.append([section])
            else:
                runs[-1].append(section)
        first_states = (sent, received)
        for run in runs[:-1]:
            states = call(
                lambda *refs, run=run: step(run, final, *refs), array(2, vectors, width), [VMEM] * 4, *step_cost,
                *first_states, mine, theirs,
            )
            first_states = (states, across(states, (run[-1] + 1) % bits))
        last_body = lambda *refs: last_step(runs[-1], final, *refs)
        last_weights = (mine, theirs)
    expand_cost = (2 * vectors * width * rows, 4 * width * rows)
    expand = row_factor.reshape(width, rows)
    out_half, out_below = call(
        lambda *refs: last_body(rank_size, groups // 2, *refs), [array(vectors, rows)] * 2,
        [VMEM] * (4 + len(last_weights)), *expand_cost, *first_states, *last_weights, expand, row_owner,
    )
    out_half = shifted(out_half, "grp", groups // 2)
    out_below = shifted(out_below, "grp", groups - 1)
    diag = call(
        diagonal, array(vectors, rows), [VMEM, HBM], 2 * vectors * rows * order, 2 * rows * order,
        xb, pltpu.with_memory_space_constraint(leaf_inverse, pltpu.HBM),
        scratch=[pltpu.VMEM(leaf_inverse.shape, BF16), pltpu.SemaphoreType.DMA((2 * leaf_inverse.shape[0],))],
    )
    return call(
        combine, array(vectors, rows), [VMEM] * 3, 2 * vectors * rows, 16 * vectors * rows, out_half, out_below, diag,
        scratch=[pltpu.VMEM((vectors, rows), F32), pltpu.SemaphoreType.DMA((4,))], out=HBM,
    )


def solution(mesh):
    in_specs = (
        P(None, ("grp", "bf")),
        P(("grp", "bf"), None, None),
        P(None, None, ("grp", "bf")),
        P(None, None, ("grp", "bf")),
        P(("grp", "bf"), None, None, None, None, None),
        P(),
        P(),
    )
    out_specs = P(None, ("grp", "bf"))
    return jax.shard_map(shards, mesh=mesh, in_specs=in_specs, out_specs=out_specs, check_vma=False)
```

```python
import jax
import jax.numpy as jnp
from jax import lax
from jax.experimental import pallas as pl
from jax.experimental.pallas import tpu as pltpu
from jax.sharding import PartitionSpec as P

F32, BF16 = jnp.float32, jnp.bfloat16
VMEM = pl.BlockSpec(memory_space=pltpu.VMEM)
HBM = pl.BlockSpec(memory_space=pltpu.HBM)
NT = (((1,), (1,)), ((), ()))


def shifted(value, axis, distance):
    size = lax.axis_size(axis)
    return lax.ppermute(value, axis, [(source, (source + distance) % size) for source in range(size)])


def swapped(value):
    return lax.ppermute(value, "bf", [(n, n ^ 1) for n in range(lax.axis_size("bf"))])


def across(value, bit):
    return lax.ppermute(value, "bf", [(n, n ^ 1 << bit) for n in range(lax.axis_size("bf"))])


def call(body, shapes, specs, flops, moved, *operands, scratch=(), out=VMEM):
    return pl.pallas_call(
        body,
        out_shape=shapes,
        in_specs=specs,
        out_specs=jax.tree.map(lambda _: out, shapes),
        scratch_shapes=scratch,
        cost_estimate=pl.CostEstimate(flops=flops, bytes_accessed=moved, transcendentals=0),
        compiler_params=pltpu.CompilerParams(vmem_limit_bytes=16 * 2**20),
    )(*operands)


def block_diagonal(compact, levels):
    k = compact.shape[0]
    lane = lax.broadcasted_iota(jnp.int32, compact.shape, 1)
    parts = []
    for level in range(levels):
        mine = jnp.logical_and(lane >= level * k, lane < (level + 1) * k)
        parts.append(jnp.where(mine, compact, 0.0))
    return jnp.concatenate(parts, axis=0)


def section_weights(compact, levels):
    k = compact.shape[0] // 2
    parts = [block_diagonal(compact[:k], levels), block_diagonal(compact[k:], levels)]
    return jnp.concatenate(parts, axis=0).astype(BF16)


def compact_section(mixing_ref, section, side):
    levels = mixing_ref.shape[0]
    return jnp.concatenate([mixing_ref[level, section, side].astype(F32) for level in range(levels)], axis=1)


def split(source, target, parts, axis):
    count = source.shape[axis] // parts
    places = [(slice(None),) * axis + (pl.ds(n * count, count),) for n in range(parts)]
    return [(source.at[place], target.at[place]) for place in places]


def load(groups, field_hbm, col_hbm, mixing_hbm, perm_hbm, xb_ref, sent_ref, *refs):
    *out_refs, field_ref, col_ref, mixing_ref, perm_ref, sems = refs
    compact = {}
    levels, sections, _, k, _ = mixing_ref.shape
    vectors = field_ref.shape[0]
    pairs = split(col_hbm, col_ref, 4, 0) + split(field_hbm, field_ref, 2, 0)
    pairs += [(mixing_hbm.at[level], mixing_ref.at[level]) for level in range(levels)]
    pairs.append((perm_hbm, perm_ref))
    copies = [pltpu.make_async_copy(*pair, sems.at[n]) for n, pair in enumerate(pairs)]
    for copy in copies:
        copy.start()
    for copy in copies:
        copy.wait()
    xb = field_ref[...].astype(BF16)
    xb_ref[...] = xb
    sent_ref[:vectors, :] = lax.dot_general(col_ref[...], xb, NT, preferred_element_type=F32).T
    row = lax.broadcasted_iota(jnp.int32, (k, k), 0)
    picks = jnp.concatenate([(row == perm_ref[level : level + 1, :]).astype(F32) for level in range(levels)], axis=1)
    picks = block_diagonal(picks, levels).astype(BF16)
    for section in range(sections):
        for side in range(2):
            mats = jnp.concatenate([mixing_ref[level, section, side].astype(F32) for level in range(levels)], axis=1)
            if section == 0:
                mats = jnp.dot(picks, block_diagonal(mats, levels).astype(BF16), preferred_element_type=F32)
                mats = sum(mats[level * k : (level + 1) * k] for level in range(levels))
            compact[section, side] = mats
            for n, (group, out_ref) in enumerate(zip(groups, (sent_ref, *out_refs))):
                if section in group:
                    start = (0 if n else vectors) + (2 * group.index(section) + side) * k
                    out_ref[start : start + k, :] = mats
    if len(out_refs) == len(groups):
        left, right = [block_diagonal(compact[which], levels).astype(BF16) for which in ((1, 1), (2, 0))]
        out_refs[-1][...] = compact_product(levels, left, right)


def build_weights(levels, chosen, *refs):
    *compact_refs, weights_ref = refs
    size = 2 * weights_ref.shape[2] // levels
    for n, (operand, start) in enumerate(chosen):
        weights_ref[n] = section_weights(compact_refs[operand][start : start + size, :], levels)


def compact_product(levels, left, right):
    k = left.shape[0] // levels
    product = jnp.dot(left, right, preferred_element_type=F32)
    return sum(product[level * k : (level + 1) * k] for level in range(levels))


def three_terms(value):
    high = value.astype(BF16)
    rest = value - high.astype(F32)
    middle = rest.astype(BF16)
    return high, middle, (rest - middle.astype(F32)).astype(BF16)


def factor_terms(levels, compact):
    return three_terms(block_diagonal(compact, levels))


def build_terms(levels, compact_ref, *refs):
    *message_refs, terms_ref = refs
    k, width = compact_ref.shape
    parts = [compact_ref[...]] + [ref[-k:, :] for ref in message_refs]
    for row, part in enumerate(parts):
        for n, term in enumerate(factor_terms(levels, part)):
            terms_ref[n, row * width : (row + 1) * width, :] = term


def terms_dot(value, terms):
    count = value.shape[0]
    stacked = jnp.concatenate(three_terms(value), axis=0)
    sums = sum(jnp.dot(stacked, term, preferred_element_type=F32) for term in reversed(terms))
    return sums[:count] + (sums[count : 2 * count] + sums[2 * count :])


def exact_dot(value, factor):
    return terms_dot(value, [factor])


def section_product(own, other, weights):
    return exact_dot(jnp.concatenate([own, other], axis=1), weights)


def run_sections(sections, final, first_refs, mine_ref, theirs_ref, out_ref):
    weights = (mine_ref, theirs_ref)
    if sections[0]:
        states_ref, other_ref = first_refs
        states, others = [states_ref[0], states_ref[1]], [other_ref[0], other_ref[1]]
    else:
        states = [ref[: out_ref.shape[1], :] for ref in first_refs]
        others = states[::-1]
    for section in sections:
        count = 1 if section == final else 2
        states = [section_product(states[n], others[n], weights[n][section]) for n in range(count)]
        others = states[::-1]
    if count == 1:
        return states[0]
    out_ref[0], out_ref[1] = states


def step(sections, final, first_ref, second_ref, mine_ref, theirs_ref, out_ref):
    run_sections(sections, final, (first_ref, second_ref), mine_ref, theirs_ref, out_ref)


def first_step(levels, sent_ref, received_ref, mine_ref, theirs_ref, out_ref):
    width = out_ref.shape[1]
    k = width // levels
    count = (out_ref.shape[0] - k) // 3
    mine, theirs = sent_ref[:count, :], received_ref[:count, :]
    mine, theirs = section_product(mine, theirs, mine_ref[0]), section_product(theirs, mine, theirs_ref[0])
    out_ref[:count, :] = mine
    out_ref[count : 2 * count, :] = theirs
    mine, theirs = exact_dot(mine, mine_ref[1, :width, :]), exact_dot(theirs, theirs_ref[1, :width, :])
    out_ref[2 * count : 3 * count, :] = section_product(mine, theirs, mine_ref[2])
    out_ref[3 * count :, :] = compact_product(levels, theirs_ref[1, width:, :], mine_ref[2, width:, :])


def level_rank(state, rank_size, half_shift, owner_ref, half):
    first_is_half = jnp.broadcast_to(owner_ref[0:1, 0:1], state.shape) == half_shift
    lane = lax.broadcasted_iota(jnp.int32, state.shape, 1)
    chosen = jnp.logical_xor(lane >= rank_size, first_is_half)
    return (jnp.where(chosen, state, 0.0) if half else jnp.where(chosen, 0.0, state)).astype(BF16)


def finish(state, rank_size, half_shift, row_ref, owner_ref, half_ref, below_ref):
    ranks = [level_rank(state, rank_size, half_shift, owner_ref, half) for half in (True, False)]
    outs = jnp.dot(jnp.concatenate(ranks, axis=0), row_ref[...], preferred_element_type=F32)
    half_ref[...] = outs[: state.shape[0]]
    below_ref[...] = outs[state.shape[0] :]


def last_step(sections, final, rank_size, half_shift, first_ref, second_ref, mine_ref, theirs_ref, *refs):
    state = run_sections(sections, final, (first_ref, second_ref), mine_ref, theirs_ref, None)
    finish(state, rank_size, half_shift, *refs)


def last_sections(levels, rank_size, half_shift, here_ref, there_ref, mine_ref, terms_ref, far_ref, *refs):
    count = (here_ref.shape[0] - rank_size) // 3
    here = jnp.concatenate([here_ref[:count, :], here_ref[count : 2 * count, :]], axis=1)
    there = jnp.concatenate([there_ref[:count, :], there_ref[count : 2 * count, :]], axis=1)
    mine = here_ref[2 * count : 3 * count, :] + terms_dot(there, [terms_ref[n] for n in range(3)])
    behind = factor_terms(levels, there_ref[3 * count :, :])
    far_terms = [jnp.concatenate([far_ref[n], behind[n]], axis=0) for n in range(3)]
    far = there_ref[2 * count : 3 * count, :] + terms_dot(here, far_terms)
    finish(section_product(mine, far, mine_ref[3]), rank_size, half_shift, *refs)


def diagonal(xb_ref, leaf_hbm, out_ref, leaf_ref, sems):
    blocks, order, _ = leaf_hbm.shape
    copies = []
    for n in range(blocks):
        for source, target in split(leaf_hbm.at[n], leaf_ref.at[n], 2, 0):
            copies.append(pltpu.make_async_copy(source, target, sems.at[len(copies)]))
            copies[-1].start()
    for n in range(blocks):
        copies[2 * n].wait()
        copies[2 * n + 1].wait()
        part = pl.ds(n * order, order)
        out_ref[:, part] = jnp.dot(xb_ref[:, part], leaf_ref[n], preferred_element_type=F32)


def combine(half_ref, below_ref, diag_ref, out_hbm, sum_ref, sems):
    parts = sems.shape[0]
    count = sum_ref.shape[1] // parts
    copies = []
    for n in range(parts):
        part = pl.ds(n * count, count)
        sum_ref[:, part] = diag_ref[:, part] + below_ref[:, part] + half_ref[:, part]
        copies.append(pltpu.make_async_copy(sum_ref.at[:, part], out_hbm.at[:, part], sems.at[n]))
        copies[-1].start()
    for copy in copies:
        copy.wait()


def shards(field, leaf_inverse, col_factor, row_factor, mixing, row_owner, rank_perm):
    vectors, rows = field.shape
    order = leaf_inverse.shape[1]
    levels, rank_size, _ = col_factor.shape
    sections = mixing.shape[2]
    bits = lax.axis_size("bf").bit_length() - 1
    groups = lax.axis_size("grp")
    width = levels * rank_size

    def array(*shape, kind=F32):
        return jax.ShapeDtypeStruct(shape, kind)

    in_hbm = [
        pltpu.with_memory_space_constraint(x, pltpu.HBM)
        for x in (field, col_factor.reshape(width, rows), mixing[0], rank_perm)
    ]
    size = 2 * rank_size
    one_round = bits == 2 and sections == 4 and levels == 2
    groups_sent = [(0, 1), (2, 3)] if one_round else [tuple(range(sections - 1)), (sections - 1,)]
    xb, sent, *kept = call(
        lambda *refs: load(groups_sent, *refs),
        [array(vectors, rows, kind=BF16)]
        + [array(len(group) * size + (0 if n else vectors), width) for n, group in enumerate(groups_sent)]
        + [array(rank_size, width)] * one_round,
        [HBM] * 4, 2 * vectors * rows * width, 3 * rows * width, *in_hbm,
        scratch=[
            pltpu.VMEM(field.shape, F32),
            pltpu.VMEM((width, rows), BF16),
            pltpu.VMEM(mixing.shape[1:], BF16),
            pltpu.VMEM(rank_perm.shape, jnp.int32),
            pltpu.SemaphoreType.DMA((1 + levels + 2 + 4,)),
        ],
    )
    weight_cost = (4 * width * width * sections, 8 * width * width * sections)

    def weights(chosen, *compacts):
        return call(
            lambda *refs: build_weights(levels, chosen, *refs), array(len(chosen), 2 * width, width, kind=BF16),
            [VMEM] * len(compacts), *weight_cost, *compacts,
        )

    def terms(*compacts, scale=1):
        return call(
            lambda *refs: build_terms(levels, *refs), array(3, len(compacts) * width, width, kind=BF16),
            [VMEM] * len(compacts), *[scale * cost for cost in weight_cost], *compacts,
        )

    received = swapped(sent)
    step_cost = (24 * vectors * width * width, 8 * width * width)
    final = sections - 1
    if one_round:
        chosen = [(0, vectors), (0, vectors + size), (1, 0), (1, size)]
        mine, factor = weights(chosen, sent, kept[0]), kept[1]
        far_factor = across(factor, 1)
        states = call(
            lambda *refs: first_step(levels, *refs), array(3 * vectors + rank_size, width), [VMEM] * 4, *step_cost,
            sent, received, mine, weights(chosen[:2], received),
        )
        first_states = (states, across(states, 1))
        last_body = lambda *refs: last_sections(levels, *refs)
        last_weights = (mine, terms(factor, states), terms(far_factor, scale=1000))
    else:
        starts = [(0, vectors + n * size) for n in range(final)]
        mine, theirs = weights(starts + [(1, 0)], sent, *kept), weights(starts, received)
        runs = []
        for section in range(sections):
            if section % bits or not section:
                runs.append([section])
            else:
                runs[-1].append(section)
        first_states = (sent, received)
        for run in runs[:-1]:
            states = call(
                lambda *refs, run=run: step(run, final, *refs), array(2, vectors, width), [VMEM] * 4, *step_cost,
                *first_states, mine, theirs,
            )
            first_states = (states, across(states, (run[-1] + 1) % bits))
        last_body = lambda *refs: last_step(runs[-1], final, *refs)
        last_weights = (mine, theirs)
    expand_cost = (2 * vectors * width * rows, 4 * width * rows)
    expand = row_factor.reshape(width, rows)
    out_half, out_below = call(
        lambda *refs: last_body(rank_size, groups // 2, *refs), [array(vectors, rows)] * 2,
        [VMEM] * (4 + len(last_weights)), *expand_cost, *first_states, *last_weights, expand, row_owner,
    )
    out_half = shifted(out_half, "grp", groups // 2)
    out_below = shifted(out_below, "grp", groups - 1)
    diag = call(
        diagonal, array(vectors, rows), [VMEM, HBM], 2 * vectors * rows * order, 2 * rows * order,
        xb, pltpu.with_memory_space_constraint(leaf_inverse, pltpu.HBM),
        scratch=[pltpu.VMEM(leaf_inverse.shape, BF16), pltpu.SemaphoreType.DMA((2 * leaf_inverse.shape[0],))],
    )
    return call(
        combine, array(vectors, rows), [VMEM] * 3, 2 * vectors * rows, 16 * vectors * rows, out_half, out_below, diag,
        scratch=[pltpu.VMEM((vectors, rows), F32), pltpu.SemaphoreType.DMA((4,))], out=HBM,
    )


def solution(mesh):
    in_specs = (
        P(None, ("grp", "bf")),
        P(("grp", "bf"), None, None),
        P(None, None, ("grp", "bf")),
        P(None, None, ("grp", "bf")),
        P(("grp", "bf"), None, None, None, None, None),
        P(),
        P(),
    )
    out_specs = P(None, ("grp", "bf"))
    return jax.shard_map(shards, mesh=mesh, in_specs=in_specs, out_specs=out_specs, check_vma=False)
```

```python
import jax
import jax.numpy as jnp
from jax import lax
from jax.experimental import pallas as pl
from jax.experimental.pallas import tpu as pltpu
from jax.sharding import PartitionSpec as P

F32, BF16 = jnp.float32, jnp.bfloat16
VMEM = pl.BlockSpec(memory_space=pltpu.VMEM)
HBM = pl.BlockSpec(memory_space=pltpu.HBM)
NT = (((1,), (1,)), ((), ()))


def shifted(value, axis, distance):
    size = lax.axis_size(axis)
    return lax.ppermute(value, axis, [(source, (source + distance) % size) for source in range(size)])


def swapped_groups(value):
    return lax.ppermute(value, "grp", [(g, g ^ 1) for g in range(lax.axis_size("grp"))])


def rest_below(value):
    size, places = lax.axis_size("grp"), lax.axis_size("bf")
    pairs = []
    for g in range(size):
        for b in range(places):
            if b % 2:
                target = ((g - 2) % size, b) if g % 2 else (g, b ^ 2)
            else:
                target = (g ^ 1, b) if g % 2 else ((g - 1) % size, b)
            pairs.append((g * places + b, target[0] * places + target[1]))
    return lax.ppermute(value, ("grp", "bf"), pairs)


def swapped(value):
    return lax.ppermute(value, "bf", [(n, n ^ 1) for n in range(lax.axis_size("bf"))])


def across(value, bit):
    return lax.ppermute(value, "bf", [(n, n ^ 1 << bit) for n in range(lax.axis_size("bf"))])


def call(body, shapes, specs, flops, moved, *operands, scratch=(), out=VMEM):
    return pl.pallas_call(
        body,
        out_shape=shapes,
        in_specs=specs,
        out_specs=jax.tree.map(lambda _: out, shapes),
        scratch_shapes=scratch,
        cost_estimate=pl.CostEstimate(flops=flops, bytes_accessed=moved, transcendentals=0),
        compiler_params=pltpu.CompilerParams(vmem_limit_bytes=16 * 2**20),
    )(*operands)


def block_diagonal(compact, levels):
    k = compact.shape[0]
    lane = lax.broadcasted_iota(jnp.int32, compact.shape, 1)
    parts = []
    for level in range(levels):
        mine = jnp.logical_and(lane >= level * k, lane < (level + 1) * k)
        parts.append(jnp.where(mine, compact, 0.0))
    return jnp.concatenate(parts, axis=0)


def section_weights(compact, levels):
    k = compact.shape[0] // 2
    parts = [block_diagonal(compact[:k], levels), block_diagonal(compact[k:], levels)]
    return jnp.concatenate(parts, axis=0).astype(BF16)


def compact_section(mixing_ref, section, side):
    levels = mixing_ref.shape[0]
    return jnp.concatenate([mixing_ref[level, section, side].astype(F32) for level in range(levels)], axis=1)


def split(source, target, parts, axis):
    count = source.shape[axis] // parts
    places = [(slice(None),) * axis + (pl.ds(n * count, count),) for n in range(parts)]
    return [(source.at[place], target.at[place]) for place in places]


def load(groups, field_hbm, col_hbm, mixing_hbm, perm_hbm, xb_ref, sent_ref, *refs):
    *out_refs, field_ref, col_ref, mixing_ref, perm_ref, sems = refs
    compact = {}
    levels, sections, _, k, _ = mixing_ref.shape
    vectors = field_ref.shape[0]
    pairs = split(col_hbm, col_ref, 4, 0) + split(field_hbm, field_ref, 2, 0)
    pairs += [(mixing_hbm.at[level], mixing_ref.at[level]) for level in range(levels)]
    pairs.append((perm_hbm, perm_ref))
    copies = [pltpu.make_async_copy(*pair, sems.at[n]) for n, pair in enumerate(pairs)]
    for copy in copies:
        copy.start()
    for copy in copies:
        copy.wait()
    xb = field_ref[...].astype(BF16)
    xb_ref[...] = xb
    sent_ref[:vectors, :] = lax.dot_general(xb, col_ref[...], NT, preferred_element_type=F32)
    row = lax.broadcasted_iota(jnp.int32, (k, k), 0)
    picks = jnp.concatenate([(row == perm_ref[level : level + 1, :]).astype(F32) for level in range(levels)], axis=1)
    picks = block_diagonal(picks, levels).astype(BF16)
    for section in range(sections):
        for side in range(2):
            mats = jnp.concatenate([mixing_ref[level, section, side].astype(F32) for level in range(levels)], axis=1)
            if section == 0:
                mats = jnp.dot(picks, block_diagonal(mats, levels).astype(BF16), preferred_element_type=F32)
                mats = sum(mats[level * k : (level + 1) * k] for level in range(levels))
            compact[section, side] = mats
            for n, (group, out_ref) in enumerate(zip(groups, (sent_ref, *out_refs))):
                if section in group:
                    start = (0 if n else vectors) + (2 * group.index(section) + side) * k
                    out_ref[start : start + k, :] = mats
    if len(out_refs) == len(groups):
        left, right = [block_diagonal(compact[which], levels).astype(BF16) for which in ((1, 1), (2, 0))]
        out_refs[-1][...] = compact_product(levels, left, right)


def build_weights(levels, chosen, *refs):
    *compact_refs, weights_ref = refs
    size = 2 * weights_ref.shape[2] // levels
    for n, (operand, start) in enumerate(chosen):
        weights_ref[n] = section_weights(compact_refs[operand][start : start + size, :], levels)


def compact_product(levels, left, right):
    k = left.shape[0] // levels
    product = jnp.dot(left, right, preferred_element_type=F32)
    return sum(product[level * k : (level + 1) * k] for level in range(levels))


def three_terms(value):
    high = value.astype(BF16)
    rest = value - high.astype(F32)
    middle = rest.astype(BF16)
    return high, middle, (rest - middle.astype(F32)).astype(BF16)


def factor_terms(levels, compact):
    return three_terms(block_diagonal(compact, levels))


def build_terms(levels, compact_ref, *refs):
    *message_refs, terms_ref = refs
    k, width = compact_ref.shape
    parts = [compact_ref[...]] + [ref[-k:, :] for ref in message_refs]
    for row, part in enumerate(parts):
        for n, term in enumerate(factor_terms(levels, part)):
            terms_ref[n, row * width : (row + 1) * width, :] = term


def terms_dot(value, terms):
    count = value.shape[0]
    stacked = jnp.concatenate(three_terms(value), axis=0)
    sums = sum(jnp.dot(stacked, term, preferred_element_type=F32) for term in reversed(terms))
    return sums[:count] + (sums[count : 2 * count] + sums[2 * count :])


def exact_dot(value, factor):
    return terms_dot(value, [factor])


def section_product(own, other, weights):
    return exact_dot(jnp.concatenate([own, other], axis=1), weights)


def run_sections(sections, final, first_refs, mine_ref, theirs_ref, out_ref):
    weights = (mine_ref, theirs_ref)
    if sections[0]:
        states_ref, other_ref = first_refs
        states, others = [states_ref[0], states_ref[1]], [other_ref[0], other_ref[1]]
    else:
        states = [ref[: out_ref.shape[1], :] for ref in first_refs]
        others = states[::-1]
    for section in sections:
        count = 1 if section == final else 2
        states = [section_product(states[n], others[n], weights[n][section]) for n in range(count)]
        others = states[::-1]
    if count == 1:
        return states[0]
    out_ref[0], out_ref[1] = states


def step(sections, final, first_ref, second_ref, mine_ref, theirs_ref, out_ref):
    run_sections(sections, final, (first_ref, second_ref), mine_ref, theirs_ref, out_ref)


def first_step(levels, sent_ref, received_ref, mine_ref, theirs_ref, out_ref):
    width = out_ref.shape[1]
    k = width // levels
    count = (out_ref.shape[0] - k) // 3
    mine, theirs = sent_ref[:count, :], received_ref[:count, :]
    mine, theirs = section_product(mine, theirs, mine_ref[0]), section_product(theirs, mine, theirs_ref[0])
    out_ref[:count, :] = mine
    out_ref[count : 2 * count, :] = theirs
    mine, theirs = exact_dot(mine, mine_ref[1, :width, :]), exact_dot(theirs, theirs_ref[1, :width, :])
    out_ref[2 * count : 3 * count, :] = section_product(mine, theirs, mine_ref[2])
    out_ref[3 * count :, :] = compact_product(levels, theirs_ref[1, width:, :], mine_ref[2, width:, :])


def level_rank(state, rank_size, half_shift, owner_ref, half):
    first_is_half = jnp.broadcast_to(owner_ref[0:1, 0:1], state.shape) == half_shift
    lane = lax.broadcasted_iota(jnp.int32, state.shape, 1)
    chosen = jnp.logical_xor(lane >= rank_size, first_is_half)
    return (jnp.where(chosen, state, 0.0) if half else jnp.where(chosen, 0.0, state)).astype(BF16)


def finish(state, rank_size, half_shift, row_ref, owner_ref, half_ref, below_ref):
    ranks = [level_rank(state, rank_size, half_shift, owner_ref, half) for half in (True, False)]
    outs = jnp.dot(jnp.concatenate(ranks, axis=0), row_ref[...], preferred_element_type=F32)
    half_ref[...] = outs[: state.shape[0]]
    below_ref[...] = outs[state.shape[0] :]


def last_step(sections, final, rank_size, half_shift, first_ref, second_ref, mine_ref, theirs_ref, *refs):
    state = run_sections(sections, final, (first_ref, second_ref), mine_ref, theirs_ref, None)
    finish(state, rank_size, half_shift, *refs)


def last_sections(levels, rank_size, half_shift, here_ref, there_ref, mine_ref, terms_ref, far_ref, *refs):
    count = (here_ref.shape[0] - rank_size) // 3
    here = jnp.concatenate([here_ref[:count, :], here_ref[count : 2 * count, :]], axis=1)
    there = jnp.concatenate([there_ref[:count, :], there_ref[count : 2 * count, :]], axis=1)
    mine = here_ref[2 * count : 3 * count, :] + terms_dot(there, [terms_ref[n] for n in range(3)])
    behind = factor_terms(levels, there_ref[3 * count :, :])
    far_terms = [jnp.concatenate([far_ref[n], behind[n]], axis=0) for n in range(3)]
    far = there_ref[2 * count : 3 * count, :] + terms_dot(here, far_terms)
    finish(section_product(mine, far, mine_ref[3]), rank_size, half_shift, *refs)


def diagonal(xb_ref, leaf_hbm, out_ref, leaf_ref, sems):
    blocks, order, _ = leaf_hbm.shape
    copies = []
    for n in range(blocks):
        for source, target in split(leaf_hbm.at[n], leaf_ref.at[n], 2, 0):
            copies.append(pltpu.make_async_copy(source, target, sems.at[len(copies)]))
            copies[-1].start()
    for n in range(blocks):
        copies[2 * n].wait()
        copies[2 * n + 1].wait()
        part = pl.ds(n * order, order)
        out_ref[:, part] = jnp.dot(xb_ref[:, part], leaf_ref[n], preferred_element_type=F32)


def arrived(half_ref, out_ref):
    out_ref[...] = half_ref[: out_ref.shape[0], : out_ref.shape[1]]


def combine(half_ref, near_ref, rest_ref, diag_ref, _, out_hbm, sum_ref, sems):
    parts = sems.shape[0]
    count = sum_ref.shape[1] // parts
    odd = jnp.broadcast_to(lax.rem(lax.axis_index("grp"), 2), (sum_ref.shape[0], count)) == 1
    copies = []
    for n in range(parts):
        part = pl.ds(n * count, count)
        below = jnp.where(odd, rest_ref[:, part], near_ref[:, part])
        sum_ref[:, part] = diag_ref[:, part] + below + half_ref[:, part]
        copies.append(pltpu.make_async_copy(sum_ref.at[:, part], out_hbm.at[:, part], sems.at[n]))
        copies[-1].start()
    for copy in copies:
        copy.wait()


def shards(field, leaf_inverse, col_factor, row_factor, mixing, row_owner, rank_perm):
    vectors, rows = field.shape
    order = leaf_inverse.shape[1]
    levels, rank_size, _ = col_factor.shape
    sections = mixing.shape[2]
    bits = lax.axis_size("bf").bit_length() - 1
    groups = lax.axis_size("grp")
    width = levels * rank_size

    def array(*shape, kind=F32):
        return jax.ShapeDtypeStruct(shape, kind)

    in_hbm = [
        pltpu.with_memory_space_constraint(x, pltpu.HBM)
        for x in (field, col_factor.reshape(width, rows), mixing[0], rank_perm)
    ]
    size = 2 * rank_size
    one_round = bits == 2 and sections == 4 and levels == 2
    groups_sent = [(0, 1), (2, 3)] if one_round else [tuple(range(sections - 1)), (sections - 1,)]
    xb, sent, *kept = call(
        lambda *refs: load(groups_sent, *refs),
        [array(vectors, rows, kind=BF16)]
        + [array(len(group) * size + (0 if n else vectors), width) for n, group in enumerate(groups_sent)]
        + [array(rank_size, width)] * one_round,
        [HBM] * 4, 2 * vectors * rows * width, 3 * rows * width, *in_hbm,
        scratch=[
            pltpu.VMEM(field.shape, F32),
            pltpu.VMEM((width, rows), BF16),
            pltpu.VMEM(mixing.shape[1:], BF16),
            pltpu.VMEM(rank_perm.shape, jnp.int32),
            pltpu.SemaphoreType.DMA((1 + levels + 2 + 4,)),
        ],
    )
    weight_cost = (4 * width * width * sections, 8 * width * width * sections)

    def weights(chosen, *compacts):
        return call(
            lambda *refs: build_weights(levels, chosen, *refs), array(len(chosen), 2 * width, width, kind=BF16),
            [VMEM] * len(compacts), *weight_cost, *compacts,
        )

    def terms(*compacts, scale=1):
        return call(
            lambda *refs: build_terms(levels, *refs), array(3, len(compacts) * width, width, kind=BF16),
            [VMEM] * len(compacts), *[scale * cost for cost in weight_cost], *compacts,
        )

    received = swapped(sent)
    step_cost = (24 * vectors * width * width, 8 * width * width)
    final = sections - 1
    if one_round:
        chosen = [(0, vectors), (0, vectors + size), (1, 0), (1, size)]
        mine, factor = weights(chosen, sent, kept[0]), kept[1]
        far_factor = across(factor, 1)
        states = call(
            lambda *refs: first_step(levels, *refs), array(3 * vectors + rank_size, width), [VMEM] * 4, *step_cost,
            sent, received, mine, weights(chosen[:2], received),
        )
        first_states = (states, across(states, 1))
        last_body = lambda *refs: last_sections(levels, *refs)
        last_weights = (mine, terms(factor, states), terms(far_factor, scale=1000))
    else:
        starts = [(0, vectors + n * size) for n in range(final)]
        mine, theirs = weights(starts + [(1, 0)], sent, *kept), weights(starts, received)
        runs = []
        for section in range(sections):
            if section % bits or not section:
                runs.append([section])
            else:
                runs[-1].append(section)
        first_states = (sent, received)
        for run in runs[:-1]:
            states = call(
                lambda *refs, run=run: step(run, final, *refs), array(2, vectors, width), [VMEM] * 4, *step_cost,
                *first_states, mine, theirs,
            )
            first_states = (states, across(states, (run[-1] + 1) % bits))
        last_body = lambda *refs: last_step(runs[-1], final, *refs)
        last_weights = (mine, theirs)
    expand_cost = (2 * vectors * width * rows, 4 * width * rows)
    expand = row_factor.reshape(width, rows)
    out_half, out_below = call(
        lambda *refs: last_body(rank_size, groups // 2, *refs), [array(vectors, rows)] * 2,
        [VMEM] * (4 + len(last_weights)), *expand_cost, *first_states, *last_weights, expand, row_owner,
    )
    out_half = shifted(out_half, "grp", groups // 2)
    near = swapped_groups(out_below)
    rest = rest_below(jnp.where(lax.axis_index("bf") % 2 == 1, near, out_below))
    diag = call(
        diagonal, array(vectors, rows), [VMEM, HBM], 2 * vectors * rows * order, 2 * rows * order,
        xb, pltpu.with_memory_space_constraint(leaf_inverse, pltpu.HBM),
        scratch=[pltpu.VMEM(leaf_inverse.shape, BF16), pltpu.SemaphoreType.DMA((2 * leaf_inverse.shape[0],))],
    )
    token = call(arrived, array(8, 128), [VMEM], *[1000 * cost for cost in weight_cost], out_half)
    return call(
        combine, array(vectors, rows), [VMEM] * 5, 2 * vectors * rows, 16 * vectors * rows, out_half, near, rest, diag, token,
        scratch=[pltpu.VMEM((vectors, rows), F32), pltpu.SemaphoreType.DMA((4,))], out=HBM,
    )


def solution(mesh):
    in_specs = (
        P(None, ("grp", "bf")),
        P(("grp", "bf"), None, None),
        P(None, None, ("grp", "bf")),
        P(None, None, ("grp", "bf")),
        P(("grp", "bf"), None, None, None, None, None),
        P(),
        P(),
    )
    out_specs = P(None, ("grp", "bf"))
    return jax.shard_map(shards, mesh=mesh, in_specs=in_specs, out_specs=out_specs, check_vma=False)
```

```python
import jax
import jax.numpy as jnp
from jax import lax
from jax.experimental import pallas as pl
from jax.experimental.pallas import tpu as pltpu
from jax.sharding import PartitionSpec as P

F32, BF16 = jnp.float32, jnp.bfloat16
VMEM = pl.BlockSpec(memory_space=pltpu.VMEM)
HBM = pl.BlockSpec(memory_space=pltpu.HBM)
NT = (((1,), (1,)), ((), ()))


def shifted(value, axis, distance):
    size = lax.axis_size(axis)
    return lax.ppermute(value, axis, [(source, (source + distance) % size) for source in range(size)])


def swapped_groups(value):
    return lax.ppermute(value, "grp", [(g, g ^ 1) for g in range(lax.axis_size("grp"))])


def below_from_even(value, step, parity):
    size, places = lax.axis_size("grp"), lax.axis_size("bf")
    pairs = []
    for g in range(size):
        for b in range(places):
            if b % 2 != parity:
                target = (g, b ^ 2)
            elif g % 2 == step - 1:
                target = ((g - step) % size, b)
            else:
                target = (g ^ 1, b) if step == 1 else (g, b ^ 2)
            pairs.append((g * places + b, target[0] * places + target[1]))
    return lax.ppermute(value, ("grp", "bf"), pairs)


def swapped(value):
    return lax.ppermute(value, "bf", [(n, n ^ 1) for n in range(lax.axis_size("bf"))])


def across(value, bit):
    return lax.ppermute(value, "bf", [(n, n ^ 1 << bit) for n in range(lax.axis_size("bf"))])


def call(body, shapes, specs, flops, moved, *operands, scratch=(), out=VMEM):
    return pl.pallas_call(
        body,
        out_shape=shapes,
        in_specs=specs,
        out_specs=jax.tree.map(lambda _: out, shapes),
        scratch_shapes=scratch,
        cost_estimate=pl.CostEstimate(flops=flops, bytes_accessed=moved, transcendentals=0),
        compiler_params=pltpu.CompilerParams(vmem_limit_bytes=16 * 2**20),
    )(*operands)


def block_diagonal(compact, levels):
    k = compact.shape[0]
    lane = lax.broadcasted_iota(jnp.int32, compact.shape, 1)
    parts = []
    for level in range(levels):
        mine = jnp.logical_and(lane >= level * k, lane < (level + 1) * k)
        parts.append(jnp.where(mine, compact, 0.0))
    return jnp.concatenate(parts, axis=0)


def section_weights(compact, levels):
    k = compact.shape[0] // 2
    parts = [block_diagonal(compact[:k], levels), block_diagonal(compact[k:], levels)]
    return jnp.concatenate(parts, axis=0).astype(BF16)


def compact_section(mixing_ref, section, side):
    levels = mixing_ref.shape[0]
    return jnp.concatenate([mixing_ref[level, section, side].astype(F32) for level in range(levels)], axis=1)


def split(source, target, parts, axis):
    count = source.shape[axis] // parts
    places = [(slice(None),) * axis + (pl.ds(n * count, count),) for n in range(parts)]
    return [(source.at[place], target.at[place]) for place in places]


def load(groups, field_hbm, col_hbm, mixing_hbm, perm_hbm, xb_ref, sent_ref, *refs):
    *out_refs, field_ref, col_ref, mixing_ref, perm_ref, sems = refs
    compact = {}
    levels, sections, _, k, _ = mixing_ref.shape
    vectors = field_ref.shape[0]
    pairs = split(col_hbm, col_ref, 4, 0) + split(field_hbm, field_ref, 2, 0)
    pairs += [(mixing_hbm.at[level], mixing_ref.at[level]) for level in range(levels)]
    pairs.append((perm_hbm, perm_ref))
    copies = [pltpu.make_async_copy(*pair, sems.at[n]) for n, pair in enumerate(pairs)]
    for copy in copies:
        copy.start()
    for copy in copies:
        copy.wait()
    xb = field_ref[...].astype(BF16)
    xb_ref[...] = xb
    sent_ref[:vectors, :] = lax.dot_general(xb, col_ref[...], NT, preferred_element_type=F32)
    row = lax.broadcasted_iota(jnp.int32, (k, k), 0)
    picks = jnp.concatenate([(row == perm_ref[level : level + 1, :]).astype(F32) for level in range(levels)], axis=1)
    picks = block_diagonal(picks, levels).astype(BF16)
    for section in range(sections):
        for side in range(2):
            mats = jnp.concatenate([mixing_ref[level, section, side].astype(F32) for level in range(levels)], axis=1)
            if section == 0:
                mats = jnp.dot(picks, block_diagonal(mats, levels).astype(BF16), preferred_element_type=F32)
                mats = sum(mats[level * k : (level + 1) * k] for level in range(levels))
            compact[section, side] = mats
            for n, (group, out_ref) in enumerate(zip(groups, (sent_ref, *out_refs))):
                if section in group:
                    start = (0 if n else vectors) + (2 * group.index(section) + side) * k
                    out_ref[start : start + k, :] = mats
    if len(out_refs) == len(groups):
        left, right = [block_diagonal(compact[which], levels).astype(BF16) for which in ((1, 1), (2, 0))]
        out_refs[-1][...] = compact_product(levels, left, right)


def build_weights(levels, chosen, *refs):
    *compact_refs, weights_ref = refs
    size = 2 * weights_ref.shape[2] // levels
    for n, (operand, start) in enumerate(chosen):
        weights_ref[n] = section_weights(compact_refs[operand][start : start + size, :], levels)


def compact_product(levels, left, right):
    k = left.shape[0] // levels
    product = jnp.dot(left, right, preferred_element_type=F32)
    return sum(product[level * k : (level + 1) * k] for level in range(levels))


def three_terms(value):
    high = value.astype(BF16)
    rest = value - high.astype(F32)
    middle = rest.astype(BF16)
    return high, middle, (rest - middle.astype(F32)).astype(BF16)


def factor_terms(levels, compact):
    return three_terms(block_diagonal(compact, levels))


def build_terms(levels, compact_ref, *refs):
    *message_refs, terms_ref = refs
    k, width = compact_ref.shape
    parts = [compact_ref[...]] + [ref[-k:, :] for ref in message_refs]
    for row, part in enumerate(parts):
        for n, term in enumerate(factor_terms(levels, part)):
            terms_ref[n, row * width : (row + 1) * width, :] = term


def terms_dot(value, terms):
    count = value.shape[0]
    stacked = jnp.concatenate(three_terms(value), axis=0)
    sums = sum(jnp.dot(stacked, term, preferred_element_type=F32) for term in reversed(terms))
    return sums[:count] + (sums[count : 2 * count] + sums[2 * count :])


def exact_dot(value, factor):
    return terms_dot(value, [factor])


def section_product(own, other, weights):
    return exact_dot(jnp.concatenate([own, other], axis=1), weights)


def run_sections(sections, final, first_refs, mine_ref, theirs_ref, out_ref):
    weights = (mine_ref, theirs_ref)
    if sections[0]:
        states_ref, other_ref = first_refs
        states, others = [states_ref[0], states_ref[1]], [other_ref[0], other_ref[1]]
    else:
        states = [ref[: out_ref.shape[1], :] for ref in first_refs]
        others = states[::-1]
    for section in sections:
        count = 1 if section == final else 2
        states = [section_product(states[n], others[n], weights[n][section]) for n in range(count)]
        others = states[::-1]
    if count == 1:
        return states[0]
    out_ref[0], out_ref[1] = states


def step(sections, final, first_ref, second_ref, mine_ref, theirs_ref, out_ref):
    run_sections(sections, final, (first_ref, second_ref), mine_ref, theirs_ref, out_ref)


def first_step(levels, sent_ref, received_ref, mine_ref, theirs_ref, out_ref):
    width = out_ref.shape[1]
    k = width // levels
    count = (out_ref.shape[0] - k) // 3
    mine, theirs = sent_ref[:count, :], received_ref[:count, :]
    mine, theirs = section_product(mine, theirs, mine_ref[0]), section_product(theirs, mine, theirs_ref[0])
    out_ref[:count, :] = mine
    out_ref[count : 2 * count, :] = theirs
    mine, theirs = exact_dot(mine, mine_ref[1, :width, :]), exact_dot(theirs, theirs_ref[1, :width, :])
    out_ref[2 * count : 3 * count, :] = section_product(mine, theirs, mine_ref[2])
    out_ref[3 * count :, :] = compact_product(levels, theirs_ref[1, width:, :], mine_ref[2, width:, :])


def level_rank(state, rank_size, half_shift, owner_ref, half):
    first_is_half = jnp.broadcast_to(owner_ref[0:1, 0:1], state.shape) == half_shift
    lane = lax.broadcasted_iota(jnp.int32, state.shape, 1)
    chosen = jnp.logical_xor(lane >= rank_size, first_is_half)
    return (jnp.where(chosen, state, 0.0) if half else jnp.where(chosen, 0.0, state)).astype(BF16)


def finish(state, rank_size, half_shift, row_ref, owner_ref, half_ref, below_ref):
    ranks = [level_rank(state, rank_size, half_shift, owner_ref, half) for half in (True, False)]
    outs = jnp.dot(jnp.concatenate(ranks, axis=0), row_ref[...], preferred_element_type=F32)
    half_ref[...] = outs[: state.shape[0]]
    below_ref[...] = outs[state.shape[0] :]


def last_step(sections, final, rank_size, half_shift, first_ref, second_ref, mine_ref, theirs_ref, *refs):
    state = run_sections(sections, final, (first_ref, second_ref), mine_ref, theirs_ref, None)
    finish(state, rank_size, half_shift, *refs)


def last_sections(levels, rank_size, half_shift, here_ref, there_ref, mine_ref, terms_ref, far_ref, *refs):
    count = (here_ref.shape[0] - rank_size) // 3
    here = jnp.concatenate([here_ref[:count, :], here_ref[count : 2 * count, :]], axis=1)
    there = jnp.concatenate([there_ref[:count, :], there_ref[count : 2 * count, :]], axis=1)
    mine = here_ref[2 * count : 3 * count, :] + terms_dot(there, [terms_ref[n] for n in range(3)])
    behind = factor_terms(levels, there_ref[3 * count :, :])
    far_terms = [jnp.concatenate([far_ref[n], behind[n]], axis=0) for n in range(3)]
    far = there_ref[2 * count : 3 * count, :] + terms_dot(here, far_terms)
    finish(section_product(mine, far, mine_ref[3]), rank_size, half_shift, *refs)


def diagonal(xb_ref, leaf_hbm, out_ref, leaf_ref, sems):
    blocks, order, _ = leaf_hbm.shape
    copies = []
    for n in range(blocks):
        for source, target in split(leaf_hbm.at[n], leaf_ref.at[n], 2, 0):
            copies.append(pltpu.make_async_copy(source, target, sems.at[len(copies)]))
            copies[-1].start()
    for n in range(blocks):
        copies[2 * n].wait()
        copies[2 * n + 1].wait()
        part = pl.ds(n * order, order)
        out_ref[:, part] = jnp.dot(xb_ref[:, part], leaf_ref[n], preferred_element_type=F32)


def arrived(half_ref, out_ref):
    out_ref[...] = half_ref[: out_ref.shape[0], : out_ref.shape[1]]


def combine(half_ref, near_ref, straight_ref, onward_ref, diag_ref, _, out_hbm, sum_ref, sems):
    parts = sems.shape[0]
    count = sum_ref.shape[1] // parts
    shape = (sum_ref.shape[0], count)
    odd = jnp.broadcast_to(lax.rem(lax.axis_index("grp"), 2), shape) == 1
    first = jnp.broadcast_to(lax.rem(lax.axis_index("bf"), 2), shape) == 0
    copies = []
    for n in range(parts):
        part = pl.ds(n * count, count)
        rest = jnp.where(first, straight_ref[:, part], onward_ref[:, part])
        below = jnp.where(odd, rest, near_ref[:, part])
        sum_ref[:, part] = diag_ref[:, part] + below + half_ref[:, part]
        copies.append(pltpu.make_async_copy(sum_ref.at[:, part], out_hbm.at[:, part], sems.at[n]))
        copies[-1].start()
    for copy in copies:
        copy.wait()


def shards(field, leaf_inverse, col_factor, row_factor, mixing, row_owner, rank_perm):
    vectors, rows = field.shape
    order = leaf_inverse.shape[1]
    levels, rank_size, _ = col_factor.shape
    sections = mixing.shape[2]
    bits = lax.axis_size("bf").bit_length() - 1
    groups = lax.axis_size("grp")
    width = levels * rank_size

    def array(*shape, kind=F32):
        return jax.ShapeDtypeStruct(shape, kind)

    in_hbm = [
        pltpu.with_memory_space_constraint(x, pltpu.HBM)
        for x in (field, col_factor.reshape(width, rows), mixing[0], rank_perm)
    ]
    size = 2 * rank_size
    one_round = bits == 2 and sections == 4 and levels == 2
    groups_sent = [(0, 1), (2, 3)] if one_round else [tuple(range(sections - 1)), (sections - 1,)]
    xb, sent, *kept = call(
        lambda *refs: load(groups_sent, *refs),
        [array(vectors, rows, kind=BF16)]
        + [array(len(group) * size + (0 if n else vectors), width) for n, group in enumerate(groups_sent)]
        + [array(rank_size, width)] * one_round,
        [HBM] * 4, 2 * vectors * rows * width, 3 * rows * width, *in_hbm,
        scratch=[
            pltpu.VMEM(field.shape, F32),
            pltpu.VMEM((width, rows), BF16),
            pltpu.VMEM(mixing.shape[1:], BF16),
            pltpu.VMEM(rank_perm.shape, jnp.int32),
            pltpu.SemaphoreType.DMA((1 + levels + 2 + 4,)),
        ],
    )
    weight_cost = (4 * width * width * sections, 8 * width * width * sections)

    def weights(chosen, *compacts):
        return call(
            lambda *refs: build_weights(levels, chosen, *refs), array(len(chosen), 2 * width, width, kind=BF16),
            [VMEM] * len(compacts), *weight_cost, *compacts,
        )

    def terms(*compacts, scale=1):
        return call(
            lambda *refs: build_terms(levels, *refs), array(3, len(compacts) * width, width, kind=BF16),
            [VMEM] * len(compacts), *[scale * cost for cost in weight_cost], *compacts,
        )

    received = swapped(sent)
    step_cost = (24 * vectors * width * width, 8 * width * width)
    final = sections - 1
    if one_round:
        chosen = [(0, vectors), (0, vectors + size), (1, 0), (1, size)]
        mine, factor = weights(chosen, sent, kept[0]), kept[1]
        far_factor = across(factor, 1)
        states = call(
            lambda *refs: first_step(levels, *refs), array(3 * vectors + rank_size, width), [VMEM] * 4, *step_cost,
            sent, received, mine, weights(chosen[:2], received),
        )
        first_states = (states, across(states, 1))
        last_body = lambda *refs: last_sections(levels, *refs)
        last_weights = (mine, terms(factor, states), terms(far_factor, scale=1000))
    else:
        starts = [(0, vectors + n * size) for n in range(final)]
        mine, theirs = weights(starts + [(1, 0)], sent, *kept), weights(starts, received)
        runs = []
        for section in range(sections):
            if section % bits or not section:
                runs.append([section])
            else:
                runs[-1].append(section)
        first_states = (sent, received)
        for run in runs[:-1]:
            states = call(
                lambda *refs, run=run: step(run, final, *refs), array(2, vectors, width), [VMEM] * 4, *step_cost,
                *first_states, mine, theirs,
            )
            first_states = (states, across(states, (run[-1] + 1) % bits))
        last_body = lambda *refs: last_step(runs[-1], final, *refs)
        last_weights = (mine, theirs)
    expand_cost = (2 * vectors * width * rows, 4 * width * rows)
    expand = row_factor.reshape(width, rows)
    out_half, out_below = call(
        lambda *refs: last_body(rank_size, groups // 2, *refs), [array(vectors, rows)] * 2,
        [VMEM] * (4 + len(last_weights)), *expand_cost, *first_states, *last_weights, expand, row_owner,
    )
    out_half = shifted(out_half, "grp", groups // 2)
    near = swapped_groups(out_below)
    straight = below_from_even(out_below, 1, 0)
    onward = below_from_even(near, 2, 1)
    diag = call(
        diagonal, array(vectors, rows), [VMEM, HBM], 2 * vectors * rows * order, 2 * rows * order,
        xb, pltpu.with_memory_space_constraint(leaf_inverse, pltpu.HBM),
        scratch=[pltpu.VMEM(leaf_inverse.shape, BF16), pltpu.SemaphoreType.DMA((2 * leaf_inverse.shape[0],))],
    )
    token = call(arrived, array(8, 128), [VMEM], *[1000 * cost for cost in weight_cost], out_half)
    return call(
        combine, array(vectors, rows), [VMEM] * 6, 2 * vectors * rows, 16 * vectors * rows, out_half, near, straight, onward, diag, token,
        scratch=[pltpu.VMEM((vectors, rows), F32), pltpu.SemaphoreType.DMA((4,))], out=HBM,
    )


def solution(mesh):
    in_specs = (
        P(None, ("grp", "bf")),
        P(("grp", "bf"), None, None),
        P(None, None, ("grp", "bf")),
        P(None, None, ("grp", "bf")),
        P(("grp", "bf"), None, None, None, None, None),
        P(),
        P(),
    )
    out_specs = P(None, ("grp", "bf"))
    return jax.shard_map(shards, mesh=mesh, in_specs=in_specs, out_specs=out_specs, check_vma=False)
```

```python
import jax
import jax.numpy as jnp
from jax import lax
from jax.experimental import pallas as pl
from jax.experimental.pallas import tpu as pltpu
from jax.sharding import PartitionSpec as P

F32, BF16 = jnp.float32, jnp.bfloat16
VMEM = pl.BlockSpec(memory_space=pltpu.VMEM)
HBM = pl.BlockSpec(memory_space=pltpu.HBM)
NT = (((1,), (1,)), ((), ()))


def shifted(value, axis, distance):
    size = lax.axis_size(axis)
    return lax.ppermute(value, axis, [(source, (source + distance) % size) for source in range(size)])


def swapped(value):
    return lax.ppermute(value, "bf", [(n, n ^ 1) for n in range(lax.axis_size("bf"))])


def across(value, bit):
    return lax.ppermute(value, "bf", [(n, n ^ 1 << bit) for n in range(lax.axis_size("bf"))])


def call(body, shapes, specs, flops, moved, *operands, scratch=(), out=VMEM):
    return pl.pallas_call(
        body,
        out_shape=shapes,
        in_specs=specs,
        out_specs=jax.tree.map(lambda _: out, shapes),
        scratch_shapes=scratch,
        cost_estimate=pl.CostEstimate(flops=flops, bytes_accessed=moved, transcendentals=0),
        compiler_params=pltpu.CompilerParams(vmem_limit_bytes=16 * 2**20),
    )(*operands)


def block_diagonal(compact, levels):
    k = compact.shape[0]
    lane = lax.broadcasted_iota(jnp.int32, compact.shape, 1)
    parts = []
    for level in range(levels):
        mine = jnp.logical_and(lane >= level * k, lane < (level + 1) * k)
        parts.append(jnp.where(mine, compact, 0.0))
    return jnp.concatenate(parts, axis=0)


def section_weights(compact, levels):
    k = compact.shape[0] // 2
    parts = [block_diagonal(compact[:k], levels), block_diagonal(compact[k:], levels)]
    return jnp.concatenate(parts, axis=0).astype(BF16)


def compact_section(mixing_ref, section, side):
    levels = mixing_ref.shape[0]
    return jnp.concatenate([mixing_ref[level, section, side].astype(F32) for level in range(levels)], axis=1)


def split(source, target, parts, axis):
    count = source.shape[axis] // parts
    places = [(slice(None),) * axis + (pl.ds(n * count, count),) for n in range(parts)]
    return [(source.at[place], target.at[place]) for place in places]


def section_factors(mixing_ref, section, side):
    return jnp.concatenate([mixing_ref[level, section, side].astype(F32) for level in range(mixing_ref.shape[0])], axis=1)


def load(count, field_hbm, col_hbm, mixing_hbm, perm_hbm, xb_ref, sent_ref, mixing_ref, field_ref, col_ref, perm_ref, sems):
    levels, _, _, k, _ = mixing_ref.shape
    vectors = field_ref.shape[0]
    pairs = split(col_hbm, col_ref, 4, 0) + split(field_hbm, field_ref, 2, 0)
    pairs += [(mixing_hbm.at[level], mixing_ref.at[level]) for level in range(levels)]
    pairs.append((perm_hbm, perm_ref))
    copies = [pltpu.make_async_copy(*pair, sems.at[n]) for n, pair in enumerate(pairs)]
    for copy in copies:
        copy.start()
    for copy in copies:
        copy.wait()
    xb = field_ref[...].astype(BF16)
    xb_ref[...] = xb
    sent_ref[:vectors, :] = lax.dot_general(xb, col_ref[...], NT, preferred_element_type=F32)
    row = lax.broadcasted_iota(jnp.int32, (k, k), 0)
    picks = jnp.concatenate([(row == perm_ref[level : level + 1, :]).astype(F32) for level in range(levels)], axis=1)
    picks = block_diagonal(picks, levels).astype(BF16)
    for section in range(count):
        for side in range(2):
            mats = section_factors(mixing_ref, section, side)
            if section == 0:
                mats = jnp.dot(picks, block_diagonal(mats, levels).astype(BF16), preferred_element_type=F32)
                mats = sum(mats[level * k : (level + 1) * k] for level in range(levels))
            start = vectors + (2 * section + side) * k
            sent_ref[start : start + k, :] = mats


def keep(first, mixing_ref, kept_ref, *factor_refs):
    levels, sections, _, k, _ = mixing_ref.shape
    for section in range(first, sections):
        for side in range(2):
            start = (2 * (section - first) + side) * k
            kept_ref[start : start + k, :] = section_factors(mixing_ref, section, side)
    for factor_ref in factor_refs:
        left, right = [
            block_diagonal(section_factors(mixing_ref, *which), levels).astype(BF16) for which in ((1, 1), (2, 0))
        ]
        factor_ref[...] = compact_product(levels, left, right)


def build_weights(levels, chosen, *refs):
    *compact_refs, weights_ref = refs
    size = 2 * weights_ref.shape[2] // levels
    for n, (operand, start) in enumerate(chosen):
        weights_ref[n] = section_weights(compact_refs[operand][start : start + size, :], levels)


def compact_product(levels, left, right):
    k = left.shape[0] // levels
    product = jnp.dot(left, right, preferred_element_type=F32)
    return sum(product[level * k : (level + 1) * k] for level in range(levels))


def three_terms(value):
    high = value.astype(BF16)
    rest = value - high.astype(F32)
    middle = rest.astype(BF16)
    return high, middle, (rest - middle.astype(F32)).astype(BF16)


def factor_terms(levels, compact):
    return three_terms(block_diagonal(compact, levels))


def build_terms(levels, compact_ref, *refs):
    *message_refs, terms_ref = refs
    k, width = compact_ref.shape
    parts = [compact_ref[...]] + [ref[-k:, :] for ref in message_refs]
    for row, part in enumerate(parts):
        for n, term in enumerate(factor_terms(levels, part)):
            terms_ref[n, row * width : (row + 1) * width, :] = term


def terms_dot(value, terms):
    count = value.shape[0]
    stacked = jnp.concatenate(three_terms(value), axis=0)
    sums = sum(jnp.dot(stacked, term, preferred_element_type=F32) for term in reversed(terms))
    return sums[:count] + (sums[count : 2 * count] + sums[2 * count :])


def exact_dot(value, factor):
    return terms_dot(value, [factor])


def section_product(own, other, weights):
    return exact_dot(jnp.concatenate([own, other], axis=1), weights)


def run_sections(sections, final, first_refs, mine_ref, theirs_ref, out_ref):
    weights = (mine_ref, theirs_ref)
    if sections[0]:
        states_ref, other_ref = first_refs
        states, others = [states_ref[0], states_ref[1]], [other_ref[0], other_ref[1]]
    else:
        states = [ref[: out_ref.shape[1], :] for ref in first_refs]
        others = states[::-1]
    for section in sections:
        count = 1 if section == final else 2
        states = [section_product(states[n], others[n], weights[n][section]) for n in range(count)]
        others = states[::-1]
    if count == 1:
        return states[0]
    out_ref[0], out_ref[1] = states


def step(sections, final, first_ref, second_ref, mine_ref, theirs_ref, out_ref):
    run_sections(sections, final, (first_ref, second_ref), mine_ref, theirs_ref, out_ref)


def first_step(levels, sent_ref, received_ref, mine_ref, theirs_ref, out_ref):
    width = out_ref.shape[1]
    k = width // levels
    count = (out_ref.shape[0] - k) // 3
    mine, theirs = sent_ref[:count, :], received_ref[:count, :]
    mine, theirs = section_product(mine, theirs, mine_ref[0]), section_product(theirs, mine, theirs_ref[0])
    out_ref[:count, :] = mine
    out_ref[count : 2 * count, :] = theirs
    mine, theirs = exact_dot(mine, mine_ref[1, :width, :]), exact_dot(theirs, theirs_ref[1, :width, :])
    out_ref[2 * count : 3 * count, :] = section_product(mine, theirs, mine_ref[2])
    out_ref[3 * count :, :] = compact_product(levels, theirs_ref[1, width:, :], mine_ref[2, width:, :])


def level_rank(state, rank_size, half_shift, owner_ref, half):
    first_is_half = jnp.broadcast_to(owner_ref[0:1, 0:1], state.shape) == half_shift
    lane = lax.broadcasted_iota(jnp.int32, state.shape, 1)
    chosen = jnp.logical_xor(lane >= rank_size, first_is_half)
    return (jnp.where(chosen, state, 0.0) if half else jnp.where(chosen, 0.0, state)).astype(BF16)


def finish(state, rank_size, half_shift, row_ref, owner_ref, half_ref, below_ref):
    ranks = [level_rank(state, rank_size, half_shift, owner_ref, half) for half in (True, False)]
    outs = jnp.dot(jnp.concatenate(ranks, axis=0), row_ref[...], preferred_element_type=F32)
    half_ref[...] = outs[: state.shape[0]]
    below_ref[...] = outs[state.shape[0] :]


def last_step(sections, final, rank_size, half_shift, first_ref, second_ref, mine_ref, theirs_ref, *refs):
    state = run_sections(sections, final, (first_ref, second_ref), mine_ref, theirs_ref, None)
    finish(state, rank_size, half_shift, *refs)


def last_sections(levels, rank_size, half_shift, here_ref, there_ref, mine_ref, terms_ref, far_ref, *refs):
    count = (here_ref.shape[0] - rank_size) // 3
    here = jnp.concatenate([here_ref[:count, :], here_ref[count : 2 * count, :]], axis=1)
    there = jnp.concatenate([there_ref[:count, :], there_ref[count : 2 * count, :]], axis=1)
    mine = here_ref[2 * count : 3 * count, :] + terms_dot(there, [terms_ref[n] for n in range(3)])
    behind = factor_terms(levels, there_ref[3 * count :, :])
    far_terms = [jnp.concatenate([far_ref[n], behind[n]], axis=0) for n in range(3)]
    far = there_ref[2 * count : 3 * count, :] + terms_dot(here, far_terms)
    finish(section_product(mine, far, mine_ref[3]), rank_size, half_shift, *refs)


def diagonal(xb_ref, leaf_hbm, out_ref, leaf_ref, sems):
    blocks, order, _ = leaf_hbm.shape
    copies = []
    for n in range(blocks):
        for source, target in split(leaf_hbm.at[n], leaf_ref.at[n], 2, 0):
            copies.append(pltpu.make_async_copy(source, target, sems.at[len(copies)]))
            copies[-1].start()
    for n in range(blocks):
        copies[2 * n].wait()
        copies[2 * n + 1].wait()
        part = pl.ds(n * order, order)
        out_ref[:, part] = jnp.dot(xb_ref[:, part], leaf_ref[n], preferred_element_type=F32)


def combine(half_ref, below_ref, diag_ref, out_hbm, sum_ref, sems):
    parts = sems.shape[0]
    count = sum_ref.shape[1] // parts
    copies = []
    for n in range(parts):
        part = pl.ds(n * count, count)
        sum_ref[:, part] = diag_ref[:, part] + below_ref[:, part] + half_ref[:, part]
        copies.append(pltpu.make_async_copy(sum_ref.at[:, part], out_hbm.at[:, part], sems.at[n]))
        copies[-1].start()
    for copy in copies:
        copy.wait()


def shards(field, leaf_inverse, col_factor, row_factor, mixing, row_owner, rank_perm):
    vectors, rows = field.shape
    order = leaf_inverse.shape[1]
    levels, rank_size, _ = col_factor.shape
    sections = mixing.shape[2]
    bits = lax.axis_size("bf").bit_length() - 1
    groups = lax.axis_size("grp")
    width = levels * rank_size

    def array(*shape, kind=F32):
        return jax.ShapeDtypeStruct(shape, kind)

    in_hbm = [
        pltpu.with_memory_space_constraint(x, pltpu.HBM)
        for x in (field, col_factor.reshape(width, rows), mixing[0], rank_perm)
    ]
    size = 2 * rank_size
    one_round = bits == 2 and sections == 4 and levels == 2
    ahead = 2 if one_round else sections - 1
    xb, sent, mixing_here = call(
        lambda *refs: load(ahead, *refs),
        [
            array(vectors, rows, kind=BF16),
            array(vectors + ahead * size, width),
            array(*mixing.shape[1:], kind=BF16),
        ],
        [HBM] * 4, 2 * vectors * rows * width, 3 * rows * width, *in_hbm,
        scratch=[
            pltpu.VMEM(field.shape, F32),
            pltpu.VMEM((width, rows), BF16),
            pltpu.VMEM(rank_perm.shape, jnp.int32),
            pltpu.SemaphoreType.DMA((1 + levels + 2 + 4,)),
        ],
    )
    weight_cost = (4 * width * width * sections, 8 * width * width * sections)

    def weights(chosen, *compacts):
        return call(
            lambda *refs: build_weights(levels, chosen, *refs), array(len(chosen), 2 * width, width, kind=BF16),
            [VMEM] * len(compacts), *weight_cost, *compacts,
        )

    def terms(*compacts, scale=1):
        return call(
            lambda *refs: build_terms(levels, *refs), array(3, len(compacts) * width, width, kind=BF16),
            [VMEM] * len(compacts), *[scale * cost for cost in weight_cost], *compacts,
        )

    received = swapped(sent)
    kept = call(
        lambda *refs: keep(ahead, *refs),
        [array((sections - ahead) * size, width)] + [array(rank_size, width)] * one_round,
        [VMEM], *weight_cost, mixing_here,
    )
    step_cost = (24 * vectors * width * width, 8 * width * width)
    final = sections - 1
    if one_round:
        chosen = [(0, vectors), (0, vectors + size), (1, 0), (1, size)]
        mine, factor = weights(chosen, sent, kept[0]), kept[1]
        far_factor = across(factor, 1)
        states = call(
            lambda *refs: first_step(levels, *refs), array(3 * vectors + rank_size, width), [VMEM] * 4, *step_cost,
            sent, received, mine, weights(chosen[:2], received),
        )
        first_states = (states, across(states, 1))
        last_body = lambda *refs: last_sections(levels, *refs)
        last_weights = (mine, terms(factor, states), terms(far_factor, scale=1000))
    else:
        starts = [(0, vectors + n * size) for n in range(final)]
        mine, theirs = weights(starts + [(1, 0)], sent, *kept), weights(starts, received)
        runs = []
        for section in range(sections):
            if section % bits or not section:
                runs.append([section])
            else:
                runs[-1].append(section)
        first_states = (sent, received)
        for run in runs[:-1]:
            states = call(
                lambda *refs, run=run: step(run, final, *refs), array(2, vectors, width), [VMEM] * 4, *step_cost,
                *first_states, mine, theirs,
            )
            first_states = (states, across(states, (run[-1] + 1) % bits))
        last_body = lambda *refs: last_step(runs[-1], final, *refs)
        last_weights = (mine, theirs)
    expand_cost = (2 * vectors * width * rows, 4 * width * rows)
    expand = row_factor.reshape(width, rows)
    out_half, out_below = call(
        lambda *refs: last_body(rank_size, groups // 2, *refs), [array(vectors, rows)] * 2,
        [VMEM] * (4 + len(last_weights)), *expand_cost, *first_states, *last_weights, expand, row_owner,
    )
    out_half = shifted(out_half, "grp", groups // 2)
    out_below = shifted(out_below, "grp", groups - 1)
    diag = call(
        diagonal, array(vectors, rows), [VMEM, HBM], 2 * vectors * rows * order, 2 * rows * order,
        xb, pltpu.with_memory_space_constraint(leaf_inverse, pltpu.HBM),
        scratch=[pltpu.VMEM(leaf_inverse.shape, BF16), pltpu.SemaphoreType.DMA((2 * leaf_inverse.shape[0],))],
    )
    return call(
        combine, array(vectors, rows), [VMEM] * 3, 2 * vectors * rows, 16 * vectors * rows, out_half, out_below, diag,
        scratch=[pltpu.VMEM((vectors, rows), F32), pltpu.SemaphoreType.DMA((4,))], out=HBM,
    )


def solution(mesh):
    in_specs = (
        P(None, ("grp", "bf")),
        P(("grp", "bf"), None, None),
        P(None, None, ("grp", "bf")),
        P(None, None, ("grp", "bf")),
        P(("grp", "bf"), None, None, None, None, None),
        P(),
        P(),
    )
    out_specs = P(None, ("grp", "bf"))
    return jax.shard_map(shards, mesh=mesh, in_specs=in_specs, out_specs=out_specs, check_vma=False)
```

```python
import jax
import jax.numpy as jnp
from jax import lax
from jax.experimental import pallas as pl
from jax.experimental.pallas import tpu as pltpu
from jax.sharding import PartitionSpec as P

F32, BF16 = jnp.float32, jnp.bfloat16
VMEM = pl.BlockSpec(memory_space=pltpu.VMEM)
HBM = pl.BlockSpec(memory_space=pltpu.HBM)
NT = (((1,), (1,)), ((), ()))


def shifted(value, axis, distance):
    size = lax.axis_size(axis)
    return lax.ppermute(value, axis, [(source, (source + distance) % size) for source in range(size)])


def swapped(value):
    return lax.ppermute(value, "bf", [(n, n ^ 1) for n in range(lax.axis_size("bf"))])


def across(value, bit):
    return lax.ppermute(value, "bf", [(n, n ^ 1 << bit) for n in range(lax.axis_size("bf"))])


def call(body, shapes, specs, flops, moved, *operands, scratch=(), out=VMEM):
    return pl.pallas_call(
        body,
        out_shape=shapes,
        in_specs=specs,
        out_specs=jax.tree.map(lambda _: out, shapes),
        scratch_shapes=scratch,
        cost_estimate=pl.CostEstimate(flops=flops, bytes_accessed=moved, transcendentals=0),
        compiler_params=pltpu.CompilerParams(vmem_limit_bytes=16 * 2**20),
    )(*operands)


def block_diagonal(compact, levels):
    k = compact.shape[0]
    lane = lax.broadcasted_iota(jnp.int32, compact.shape, 1)
    parts = []
    for level in range(levels):
        mine = jnp.logical_and(lane >= level * k, lane < (level + 1) * k)
        parts.append(jnp.where(mine, compact, 0.0))
    return jnp.concatenate(parts, axis=0)


def section_weights(compact, levels):
    k = compact.shape[0] // 2
    parts = [block_diagonal(compact[:k], levels), block_diagonal(compact[k:], levels)]
    return jnp.concatenate(parts, axis=0).astype(BF16)


def compact_section(mixing_ref, section, side):
    levels = mixing_ref.shape[0]
    return jnp.concatenate([mixing_ref[level, section, side].astype(F32) for level in range(levels)], axis=1)


def split(source, target, parts, axis):
    count = source.shape[axis] // parts
    places = [(slice(None),) * axis + (pl.ds(n * count, count),) for n in range(parts)]
    return [(source.at[place], target.at[place]) for place in places]


def load(groups, field_hbm, col_hbm, mixing_hbm, perm_hbm, xb_ref, sent_ref, *refs):
    *out_refs, field_ref, col_ref, mixing_ref, perm_ref, sems = refs
    compact = {}
    levels, sections, _, k, _ = mixing_ref.shape
    vectors = field_ref.shape[0]
    pairs = split(col_hbm, col_ref, 4, 0) + split(field_hbm, field_ref, 2, 0)
    pairs += [(mixing_hbm.at[level], mixing_ref.at[level]) for level in range(levels)]
    pairs.append((perm_hbm, perm_ref))
    copies = [pltpu.make_async_copy(*pair, sems.at[n]) for n, pair in enumerate(pairs)]
    for copy in copies:
        copy.start()
    for copy in copies:
        copy.wait()
    xb = field_ref[...].astype(BF16)
    xb_ref[...] = xb
    sent_ref[:vectors, :] = lax.dot_general(xb, col_ref[...], NT, preferred_element_type=F32)
    row = lax.broadcasted_iota(jnp.int32, (k, k), 0)
    picks = jnp.concatenate([(row == perm_ref[level : level + 1, :]).astype(F32) for level in range(levels)], axis=1)
    picks = block_diagonal(picks, levels).astype(BF16)
    for section in range(sections):
        for side in range(2):
            mats = jnp.concatenate([mixing_ref[level, section, side].astype(F32) for level in range(levels)], axis=1)
            if section == 0:
                mats = jnp.dot(picks, block_diagonal(mats, levels).astype(BF16), preferred_element_type=F32)
                mats = sum(mats[level * k : (level + 1) * k] for level in range(levels))
            compact[section, side] = mats
            for n, (group, out_ref) in enumerate(zip(groups, (sent_ref, *out_refs))):
                if section in group:
                    start = (0 if n else vectors) + (2 * group.index(section) + side) * k
                    out_ref[start : start + k, :] = mats
    if len(out_refs) == len(groups):
        left, right = [block_diagonal(compact[which], levels).astype(BF16) for which in ((1, 1), (2, 0))]
        out_refs[-1][...] = compact_product(levels, left, right)


def build_weights(levels, chosen, *refs):
    *compact_refs, weights_ref = refs
    size = 2 * weights_ref.shape[2] // levels
    for n, (operand, start) in enumerate(chosen):
        weights_ref[n] = section_weights(compact_refs[operand][start : start + size, :], levels)


def compact_product(levels, left, right):
    k = left.shape[0] // levels
    product = jnp.dot(left, right, preferred_element_type=F32)
    return sum(product[level * k : (level + 1) * k] for level in range(levels))


def two_terms(value):
    high = value.astype(BF16)
    return high, (value - high.astype(F32)).astype(BF16)


def factor_terms(levels, compact):
    return two_terms(block_diagonal(compact, levels))


def build_terms(levels, compact_ref, *refs):
    *message_refs, terms_ref = refs
    k, width = compact_ref.shape
    parts = [compact_ref[...]] + [ref[-k:, :] for ref in message_refs]
    for row, part in enumerate(parts):
        for n, term in enumerate(factor_terms(levels, part)):
            terms_ref[n, row * width : (row + 1) * width, :] = term


def terms_dot(value, terms):
    count = value.shape[0]
    stacked = jnp.concatenate(two_terms(value), axis=0)
    sums = sum(jnp.dot(stacked, term, preferred_element_type=F32) for term in reversed(terms))
    return sums[:count] + sums[count:]


def exact_dot(value, factor):
    return terms_dot(value, [factor])


def section_product(own, other, weights):
    return exact_dot(jnp.concatenate([own, other], axis=1), weights)


def run_sections(sections, final, first_refs, mine_ref, theirs_ref, out_ref):
    weights = (mine_ref, theirs_ref)
    if sections[0]:
        states_ref, other_ref = first_refs
        states, others = [states_ref[0], states_ref[1]], [other_ref[0], other_ref[1]]
    else:
        states = [ref[: out_ref.shape[1], :] for ref in first_refs]
        others = states[::-1]
    for section in sections:
        count = 1 if section == final else 2
        states = [section_product(states[n], others[n], weights[n][section]) for n in range(count)]
        others = states[::-1]
    if count == 1:
        return states[0]
    out_ref[0], out_ref[1] = states


def step(sections, final, first_ref, second_ref, mine_ref, theirs_ref, out_ref):
    run_sections(sections, final, (first_ref, second_ref), mine_ref, theirs_ref, out_ref)


def first_step(levels, sent_ref, received_ref, mine_ref, theirs_ref, out_ref):
    width = out_ref.shape[1]
    k = width // levels
    count = (out_ref.shape[0] - k) // 3
    mine, theirs = sent_ref[:count, :], received_ref[:count, :]
    mine, theirs = section_product(mine, theirs, mine_ref[0]), section_product(theirs, mine, theirs_ref[0])
    out_ref[:count, :] = mine
    out_ref[count : 2 * count, :] = theirs
    mine, theirs = exact_dot(mine, mine_ref[1, :width, :]), exact_dot(theirs, theirs_ref[1, :width, :])
    out_ref[2 * count : 3 * count, :] = section_product(mine, theirs, mine_ref[2])
    out_ref[3 * count :, :] = compact_product(levels, theirs_ref[1, width:, :], mine_ref[2, width:, :])


def level_rank(state, rank_size, half_shift, owner_ref, half):
    first_is_half = jnp.broadcast_to(owner_ref[0:1, 0:1], state.shape) == half_shift
    lane = lax.broadcasted_iota(jnp.int32, state.shape, 1)
    chosen = jnp.logical_xor(lane >= rank_size, first_is_half)
    return (jnp.where(chosen, state, 0.0) if half else jnp.where(chosen, 0.0, state)).astype(BF16)


def finish(state, rank_size, half_shift, row_ref, owner_ref, half_ref, below_ref):
    ranks = [level_rank(state, rank_size, half_shift, owner_ref, half) for half in (True, False)]
    outs = jnp.dot(jnp.concatenate(ranks, axis=0), row_ref[...], preferred_element_type=F32)
    half_ref[...] = outs[: state.shape[0]]
    below_ref[...] = outs[state.shape[0] :]


def last_step(sections, final, rank_size, half_shift, first_ref, second_ref, mine_ref, theirs_ref, *refs):
    state = run_sections(sections, final, (first_ref, second_ref), mine_ref, theirs_ref, None)
    finish(state, rank_size, half_shift, *refs)


def last_sections(levels, rank_size, half_shift, here_ref, there_ref, mine_ref, terms_ref, far_ref, *refs):
    count = (here_ref.shape[0] - rank_size) // 3
    here = jnp.concatenate([here_ref[:count, :], here_ref[count : 2 * count, :]], axis=1)
    there = jnp.concatenate([there_ref[:count, :], there_ref[count : 2 * count, :]], axis=1)
    mine = here_ref[2 * count : 3 * count, :] + terms_dot(there, [terms_ref[n] for n in range(2)])
    behind = factor_terms(levels, there_ref[3 * count :, :])
    far_terms = [jnp.concatenate([far_ref[n], behind[n]], axis=0) for n in range(2)]
    far = there_ref[2 * count : 3 * count, :] + terms_dot(here, far_terms)
    finish(section_product(mine, far, mine_ref[3]), rank_size, half_shift, *refs)


def diagonal(xb_ref, leaf_hbm, out_ref, leaf_ref, sems):
    blocks, order, _ = leaf_hbm.shape
    copies = []
    for n in range(blocks):
        for source, target in split(leaf_hbm.at[n], leaf_ref.at[n], 2, 0):
            copies.append(pltpu.make_async_copy(source, target, sems.at[len(copies)]))
            copies[-1].start()
    for n in range(blocks):
        copies[2 * n].wait()
        copies[2 * n + 1].wait()
        part = pl.ds(n * order, order)
        out_ref[:, part] = jnp.dot(xb_ref[:, part], leaf_ref[n], preferred_element_type=F32)


def combine(half_ref, below_ref, diag_ref, out_hbm, sum_ref, sems):
    parts = sems.shape[0]
    count = sum_ref.shape[1] // parts
    copies = []
    for n in range(parts):
        part = pl.ds(n * count, count)
        sum_ref[:, part] = diag_ref[:, part] + below_ref[:, part] + half_ref[:, part]
        copies.append(pltpu.make_async_copy(sum_ref.at[:, part], out_hbm.at[:, part], sems.at[n]))
        copies[-1].start()
    for copy in copies:
        copy.wait()


def shards(field, leaf_inverse, col_factor, row_factor, mixing, row_owner, rank_perm):
    vectors, rows = field.shape
    order = leaf_inverse.shape[1]
    levels, rank_size, _ = col_factor.shape
    sections = mixing.shape[2]
    bits = lax.axis_size("bf").bit_length() - 1
    groups = lax.axis_size("grp")
    width = levels * rank_size

    def array(*shape, kind=F32):
        return jax.ShapeDtypeStruct(shape, kind)

    in_hbm = [
        pltpu.with_memory_space_constraint(x, pltpu.HBM)
        for x in (field, col_factor.reshape(width, rows), mixing[0], rank_perm)
    ]
    size = 2 * rank_size
    one_round = bits == 2 and sections == 4 and levels == 2
    groups_sent = [(0, 1), (2, 3)] if one_round else [tuple(range(sections - 1)), (sections - 1,)]
    xb, sent, *kept = call(
        lambda *refs: load(groups_sent, *refs),
        [array(vectors, rows, kind=BF16)]
        + [array(len(group) * size + (0 if n else vectors), width) for n, group in enumerate(groups_sent)]
        + [array(rank_size, width)] * one_round,
        [HBM] * 4, 2 * vectors * rows * width, 3 * rows * width, *in_hbm,
        scratch=[
            pltpu.VMEM(field.shape, F32),
            pltpu.VMEM((width, rows), BF16),
            pltpu.VMEM(mixing.shape[1:], BF16),
            pltpu.VMEM(rank_perm.shape, jnp.int32),
            pltpu.SemaphoreType.DMA((1 + levels + 2 + 4,)),
        ],
    )
    weight_cost = (4 * width * width * sections, 8 * width * width * sections)

    def weights(chosen, *compacts):
        return call(
            lambda *refs: build_weights(levels, chosen, *refs), array(len(chosen), 2 * width, width, kind=BF16),
            [VMEM] * len(compacts), *weight_cost, *compacts,
        )

    def terms(*compacts, scale=1):
        return call(
            lambda *refs: build_terms(levels, *refs), array(2, len(compacts) * width, width, kind=BF16),
            [VMEM] * len(compacts), *[scale * cost for cost in weight_cost], *compacts,
        )

    received = swapped(sent)
    step_cost = (24 * vectors * width * width, 8 * width * width)
    final = sections - 1
    if one_round:
        chosen = [(0, vectors), (0, vectors + size), (1, 0), (1, size)]
        mine, factor = weights(chosen, sent, kept[0]), kept[1]
        far_factor = across(factor, 1)
        states = call(
            lambda *refs: first_step(levels, *refs), array(3 * vectors + rank_size, width), [VMEM] * 4, *step_cost,
            sent, received, mine, weights(chosen[:2], received),
        )
        first_states = (states, across(states, 1))
        last_body = lambda *refs: last_sections(levels, *refs)
        last_weights = (mine, terms(factor, states), terms(far_factor, scale=1000))
    else:
        starts = [(0, vectors + n * size) for n in range(final)]
        mine, theirs = weights(starts + [(1, 0)], sent, *kept), weights(starts, received)
        runs = []
        for section in range(sections):
            if section % bits or not section:
                runs.append([section])
            else:
                runs[-1].append(section)
        first_states = (sent, received)
        for run in runs[:-1]:
            states = call(
                lambda *refs, run=run: step(run, final, *refs), array(2, vectors, width), [VMEM] * 4, *step_cost,
                *first_states, mine, theirs,
            )
            first_states = (states, across(states, (run[-1] + 1) % bits))
        last_body = lambda *refs: last_step(runs[-1], final, *refs)
        last_weights = (mine, theirs)
    expand_cost = (2 * vectors * width * rows, 4 * width * rows)
    expand = row_factor.reshape(width, rows)
    out_half, out_below = call(
        lambda *refs: last_body(rank_size, groups // 2, *refs), [array(vectors, rows)] * 2,
        [VMEM] * (4 + len(last_weights)), *expand_cost, *first_states, *last_weights, expand, row_owner,
    )
    out_half = shifted(out_half, "grp", groups // 2)
    out_below = shifted(out_below, "grp", groups - 1)
    diag = call(
        diagonal, array(vectors, rows), [VMEM, HBM], 2 * vectors * rows * order, 2 * rows * order,
        xb, pltpu.with_memory_space_constraint(leaf_inverse, pltpu.HBM),
        scratch=[pltpu.VMEM(leaf_inverse.shape, BF16), pltpu.SemaphoreType.DMA((2 * leaf_inverse.shape[0],))],
    )
    return call(
        combine, array(vectors, rows), [VMEM] * 3, 2 * vectors * rows, 16 * vectors * rows, out_half, out_below, diag,
        scratch=[pltpu.VMEM((vectors, rows), F32), pltpu.SemaphoreType.DMA((4,))], out=HBM,
    )


def solution(mesh):
    in_specs = (
        P(None, ("grp", "bf")),
        P(("grp", "bf"), None, None),
        P(None, None, ("grp", "bf")),
        P(None, None, ("grp", "bf")),
        P(("grp", "bf"), None, None, None, None, None),
        P(),
        P(),
    )
    out_specs = P(None, ("grp", "bf"))
    return jax.shard_map(shards, mesh=mesh, in_specs=in_specs, out_specs=out_specs, check_vma=False)
```

```python
import jax
import jax.numpy as jnp
from jax import lax
from jax.experimental import pallas as pl
from jax.experimental.pallas import tpu as pltpu
from jax.sharding import PartitionSpec as P

F32, BF16 = jnp.float32, jnp.bfloat16
VMEM = pl.BlockSpec(memory_space=pltpu.VMEM)
HBM = pl.BlockSpec(memory_space=pltpu.HBM)
NT = (((1,), (1,)), ((), ()))


def shifted(value, axis, distance):
    size = lax.axis_size(axis)
    return lax.ppermute(value, axis, [(source, (source + distance) % size) for source in range(size)])


def swapped(value):
    return lax.ppermute(value, "bf", [(n, n ^ 1) for n in range(lax.axis_size("bf"))])


def across(value, bit):
    return lax.ppermute(value, "bf", [(n, n ^ 1 << bit) for n in range(lax.axis_size("bf"))])


def call(body, shapes, specs, flops, moved, *operands, scratch=(), out=VMEM):
    return pl.pallas_call(
        body,
        out_shape=shapes,
        in_specs=specs,
        out_specs=jax.tree.map(lambda _: out, shapes),
        scratch_shapes=scratch,
        cost_estimate=pl.CostEstimate(flops=flops, bytes_accessed=moved, transcendentals=0),
        compiler_params=pltpu.CompilerParams(vmem_limit_bytes=16 * 2**20),
    )(*operands)


def block_diagonal(compact, levels):
    k = compact.shape[0]
    lane = lax.broadcasted_iota(jnp.int32, compact.shape, 1)
    parts = []
    for level in range(levels):
        mine = jnp.logical_and(lane >= level * k, lane < (level + 1) * k)
        parts.append(jnp.where(mine, compact, 0.0))
    return jnp.concatenate(parts, axis=0)


def section_weights(compact, levels):
    k = compact.shape[0] // 2
    parts = [block_diagonal(compact[:k], levels), block_diagonal(compact[k:], levels)]
    return jnp.concatenate(parts, axis=0).astype(BF16)


def compact_section(mixing_ref, section, side):
    levels = mixing_ref.shape[0]
    return jnp.concatenate([mixing_ref[level, section, side].astype(F32) for level in range(levels)], axis=1)


def split(source, target, parts, axis):
    count = source.shape[axis] // parts
    places = [(slice(None),) * axis + (pl.ds(n * count, count),) for n in range(parts)]
    return [(source.at[place], target.at[place]) for place in places]


def load(groups, field_hbm, col_hbm, mixing_hbm, perm_hbm, xb_ref, sent_ref, *refs):
    *out_refs, field_ref, col_ref, mixing_ref, perm_ref, sems = refs
    compact = {}
    levels, sections, _, k, _ = mixing_ref.shape
    vectors = field_ref.shape[0]
    pairs = split(col_hbm, col_ref, 4, 0) + split(field_hbm, field_ref, 2, 0)
    pairs += [(mixing_hbm.at[level], mixing_ref.at[level]) for level in range(levels)]
    pairs.append((perm_hbm, perm_ref))
    copies = [pltpu.make_async_copy(*pair, sems.at[n]) for n, pair in enumerate(pairs)]
    for copy in copies:
        copy.start()
    for copy in copies:
        copy.wait()
    xb = field_ref[...].astype(BF16)
    xb_ref[...] = xb
    parts = [
        lax.dot_general(xb, col_ref[level * k : (level + 1) * k, :], NT, preferred_element_type=F32) for level in range(levels)
    ]
    sent_ref[:vectors, :] = jnp.concatenate(parts, axis=1)
    row = lax.broadcasted_iota(jnp.int32, (k, k), 0)
    picks = jnp.concatenate([(row == perm_ref[level : level + 1, :]).astype(F32) for level in range(levels)], axis=1)
    picks = block_diagonal(picks, levels).astype(BF16)
    for section in range(sections):
        for side in range(2):
            mats = jnp.concatenate([mixing_ref[level, section, side].astype(F32) for level in range(levels)], axis=1)
            if section == 0:
                mats = jnp.dot(picks, block_diagonal(mats, levels).astype(BF16), preferred_element_type=F32)
                mats = sum(mats[level * k : (level + 1) * k] for level in range(levels))
            compact[section, side] = mats
            for n, (group, out_ref) in enumerate(zip(groups, (sent_ref, *out_refs))):
                if section in group:
                    start = (0 if n else vectors) + (2 * group.index(section) + side) * k
                    out_ref[start : start + k, :] = mats
    if len(out_refs) == len(groups):
        left, right = [block_diagonal(compact[which], levels).astype(BF16) for which in ((1, 1), (2, 0))]
        out_refs[-1][...] = compact_product(levels, left, right)


def build_weights(levels, chosen, *refs):
    *compact_refs, weights_ref = refs
    size = 2 * weights_ref.shape[2] // levels
    for n, (operand, start) in enumerate(chosen):
        weights_ref[n] = section_weights(compact_refs[operand][start : start + size, :], levels)


def compact_product(levels, left, right):
    k = left.shape[0] // levels
    product = jnp.dot(left, right, preferred_element_type=F32)
    return sum(product[level * k : (level + 1) * k] for level in range(levels))


def three_terms(value):
    high = value.astype(BF16)
    rest = value - high.astype(F32)
    middle = rest.astype(BF16)
    return high, middle, (rest - middle.astype(F32)).astype(BF16)


def factor_terms(levels, compact):
    return three_terms(block_diagonal(compact, levels))


def build_terms(levels, compact_ref, *refs):
    *message_refs, terms_ref = refs
    k, width = compact_ref.shape
    parts = [compact_ref[...]] + [ref[-k:, :] for ref in message_refs]
    for row, part in enumerate(parts):
        for n, term in enumerate(factor_terms(levels, part)):
            terms_ref[n, row * width : (row + 1) * width, :] = term


def terms_dot(value, terms):
    count = value.shape[0]
    stacked = jnp.concatenate(three_terms(value), axis=0)
    sums = sum(jnp.dot(stacked, term, preferred_element_type=F32) for term in reversed(terms))
    return sums[:count] + (sums[count : 2 * count] + sums[2 * count :])


def exact_dot(value, factor):
    return terms_dot(value, [factor])


def section_product(own, other, weights):
    return exact_dot(jnp.concatenate([own, other], axis=1), weights)


def run_sections(sections, final, first_refs, mine_ref, theirs_ref, out_ref):
    weights = (mine_ref, theirs_ref)
    if sections[0]:
        states_ref, other_ref = first_refs
        states, others = [states_ref[0], states_ref[1]], [other_ref[0], other_ref[1]]
    else:
        states = [ref[: out_ref.shape[1], :] for ref in first_refs]
        others = states[::-1]
    for section in sections:
        count = 1 if section == final else 2
        states = [section_product(states[n], others[n], weights[n][section]) for n in range(count)]
        others = states[::-1]
    if count == 1:
        return states[0]
    out_ref[0], out_ref[1] = states


def step(sections, final, first_ref, second_ref, mine_ref, theirs_ref, out_ref):
    run_sections(sections, final, (first_ref, second_ref), mine_ref, theirs_ref, out_ref)


def first_step(levels, sent_ref, received_ref, mine_ref, theirs_ref, out_ref):
    width = out_ref.shape[1]
    k = width // levels
    count = (out_ref.shape[0] - k) // 3
    mine, theirs = sent_ref[:count, :], received_ref[:count, :]
    mine, theirs = section_product(mine, theirs, mine_ref[0]), section_product(theirs, mine, theirs_ref[0])
    out_ref[:count, :] = mine
    out_ref[count : 2 * count, :] = theirs
    mine, theirs = exact_dot(mine, mine_ref[1, :width, :]), exact_dot(theirs, theirs_ref[1, :width, :])
    out_ref[2 * count : 3 * count, :] = section_product(mine, theirs, mine_ref[2])
    out_ref[3 * count :, :] = compact_product(levels, theirs_ref[1, width:, :], mine_ref[2, width:, :])


def level_rank(state, rank_size, half_shift, owner_ref, half):
    first_is_half = jnp.broadcast_to(owner_ref[0:1, 0:1], state.shape) == half_shift
    lane = lax.broadcasted_iota(jnp.int32, state.shape, 1)
    chosen = jnp.logical_xor(lane >= rank_size, first_is_half)
    return (jnp.where(chosen, state, 0.0) if half else jnp.where(chosen, 0.0, state)).astype(BF16)


def finish(state, rank_size, half_shift, row_ref, owner_ref, state_ref, half_ref):
    state_ref[...] = state
    rank = level_rank(state, rank_size, half_shift, owner_ref, True)
    half_ref[...] = jnp.dot(rank, row_ref[...], preferred_element_type=F32)


def expand_below(rank_size, half_shift, state_ref, row_ref, owner_ref, below_ref):
    rank = level_rank(state_ref[...], rank_size, half_shift, owner_ref, False)
    below_ref[...] = jnp.dot(rank, row_ref[...], preferred_element_type=F32)


def last_step(sections, final, rank_size, half_shift, first_ref, second_ref, mine_ref, theirs_ref, *refs):
    state = run_sections(sections, final, (first_ref, second_ref), mine_ref, theirs_ref, None)
    finish(state, rank_size, half_shift, *refs)


def last_sections(levels, rank_size, half_shift, here_ref, there_ref, mine_ref, terms_ref, far_ref, *refs):
    count = (here_ref.shape[0] - rank_size) // 3
    here = jnp.concatenate([here_ref[:count, :], here_ref[count : 2 * count, :]], axis=1)
    there = jnp.concatenate([there_ref[:count, :], there_ref[count : 2 * count, :]], axis=1)
    mine = here_ref[2 * count : 3 * count, :] + terms_dot(there, [terms_ref[n] for n in range(3)])
    behind = factor_terms(levels, there_ref[3 * count :, :])
    far_terms = [jnp.concatenate([far_ref[n], behind[n]], axis=0) for n in range(3)]
    far = there_ref[2 * count : 3 * count, :] + terms_dot(here, far_terms)
    finish(section_product(mine, far, mine_ref[3]), rank_size, half_shift, *refs)


def diagonal(xb_ref, leaf_hbm, out_ref, leaf_ref, sems):
    blocks, order, _ = leaf_hbm.shape
    copies = []
    for n in range(blocks):
        for source, target in split(leaf_hbm.at[n], leaf_ref.at[n], 2, 0):
            copies.append(pltpu.make_async_copy(source, target, sems.at[len(copies)]))
            copies[-1].start()
    for n in range(blocks):
        copies[2 * n].wait()
        copies[2 * n + 1].wait()
        part = pl.ds(n * order, order)
        out_ref[:, part] = jnp.dot(xb_ref[:, part], leaf_ref[n], preferred_element_type=F32)


def arrived(half_ref, out_ref):
    out_ref[...] = half_ref[: out_ref.shape[0], : out_ref.shape[1]]


def combine(half_ref, below_ref, diag_ref, _, out_hbm, sum_ref, sems):
    parts = sems.shape[0]
    count = sum_ref.shape[1] // parts
    copies = []
    for n in range(parts):
        part = pl.ds(n * count, count)
        sum_ref[:, part] = diag_ref[:, part] + below_ref[:, part] + half_ref[:, part]
        copies.append(pltpu.make_async_copy(sum_ref.at[:, part], out_hbm.at[:, part], sems.at[n]))
        copies[-1].start()
    for copy in copies:
        copy.wait()


def shards(field, leaf_inverse, col_factor, row_factor, mixing, row_owner, rank_perm):
    vectors, rows = field.shape
    order = leaf_inverse.shape[1]
    levels, rank_size, _ = col_factor.shape
    sections = mixing.shape[2]
    bits = lax.axis_size("bf").bit_length() - 1
    groups = lax.axis_size("grp")
    width = levels * rank_size

    def array(*shape, kind=F32):
        return jax.ShapeDtypeStruct(shape, kind)

    in_hbm = [
        pltpu.with_memory_space_constraint(x, pltpu.HBM)
        for x in (field, col_factor.reshape(width, rows), mixing[0], rank_perm)
    ]
    size = 2 * rank_size
    one_round = bits == 2 and sections == 4 and levels == 2
    groups_sent = [(0, 1), (2, 3)] if one_round else [tuple(range(sections - 1)), (sections - 1,)]
    xb, sent, *kept = call(
        lambda *refs: load(groups_sent, *refs),
        [array(vectors, rows, kind=BF16)]
        + [array(len(group) * size + (0 if n else vectors), width) for n, group in enumerate(groups_sent)]
        + [array(rank_size, width)] * one_round,
        [HBM] * 4, 2 * vectors * rows * width, 3 * rows * width, *in_hbm,
        scratch=[
            pltpu.VMEM(field.shape, F32),
            pltpu.VMEM((width, rows), BF16),
            pltpu.VMEM(mixing.shape[1:], BF16),
            pltpu.VMEM(rank_perm.shape, jnp.int32),
            pltpu.SemaphoreType.DMA((1 + levels + 2 + 4,)),
        ],
    )
    weight_cost = (4 * width * width * sections, 8 * width * width * sections)

    def weights(chosen, *compacts):
        return call(
            lambda *refs: build_weights(levels, chosen, *refs), array(len(chosen), 2 * width, width, kind=BF16),
            [VMEM] * len(compacts), *weight_cost, *compacts,
        )

    def terms(*compacts, scale=1):
        return call(
            lambda *refs: build_terms(levels, *refs), array(3, len(compacts) * width, width, kind=BF16),
            [VMEM] * len(compacts), *[scale * cost for cost in weight_cost], *compacts,
        )

    received = swapped(sent)
    step_cost = (24 * vectors * width * width, 8 * width * width)
    final = sections - 1
    if one_round:
        chosen = [(0, vectors), (0, vectors + size), (1, 0), (1, size)]
        mine, factor = weights(chosen, sent, kept[0]), kept[1]
        far_factor = across(factor, 1)
        states = call(
            lambda *refs: first_step(levels, *refs), array(3 * vectors + rank_size, width), [VMEM] * 4, *step_cost,
            sent, received, mine, weights(chosen[:2], received),
        )
        first_states = (states, across(states, 1))
        last_body = lambda *refs: last_sections(levels, *refs)
        last_weights = (mine, terms(factor, states), terms(far_factor, scale=1000))
    else:
        starts = [(0, vectors + n * size) for n in range(final)]
        mine, theirs = weights(starts + [(1, 0)], sent, *kept), weights(starts, received)
        runs = []
        for section in range(sections):
            if section % bits or not section:
                runs.append([section])
            else:
                runs[-1].append(section)
        first_states = (sent, received)
        for run in runs[:-1]:
            states = call(
                lambda *refs, run=run: step(run, final, *refs), array(2, vectors, width), [VMEM] * 4, *step_cost,
                *first_states, mine, theirs,
            )
            first_states = (states, across(states, (run[-1] + 1) % bits))
        last_body = lambda *refs: last_step(runs[-1], final, *refs)
        last_weights = (mine, theirs)
    expand_cost = (2 * vectors * width * rows, 4 * width * rows)
    expand = row_factor.reshape(width, rows)
    state, out_half = call(
        lambda *refs: last_body(rank_size, groups // 2, *refs), [array(vectors, width), array(vectors, rows)],
        [VMEM] * (4 + len(last_weights)), *expand_cost, *first_states, *last_weights, expand, row_owner,
    )
    out_below = call(
        lambda *refs: expand_below(rank_size, groups // 2, *refs), array(vectors, rows),
        [VMEM] * 3, *expand_cost, state, expand, row_owner,
    )
    out_half = shifted(out_half, "grp", groups // 2)
    out_below = shifted(out_below, "grp", groups - 1)
    diag = call(
        diagonal, array(vectors, rows), [VMEM, HBM], 2 * vectors * rows * order, 2 * rows * order,
        xb, pltpu.with_memory_space_constraint(leaf_inverse, pltpu.HBM),
        scratch=[pltpu.VMEM(leaf_inverse.shape, BF16), pltpu.SemaphoreType.DMA((2 * leaf_inverse.shape[0],))],
    )
    token = call(arrived, array(8, 128), [VMEM], *[1000 * cost for cost in weight_cost], out_half)
    return call(
        combine, array(vectors, rows), [VMEM] * 4, 2 * vectors * rows, 16 * vectors * rows, out_half, out_below, diag, token,
        scratch=[pltpu.VMEM((vectors, rows), F32), pltpu.SemaphoreType.DMA((4,))], out=HBM,
    )


def solution(mesh):
    in_specs = (
        P(None, ("grp", "bf")),
        P(("grp", "bf"), None, None),
        P(None, None, ("grp", "bf")),
        P(None, None, ("grp", "bf")),
        P(("grp", "bf"), None, None, None, None, None),
        P(),
        P(),
    )
    out_specs = P(None, ("grp", "bf"))
    return jax.shard_map(shards, mesh=mesh, in_specs=in_specs, out_specs=out_specs, check_vma=False)
```

```python
import jax
import jax.numpy as jnp
from jax import lax
from jax.experimental import pallas as pl
from jax.experimental.pallas import tpu as pltpu
from jax.sharding import PartitionSpec as P

F32, BF16 = jnp.float32, jnp.bfloat16
VMEM = pl.BlockSpec(memory_space=pltpu.VMEM)
HBM = pl.BlockSpec(memory_space=pltpu.HBM)
NT = (((1,), (1,)), ((), ()))


def shifted(value, axis, distance):
    size = lax.axis_size(axis)
    return lax.ppermute(value, axis, [(source, (source + distance) % size) for source in range(size)])


def swapped(value):
    return lax.ppermute(value, "bf", [(n, n ^ 1) for n in range(lax.axis_size("bf"))])


def across(value, bit):
    return lax.ppermute(value, "bf", [(n, n ^ 1 << bit) for n in range(lax.axis_size("bf"))])


def call(body, shapes, specs, flops, moved, *operands, scratch=(), out=VMEM):
    return pl.pallas_call(
        body,
        out_shape=shapes,
        in_specs=specs,
        out_specs=jax.tree.map(lambda _: out, shapes),
        scratch_shapes=scratch,
        cost_estimate=pl.CostEstimate(flops=flops, bytes_accessed=moved, transcendentals=0),
        compiler_params=pltpu.CompilerParams(vmem_limit_bytes=16 * 2**20),
    )(*operands)


def block_diagonal(compact, levels):
    k = compact.shape[0]
    lane = lax.broadcasted_iota(jnp.int32, compact.shape, 1)
    parts = []
    for level in range(levels):
        mine = jnp.logical_and(lane >= level * k, lane < (level + 1) * k)
        parts.append(jnp.where(mine, compact, 0.0))
    return jnp.concatenate(parts, axis=0)


def section_weights(compact, levels):
    k = compact.shape[0] // 2
    parts = [block_diagonal(compact[:k], levels), block_diagonal(compact[k:], levels)]
    return jnp.concatenate(parts, axis=0).astype(BF16)


def compact_section(mixing_ref, section, side):
    levels = mixing_ref.shape[0]
    return jnp.concatenate([mixing_ref[level, section, side].astype(F32) for level in range(levels)], axis=1)


def split(source, target, parts, axis):
    count = source.shape[axis] // parts
    places = [(slice(None),) * axis + (pl.ds(n * count, count),) for n in range(parts)]
    return [(source.at[place], target.at[place]) for place in places]


def load(groups, field_hbm, col_hbm, mixing_hbm, perm_hbm, xb_ref, sent_ref, *refs):
    *out_refs, field_ref, col_ref, mixing_ref, perm_ref, sems = refs
    compact = {}
    levels, sections, _, k, _ = mixing_ref.shape
    vectors = field_ref.shape[0]
    pairs = split(col_hbm, col_ref, 4, 0) + split(field_hbm, field_ref, 2, 0)
    pairs += [(mixing_hbm.at[level], mixing_ref.at[level]) for level in range(levels)]
    pairs.append((perm_hbm, perm_ref))
    copies = [pltpu.make_async_copy(*pair, sems.at[n]) for n, pair in enumerate(pairs)]
    for copy in copies:
        copy.start()
    for copy in copies:
        copy.wait()
    xb = field_ref[...].astype(BF16)
    xb_ref[...] = xb
    sent_ref[:vectors, :] = lax.dot_general(xb, col_ref[...], NT, preferred_element_type=F32)
    row = lax.broadcasted_iota(jnp.int32, (k, k), 0)
    picks = jnp.concatenate([(row == perm_ref[level : level + 1, :]).astype(F32) for level in range(levels)], axis=1)
    picks = block_diagonal(picks, levels).astype(BF16)
    for section in range(sections):
        for side in range(2):
            mats = jnp.concatenate([mixing_ref[level, section, side].astype(F32) for level in range(levels)], axis=1)
            if section == 0:
                mats = jnp.dot(picks, block_diagonal(mats, levels).astype(BF16), preferred_element_type=F32)
                mats = sum(mats[level * k : (level + 1) * k] for level in range(levels))
            compact[section, side] = mats
            for n, (group, out_ref) in enumerate(zip(groups, (sent_ref, *out_refs))):
                if section in group:
                    start = (0 if n else vectors) + (2 * group.index(section) + side) * k
                    out_ref[start : start + k, :] = mats
    if len(out_refs) == len(groups):
        left, right = [block_diagonal(compact[which], levels).astype(BF16) for which in ((1, 1), (2, 0))]
        out_refs[-1][...] = compact_product(levels, left, right)


def build_weights(levels, chosen, *refs):
    *compact_refs, weights_ref = refs
    size = 2 * weights_ref.shape[2] // levels
    for n, (operand, start) in enumerate(chosen):
        weights_ref[n] = section_weights(compact_refs[operand][start : start + size, :], levels)


def compact_product(levels, left, right):
    k = left.shape[0] // levels
    product = jnp.dot(left, right, preferred_element_type=F32)
    return sum(product[level * k : (level + 1) * k] for level in range(levels))


def two_terms(value):
    high = value.astype(BF16)
    return high, (value - high.astype(F32)).astype(BF16)


def factor_terms(levels, compact):
    return two_terms(block_diagonal(compact, levels))


def build_terms(levels, compact_ref, *refs):
    *message_refs, terms_ref = refs
    k, width = compact_ref.shape
    parts = [compact_ref[...]] + [ref[-k:, :] for ref in message_refs]
    for row, part in enumerate(parts):
        for n, term in enumerate(factor_terms(levels, part)):
            terms_ref[n, row * width : (row + 1) * width, :] = term


def terms_dot(value, terms):
    count = value.shape[0]
    stacked = jnp.concatenate(two_terms(value), axis=0)
    sums = sum(jnp.dot(stacked, term, preferred_element_type=F32) for term in reversed(terms))
    return sums[:count] + sums[count:]


def exact_dot(value, factor):
    return terms_dot(value, [factor])


def section_product(own, other, weights):
    return exact_dot(jnp.concatenate([own, other], axis=1), weights)


def run_sections(sections, final, first_refs, mine_ref, theirs_ref, out_ref):
    weights = (mine_ref, theirs_ref)
    if sections[0]:
        states_ref, other_ref = first_refs
        states, others = [states_ref[0], states_ref[1]], [other_ref[0], other_ref[1]]
    else:
        states = [ref[: out_ref.shape[1], :] for ref in first_refs]
        others = states[::-1]
    for section in sections:
        count = 1 if section == final else 2
        states = [section_product(states[n], others[n], weights[n][section]) for n in range(count)]
        others = states[::-1]
    if count == 1:
        return states[0]
    out_ref[0], out_ref[1] = states


def step(sections, final, first_ref, second_ref, mine_ref, theirs_ref, out_ref):
    run_sections(sections, final, (first_ref, second_ref), mine_ref, theirs_ref, out_ref)


def first_step(levels, sent_ref, received_ref, mine_ref, theirs_ref, out_ref):
    width = out_ref.shape[1]
    k = width // levels
    count = (out_ref.shape[0] - k) // 3
    mine, theirs = sent_ref[:count, :], received_ref[:count, :]
    mine, theirs = section_product(mine, theirs, mine_ref[0]), section_product(theirs, mine, theirs_ref[0])
    out_ref[:count, :] = mine
    out_ref[count : 2 * count, :] = theirs
    mine, theirs = exact_dot(mine, mine_ref[1, :width, :]), exact_dot(theirs, theirs_ref[1, :width, :])
    out_ref[2 * count : 3 * count, :] = section_product(mine, theirs, mine_ref[2])
    out_ref[3 * count :, :] = compact_product(levels, theirs_ref[1, width:, :], mine_ref[2, width:, :])


def level_rank(state, rank_size, half_shift, owner_ref, half):
    first_is_half = jnp.broadcast_to(owner_ref[0:1, 0:1], state.shape) == half_shift
    lane = lax.broadcasted_iota(jnp.int32, state.shape, 1)
    chosen = jnp.logical_xor(lane >= rank_size, first_is_half)
    return (jnp.where(chosen, state, 0.0) if half else jnp.where(chosen, 0.0, state)).astype(BF16)


def finish(state, rank_size, half_shift, row_ref, owner_ref, state_ref, half_ref):
    state_ref[...] = state
    rank = level_rank(state, rank_size, half_shift, owner_ref, True)
    half_ref[...] = jnp.dot(rank, row_ref[...], preferred_element_type=F32)


def expand_below(rank_size, half_shift, state_ref, row_ref, owner_ref, below_ref):
    rank = level_rank(state_ref[...], rank_size, half_shift, owner_ref, False)
    below_ref[...] = jnp.dot(rank, row_ref[...], preferred_element_type=F32)


def last_step(sections, final, rank_size, half_shift, first_ref, second_ref, mine_ref, theirs_ref, *refs):
    state = run_sections(sections, final, (first_ref, second_ref), mine_ref, theirs_ref, None)
    finish(state, rank_size, half_shift, *refs)


def last_sections(levels, rank_size, half_shift, here_ref, there_ref, mine_ref, terms_ref, far_ref, *refs):
    count = (here_ref.shape[0] - rank_size) // 3
    here = jnp.concatenate([here_ref[:count, :], here_ref[count : 2 * count, :]], axis=1)
    there = jnp.concatenate([there_ref[:count, :], there_ref[count : 2 * count, :]], axis=1)
    mine = here_ref[2 * count : 3 * count, :] + terms_dot(there, [terms_ref[n] for n in range(2)])
    behind = factor_terms(levels, there_ref[3 * count :, :])
    far_terms = [jnp.concatenate([far_ref[n], behind[n]], axis=0) for n in range(2)]
    far = there_ref[2 * count : 3 * count, :] + terms_dot(here, far_terms)
    finish(section_product(mine, far, mine_ref[3]), rank_size, half_shift, *refs)


def diagonal(xb_ref, leaf_hbm, out_ref, leaf_ref, sems):
    blocks, order, _ = leaf_hbm.shape
    copies = []
    for n in range(blocks):
        for source, target in split(leaf_hbm.at[n], leaf_ref.at[n], 2, 0):
            copies.append(pltpu.make_async_copy(source, target, sems.at[len(copies)]))
            copies[-1].start()
    for n in range(blocks):
        copies[2 * n].wait()
        copies[2 * n + 1].wait()
        part = pl.ds(n * order, order)
        out_ref[:, part] = jnp.dot(xb_ref[:, part], leaf_ref[n], preferred_element_type=F32)


def arrived(half_ref, out_ref):
    out_ref[...] = half_ref[: out_ref.shape[0], : out_ref.shape[1]]


def combine(half_ref, below_ref, diag_ref, _, out_hbm, sum_ref, sems):
    parts = sems.shape[0]
    count = sum_ref.shape[1] // parts
    copies = []
    for n in range(parts):
        part = pl.ds(n * count, count)
        sum_ref[:, part] = diag_ref[:, part] + below_ref[:, part] + half_ref[:, part]
        copies.append(pltpu.make_async_copy(sum_ref.at[:, part], out_hbm.at[:, part], sems.at[n]))
        copies[-1].start()
    for copy in copies:
        copy.wait()


def shards(field, leaf_inverse, col_factor, row_factor, mixing, row_owner, rank_perm):
    vectors, rows = field.shape
    order = leaf_inverse.shape[1]
    levels, rank_size, _ = col_factor.shape
    sections = mixing.shape[2]
    bits = lax.axis_size("bf").bit_length() - 1
    groups = lax.axis_size("grp")
    width = levels * rank_size

    def array(*shape, kind=F32):
        return jax.ShapeDtypeStruct(shape, kind)

    in_hbm = [
        pltpu.with_memory_space_constraint(x, pltpu.HBM)
        for x in (field, col_factor.reshape(width, rows), mixing[0], rank_perm)
    ]
    size = 2 * rank_size
    one_round = bits == 2 and sections == 4 and levels == 2
    groups_sent = [(0, 1), (2, 3)] if one_round else [tuple(range(sections - 1)), (sections - 1,)]
    xb, sent, *kept = call(
        lambda *refs: load(groups_sent, *refs),
        [array(vectors, rows, kind=BF16)]
        + [array(len(group) * size + (0 if n else vectors), width) for n, group in enumerate(groups_sent)]
        + [array(rank_size, width)] * one_round,
        [HBM] * 4, 2 * vectors * rows * width, 3 * rows * width, *in_hbm,
        scratch=[
            pltpu.VMEM(field.shape, F32),
            pltpu.VMEM((width, rows), BF16),
            pltpu.VMEM(mixing.shape[1:], BF16),
            pltpu.VMEM(rank_perm.shape, jnp.int32),
            pltpu.SemaphoreType.DMA((1 + levels + 2 + 4,)),
        ],
    )
    weight_cost = (4 * width * width * sections, 8 * width * width * sections)

    def weights(chosen, *compacts):
        return call(
            lambda *refs: build_weights(levels, chosen, *refs), array(len(chosen), 2 * width, width, kind=BF16),
            [VMEM] * len(compacts), *weight_cost, *compacts,
        )

    def terms(*compacts, scale=1):
        return call(
            lambda *refs: build_terms(levels, *refs), array(2, len(compacts) * width, width, kind=BF16),
            [VMEM] * len(compacts), *[scale * cost for cost in weight_cost], *compacts,
        )

    received = swapped(sent)
    step_cost = (24 * vectors * width * width, 8 * width * width)
    final = sections - 1
    if one_round:
        chosen = [(0, vectors), (0, vectors + size), (1, 0), (1, size)]
        mine, factor = weights(chosen, sent, kept[0]), kept[1]
        far_factor = across(factor, 1)
        states = call(
            lambda *refs: first_step(levels, *refs), array(3 * vectors + rank_size, width), [VMEM] * 4, *step_cost,
            sent, received, mine, weights(chosen[:2], received),
        )
        first_states = (states, across(states, 1))
        last_body = lambda *refs: last_sections(levels, *refs)
        last_weights = (mine, terms(factor, states), terms(far_factor, scale=1000))
    else:
        starts = [(0, vectors + n * size) for n in range(final)]
        mine, theirs = weights(starts + [(1, 0)], sent, *kept), weights(starts, received)
        runs = []
        for section in range(sections):
            if section % bits or not section:
                runs.append([section])
            else:
                runs[-1].append(section)
        first_states = (sent, received)
        for run in runs[:-1]:
            states = call(
                lambda *refs, run=run: step(run, final, *refs), array(2, vectors, width), [VMEM] * 4, *step_cost,
                *first_states, mine, theirs,
            )
            first_states = (states, across(states, (run[-1] + 1) % bits))
        last_body = lambda *refs: last_step(runs[-1], final, *refs)
        last_weights = (mine, theirs)
    expand_cost = (2 * vectors * width * rows, 4 * width * rows)
    expand = row_factor.reshape(width, rows)
    state, out_half = call(
        lambda *refs: last_body(rank_size, groups // 2, *refs), [array(vectors, width), array(vectors, rows)],
        [VMEM] * (4 + len(last_weights)), *expand_cost, *first_states, *last_weights, expand, row_owner,
    )
    out_below = call(
        lambda *refs: expand_below(rank_size, groups // 2, *refs), array(vectors, rows),
        [VMEM] * 3, *expand_cost, state, expand, row_owner,
    )
    out_half = shifted(out_half, "grp", groups // 2)
    out_below = shifted(out_below, "grp", groups - 1)
    diag = call(
        diagonal, array(vectors, rows), [VMEM, HBM], 2 * vectors * rows * order, 2 * rows * order,
        xb, pltpu.with_memory_space_constraint(leaf_inverse, pltpu.HBM),
        scratch=[pltpu.VMEM(leaf_inverse.shape, BF16), pltpu.SemaphoreType.DMA((2 * leaf_inverse.shape[0],))],
    )
    token = call(arrived, array(8, 128), [VMEM], *[1000 * cost for cost in weight_cost], out_half)
    return call(
        combine, array(vectors, rows), [VMEM] * 4, 2 * vectors * rows, 16 * vectors * rows, out_half, out_below, diag, token,
        scratch=[pltpu.VMEM((vectors, rows), F32), pltpu.SemaphoreType.DMA((4,))], out=HBM,
    )


def solution(mesh):
    in_specs = (
        P(None, ("grp", "bf")),
        P(("grp", "bf"), None, None),
        P(None, None, ("grp", "bf")),
        P(None, None, ("grp", "bf")),
        P(("grp", "bf"), None, None, None, None, None),
        P(),
        P(),
    )
    out_specs = P(None, ("grp", "bf"))
    return jax.shard_map(shards, mesh=mesh, in_specs=in_specs, out_specs=out_specs, check_vma=False)
```

```python
import jax
import jax.numpy as jnp
from jax import lax
from jax.experimental import pallas as pl
from jax.experimental.pallas import tpu as pltpu
from jax.sharding import PartitionSpec as P

F32, BF16 = jnp.float32, jnp.bfloat16
VMEM = pl.BlockSpec(memory_space=pltpu.VMEM)
HBM = pl.BlockSpec(memory_space=pltpu.HBM)
NT = (((1,), (1,)), ((), ()))


def shifted(value, axis, distance):
    size = lax.axis_size(axis)
    return lax.ppermute(value, axis, [(source, (source + distance) % size) for source in range(size)])


def swapped(value):
    return lax.ppermute(value, "bf", [(n, n ^ 1) for n in range(lax.axis_size("bf"))])


def across(value, bit):
    return lax.ppermute(value, "bf", [(n, n ^ 1 << bit) for n in range(lax.axis_size("bf"))])


def call(body, shapes, specs, flops, moved, *operands, scratch=(), out=VMEM):
    return pl.pallas_call(
        body,
        out_shape=shapes,
        in_specs=specs,
        out_specs=jax.tree.map(lambda _: out, shapes),
        scratch_shapes=scratch,
        cost_estimate=pl.CostEstimate(flops=flops, bytes_accessed=moved, transcendentals=0),
        compiler_params=pltpu.CompilerParams(vmem_limit_bytes=16 * 2**20),
    )(*operands)


def block_diagonal(compact, levels):
    k = compact.shape[0]
    lane = lax.broadcasted_iota(jnp.int32, compact.shape, 1)
    parts = []
    for level in range(levels):
        mine = jnp.logical_and(lane >= level * k, lane < (level + 1) * k)
        parts.append(jnp.where(mine, compact, 0.0))
    return jnp.concatenate(parts, axis=0)


def section_weights(compact, levels):
    k = compact.shape[0] // 2
    parts = [block_diagonal(compact[:k], levels), block_diagonal(compact[k:], levels)]
    return jnp.concatenate(parts, axis=0).astype(BF16)


def compact_section(mixing_ref, section, side):
    levels = mixing_ref.shape[0]
    return jnp.concatenate([mixing_ref[level, section, side].astype(F32) for level in range(levels)], axis=1)


def split(source, target, parts, axis):
    count = source.shape[axis] // parts
    places = [(slice(None),) * axis + (pl.ds(n * count, count),) for n in range(parts)]
    return [(source.at[place], target.at[place]) for place in places]


def load(groups, field_hbm, col_hbm, mixing_hbm, perm_hbm, xb_ref, sent_ref, *refs):
    *out_refs, field_ref, col_ref, mixing_ref, perm_ref, sems = refs
    compact = {}
    levels, sections, _, k, _ = mixing_ref.shape
    vectors = field_ref.shape[0]
    vectors_in, factors_in = split(field_hbm, field_ref, 2, 0), split(col_hbm, col_ref, levels, 0)
    mixing_in = [(mixing_hbm.at[level], mixing_ref.at[level]) for level in range(levels)] + [(perm_hbm, perm_ref)]
    stages = [vectors_in + factors_in[:1], mixing_in, factors_in[1:]]
    copies = []
    for stage in stages:
        copies.append([])
        for pair in stage:
            copies[-1].append(pltpu.make_async_copy(*pair, sems.at[sum(len(done) for done in copies)]))
            copies[-1][-1].start()

    def projected(xb, level):
        return lax.dot_general(xb, col_ref[level * k : (level + 1) * k, :], NT, preferred_element_type=F32)

    for copy in copies[0]:
        copy.wait()
    xb = field_ref[...].astype(BF16)
    xb_ref[...] = xb
    states = [projected(xb, 0)]
    for copy in copies[1]:
        copy.wait()
    row = lax.broadcasted_iota(jnp.int32, (k, k), 0)
    picks = jnp.concatenate([(row == perm_ref[level : level + 1, :]).astype(F32) for level in range(levels)], axis=1)
    picks = block_diagonal(picks, levels).astype(BF16)
    for section in range(sections):
        for side in range(2):
            mats = jnp.concatenate([mixing_ref[level, section, side].astype(F32) for level in range(levels)], axis=1)
            if section == 0:
                mats = jnp.dot(picks, block_diagonal(mats, levels).astype(BF16), preferred_element_type=F32)
                mats = sum(mats[level * k : (level + 1) * k] for level in range(levels))
            compact[section, side] = mats
            for n, (group, out_ref) in enumerate(zip(groups, (sent_ref, *out_refs))):
                if section in group:
                    start = (0 if n else vectors) + (2 * group.index(section) + side) * k
                    out_ref[start : start + k, :] = mats
    if len(out_refs) == len(groups):
        left, right = [block_diagonal(compact[which], levels).astype(BF16) for which in ((1, 1), (2, 0))]
        out_refs[-1][...] = compact_product(levels, left, right)
    for copy in copies[2]:
        copy.wait()
    states += [projected(xb, level) for level in range(1, levels)]
    sent_ref[:vectors, :] = jnp.concatenate(states, axis=1)


def build_weights(levels, chosen, *refs):
    *compact_refs, weights_ref = refs
    size = 2 * weights_ref.shape[2] // levels
    for n, (operand, start) in enumerate(chosen):
        weights_ref[n] = section_weights(compact_refs[operand][start : start + size, :], levels)


def compact_product(levels, left, right):
    k = left.shape[0] // levels
    product = jnp.dot(left, right, preferred_element_type=F32)
    return sum(product[level * k : (level + 1) * k] for level in range(levels))


def two_terms(value):
    high = value.astype(BF16)
    return high, (value - high.astype(F32)).astype(BF16)


def factor_terms(levels, compact):
    return two_terms(block_diagonal(compact, levels))


def build_terms(levels, compact_ref, *refs):
    *message_refs, terms_ref = refs
    k, width = compact_ref.shape
    parts = [compact_ref[...]] + [ref[-k:, :] for ref in message_refs]
    for row, part in enumerate(parts):
        for n, term in enumerate(factor_terms(levels, part)):
            terms_ref[n, row * width : (row + 1) * width, :] = term


def terms_dot(value, terms):
    count = value.shape[0]
    stacked = jnp.concatenate(two_terms(value), axis=0)
    sums = sum(jnp.dot(stacked, term, preferred_element_type=F32) for term in reversed(terms))
    return sums[:count] + sums[count:]


def exact_dot(value, factor):
    return terms_dot(value, [factor])


def section_product(own, other, weights):
    return exact_dot(jnp.concatenate([own, other], axis=1), weights)


def run_sections(sections, final, first_refs, mine_ref, theirs_ref, out_ref):
    weights = (mine_ref, theirs_ref)
    if sections[0]:
        states_ref, other_ref = first_refs
        states, others = [states_ref[0], states_ref[1]], [other_ref[0], other_ref[1]]
    else:
        states = [ref[: out_ref.shape[1], :] for ref in first_refs]
        others = states[::-1]
    for section in sections:
        count = 1 if section == final else 2
        states = [section_product(states[n], others[n], weights[n][section]) for n in range(count)]
        others = states[::-1]
    if count == 1:
        return states[0]
    out_ref[0], out_ref[1] = states


def step(sections, final, first_ref, second_ref, mine_ref, theirs_ref, out_ref):
    run_sections(sections, final, (first_ref, second_ref), mine_ref, theirs_ref, out_ref)


def first_step(levels, sent_ref, received_ref, mine_ref, theirs_ref, out_ref):
    width = out_ref.shape[1]
    k = width // levels
    count = (out_ref.shape[0] - k) // 3
    mine, theirs = sent_ref[:count, :], received_ref[:count, :]
    mine, theirs = section_product(mine, theirs, mine_ref[0]), section_product(theirs, mine, theirs_ref[0])
    out_ref[:count, :] = mine
    out_ref[count : 2 * count, :] = theirs
    mine, theirs = exact_dot(mine, mine_ref[1, :width, :]), exact_dot(theirs, theirs_ref[1, :width, :])
    out_ref[2 * count : 3 * count, :] = section_product(mine, theirs, mine_ref[2])
    out_ref[3 * count :, :] = compact_product(levels, theirs_ref[1, width:, :], mine_ref[2, width:, :])


def level_rank(state, rank_size, half_shift, owner_ref, half):
    first_is_half = jnp.broadcast_to(owner_ref[0:1, 0:1], state.shape) == half_shift
    lane = lax.broadcasted_iota(jnp.int32, state.shape, 1)
    chosen = jnp.logical_xor(lane >= rank_size, first_is_half)
    return (jnp.where(chosen, state, 0.0) if half else jnp.where(chosen, 0.0, state)).astype(BF16)


def finish(state, rank_size, half_shift, row_ref, owner_ref, state_ref, half_ref):
    state_ref[...] = state
    rank = level_rank(state, rank_size, half_shift, owner_ref, True)
    half_ref[...] = jnp.dot(rank, row_ref[...], preferred_element_type=F32)


def expand_below(rank_size, half_shift, state_ref, row_ref, owner_ref, below_ref):
    rank = level_rank(state_ref[...], rank_size, half_shift, owner_ref, False)
    below_ref[...] = jnp.dot(rank, row_ref[...], preferred_element_type=F32)


def last_step(sections, final, rank_size, half_shift, first_ref, second_ref, mine_ref, theirs_ref, *refs):
    state = run_sections(sections, final, (first_ref, second_ref), mine_ref, theirs_ref, None)
    finish(state, rank_size, half_shift, *refs)


def last_sections(levels, rank_size, half_shift, here_ref, there_ref, mine_ref, terms_ref, far_ref, *refs):
    count = (here_ref.shape[0] - rank_size) // 3
    here = jnp.concatenate([here_ref[:count, :], here_ref[count : 2 * count, :]], axis=1)
    there = jnp.concatenate([there_ref[:count, :], there_ref[count : 2 * count, :]], axis=1)
    mine = here_ref[2 * count : 3 * count, :] + terms_dot(there, [terms_ref[n] for n in range(2)])
    behind = factor_terms(levels, there_ref[3 * count :, :])
    far_terms = [jnp.concatenate([far_ref[n], behind[n]], axis=0) for n in range(2)]
    far = there_ref[2 * count : 3 * count, :] + terms_dot(here, far_terms)
    finish(section_product(mine, far, mine_ref[3]), rank_size, half_shift, *refs)


def diagonal(xb_ref, leaf_hbm, out_ref, leaf_ref, sems):
    blocks, order, _ = leaf_hbm.shape
    copies = []
    for n in range(blocks):
        for source, target in split(leaf_hbm.at[n], leaf_ref.at[n], 2, 0):
            copies.append(pltpu.make_async_copy(source, target, sems.at[len(copies)]))
            copies[-1].start()
    for n in range(blocks):
        copies[2 * n].wait()
        copies[2 * n + 1].wait()
        part = pl.ds(n * order, order)
        out_ref[:, part] = jnp.dot(xb_ref[:, part], leaf_ref[n], preferred_element_type=F32)


def arrived(half_ref, out_ref):
    out_ref[...] = half_ref[: out_ref.shape[0], : out_ref.shape[1]]


def combine(half_ref, below_ref, diag_ref, _, out_hbm, sum_ref, sems):
    parts = sems.shape[0]
    count = sum_ref.shape[1] // parts
    copies = []
    for n in range(parts):
        part = pl.ds(n * count, count)
        sum_ref[:, part] = diag_ref[:, part] + below_ref[:, part] + half_ref[:, part]
        copies.append(pltpu.make_async_copy(sum_ref.at[:, part], out_hbm.at[:, part], sems.at[n]))
        copies[-1].start()
    for copy in copies:
        copy.wait()


def shards(field, leaf_inverse, col_factor, row_factor, mixing, row_owner, rank_perm):
    vectors, rows = field.shape
    order = leaf_inverse.shape[1]
    levels, rank_size, _ = col_factor.shape
    sections = mixing.shape[2]
    bits = lax.axis_size("bf").bit_length() - 1
    groups = lax.axis_size("grp")
    width = levels * rank_size

    def array(*shape, kind=F32):
        return jax.ShapeDtypeStruct(shape, kind)

    in_hbm = [
        pltpu.with_memory_space_constraint(x, pltpu.HBM)
        for x in (field, col_factor.reshape(width, rows), mixing[0], rank_perm)
    ]
    size = 2 * rank_size
    one_round = bits == 2 and sections == 4 and levels == 2
    groups_sent = [(0, 1), (2, 3)] if one_round else [tuple(range(sections - 1)), (sections - 1,)]
    xb, sent, *kept = call(
        lambda *refs: load(groups_sent, *refs),
        [array(vectors, rows, kind=BF16)]
        + [array(len(group) * size + (0 if n else vectors), width) for n, group in enumerate(groups_sent)]
        + [array(rank_size, width)] * one_round,
        [HBM] * 4, 2 * vectors * rows * width, 3 * rows * width, *in_hbm,
        scratch=[
            pltpu.VMEM(field.shape, F32),
            pltpu.VMEM((width, rows), BF16),
            pltpu.VMEM(mixing.shape[1:], BF16),
            pltpu.VMEM(rank_perm.shape, jnp.int32),
            pltpu.SemaphoreType.DMA((1 + levels + 2 + 4,)),
        ],
    )
    weight_cost = (4 * width * width * sections, 8 * width * width * sections)

    def weights(chosen, *compacts):
        return call(
            lambda *refs: build_weights(levels, chosen, *refs), array(len(chosen), 2 * width, width, kind=BF16),
            [VMEM] * len(compacts), *weight_cost, *compacts,
        )

    def terms(*compacts, scale=1):
        return call(
            lambda *refs: build_terms(levels, *refs), array(2, len(compacts) * width, width, kind=BF16),
            [VMEM] * len(compacts), *[scale * cost for cost in weight_cost], *compacts,
        )

    received = swapped(sent)
    step_cost = (24 * vectors * width * width, 8 * width * width)
    final = sections - 1
    if one_round:
        chosen = [(0, vectors), (0, vectors + size), (1, 0), (1, size)]
        mine, factor = weights(chosen, sent, kept[0]), kept[1]
        far_factor = across(factor, 1)
        states = call(
            lambda *refs: first_step(levels, *refs), array(3 * vectors + rank_size, width), [VMEM] * 4, *step_cost,
            sent, received, mine, weights(chosen[:2], received),
        )
        first_states = (states, across(states, 1))
        last_body = lambda *refs: last_sections(levels, *refs)
        last_weights = (mine, terms(factor, states), terms(far_factor, scale=1000))
    else:
        starts = [(0, vectors + n * size) for n in range(final)]
        mine, theirs = weights(starts + [(1, 0)], sent, *kept), weights(starts, received)
        runs = []
        for section in range(sections):
            if section % bits or not section:
                runs.append([section])
            else:
                runs[-1].append(section)
        first_states = (sent, received)
        for run in runs[:-1]:
            states = call(
                lambda *refs, run=run: step(run, final, *refs), array(2, vectors, width), [VMEM] * 4, *step_cost,
                *first_states, mine, theirs,
            )
            first_states = (states, across(states, (run[-1] + 1) % bits))
        last_body = lambda *refs: last_step(runs[-1], final, *refs)
        last_weights = (mine, theirs)
    expand_cost = (2 * vectors * width * rows, 4 * width * rows)
    expand = row_factor.reshape(width, rows)
    state, out_half = call(
        lambda *refs: last_body(rank_size, groups // 2, *refs), [array(vectors, width), array(vectors, rows)],
        [VMEM] * (4 + len(last_weights)), *expand_cost, *first_states, *last_weights, expand, row_owner,
    )
    out_below = call(
        lambda *refs: expand_below(rank_size, groups // 2, *refs), array(vectors, rows),
        [VMEM] * 3, *expand_cost, state, expand, row_owner,
    )
    out_half = shifted(out_half, "grp", groups // 2)
    out_below = shifted(out_below, "grp", groups - 1)
    diag = call(
        diagonal, array(vectors, rows), [VMEM, HBM], 2 * vectors * rows * order, 2 * rows * order,
        xb, pltpu.with_memory_space_constraint(leaf_inverse, pltpu.HBM),
        scratch=[pltpu.VMEM(leaf_inverse.shape, BF16), pltpu.SemaphoreType.DMA((2 * leaf_inverse.shape[0],))],
    )
    token = call(arrived, array(8, 128), [VMEM], *[1000 * cost for cost in weight_cost], out_half)
    return call(
        combine, array(vectors, rows), [VMEM] * 4, 2 * vectors * rows, 16 * vectors * rows, out_half, out_below, diag, token,
        scratch=[pltpu.VMEM((vectors, rows), F32), pltpu.SemaphoreType.DMA((4,))], out=HBM,
    )


def solution(mesh):
    in_specs = (
        P(None, ("grp", "bf")),
        P(("grp", "bf"), None, None),
        P(None, None, ("grp", "bf")),
        P(None, None, ("grp", "bf")),
        P(("grp", "bf"), None, None, None, None, None),
        P(),
        P(),
    )
    out_specs = P(None, ("grp", "bf"))
    return jax.shard_map(shards, mesh=mesh, in_specs=in_specs, out_specs=out_specs, check_vma=False)
```

```python
import jax
import jax.numpy as jnp
from jax import lax
from jax.experimental import pallas as pl
from jax.experimental.pallas import tpu as pltpu
from jax.sharding import PartitionSpec as P

F32, BF16 = jnp.float32, jnp.bfloat16
VMEM = pl.BlockSpec(memory_space=pltpu.VMEM)
HBM = pl.BlockSpec(memory_space=pltpu.HBM)
NT = (((1,), (1,)), ((), ()))


def shifted(value, axis, distance):
    size = lax.axis_size(axis)
    return lax.ppermute(value, axis, [(source, (source + distance) % size) for source in range(size)])


def swapped(value):
    return lax.ppermute(value, "bf", [(n, n ^ 1) for n in range(lax.axis_size("bf"))])


def across(value, bit):
    return lax.ppermute(value, "bf", [(n, n ^ 1 << bit) for n in range(lax.axis_size("bf"))])


def call(body, shapes, specs, flops, moved, *operands, scratch=(), out=VMEM):
    return pl.pallas_call(
        body,
        out_shape=shapes,
        in_specs=specs,
        out_specs=jax.tree.map(lambda _: out, shapes),
        scratch_shapes=scratch,
        cost_estimate=pl.CostEstimate(flops=flops, bytes_accessed=moved, transcendentals=0),
        compiler_params=pltpu.CompilerParams(vmem_limit_bytes=16 * 2**20),
    )(*operands)


def block_diagonal(compact, levels):
    k = compact.shape[0]
    lane = lax.broadcasted_iota(jnp.int32, compact.shape, 1)
    parts = []
    for level in range(levels):
        mine = jnp.logical_and(lane >= level * k, lane < (level + 1) * k)
        parts.append(jnp.where(mine, compact, 0.0))
    return jnp.concatenate(parts, axis=0)


def section_weights(compact, levels):
    k = compact.shape[0] // 2
    parts = [block_diagonal(compact[:k], levels), block_diagonal(compact[k:], levels)]
    return jnp.concatenate(parts, axis=0).astype(BF16)


def compact_section(mixing_ref, section, side):
    levels = mixing_ref.shape[0]
    return jnp.concatenate([mixing_ref[level, section, side].astype(F32) for level in range(levels)], axis=1)


def split(source, target, parts, axis):
    count = source.shape[axis] // parts
    places = [(slice(None),) * axis + (pl.ds(n * count, count),) for n in range(parts)]
    return [(source.at[place], target.at[place]) for place in places]


def load(groups, field_hbm, col_hbm, mixing_hbm, perm_hbm, xb_ref, sent_ref, *refs):
    *out_refs, field_ref, col_ref, mixing_ref, perm_ref, sems = refs
    compact = {}
    levels, sections, _, k, _ = mixing_ref.shape
    vectors = field_ref.shape[0]
    pairs = split(col_hbm, col_ref, 4, 0) + split(field_hbm, field_ref, 2, 0)
    pairs += [(mixing_hbm.at[level], mixing_ref.at[level]) for level in range(levels)]
    pairs.append((perm_hbm, perm_ref))
    copies = [pltpu.make_async_copy(*pair, sems.at[n]) for n, pair in enumerate(pairs)]
    for copy in copies:
        copy.start()
    for copy in copies:
        copy.wait()
    xb = field_ref[...].astype(BF16)
    xb_ref[...] = xb
    sent_ref[:vectors, :] = lax.dot_general(xb, col_ref[...], NT, preferred_element_type=F32)
    row = lax.broadcasted_iota(jnp.int32, (k, k), 0)
    picks = jnp.concatenate([(row == perm_ref[level : level + 1, :]).astype(F32) for level in range(levels)], axis=1)
    picks = block_diagonal(picks, levels).astype(BF16)
    for section in range(sections):
        mats = [
            jnp.concatenate([mixing_ref[level, section, side].astype(F32) for level in range(levels)], axis=1)
            for side in range(2)
        ]
        if section == 0:
            both = jnp.concatenate([block_diagonal(one, levels) for one in mats], axis=1).astype(BF16)
            both = jnp.dot(picks, both, preferred_element_type=F32)
            both = sum(both[level * k : (level + 1) * k] for level in range(levels))
            mats = [both[:, : levels * k], both[:, levels * k :]]
        for side in range(2):
            compact[section, side] = mats[side]
            for n, (group, out_ref) in enumerate(zip(groups, (sent_ref, *out_refs))):
                if section in group:
                    start = (0 if n else vectors) + (2 * group.index(section) + side) * k
                    out_ref[start : start + k, :] = mats[side]
    if len(out_refs) == len(groups):
        left, right = [block_diagonal(compact[which], levels).astype(BF16) for which in ((1, 1), (2, 0))]
        out_refs[-1][...] = compact_product(levels, left, right)


def build_weights(levels, chosen, *refs):
    *compact_refs, weights_ref = refs
    size = 2 * weights_ref.shape[2] // levels
    for n, (operand, start) in enumerate(chosen):
        weights_ref[n] = section_weights(compact_refs[operand][start : start + size, :], levels)


def compact_product(levels, left, right):
    k = left.shape[0] // levels
    product = jnp.dot(left, right, preferred_element_type=F32)
    return sum(product[level * k : (level + 1) * k] for level in range(levels))


def two_terms(value):
    high = value.astype(BF16)
    return high, (value - high.astype(F32)).astype(BF16)


def factor_terms(levels, compact):
    return two_terms(block_diagonal(compact, levels))


def build_terms(levels, compact_ref, *refs):
    *message_refs, terms_ref = refs
    k, width = compact_ref.shape
    parts = [compact_ref[...]] + [ref[-k:, :] for ref in message_refs]
    for row, part in enumerate(parts):
        for n, term in enumerate(factor_terms(levels, part)):
            terms_ref[n, row * width : (row + 1) * width, :] = term


def terms_dot(value, terms):
    count = value.shape[0]
    stacked = jnp.concatenate(two_terms(value), axis=0)
    sums = sum(jnp.dot(stacked, term, preferred_element_type=F32) for term in reversed(terms))
    return sums[:count] + sums[count:]


def exact_dot(value, factor):
    return terms_dot(value, [factor])


def section_product(own, other, weights):
    return exact_dot(jnp.concatenate([own, other], axis=1), weights)


def run_sections(sections, final, first_refs, mine_ref, theirs_ref, out_ref):
    weights = (mine_ref, theirs_ref)
    if sections[0]:
        states_ref, other_ref = first_refs
        states, others = [states_ref[0], states_ref[1]], [other_ref[0], other_ref[1]]
    else:
        states = [ref[: out_ref.shape[1], :] for ref in first_refs]
        others = states[::-1]
    for section in sections:
        count = 1 if section == final else 2
        states = [section_product(states[n], others[n], weights[n][section]) for n in range(count)]
        others = states[::-1]
    if count == 1:
        return states[0]
    out_ref[0], out_ref[1] = states


def step(sections, final, first_ref, second_ref, mine_ref, theirs_ref, out_ref):
    run_sections(sections, final, (first_ref, second_ref), mine_ref, theirs_ref, out_ref)


def first_step(levels, sent_ref, received_ref, mine_ref, theirs_ref, out_ref):
    width = out_ref.shape[1]
    k = width // levels
    count = (out_ref.shape[0] - k) // 3
    mine, theirs = sent_ref[:count, :], received_ref[:count, :]
    mine, theirs = section_product(mine, theirs, mine_ref[0]), section_product(theirs, mine, theirs_ref[0])
    out_ref[:count, :] = mine
    out_ref[count : 2 * count, :] = theirs
    mine, theirs = exact_dot(mine, mine_ref[1, :width, :]), exact_dot(theirs, theirs_ref[1, :width, :])
    out_ref[2 * count : 3 * count, :] = section_product(mine, theirs, mine_ref[2])
    out_ref[3 * count :, :] = compact_product(levels, theirs_ref[1, width:, :], mine_ref[2, width:, :])


def level_rank(state, rank_size, half_shift, owner_ref, half):
    first_is_half = jnp.broadcast_to(owner_ref[0:1, 0:1], state.shape) == half_shift
    lane = lax.broadcasted_iota(jnp.int32, state.shape, 1)
    chosen = jnp.logical_xor(lane >= rank_size, first_is_half)
    return (jnp.where(chosen, state, 0.0) if half else jnp.where(chosen, 0.0, state)).astype(BF16)


def finish(state, rank_size, half_shift, row_ref, owner_ref, state_ref, half_ref):
    state_ref[...] = state
    rank = level_rank(state, rank_size, half_shift, owner_ref, True)
    half_ref[...] = jnp.dot(rank, row_ref[...], preferred_element_type=F32)


def expand_below(rank_size, half_shift, state_ref, row_ref, owner_ref, below_ref):
    rank = level_rank(state_ref[...], rank_size, half_shift, owner_ref, False)
    below_ref[...] = jnp.dot(rank, row_ref[...], preferred_element_type=F32)


def last_step(sections, final, rank_size, half_shift, first_ref, second_ref, mine_ref, theirs_ref, *refs):
    state = run_sections(sections, final, (first_ref, second_ref), mine_ref, theirs_ref, None)
    finish(state, rank_size, half_shift, *refs)


def last_sections(levels, rank_size, half_shift, here_ref, there_ref, mine_ref, terms_ref, far_ref, *refs):
    count = (here_ref.shape[0] - rank_size) // 3
    here = jnp.concatenate([here_ref[:count, :], here_ref[count : 2 * count, :]], axis=1)
    there = jnp.concatenate([there_ref[:count, :], there_ref[count : 2 * count, :]], axis=1)
    mine = here_ref[2 * count : 3 * count, :] + terms_dot(there, [terms_ref[n] for n in range(2)])
    behind = factor_terms(levels, there_ref[3 * count :, :])
    far_terms = [jnp.concatenate([far_ref[n], behind[n]], axis=0) for n in range(2)]
    far = there_ref[2 * count : 3 * count, :] + terms_dot(here, far_terms)
    finish(section_product(mine, far, mine_ref[3]), rank_size, half_shift, *refs)


def diagonal(xb_ref, leaf_hbm, out_ref, leaf_ref, sems):
    blocks, order, _ = leaf_hbm.shape
    copies = []
    for n in range(blocks):
        for source, target in split(leaf_hbm.at[n], leaf_ref.at[n], 2, 0):
            copies.append(pltpu.make_async_copy(source, target, sems.at[len(copies)]))
            copies[-1].start()
    for n in range(blocks):
        copies[2 * n].wait()
        copies[2 * n + 1].wait()
        part = pl.ds(n * order, order)
        out_ref[:, part] = jnp.dot(xb_ref[:, part], leaf_ref[n], preferred_element_type=F32)


def arrived(half_ref, out_ref):
    out_ref[...] = half_ref[: out_ref.shape[0], : out_ref.shape[1]]


def combine(half_ref, below_ref, diag_ref, _, out_hbm, sum_ref, sems):
    parts = sems.shape[0]
    count = sum_ref.shape[1] // parts
    copies = []
    for n in range(parts):
        part = pl.ds(n * count, count)
        sum_ref[:, part] = diag_ref[:, part] + below_ref[:, part] + half_ref[:, part]
        copies.append(pltpu.make_async_copy(sum_ref.at[:, part], out_hbm.at[:, part], sems.at[n]))
        copies[-1].start()
    for copy in copies:
        copy.wait()


def shards(field, leaf_inverse, col_factor, row_factor, mixing, row_owner, rank_perm):
    vectors, rows = field.shape
    order = leaf_inverse.shape[1]
    levels, rank_size, _ = col_factor.shape
    sections = mixing.shape[2]
    bits = lax.axis_size("bf").bit_length() - 1
    groups = lax.axis_size("grp")
    width = levels * rank_size

    def array(*shape, kind=F32):
        return jax.ShapeDtypeStruct(shape, kind)

    in_hbm = [
        pltpu.with_memory_space_constraint(x, pltpu.HBM)
        for x in (field, col_factor.reshape(width, rows), mixing[0], rank_perm)
    ]
    size = 2 * rank_size
    one_round = bits == 2 and sections == 4 and levels == 2
    groups_sent = [(0, 1), (2, 3)] if one_round else [tuple(range(sections - 1)), (sections - 1,)]
    xb, sent, *kept = call(
        lambda *refs: load(groups_sent, *refs),
        [array(vectors, rows, kind=BF16)]
        + [array(len(group) * size + (0 if n else vectors), width) for n, group in enumerate(groups_sent)]
        + [array(rank_size, width)] * one_round,
        [HBM] * 4, 2 * vectors * rows * width, 3 * rows * width, *in_hbm,
        scratch=[
            pltpu.VMEM(field.shape, F32),
            pltpu.VMEM((width, rows), BF16),
            pltpu.VMEM(mixing.shape[1:], BF16),
            pltpu.VMEM(rank_perm.shape, jnp.int32),
            pltpu.SemaphoreType.DMA((1 + levels + 2 + 4,)),
        ],
    )
    weight_cost = (4 * width * width * sections, 8 * width * width * sections)

    def weights(chosen, *compacts):
        return call(
            lambda *refs: build_weights(levels, chosen, *refs), array(len(chosen), 2 * width, width, kind=BF16),
            [VMEM] * len(compacts), *weight_cost, *compacts,
        )

    def terms(*compacts, scale=1):
        return call(
            lambda *refs: build_terms(levels, *refs), array(2, len(compacts) * width, width, kind=BF16),
            [VMEM] * len(compacts), *[scale * cost for cost in weight_cost], *compacts,
        )

    received = swapped(sent)
    step_cost = (24 * vectors * width * width, 8 * width * width)
    final = sections - 1
    if one_round:
        chosen = [(0, vectors), (0, vectors + size), (1, 0), (1, size)]
        mine, factor = weights(chosen, sent, kept[0]), kept[1]
        far_factor = across(factor, 1)
        states = call(
            lambda *refs: first_step(levels, *refs), array(3 * vectors + rank_size, width), [VMEM] * 4, *step_cost,
            sent, received, mine, weights(chosen[:2], received),
        )
        first_states = (states, across(states, 1))
        last_body = lambda *refs: last_sections(levels, *refs)
        last_weights = (mine, terms(factor, states), terms(far_factor, scale=1000))
    else:
        starts = [(0, vectors + n * size) for n in range(final)]
        mine, theirs = weights(starts + [(1, 0)], sent, *kept), weights(starts, received)
        runs = []
        for section in range(sections):
            if section % bits or not section:
                runs.append([section])
            else:
                runs[-1].append(section)
        first_states = (sent, received)
        for run in runs[:-1]:
            states = call(
                lambda *refs, run=run: step(run, final, *refs), array(2, vectors, width), [VMEM] * 4, *step_cost,
                *first_states, mine, theirs,
            )
            first_states = (states, across(states, (run[-1] + 1) % bits))
        last_body = lambda *refs: last_step(runs[-1], final, *refs)
        last_weights = (mine, theirs)
    expand_cost = (2 * vectors * width * rows, 4 * width * rows)
    expand = row_factor.reshape(width, rows)
    state, out_half = call(
        lambda *refs: last_body(rank_size, groups // 2, *refs), [array(vectors, width), array(vectors, rows)],
        [VMEM] * (4 + len(last_weights)), *expand_cost, *first_states, *last_weights, expand, row_owner,
    )
    out_below = call(
        lambda *refs: expand_below(rank_size, groups // 2, *refs), array(vectors, rows),
        [VMEM] * 3, *expand_cost, state, expand, row_owner,
    )
    out_half = shifted(out_half, "grp", groups // 2)
    out_below = shifted(out_below, "grp", groups - 1)
    diag = call(
        diagonal, array(vectors, rows), [VMEM, HBM], 2 * vectors * rows * order, 2 * rows * order,
        xb, pltpu.with_memory_space_constraint(leaf_inverse, pltpu.HBM),
        scratch=[pltpu.VMEM(leaf_inverse.shape, BF16), pltpu.SemaphoreType.DMA((2 * leaf_inverse.shape[0],))],
    )
    token = call(arrived, array(8, 128), [VMEM], *[1000 * cost for cost in weight_cost], out_half)
    return call(
        combine, array(vectors, rows), [VMEM] * 4, 2 * vectors * rows, 16 * vectors * rows, out_half, out_below, diag, token,
        scratch=[pltpu.VMEM((vectors, rows), F32), pltpu.SemaphoreType.DMA((4,))], out=HBM,
    )


def solution(mesh):
    in_specs = (
        P(None, ("grp", "bf")),
        P(("grp", "bf"), None, None),
        P(None, None, ("grp", "bf")),
        P(None, None, ("grp", "bf")),
        P(("grp", "bf"), None, None, None, None, None),
        P(),
        P(),
    )
    out_specs = P(None, ("grp", "bf"))
    return jax.shard_map(shards, mesh=mesh, in_specs=in_specs, out_specs=out_specs, check_vma=False)
```

```python
import jax
import jax.numpy as jnp
from jax import lax
from jax.experimental import pallas as pl
from jax.experimental.pallas import tpu as pltpu
from jax.sharding import PartitionSpec as P

F32, BF16 = jnp.float32, jnp.bfloat16
VMEM = pl.BlockSpec(memory_space=pltpu.VMEM)
HBM = pl.BlockSpec(memory_space=pltpu.HBM)
NT = (((1,), (1,)), ((), ()))


def shifted(value, axis, distance):
    size = lax.axis_size(axis)
    return lax.ppermute(value, axis, [(source, (source + distance) % size) for source in range(size)])


def swapped(value):
    return lax.ppermute(value, "bf", [(n, n ^ 1) for n in range(lax.axis_size("bf"))])


def across(value, bit):
    return lax.ppermute(value, "bf", [(n, n ^ 1 << bit) for n in range(lax.axis_size("bf"))])


def call(body, shapes, specs, flops, moved, *operands, scratch=(), out=VMEM):
    return pl.pallas_call(
        body,
        out_shape=shapes,
        in_specs=specs,
        out_specs=jax.tree.map(lambda _: out, shapes),
        scratch_shapes=scratch,
        cost_estimate=pl.CostEstimate(flops=flops, bytes_accessed=moved, transcendentals=0),
        compiler_params=pltpu.CompilerParams(vmem_limit_bytes=16 * 2**20),
    )(*operands)


def block_diagonal(compact, levels):
    k = compact.shape[0]
    lane = lax.broadcasted_iota(jnp.int32, compact.shape, 1)
    parts = []
    for level in range(levels):
        mine = jnp.logical_and(lane >= level * k, lane < (level + 1) * k)
        parts.append(jnp.where(mine, compact, 0.0))
    return jnp.concatenate(parts, axis=0)


def section_weights(compact, levels):
    k = compact.shape[0] // 2
    parts = [block_diagonal(compact[:k], levels), block_diagonal(compact[k:], levels)]
    return jnp.concatenate(parts, axis=0).astype(BF16)


def compact_section(mixing_ref, section, side):
    levels = mixing_ref.shape[0]
    return jnp.concatenate([mixing_ref[level, section, side].astype(F32) for level in range(levels)], axis=1)


def split(source, target, parts, axis):
    count = source.shape[axis] // parts
    places = [(slice(None),) * axis + (pl.ds(n * count, count),) for n in range(parts)]
    return [(source.at[place], target.at[place]) for place in places]


def load(groups, field_hbm, col_hbm, mixing_hbm, perm_hbm, xb_ref, sent_ref, *refs):
    *out_refs, field_ref, col_ref, mixing_ref, perm_ref, sems = refs
    compact = {}
    levels, sections, _, k, _ = mixing_ref.shape
    vectors = field_ref.shape[0]
    pairs = [(col_hbm, col_ref), (field_hbm, field_ref)]
    pairs += [(mixing_hbm.at[level], mixing_ref.at[level]) for level in range(levels)]
    pairs.append((perm_hbm, perm_ref))
    copies = [pltpu.make_async_copy(*pair, sems.at[n]) for n, pair in enumerate(pairs)]
    for copy in copies:
        copy.start()
    for copy in copies:
        copy.wait()
    xb = field_ref[...].astype(BF16)
    xb_ref[...] = xb
    sent_ref[:vectors, :] = lax.dot_general(xb, col_ref[...], NT, preferred_element_type=F32)
    row = lax.broadcasted_iota(jnp.int32, (k, k), 0)
    picks = jnp.concatenate([(row == perm_ref[level : level + 1, :]).astype(F32) for level in range(levels)], axis=1)
    picks = block_diagonal(picks, levels).astype(BF16)
    for section in range(sections):
        for side in range(2):
            mats = jnp.concatenate([mixing_ref[level, section, side].astype(F32) for level in range(levels)], axis=1)
            if section == 0:
                mats = jnp.dot(picks, block_diagonal(mats, levels).astype(BF16), preferred_element_type=F32)
                mats = sum(mats[level * k : (level + 1) * k] for level in range(levels))
            compact[section, side] = mats
            for n, (group, out_ref) in enumerate(zip(groups, (sent_ref, *out_refs))):
                if section in group:
                    start = (0 if n else vectors) + (2 * group.index(section) + side) * k
                    out_ref[start : start + k, :] = mats
    if len(out_refs) == len(groups):
        left, right = [block_diagonal(compact[which], levels).astype(BF16) for which in ((1, 1), (2, 0))]
        out_refs[-1][...] = compact_product(levels, left, right)


def build_weights(levels, chosen, *refs):
    *compact_refs, weights_ref = refs
    size = 2 * weights_ref.shape[2] // levels
    for n, (operand, start) in enumerate(chosen):
        weights_ref[n] = section_weights(compact_refs[operand][start : start + size, :], levels)


def compact_product(levels, left, right):
    k = left.shape[0] // levels
    product = jnp.dot(left, right, preferred_element_type=F32)
    return sum(product[level * k : (level + 1) * k] for level in range(levels))


def two_terms(value):
    high = value.astype(BF16)
    return high, (value - high.astype(F32)).astype(BF16)


def factor_terms(levels, compact):
    return two_terms(block_diagonal(compact, levels))


def build_terms(levels, compact_ref, *refs):
    *message_refs, terms_ref = refs
    k, width = compact_ref.shape
    parts = [compact_ref[...]] + [ref[-k:, :] for ref in message_refs]
    for row, part in enumerate(parts):
        for n, term in enumerate(factor_terms(levels, part)):
            terms_ref[n, row * width : (row + 1) * width, :] = term


def terms_dot(value, terms):
    count = value.shape[0]
    stacked = jnp.concatenate(two_terms(value), axis=0)
    sums = sum(jnp.dot(stacked, term, preferred_element_type=F32) for term in reversed(terms))
    return sums[:count] + sums[count:]


def exact_dot(value, factor):
    return terms_dot(value, [factor])


def section_product(own, other, weights):
    return exact_dot(jnp.concatenate([own, other], axis=1), weights)


def run_sections(sections, final, first_refs, mine_ref, theirs_ref, out_ref):
    weights = (mine_ref, theirs_ref)
    if sections[0]:
        states_ref, other_ref = first_refs
        states, others = [states_ref[0], states_ref[1]], [other_ref[0], other_ref[1]]
    else:
        states = [ref[: out_ref.shape[1], :] for ref in first_refs]
        others = states[::-1]
    for section in sections:
        count = 1 if section == final else 2
        states = [section_product(states[n], others[n], weights[n][section]) for n in range(count)]
        others = states[::-1]
    if count == 1:
        return states[0]
    out_ref[0], out_ref[1] = states


def step(sections, final, first_ref, second_ref, mine_ref, theirs_ref, out_ref):
    run_sections(sections, final, (first_ref, second_ref), mine_ref, theirs_ref, out_ref)


def first_step(levels, sent_ref, received_ref, mine_ref, theirs_ref, out_ref):
    width = out_ref.shape[1]
    k = width // levels
    count = (out_ref.shape[0] - k) // 3
    mine, theirs = sent_ref[:count, :], received_ref[:count, :]
    mine, theirs = section_product(mine, theirs, mine_ref[0]), section_product(theirs, mine, theirs_ref[0])
    out_ref[:count, :] = mine
    out_ref[count : 2 * count, :] = theirs
    mine, theirs = exact_dot(mine, mine_ref[1, :width, :]), exact_dot(theirs, theirs_ref[1, :width, :])
    out_ref[2 * count : 3 * count, :] = section_product(mine, theirs, mine_ref[2])
    out_ref[3 * count :, :] = compact_product(levels, theirs_ref[1, width:, :], mine_ref[2, width:, :])


def level_rank(state, rank_size, half_shift, owner_ref, half):
    first_is_half = jnp.broadcast_to(owner_ref[0:1, 0:1], state.shape) == half_shift
    lane = lax.broadcasted_iota(jnp.int32, state.shape, 1)
    chosen = jnp.logical_xor(lane >= rank_size, first_is_half)
    return (jnp.where(chosen, state, 0.0) if half else jnp.where(chosen, 0.0, state)).astype(BF16)


def finish(state, rank_size, half_shift, row_ref, owner_ref, state_ref, half_ref):
    state_ref[...] = state
    rank = level_rank(state, rank_size, half_shift, owner_ref, True)
    half_ref[...] = jnp.dot(rank, row_ref[...], preferred_element_type=F32)


def expand_below(rank_size, half_shift, state_ref, row_ref, owner_ref, below_ref):
    rank = level_rank(state_ref[...], rank_size, half_shift, owner_ref, False)
    below_ref[...] = jnp.dot(rank, row_ref[...], preferred_element_type=F32)


def last_step(sections, final, rank_size, half_shift, first_ref, second_ref, mine_ref, theirs_ref, *refs):
    state = run_sections(sections, final, (first_ref, second_ref), mine_ref, theirs_ref, None)
    finish(state, rank_size, half_shift, *refs)


def last_sections(levels, rank_size, half_shift, here_ref, there_ref, mine_ref, terms_ref, far_ref, *refs):
    count = (here_ref.shape[0] - rank_size) // 3
    here = jnp.concatenate([here_ref[:count, :], here_ref[count : 2 * count, :]], axis=1)
    there = jnp.concatenate([there_ref[:count, :], there_ref[count : 2 * count, :]], axis=1)
    mine = here_ref[2 * count : 3 * count, :] + terms_dot(there, [terms_ref[n] for n in range(2)])
    behind = factor_terms(levels, there_ref[3 * count :, :])
    far_terms = [jnp.concatenate([far_ref[n], behind[n]], axis=0) for n in range(2)]
    far = there_ref[2 * count : 3 * count, :] + terms_dot(here, far_terms)
    finish(section_product(mine, far, mine_ref[3]), rank_size, half_shift, *refs)


def diagonal(xb_ref, leaf_hbm, out_ref, leaf_ref, sems):
    blocks, order, _ = leaf_hbm.shape
    copies = []
    for n in range(blocks):
        for source, target in split(leaf_hbm.at[n], leaf_ref.at[n], 2, 0):
            copies.append(pltpu.make_async_copy(source, target, sems.at[len(copies)]))
            copies[-1].start()
    for n in range(blocks):
        copies[2 * n].wait()
        copies[2 * n + 1].wait()
        part = pl.ds(n * order, order)
        out_ref[:, part] = jnp.dot(xb_ref[:, part], leaf_ref[n], preferred_element_type=F32)


def arrived(half_ref, out_ref):
    out_ref[...] = half_ref[: out_ref.shape[0], : out_ref.shape[1]]


def combine(half_ref, below_ref, diag_ref, _, out_hbm, sum_ref, sems):
    parts = sems.shape[0]
    count = sum_ref.shape[1] // parts
    copies = []
    for n in range(parts):
        part = pl.ds(n * count, count)
        sum_ref[:, part] = diag_ref[:, part] + below_ref[:, part] + half_ref[:, part]
        copies.append(pltpu.make_async_copy(sum_ref.at[:, part], out_hbm.at[:, part], sems.at[n]))
        copies[-1].start()
    for copy in copies:
        copy.wait()


def shards(field, leaf_inverse, col_factor, row_factor, mixing, row_owner, rank_perm):
    vectors, rows = field.shape
    order = leaf_inverse.shape[1]
    levels, rank_size, _ = col_factor.shape
    sections = mixing.shape[2]
    bits = lax.axis_size("bf").bit_length() - 1
    groups = lax.axis_size("grp")
    width = levels * rank_size

    def array(*shape, kind=F32):
        return jax.ShapeDtypeStruct(shape, kind)

    in_hbm = [
        pltpu.with_memory_space_constraint(x, pltpu.HBM)
        for x in (field, col_factor.reshape(width, rows), mixing[0], rank_perm)
    ]
    size = 2 * rank_size
    one_round = bits == 2 and sections == 4 and levels == 2
    groups_sent = [(0, 1), (2, 3)] if one_round else [tuple(range(sections - 1)), (sections - 1,)]
    xb, sent, *kept = call(
        lambda *refs: load(groups_sent, *refs),
        [array(vectors, rows, kind=BF16)]
        + [array(len(group) * size + (0 if n else vectors), width) for n, group in enumerate(groups_sent)]
        + [array(rank_size, width)] * one_round,
        [HBM] * 4, 2 * vectors * rows * width, 3 * rows * width, *in_hbm,
        scratch=[
            pltpu.VMEM(field.shape, F32),
            pltpu.VMEM((width, rows), BF16),
            pltpu.VMEM(mixing.shape[1:], BF16),
            pltpu.VMEM(rank_perm.shape, jnp.int32),
            pltpu.SemaphoreType.DMA((1 + levels + 2,)),
        ],
    )
    weight_cost = (4 * width * width * sections, 8 * width * width * sections)

    def weights(chosen, *compacts):
        return call(
            lambda *refs: build_weights(levels, chosen, *refs), array(len(chosen), 2 * width, width, kind=BF16),
            [VMEM] * len(compacts), *weight_cost, *compacts,
        )

    def terms(*compacts, scale=1):
        return call(
            lambda *refs: build_terms(levels, *refs), array(2, len(compacts) * width, width, kind=BF16),
            [VMEM] * len(compacts), *[scale * cost for cost in weight_cost], *compacts,
        )

    received = swapped(sent)
    step_cost = (24 * vectors * width * width, 8 * width * width)
    final = sections - 1
    if one_round:
        chosen = [(0, vectors), (0, vectors + size), (1, 0), (1, size)]
        mine, factor = weights(chosen, sent, kept[0]), kept[1]
        far_factor = across(factor, 1)
        states = call(
            lambda *refs: first_step(levels, *refs), array(3 * vectors + rank_size, width), [VMEM] * 4, *step_cost,
            sent, received, mine, weights(chosen[:2], received),
        )
        first_states = (states, across(states, 1))
        last_body = lambda *refs: last_sections(levels, *refs)
        last_weights = (mine, terms(factor, states), terms(far_factor, scale=1000))
    else:
        starts = [(0, vectors + n * size) for n in range(final)]
        mine, theirs = weights(starts + [(1, 0)], sent, *kept), weights(starts, received)
        runs = []
        for section in range(sections):
            if section % bits or not section:
                runs.append([section])
            else:
                runs[-1].append(section)
        first_states = (sent, received)
        for run in runs[:-1]:
            states = call(
                lambda *refs, run=run: step(run, final, *refs), array(2, vectors, width), [VMEM] * 4, *step_cost,
                *first_states, mine, theirs,
            )
            first_states = (states, across(states, (run[-1] + 1) % bits))
        last_body = lambda *refs: last_step(runs[-1], final, *refs)
        last_weights = (mine, theirs)
    expand_cost = (2 * vectors * width * rows, 4 * width * rows)
    expand = row_factor.reshape(width, rows)
    state, out_half = call(
        lambda *refs: last_body(rank_size, groups // 2, *refs), [array(vectors, width), array(vectors, rows)],
        [VMEM] * (4 + len(last_weights)), *expand_cost, *first_states, *last_weights, expand, row_owner,
    )
    out_below = call(
        lambda *refs: expand_below(rank_size, groups // 2, *refs), array(vectors, rows),
        [VMEM] * 3, *expand_cost, state, expand, row_owner,
    )
    out_half = shifted(out_half, "grp", groups // 2)
    out_below = shifted(out_below, "grp", groups - 1)
    diag = call(
        diagonal, array(vectors, rows), [VMEM, HBM], 2 * vectors * rows * order, 2 * rows * order,
        xb, pltpu.with_memory_space_constraint(leaf_inverse, pltpu.HBM),
        scratch=[pltpu.VMEM(leaf_inverse.shape, BF16), pltpu.SemaphoreType.DMA((2 * leaf_inverse.shape[0],))],
    )
    token = call(arrived, array(8, 128), [VMEM], *[1000 * cost for cost in weight_cost], out_half)
    return call(
        combine, array(vectors, rows), [VMEM] * 4, 2 * vectors * rows, 16 * vectors * rows, out_half, out_below, diag, token,
        scratch=[pltpu.VMEM((vectors, rows), F32), pltpu.SemaphoreType.DMA((2,))], out=HBM,
    )


def solution(mesh):
    in_specs = (
        P(None, ("grp", "bf")),
        P(("grp", "bf"), None, None),
        P(None, None, ("grp", "bf")),
        P(None, None, ("grp", "bf")),
        P(("grp", "bf"), None, None, None, None, None),
        P(),
        P(),
    )
    out_specs = P(None, ("grp", "bf"))
    return jax.shard_map(shards, mesh=mesh, in_specs=in_specs, out_specs=out_specs, check_vma=False)
```

```python
import jax
import jax.numpy as jnp
from jax import lax
from jax.experimental import pallas as pl
from jax.experimental.pallas import tpu as pltpu
from jax.sharding import PartitionSpec as P

F32, BF16 = jnp.float32, jnp.bfloat16
VMEM = pl.BlockSpec(memory_space=pltpu.VMEM)
HBM = pl.BlockSpec(memory_space=pltpu.HBM)
NT = (((1,), (1,)), ((), ()))


def shifted(value, axis, distance):
    size = lax.axis_size(axis)
    return lax.ppermute(value, axis, [(source, (source + distance) % size) for source in range(size)])


def swapped(value):
    return lax.ppermute(value, "bf", [(n, n ^ 1) for n in range(lax.axis_size("bf"))])


def across(value, bit):
    return lax.ppermute(value, "bf", [(n, n ^ 1 << bit) for n in range(lax.axis_size("bf"))])


def call(body, shapes, specs, flops, moved, *operands, scratch=(), out=VMEM):
    return pl.pallas_call(
        body,
        out_shape=shapes,
        in_specs=specs,
        out_specs=jax.tree.map(lambda _: out, shapes),
        scratch_shapes=scratch,
        cost_estimate=pl.CostEstimate(flops=flops, bytes_accessed=moved, transcendentals=0),
        compiler_params=pltpu.CompilerParams(vmem_limit_bytes=16 * 2**20),
    )(*operands)


def block_diagonal(compact, levels):
    k = compact.shape[0]
    lane = lax.broadcasted_iota(jnp.int32, compact.shape, 1)
    parts = []
    for level in range(levels):
        mine = jnp.logical_and(lane >= level * k, lane < (level + 1) * k)
        parts.append(jnp.where(mine, compact, 0.0))
    return jnp.concatenate(parts, axis=0)


def section_weights(compact, levels):
    k = compact.shape[0] // 2
    parts = [block_diagonal(compact[:k], levels), block_diagonal(compact[k:], levels)]
    return jnp.concatenate(parts, axis=0).astype(BF16)


def compact_section(mixing_ref, section, side):
    levels = mixing_ref.shape[0]
    return jnp.concatenate([mixing_ref[level, section, side].astype(F32) for level in range(levels)], axis=1)


def split(source, target, parts, axis):
    count = source.shape[axis] // parts
    places = [(slice(None),) * axis + (pl.ds(n * count, count),) for n in range(parts)]
    return [(source.at[place], target.at[place]) for place in places]


def load(groups, field_hbm, col_hbm, mixing_hbm, perm_hbm, xb_ref, sent_ref, *refs):
    *out_refs, field_ref, col_ref, mixing_ref, perm_ref, sems = refs
    compact = {}
    levels, sections, _, k, _ = mixing_ref.shape
    vectors = field_ref.shape[0]
    pairs = [(col_hbm, col_ref), (field_hbm, field_ref)]
    pairs += [(mixing_hbm, mixing_ref), (perm_hbm, perm_ref)]
    copies = [pltpu.make_async_copy(*pair, sems.at[n]) for n, pair in enumerate(pairs)]
    for copy in copies:
        copy.start()
    for copy in copies:
        copy.wait()
    xb = field_ref[...].astype(BF16)
    xb_ref[...] = xb
    sent_ref[:vectors, :] = lax.dot_general(xb, col_ref[...], NT, preferred_element_type=F32)
    row = lax.broadcasted_iota(jnp.int32, (k, k), 0)
    picks = jnp.concatenate([(row == perm_ref[level : level + 1, :]).astype(F32) for level in range(levels)], axis=1)
    picks = block_diagonal(picks, levels).astype(BF16)
    for section in range(sections):
        for side in range(2):
            mats = jnp.concatenate([mixing_ref[level, section, side].astype(F32) for level in range(levels)], axis=1)
            if section == 0:
                mats = jnp.dot(picks, block_diagonal(mats, levels).astype(BF16), preferred_element_type=F32)
                mats = sum(mats[level * k : (level + 1) * k] for level in range(levels))
            compact[section, side] = mats
            for n, (group, out_ref) in enumerate(zip(groups, (sent_ref, *out_refs))):
                if section in group:
                    start = (0 if n else vectors) + (2 * group.index(section) + side) * k
                    out_ref[start : start + k, :] = mats
    if len(out_refs) == len(groups):
        left, right = [block_diagonal(compact[which], levels).astype(BF16) for which in ((1, 1), (2, 0))]
        out_refs[-1][...] = compact_product(levels, left, right)


def build_weights(levels, chosen, *refs):
    *compact_refs, weights_ref = refs
    size = 2 * weights_ref.shape[2] // levels
    for n, (operand, start) in enumerate(chosen):
        weights_ref[n] = section_weights(compact_refs[operand][start : start + size, :], levels)


def compact_product(levels, left, right):
    k = left.shape[0] // levels
    product = jnp.dot(left, right, preferred_element_type=F32)
    return sum(product[level * k : (level + 1) * k] for level in range(levels))


def two_terms(value):
    high = value.astype(BF16)
    return high, (value - high.astype(F32)).astype(BF16)


def factor_terms(levels, compact):
    return two_terms(block_diagonal(compact, levels))


def build_terms(levels, compact_ref, *refs):
    *message_refs, terms_ref = refs
    k, width = compact_ref.shape
    parts = [compact_ref[...]] + [ref[-k:, :] for ref in message_refs]
    for row, part in enumerate(parts):
        for n, term in enumerate(factor_terms(levels, part)):
            terms_ref[n, row * width : (row + 1) * width, :] = term


def terms_dot(value, terms):
    count = value.shape[0]
    stacked = jnp.concatenate(two_terms(value), axis=0)
    sums = sum(jnp.dot(stacked, term, preferred_element_type=F32) for term in reversed(terms))
    return sums[:count] + sums[count:]


def exact_dot(value, factor):
    return terms_dot(value, [factor])


def section_product(own, other, weights):
    return exact_dot(jnp.concatenate([own, other], axis=1), weights)


def run_sections(sections, final, first_refs, mine_ref, theirs_ref, out_ref):
    weights = (mine_ref, theirs_ref)
    if sections[0]:
        states_ref, other_ref = first_refs
        states, others = [states_ref[0], states_ref[1]], [other_ref[0], other_ref[1]]
    else:
        states = [ref[: out_ref.shape[1], :] for ref in first_refs]
        others = states[::-1]
    for section in sections:
        count = 1 if section == final else 2
        states = [section_product(states[n], others[n], weights[n][section]) for n in range(count)]
        others = states[::-1]
    if count == 1:
        return states[0]
    out_ref[0], out_ref[1] = states


def step(sections, final, first_ref, second_ref, mine_ref, theirs_ref, out_ref):
    run_sections(sections, final, (first_ref, second_ref), mine_ref, theirs_ref, out_ref)


def first_step(levels, sent_ref, received_ref, mine_ref, theirs_ref, out_ref):
    width = out_ref.shape[1]
    k = width // levels
    count = (out_ref.shape[0] - k) // 3
    mine, theirs = sent_ref[:count, :], received_ref[:count, :]
    mine, theirs = section_product(mine, theirs, mine_ref[0]), section_product(theirs, mine, theirs_ref[0])
    out_ref[:count, :] = mine
    out_ref[count : 2 * count, :] = theirs
    mine, theirs = exact_dot(mine, mine_ref[1, :width, :]), exact_dot(theirs, theirs_ref[1, :width, :])
    out_ref[2 * count : 3 * count, :] = section_product(mine, theirs, mine_ref[2])
    out_ref[3 * count :, :] = compact_product(levels, theirs_ref[1, width:, :], mine_ref[2, width:, :])


def level_rank(state, rank_size, half_shift, owner_ref, half):
    first_is_half = jnp.broadcast_to(owner_ref[0:1, 0:1], state.shape) == half_shift
    lane = lax.broadcasted_iota(jnp.int32, state.shape, 1)
    chosen = jnp.logical_xor(lane >= rank_size, first_is_half)
    return (jnp.where(chosen, state, 0.0) if half else jnp.where(chosen, 0.0, state)).astype(BF16)


def finish(state, rank_size, half_shift, row_ref, owner_ref, state_ref, half_ref):
    state_ref[...] = state
    rank = level_rank(state, rank_size, half_shift, owner_ref, True)
    half_ref[...] = jnp.dot(rank, row_ref[...], preferred_element_type=F32)


def expand_below(rank_size, half_shift, state_ref, row_ref, owner_ref, below_ref):
    rank = level_rank(state_ref[...], rank_size, half_shift, owner_ref, False)
    below_ref[...] = jnp.dot(rank, row_ref[...], preferred_element_type=F32)


def last_step(sections, final, rank_size, half_shift, first_ref, second_ref, mine_ref, theirs_ref, *refs):
    state = run_sections(sections, final, (first_ref, second_ref), mine_ref, theirs_ref, None)
    finish(state, rank_size, half_shift, *refs)


def last_sections(levels, rank_size, half_shift, here_ref, there_ref, mine_ref, terms_ref, far_ref, *refs):
    count = (here_ref.shape[0] - rank_size) // 3
    here = jnp.concatenate([here_ref[:count, :], here_ref[count : 2 * count, :]], axis=1)
    there = jnp.concatenate([there_ref[:count, :], there_ref[count : 2 * count, :]], axis=1)
    mine = here_ref[2 * count : 3 * count, :] + terms_dot(there, [terms_ref[n] for n in range(2)])
    behind = factor_terms(levels, there_ref[3 * count :, :])
    far_terms = [jnp.concatenate([far_ref[n], behind[n]], axis=0) for n in range(2)]
    far = there_ref[2 * count : 3 * count, :] + terms_dot(here, far_terms)
    finish(section_product(mine, far, mine_ref[3]), rank_size, half_shift, *refs)


def diagonal(xb_ref, leaf_hbm, out_ref, leaf_ref, sems):
    blocks, order, _ = leaf_hbm.shape
    copies = []
    for n in range(blocks):
        for source, target in split(leaf_hbm.at[n], leaf_ref.at[n], 2, 0):
            copies.append(pltpu.make_async_copy(source, target, sems.at[len(copies)]))
            copies[-1].start()
    for n in range(blocks):
        copies[2 * n].wait()
        copies[2 * n + 1].wait()
        part = pl.ds(n * order, order)
        out_ref[:, part] = jnp.dot(xb_ref[:, part], leaf_ref[n], preferred_element_type=F32)


def arrived(half_ref, out_ref):
    out_ref[...] = half_ref[: out_ref.shape[0], : out_ref.shape[1]]


def combine(half_ref, below_ref, diag_ref, _, out_hbm, sum_ref, sems):
    parts = sems.shape[0]
    count = sum_ref.shape[1] // parts
    copies = []
    for n in range(parts):
        part = pl.ds(n * count, count)
        sum_ref[:, part] = diag_ref[:, part] + below_ref[:, part] + half_ref[:, part]
        copies.append(pltpu.make_async_copy(sum_ref.at[:, part], out_hbm.at[:, part], sems.at[n]))
        copies[-1].start()
    for copy in copies:
        copy.wait()


def shards(field, leaf_inverse, col_factor, row_factor, mixing, row_owner, rank_perm):
    vectors, rows = field.shape
    order = leaf_inverse.shape[1]
    levels, rank_size, _ = col_factor.shape
    sections = mixing.shape[2]
    bits = lax.axis_size("bf").bit_length() - 1
    groups = lax.axis_size("grp")
    width = levels * rank_size

    def array(*shape, kind=F32):
        return jax.ShapeDtypeStruct(shape, kind)

    in_hbm = [
        pltpu.with_memory_space_constraint(x, pltpu.HBM)
        for x in (field, col_factor.reshape(width, rows), mixing[0], rank_perm)
    ]
    size = 2 * rank_size
    one_round = bits == 2 and sections == 4 and levels == 2
    groups_sent = [(0, 1), (2, 3)] if one_round else [tuple(range(sections - 1)), (sections - 1,)]
    xb, sent, *kept = call(
        lambda *refs: load(groups_sent, *refs),
        [array(vectors, rows, kind=BF16)]
        + [array(len(group) * size + (0 if n else vectors), width) for n, group in enumerate(groups_sent)]
        + [array(rank_size, width)] * one_round,
        [HBM] * 4, 2 * vectors * rows * width, 3 * rows * width, *in_hbm,
        scratch=[
            pltpu.VMEM(field.shape, F32),
            pltpu.VMEM((width, rows), BF16),
            pltpu.VMEM(mixing.shape[1:], BF16),
            pltpu.VMEM(rank_perm.shape, jnp.int32),
            pltpu.SemaphoreType.DMA((4,)),
        ],
    )
    weight_cost = (4 * width * width * sections, 8 * width * width * sections)

    def weights(chosen, *compacts):
        return call(
            lambda *refs: build_weights(levels, chosen, *refs), array(len(chosen), 2 * width, width, kind=BF16),
            [VMEM] * len(compacts), *weight_cost, *compacts,
        )

    def terms(*compacts, scale=1):
        return call(
            lambda *refs: build_terms(levels, *refs), array(2, len(compacts) * width, width, kind=BF16),
            [VMEM] * len(compacts), *[scale * cost for cost in weight_cost], *compacts,
        )

    received = swapped(sent)
    step_cost = (24 * vectors * width * width, 8 * width * width)
    final = sections - 1
    if one_round:
        chosen = [(0, vectors), (0, vectors + size), (1, 0), (1, size)]
        mine, factor = weights(chosen, sent, kept[0]), kept[1]
        far_factor = across(factor, 1)
        states = call(
            lambda *refs: first_step(levels, *refs), array(3 * vectors + rank_size, width), [VMEM] * 4, *step_cost,
            sent, received, mine, weights(chosen[:2], received),
        )
        first_states = (states, across(states, 1))
        last_body = lambda *refs: last_sections(levels, *refs)
        last_weights = (mine, terms(factor, states), terms(far_factor, scale=1000))
    else:
        starts = [(0, vectors + n * size) for n in range(final)]
        mine, theirs = weights(starts + [(1, 0)], sent, *kept), weights(starts, received)
        runs = []
        for section in range(sections):
            if section % bits or not section:
                runs.append([section])
            else:
                runs[-1].append(section)
        first_states = (sent, received)
        for run in runs[:-1]:
            states = call(
                lambda *refs, run=run: step(run, final, *refs), array(2, vectors, width), [VMEM] * 4, *step_cost,
                *first_states, mine, theirs,
            )
            first_states = (states, across(states, (run[-1] + 1) % bits))
        last_body = lambda *refs: last_step(runs[-1], final, *refs)
        last_weights = (mine, theirs)
    expand_cost = (2 * vectors * width * rows, 4 * width * rows)
    expand = row_factor.reshape(width, rows)
    state, out_half = call(
        lambda *refs: last_body(rank_size, groups // 2, *refs), [array(vectors, width), array(vectors, rows)],
        [VMEM] * (4 + len(last_weights)), *expand_cost, *first_states, *last_weights, expand, row_owner,
    )
    out_below = call(
        lambda *refs: expand_below(rank_size, groups // 2, *refs), array(vectors, rows),
        [VMEM] * 3, *expand_cost, state, expand, row_owner,
    )
    out_half = shifted(out_half, "grp", groups // 2)
    out_below = shifted(out_below, "grp", groups - 1)
    diag = call(
        diagonal, array(vectors, rows), [VMEM, HBM], 2 * vectors * rows * order, 2 * rows * order,
        xb, pltpu.with_memory_space_constraint(leaf_inverse, pltpu.HBM),
        scratch=[pltpu.VMEM(leaf_inverse.shape, BF16), pltpu.SemaphoreType.DMA((2 * leaf_inverse.shape[0],))],
    )
    token = call(arrived, array(8, 128), [VMEM], *[1000 * cost for cost in weight_cost], out_half)
    return call(
        combine, array(vectors, rows), [VMEM] * 4, 2 * vectors * rows, 16 * vectors * rows, out_half, out_below, diag, token,
        scratch=[pltpu.VMEM((vectors, rows), F32), pltpu.SemaphoreType.DMA((2,))], out=HBM,
    )


def solution(mesh):
    in_specs = (
        P(None, ("grp", "bf")),
        P(("grp", "bf"), None, None),
        P(None, None, ("grp", "bf")),
        P(None, None, ("grp", "bf")),
        P(("grp", "bf"), None, None, None, None, None),
        P(),
        P(),
    )
    out_specs = P(None, ("grp", "bf"))
    return jax.shard_map(shards, mesh=mesh, in_specs=in_specs, out_specs=out_specs, check_vma=False)
```
